32 devices in a mesh: gx: 4 (over z), gy: 8 (over y, x, core).
Axes of the slice: x: 2, y: 2, z: 4, core: 2. Of those that a mesh axis runs over, the one named last changes fastest.
Arguments:
- cot_vort: float32 [3, 16, 1536, 1024], P(None, None, 'gy', 'gx'), may hold values from -6 to 6
- cot_vel: float32 [3, 16, 1536, 1024], P(None, None, 'gy', 'gx'), may hold values from -6 to 6
- vorticity: bfloat16 [3, 16, 1536, 1024], P(None, None, 'gy', 'gx'), may hold values from -6 to 6
- velocity: bfloat16 [3, 16, 1536, 1024], P(None, None, 'gy', 'gx'), may hold values from -6 to 6
Outputs:
- grad_vort: float32 [3, 16, 1536, 1024], P(None, None, 'gy', 'gx')
- grad_vel: float32 [3, 16, 1536, 1024], P(None, None, 'gy', 'gx')
The draws below stay inside these ranges and needn't reach their ends.
All inputs are finite; a program needn't handle non-finite values.
Results may differ from the reference program's by a relative error of at most 0.008.
Values may be sent and summed in bfloat16 or wider, within the bound.
No kernel may reach another device: no remote copies, remote signals or barrier semaphores. Data moves between devices by JAX's collectives and lax.ppermute only.
A program may use at most 256 MiB of HBM per device.

```python
import math
import jax
import jax.numpy as jnp
from jax import lax

X = 1024
Y = 1536
Z = 16


def level_of(rng, dims, pieces, least, top_value):
    level = 1.0
    for position, parts in pieces:
        heights = jax.random.uniform(jax.random.fold_in(jax.random.fold_in(rng, 6), position), (parts,), jnp.float32, least / len(pieces), top_value / len(pieces))
        level = level * jnp.repeat(jnp.exp(heights), dims[position] // parts).reshape((-1,) + (1,) * (len(dims) - 1 - position))
    return level


def bell_draw(key, extent, spread, reach, pieces=(), kind=jnp.bfloat16):
    result = spread * jax.random.normal(key, extent, jnp.float32)
    if pieces:
        result = result * level_of(key, extent, pieces, -0.22, 0.18)
    return jnp.clip(result, -reach, reach).astype(kind)


def setup_inputs(seed: int = 0) -> dict:
    seeds = jax.random.split(jax.random.key(seed), 5)
    cot_vort = bell_draw(seeds[0], (3, Z, Y, X), 1.0, 6.0, ((2, 8), (3, 4)), jnp.float32)
    cot_vel = bell_draw(seeds[1], (3, Z, Y, X), 1.0, 6.0, ((2, 8), (3, 4)), jnp.float32)
    vorticity = bell_draw(seeds[2], (3, Z, Y, X), 1.0, 6.0, ((2, 8), (3, 4)))
    velocity = bell_draw(seeds[3], (3, Z, Y, X), 1.0, 6.0, ((2, 8), (3, 4)))
    return {"cot_vort": cot_vort, "cot_vel": cot_vel, "vorticity": vorticity, "velocity": velocity}


step_size = 0.5


def rounded(value):
    return lax.optimization_barrier(value.astype(jnp.bfloat16)).astype(jnp.float32)


def phase_tables(first_index, second, length):
    product = (first_index[:, None] * second[None, :]) % length
    angles = product.astype(jnp.float32) * (2.0 * math.pi / length)
    return jnp.cos(angles), jnp.sin(angles)


def wave_numbers(indices, length):
    signed = jnp.where(indices < length // 2, indices, indices - length)
    retained = jnp.where(indices == length // 2, 0.0, 1.0).astype(jnp.float32)
    return signed.astype(jnp.float32) * (2.0 * math.pi / length), retained


def along_depth(stacked, cosine, sine, sign):
    cos_part = jnp.einsum("zk,czrmx->ckrmx", cosine, stacked, precision=lax.Precision.HIGHEST)
    sin_part = jnp.einsum("zk,czrmx->ckrmx", sine, stacked, precision=lax.Precision.HIGHEST)
    real_part = cos_part[:, :, 0] + sign * sin_part[:, :, 1]
    imag_part = cos_part[:, :, 1] - sign * sin_part[:, :, 0]
    return rounded(jnp.stack([real_part, imag_part], 2))


def along_width(real_part, imag_part, cosine, sine, sign):
    high = lax.Precision.HIGHEST
    out_real = jnp.dot(real_part, cosine, precision=high) + sign * jnp.dot(imag_part, sine, precision=high)
    out_imag = jnp.dot(imag_part, cosine, precision=high) - sign * jnp.dot(real_part, sine, precision=high)
    return out_real, out_imag


def curl_solve(real_part, imag_part, wave_x, wave_y, wave_z, retained):
    square = wave_x * wave_x + wave_y * wave_y + wave_z * wave_z
    weight = jnp.where(square > 0, retained / jnp.where(square > 0, square, 1.0), 0.0)

    def cross(vector):
        return jnp.stack([wave_y * vector[2] - wave_z * vector[1], wave_z * vector[0] - wave_x * vector[2], wave_x * vector[1] - wave_y * vector[0]])

    return -cross(imag_part) * weight, cross(real_part) * weight


def slope_whole(values, axis_number):
    return (jnp.roll(values, -1, axis_number) - jnp.roll(values, 1, axis_number)) * 0.5


def reference(cot_vort, cot_vel, vorticity, velocity):
    half_modes = Y // 2
    packed = rounded(cot_vel)
    row_index = jnp.arange(Y, dtype=jnp.int32)
    mode_index = jnp.arange(half_modes, dtype=jnp.int32)
    cosine_y, sine_y = phase_tables(row_index, mode_index, Y)
    forward_y = rounded(jnp.concatenate([cosine_y, -sine_y], 1))
    yspectrum = rounded(jnp.einsum("czyx,ym->czmx", packed, forward_y, precision=lax.Precision.HIGHEST))
    yspectrum = yspectrum.reshape(3, Z, 2, half_modes, X)
    depth_index = jnp.arange(Z, dtype=jnp.int32)
    cosine_z, sine_z = phase_tables(depth_index, depth_index, Z)
    cosine_z = rounded(cosine_z)
    sine_z = rounded(sine_z)
    zspectrum = along_depth(yspectrum, cosine_z, sine_z, 1.0)
    width_index = jnp.arange(X, dtype=jnp.int32)
    cosine_x, sine_x = phase_tables(width_index, width_index, X)
    cosine_x = rounded(cosine_x)
    sine_x = rounded(sine_x)
    xreal, ximag = along_width(zspectrum[:, :, 0], zspectrum[:, :, 1], cosine_x, sine_x, 1.0)
    wave_x, keep_x = wave_numbers(width_index, X)
    wave_z, keep_z = wave_numbers(depth_index, Z)
    wave_y = mode_index.astype(jnp.float32) * (2.0 * math.pi / Y)
    filtered_real, filtered_imag = curl_solve(xreal, ximag, wave_x[None, None, :], wave_y[None, :, None], wave_z[:, None, None], keep_z[:, None, None] * keep_x[None, None, :])
    back_real, back_imag = along_width(rounded(filtered_real), rounded(filtered_imag), cosine_x, sine_x, -1.0)
    xback = rounded(jnp.stack([back_real, back_imag], 2))
    zback = along_depth(xback, cosine_z, sine_z, -1.0)
    cosine_b, sine_b = phase_tables(mode_index, row_index, Y)
    doubling = jnp.where(mode_index == 0, 1.0, 2.0).astype(jnp.float32)[:, None]
    inverse_y = rounded(jnp.stack([cosine_b * doubling, -sine_b * doubling], 0))
    spatial = jnp.einsum("czrmx,rmy->czyx", zback, inverse_y, precision=lax.Precision.HIGHEST)
    spectral = rounded(spatial * (1.0 / (X * Y * Z)))
    adjoint = cot_vort + spectral
    velocity_full = velocity.astype(jnp.float32)
    vorticity_full = vorticity.astype(jnp.float32)
    axes_order = (3, 2, 1)
    grad_vort = jnp.stack([adjoint[j] + step_size * jnp.sum(adjoint * slope_whole(velocity_full, axes_order[j]), 0) for j in range(3)])
    total = jnp.zeros_like(adjoint)
    for j in range(3):
        total = total + slope_whole(vorticity_full[j:j + 1] * adjoint, axes_order[j])
    grad_vel = -step_size * total
    return grad_vort, grad_vel
```

```python
import math

import jax
import jax.numpy as jnp
import ml_dtypes
import numpy as np
from jax import lax
from jax.experimental import pallas as pl
from jax.experimental.pallas import tpu as pltpu
from jax.sharding import PartitionSpec as P

X = 1024
Y = 1536
Z = 16
HALF_X = X // 2
HALF_Y = Y // 2
KZ = Z // 2

step_size = 0.5

f32 = jnp.float32
bf16 = jnp.bfloat16

FORWARD_ORDER = (0, 1, 2)
BACK_ORDER = (2, 0, 1)


def params(megabytes=40, **extra):
    return pltpu.CompilerParams(vmem_limit_bytes=megabytes * 1024 * 1024, **extra)


def cost(flops, nbytes):
    return pl.CostEstimate(flops=int(flops), bytes_accessed=int(nbytes), transcendentals=0)


def trig(first, second, length):
    angle = (np.outer(first, second) % length) * (2.0 * math.pi / length)
    return np.cos(angle), np.sin(angle)


def y_tables(blocks):
    cosine, sine = trig(np.arange(HALF_Y), np.arange(Y), Y)
    both = np.stack([cosine.reshape(blocks, -1, Y), sine.reshape(blocks, -1, Y)], 1).reshape(Y, Y)
    both = both.astype(ml_dtypes.bfloat16)
    return both, np.ascontiguousarray(both.T)


def x_tables():
    cosine, sine = trig(np.arange(X), np.arange(HALF_X), X)
    both = np.concatenate([cosine, sine], 1).astype(ml_dtypes.bfloat16)
    return both, np.ascontiguousarray(both.T)


def slope_matrix(size):
    return ((np.eye(size, k=-1) - np.eye(size, k=1)) * 0.5).astype(ml_dtypes.bfloat16)


def combine(terms):
    total = None
    for factor, value in terms:
        if abs(factor) < 1e-12:
            continue
        if abs(factor - 1.0) < 1e-12:
            part = value
        elif abs(factor + 1.0) < 1e-12:
            part = -value
        else:
            part = value * factor
        total = part if total is None else total + part
    return total


def depth_forward(values):
    even = [values[0]] + [values[n] + values[Z - n] for n in range(1, 8)] + [values[8]]
    odd = [None] + [values[n] - values[Z - n] for n in range(1, 8)]
    even_sum = [even[n] + even[8 - n] for n in range(4)] + [even[4]]
    even_dif = [even[n] - even[8 - n] for n in range(4)]
    odd_sum = [None] + [odd[n] + odd[8 - n] for n in range(1, 4)] + [odd[4]]
    odd_dif = [None] + [odd[n] - odd[8 - n] for n in range(1, 4)]
    result = []
    for k in range(KZ):
        folded = even_sum if k % 2 == 0 else even_dif
        cos_part = combine([(math.cos(math.pi * k * n / 8), folded[n]) for n in range(len(folded))])
        folded = odd_dif if k % 2 == 0 else odd_sum
        sin_part = combine(
            [(math.sin(math.pi * k * n / 8), folded[n]) for n in range(1, len(folded))]
        )
        result.append((cos_part, sin_part))
    return result


def depth_inverse(cos_parts, sin_parts):
    layers = [None] * Z
    cos_sum, sin_sum = [None] * 9, [None] * 9
    for n in range(5):
        evens = combine([(math.cos(math.pi * k * n / 8), cos_parts[k]) for k in range(0, KZ, 2)])
        odds = combine([(math.cos(math.pi * k * n / 8), cos_parts[k]) for k in range(1, KZ, 2)])
        if n == 4:
            cos_sum[4] = evens
        else:
            cos_sum[n] = evens + odds
            cos_sum[8 - n] = evens - odds
    for n in range(1, 5):
        evens = combine([(math.sin(math.pi * k * n / 8), sin_parts[k]) for k in range(0, KZ, 2)])
        odds = combine([(math.sin(math.pi * k * n / 8), sin_parts[k]) for k in range(1, KZ, 2)])
        if n == 4:
            sin_sum[4] = odds
        else:
            sin_sum[n] = odds + evens
            sin_sum[8 - n] = odds - evens
    layers[0], layers[8] = cos_sum[0], cos_sum[8]
    for n in range(1, 8):
        layers[n] = cos_sum[n] + sin_sum[n]
        layers[Z - n] = cos_sum[n] - sin_sum[n]
    return layers


ROWS = 32


def depth_forward_kernel(values_ref, planes_ref):
    height = values_ref.shape[2]
    rows = min(16, height)
    for start in range(0, height, rows):
        part = pl.ds(start, rows)
        spectrum = depth_forward([values_ref[0, n, part, :] for n in range(Z)])
        for k, (cos_part, sin_part) in enumerate(spectrum):
            planes_ref[2 * k, part, :] = cos_part.astype(bf16)
            if sin_part is None:
                sin_part = jnp.zeros_like(cos_part)
            planes_ref[2 * k + 1, part, :] = sin_part.astype(bf16)


def depth_transform(values, component):
    _, _, height, width = values.shape
    return pl.pallas_call(
        depth_forward_kernel,
        grid=(height // ROWS,),
        in_specs=[pl.BlockSpec((1, Z, ROWS, width), lambda j: (component, 0, j, 0))],
        out_specs=pl.BlockSpec((Z, ROWS, width), lambda j: (0, j, 0)),
        out_shape=jax.ShapeDtypeStruct((Z, height, width), bf16),
        compiler_params=params(),
        cost_estimate=cost(6 * Z * height * width, 6 * Z * height * width),
        name="depth_transform",
    )(values)


def y_forward_kernel(table_ref, columns_ref, modes_ref):
    planes = columns_ref.shape[1]
    width = columns_ref.shape[3]
    for plane in range(planes):
        column = columns_ref[:, plane].reshape(Y, width)
        modes = jnp.dot(table_ref[...], column, preferred_element_type=f32)
        modes_ref[0, :, plane] = modes.astype(bf16).reshape(modes_ref.shape[1:2] + modes_ref.shape[3:])


def y_transform(table, columns, blocks, halves):
    _, planes, _, width = columns.shape
    modes = HALF_Y // (blocks * halves)
    rows = Y // blocks
    return pl.pallas_call(
        y_forward_kernel,
        grid=(blocks,),
        in_specs=[
            pl.BlockSpec((rows, Y), lambda j: (j, 0)),
            pl.BlockSpec(columns.shape, lambda j: (0, 0, 0, 0)),
        ],
        out_specs=pl.BlockSpec((1, halves, planes, 2, modes, width), lambda j: (j, 0, 0, 0, 0, 0)),
        out_shape=jax.ShapeDtypeStruct((blocks, halves, planes, 2, modes, width), bf16),
        compiler_params=params(),
        cost_estimate=cost(2 * planes * Y * Y * width, 2 * Y * Y + 4 * planes * Y * width),
        name="y_transform",
    )(table, columns)


def y_inverse_kernel(table_ref, modes_ref, rows_ref):
    planes = modes_ref.shape[2]
    width = modes_ref.shape[5]
    count, _, height, _ = rows_ref.shape
    for plane in range(planes):
        modes = modes_ref[:, :, plane].reshape(Y, width)
        rows = jnp.dot(table_ref[...], modes, preferred_element_type=f32)
        rows_ref[:, plane] = rows.astype(bf16).reshape(count, height, width)


def y_inverse(table, modes, size_y):
    planes, width = modes.shape[2], modes.shape[5]
    height = Y // size_y
    count = max(1, 384 // height)
    return pl.pallas_call(
        y_inverse_kernel,
        grid=(size_y // count,),
        in_specs=[
            pl.BlockSpec((count * height, Y), lambda j: (j, 0)),
            pl.BlockSpec(modes.shape, lambda j: (0, 0, 0, 0, 0, 0)),
        ],
        out_specs=pl.BlockSpec((count, planes, height, width), lambda j: (j, 0, 0, 0)),
        out_shape=jax.ShapeDtypeStruct((size_y, planes, height, width), bf16),
        compiler_params=params(),
        cost_estimate=cost(2 * planes * Y * Y * width, 2 * Y * Y + 4 * planes * Y * width),
        name="y_inverse",
    )(table, modes)


def x_forward_kernel(table_ref, modes_ref, spectrum_ref):
    blocks, _, _, modes, width = modes_ref.shape
    rows = jnp.concatenate(
        [modes_ref[block, 0].reshape(2 * modes, width) for block in range(blocks)], axis=1
    )
    spectrum = jnp.dot(rows, table_ref[...], preferred_element_type=f32)
    spectrum_ref[0] = spectrum.reshape(2, modes, X)


def x_transform(table, modes):
    blocks, _, _, count, width = modes.shape
    return pl.pallas_call(
        x_forward_kernel,
        grid=(2,),
        in_specs=[
            pl.BlockSpec((X, X), lambda j: (0, 0)),
            pl.BlockSpec((blocks, 1, 2, count, width), lambda j: (0, j, 0, 0, 0)),
        ],
        out_specs=pl.BlockSpec((1, 2, count, X), lambda j: (j, 0, 0, 0)),
        out_shape=jax.ShapeDtypeStruct((2, 2, count, X), f32),
        compiler_params=params(),
        cost_estimate=cost(8 * count * X * X, 2 * X * X + 24 * count * X),
        name="x_transform",
    )(table, modes)


def turned(field, axis, tz, ty, tx, wave):
    index = [tz, ty, tx]
    sign = 1.0 if index[axis] == 0 else -1.0
    index[axis] = 1 - index[axis]
    value = field[index[0], index[1], :, index[2] * HALF_X : (index[2] + 1) * HALF_X]
    return value * (wave * sign)


CURL = {
    0: ((1, 2), (0, 1)),
    1: ((0, 0), (2, 2)),
    2: ((2, 1), (1, 0)),
}


def curl_kernel(axes, where_ref, table_ref, plus_ref, minus_ref, back_ref):
    blocks, _, _, count, width = back_ref.shape
    base = where_ref[0] + pl.program_id(0) * count
    depth = where_ref[1]
    mode_y = lax.broadcasted_iota(jnp.int32, (count, HALF_X), 0) + base
    mode_x = lax.broadcasted_iota(jnp.int32, (count, HALF_X), 1)
    wave_y = mode_y.astype(f32) * (2.0 * math.pi / Y)
    wave_x = mode_x.astype(f32) * (2.0 * math.pi / X)
    wave_z = jnp.full((count, HALF_X), depth, jnp.int32).astype(f32) * (2.0 * math.pi / Z)
    square = wave_x * wave_x + wave_y * wave_y + wave_z * wave_z
    doubling = (
        jnp.where(mode_x == 0, 1.0, 2.0)
        * jnp.where(mode_y == 0, 1.0, 2.0)
        * jnp.where(wave_z == 0.0, 1.0, 2.0)
    )
    weight = jnp.where(square > 0, doubling / jnp.where(square > 0, square, 1.0), 0.0)
    waves = [wave_z * weight, wave_y * weight, wave_x * weight]
    rows = []
    for tz in range(2):
        for ty in range(2):
            parts = []
            for tx in range(2):
                parts.append(
                    (
                        turned(plus_ref, axes[0], tz, ty, tx, waves[axes[0]])
                        - turned(minus_ref, axes[1], tz, ty, tx, waves[axes[1]])
                    ).astype(bf16)
                )
            rows.append(jnp.concatenate(parts, axis=1))
    rows = jnp.concatenate(rows, axis=0)
    back = jnp.dot(rows, table_ref[...], preferred_element_type=f32).astype(bf16)
    for block in range(blocks):
        back_ref[block] = back[:, block * width : (block + 1) * width].reshape(2, 2, count, width)


def curl_inverse(where, table, spectra, component, blocks):
    (plus_axis, plus), (minus_axis, minus) = CURL[component]
    total = spectra[plus].shape[2]
    width = X // blocks
    count = 96 if total % 96 == 0 else total
    spec = pl.BlockSpec((2, 2, count, X), lambda j: (0, 0, j, 0))

    def kernel(*refs):
        curl_kernel((plus_axis, minus_axis), *refs)

    return pl.pallas_call(
        kernel,
        grid=(total // count,),
        in_specs=[
            pl.BlockSpec(memory_space=pltpu.SMEM),
            pl.BlockSpec((X, X), lambda j: (0, 0)),
            spec,
            spec,
        ],
        out_specs=pl.BlockSpec((blocks, 2, 2, count, width), lambda j: (0, 0, 0, j, 0)),
        out_shape=jax.ShapeDtypeStruct((blocks, 2, 2, total, width), bf16),
        compiler_params=params(),
        cost_estimate=cost(8 * total * X * X, 2 * X * X + 40 * total * X),
        name="curl_inverse",
    )(where, table, spectra[plus], spectra[minus])


def side_columns(planes):
    width = planes[0].shape[1]
    row = lax.broadcasted_iota(jnp.int32, (2 * Z, width), 0)
    lane = lax.broadcasted_iota(jnp.int32, (2 * Z, width), 1)
    total = None
    for n in range(Z):
        pick = ((row == n) & (lane == 0)) | ((row == n + Z) & (lane == width - 1))
        part = lax.dot_general(
            pick.astype(f32).astype(bf16),
            planes[n],
            (((1,), (1,)), ((), ())),
            preferred_element_type=f32,
        )
        total = part if total is None else total + part
    return total[:Z].astype(bf16), total[Z:].astype(bf16)


def spread_columns(low, high, n, width):
    row = lax.broadcasted_iota(jnp.int32, (2 * Z, width), 0)
    lane = lax.broadcasted_iota(jnp.int32, (2 * Z, width), 1)
    place = jnp.where((row == n) & (lane == 0), -0.5, 0.0) + jnp.where(
        (row == n + Z) & (lane == width - 1), 0.5, 0.0
    )
    both = jnp.concatenate([low, high], axis=0).astype(bf16)
    return lax.dot_general(
        both, place.astype(bf16), (((0,), (0,)), ((), ())), preferred_element_type=f32
    )


def edges_kernel(field_ref, first_column_ref, last_column_ref):
    first, last = side_columns([field_ref[0, n] for n in range(Z)])
    first_column_ref[0] = first
    last_column_ref[0] = last


def edge_columns(field, components):
    _, _, height, width = field.shape
    shape = jax.ShapeDtypeStruct((components, Z, height), bf16)
    spec = pl.BlockSpec((1, Z, height), lambda i: (i, 0, 0))
    return pl.pallas_call(
        edges_kernel,
        grid=(components,),
        in_specs=[pl.BlockSpec((1, Z, height, width), lambda i: (i, 0, 0, 0))],
        out_specs=[spec, spec],
        out_shape=[shape, shape],
        compiler_params=params(),
        cost_estimate=cost(
            components * 64 * Z * height * width, 2 * components * Z * height * width
        ),
        name="edge_columns",
    )(field)


def exchange(first, last, axis):
    count = lax.axis_size(axis)
    up = [(i, (i + 1) % count) for i in range(count)]
    down = [((i + 1) % count, i) for i in range(count)]
    return lax.ppermute(last, axis, up), lax.ppermute(first, axis, down)


def adjoint_kernel(planes_ref, cotangent_ref, adjoint_ref, first_x, last_x, first_y, last_y):
    height = planes_ref.shape[1]
    scale = 1.0 / (X * Y * Z)
    rows = 16
    for start in range(0, height, rows):
        part = pl.ds(start, rows)
        layers = depth_inverse(
            [planes_ref[2 * k, part, :].astype(f32) for k in range(KZ)],
            [planes_ref[2 * k + 1, part, :].astype(f32) for k in range(KZ)],
        )
        for n in range(Z):
            adjoint_ref[n, part, :] = cotangent_ref[0, n, part, :] + layers[n] * scale
    first, last = side_columns([adjoint_ref[n].astype(bf16) for n in range(Z)])
    first_x[...] = first
    last_x[...] = last
    first_y[...] = jnp.concatenate([adjoint_ref[n, 0:1, :] for n in range(Z)], 0).astype(bf16)
    last_y[...] = jnp.concatenate(
        [adjoint_ref[n, height - 1 : height, :] for n in range(Z)], 0
    ).astype(bf16)


def make_adjoint(planes, cotangent, component):
    _, height, width = planes.shape
    column = jax.ShapeDtypeStruct((Z, height), bf16)
    row = jax.ShapeDtypeStruct((Z, width), bf16)
    column_spec = pl.BlockSpec((Z, height), lambda j: (0, 0))
    row_spec = pl.BlockSpec((Z, width), lambda j: (0, 0))
    return pl.pallas_call(
        adjoint_kernel,
        grid=(1,),
        in_specs=[
            pl.BlockSpec((Z, height, width), lambda j: (0, 0, 0)),
            pl.BlockSpec((1, Z, height, width), lambda j: (component, 0, 0, 0)),
        ],
        out_specs=[
            pl.BlockSpec((Z, height, width), lambda j: (0, 0, 0)),
            column_spec,
            column_spec,
            row_spec,
            row_spec,
        ],
        out_shape=[
            jax.ShapeDtypeStruct((Z, height, width), f32),
            column,
            column,
            row,
            row,
        ],
        compiler_params=params(),
        cost_estimate=cost(70 * Z * height * width, 10 * Z * height * width),
        name="make_adjoint",
    )(planes, cotangent)


def pick_row(rows, n):
    index = lax.broadcasted_iota(jnp.int32, rows.shape, 0)
    return jnp.sum(jnp.where(index == n, rows.astype(f32), 0.0), axis=0, keepdims=True)


def end_rows(low, high, height):
    row = lax.broadcasted_iota(jnp.int32, (height, low.shape[1]), 0)
    return jnp.where(row == 0, low * -0.5, 0.0) + jnp.where(row == height - 1, high * 0.5, 0.0)


def grad_vort_kernel(
    component, slope_x, slope_y, velocity, adjoint, low_x, high_x, low_y, high_y, *refs
):
    before, after = refs if len(refs) == 2 else (None, refs[0])
    height, width = velocity.shape[2], velocity.shape[3]
    n = pl.program_id(0)
    above = lax.rem(n + 1, Z)
    below = lax.rem(n + Z - 1, Z)
    here = velocity[0, n]
    value = adjoint[0]
    half = value * step_size
    along_x = jnp.dot(here, slope_x[...], preferred_element_type=f32)
    along_x = along_x + spread_columns(low_x[0], high_x[0], n, width)
    along_y = jnp.dot(slope_y[...], here, preferred_element_type=f32)
    along_y = along_y + end_rows(
        pick_row(low_y[0], n), pick_row(high_y[0], n), height
    )
    along_z = (velocity[0, above].astype(f32) - velocity[0, below].astype(f32)) * 0.5
    for j, slope in enumerate((along_x, along_y, along_z)):
        term = half * slope
        if j == component:
            term = term + value
        if before is not None:
            term = before[j, 0] + term
        after[j, 0] = term


def add_grad_vort(component, slopes, velocity, adjoint, halos, before):
    _, _, height, width = velocity.shape
    slope_x, slope_y = slopes
    whole = lambda shape: pl.BlockSpec(shape, lambda n: (0,) * len(shape))
    column = pl.BlockSpec((1, Z, height), lambda n: (component, 0, 0))
    row = pl.BlockSpec((1, Z, width), lambda n: (component, 0, 0))
    sums = pl.BlockSpec((3, 1, height, width), lambda n: (0, n, 0, 0))
    operands = [slope_x, slope_y, velocity, adjoint, *halos]
    in_specs = [
        whole((width, width)),
        whole((height, height)),
        pl.BlockSpec((1, Z, height, width), lambda n: (component, 0, 0, 0)),
        pl.BlockSpec((1, height, width), lambda n: (n, 0, 0)),
        column,
        column,
        row,
        row,
    ]
    aliases = {}
    if before is not None:
        aliases = {len(operands): 0}
        operands.append(before)
        in_specs.append(sums)

    def kernel(*refs):
        grad_vort_kernel(component, *refs)

    return pl.pallas_call(
        kernel,
        grid=(Z,),
        in_specs=in_specs,
        out_specs=sums,
        out_shape=jax.ShapeDtypeStruct((3, Z, height, width), f32),
        input_output_aliases=aliases,
        compiler_params=params(),
        cost_estimate=cost(
            2 * Z * height * width * (width + height), Z * height * width * (18 + 12 * len(aliases))
        ),
        name="add_grad_vort",
    )(*operands)


def grad_vel_kernel(
    slope_x,
    vorticity,
    vorticity_above,
    vorticity_below,
    adjoint,
    vort_low_x,
    vort_high_x,
    vort_low_y,
    vort_high_y,
    low_x,
    high_x,
    low_y,
    high_y,
    *refs,
):
    after, padded = refs[-2:]
    _, _, height, width = vorticity.shape
    n = pl.program_id(0)
    above = lax.rem(n + 1, Z)
    below = lax.rem(n + Z - 1, Z)
    value = adjoint[n]

    product = vorticity[0, 0].astype(f32) * value
    coarse = product.astype(bf16)
    fine = (product - coarse.astype(f32)).astype(bf16)
    total = jnp.dot(coarse, slope_x[...], preferred_element_type=f32)
    total = total + jnp.dot(fine, slope_x[...], preferred_element_type=f32)
    low = vort_low_x[...].astype(f32) * low_x[...].astype(f32)
    high = vort_high_x[...].astype(f32) * high_x[...].astype(f32)
    total = total + spread_columns(low, high, n, width)

    padded[8 : 8 + height, :] = vorticity[1, 0].astype(f32) * value
    padded[7:8, :] = pick_row(vort_low_y[...], n) * pick_row(low_y[...], n)
    padded[8 + height : 9 + height, :] = pick_row(vort_high_y[...], n) * pick_row(high_y[...], n)
    total = total + (padded[9 : 9 + height, :] - padded[7 : 7 + height, :]) * 0.5

    total = total + (
        vorticity_above[0, 0].astype(f32) * adjoint[above]
        - vorticity_below[0, 0].astype(f32) * adjoint[below]
    ) * 0.5
    after[0, 0] = total * -step_size


def write_grad_vel(component, slope_x, vorticity, adjoint, vort_halos, halos, before):
    _, _, height, width = vorticity.shape
    whole = lambda shape: pl.BlockSpec(shape, lambda n: (0,) * len(shape))
    column = whole((Z, height))
    row = whole((Z, width))
    operands = [slope_x, vorticity, vorticity, vorticity, adjoint, *vort_halos, *halos]
    in_specs = [
        whole((width, width)),
        pl.BlockSpec((2, 1, height, width), lambda n: (0, n, 0, 0)),
        pl.BlockSpec((1, 1, height, width), lambda n: (2, lax.rem(n + 1, Z), 0, 0)),
        pl.BlockSpec((1, 1, height, width), lambda n: (2, lax.rem(n + Z - 1, Z), 0, 0)),
        whole((Z, height, width)),
        column,
        column,
        row,
        row,
        column,
        column,
        row,
        row,
    ]
    aliases = {}
    if before is not None:
        aliases = {len(operands): 0}
        operands.append(before)
        in_specs.append(pl.BlockSpec(memory_space=pl.ANY))
    return pl.pallas_call(
        grad_vel_kernel,
        grid=(Z,),
        in_specs=in_specs,
        out_specs=pl.BlockSpec((1, 1, height, width), lambda n: (component, n, 0, 0)),
        out_shape=jax.ShapeDtypeStruct((3, Z, height, width), f32),
        input_output_aliases=aliases,
        scratch_shapes=[pltpu.VMEM((height + 16, width), f32)],
        compiler_params=params(),
        cost_estimate=cost(4 * Z * height * width * width, Z * height * width * 16),
        name="write_grad_vel",
    )(*operands)


def pair_exchange(parts, axis, mine):
    count = lax.axis_size(axis)
    kept = lax.dynamic_index_in_dim(parts, mine, 1, keepdims=False)
    sent = lax.dynamic_index_in_dim(parts, 1 - mine, 1, keepdims=False)
    got = lax.ppermute(sent, axis, [(i, i ^ 1) for i in range(count)])
    return jnp.where(mine == 0, jnp.stack([kept, got], 1), jnp.stack([got, kept], 1))


def local(cot_vort, cot_vel, vorticity, velocity):
    size_x = lax.axis_size("gx")
    size_y = lax.axis_size("gy")
    planes = Z // size_y
    halves = size_y // KZ
    _, _, height, width = cot_vel.shape
    modes = HALF_Y // (size_x * halves)
    place_x = lax.axis_index("gx")
    place_y = lax.axis_index("gy")
    half = lax.rem(place_y, halves)
    where = jnp.stack([(place_x * halves + half) * modes, place_y // halves]).astype(jnp.int32)

    y_table, y_back_table = y_tables(size_x * halves)
    x_table, x_back_table = x_tables()
    slope_x = slope_matrix(width)
    slope_y = np.ascontiguousarray(slope_matrix(height).T)

    velocity_first, velocity_last = edge_columns(velocity, 3)
    vorticity_first, vorticity_last = edge_columns(vorticity, 1)
    low_x, high_x = exchange(
        jnp.concatenate([velocity_first, vorticity_first]),
        jnp.concatenate([velocity_last, vorticity_last]),
        "gx",
    )
    low_y, high_y = exchange(
        jnp.concatenate([velocity[:, :, 0], vorticity[1:2, :, 0]]),
        jnp.concatenate([velocity[:, :, height - 1], vorticity[1:2, :, height - 1]]),
        "gy",
    )
    velocity_halos = (low_x, high_x, low_y, high_y)
    vorticity_halos = (low_x[3], high_x[3], low_y[3], high_y[3])

    spectra = {}
    for component in FORWARD_ORDER:
        layers = depth_transform(cot_vel, component)
        columns = lax.all_to_all(
            layers.reshape(size_y, planes, height, width), "gy", 0, 0, tiled=True
        )
        coefficients = y_transform(y_table, columns, size_x, halves)
        if halves == 1:
            coefficients = coefficients.reshape(size_x, 2, 2, modes, width)
        else:
            coefficients = pair_exchange(
                coefficients.reshape(size_x, 2, 2, modes, width), "gy", half
            )
        lines = lax.all_to_all(coefficients, "gx", 0, 0, tiled=True)
        spectra[component] = x_transform(x_table, lines)

    grad_vort = None
    grad_vel = None
    for component in BACK_ORDER:
        filtered = curl_inverse(where, x_back_table, spectra, component, size_x)
        returned = lax.all_to_all(filtered, "gx", 0, 0, tiled=True)
        if halves == 1:
            returned = returned.reshape(size_x, 1, 2, 2, modes, width)
        else:
            returned = pair_exchange(returned, "gy", half)[:, :, None]
        rows = y_inverse(y_back_table, returned, size_y)
        layers = lax.all_to_all(rows, "gy", 0, 0, tiled=True)
        adjoint, first_x, last_x, first_y, last_y = make_adjoint(
            layers.reshape(Z, height, width), cot_vort, component
        )
        halos = exchange(first_x, last_x, "gx") + exchange(first_y, last_y, "gy")
        grad_vort = add_grad_vort(
            component, (slope_x, slope_y), velocity, adjoint, velocity_halos, grad_vort
        )
        grad_vel = write_grad_vel(
            component, slope_x, vorticity, adjoint, vorticity_halos, halos, grad_vel
        )
    return grad_vort, grad_vel


def solution(mesh):
    spec = P(None, None, "gy", "gx")
    return jax.shard_map(
        local,
        mesh=mesh,
        in_specs=(spec, spec, spec, spec),
        out_specs=(spec, spec),
        check_vma=False,
    )
```

```python
import math

import jax
import jax.numpy as jnp
import ml_dtypes
import numpy as np
from jax import lax
from jax.experimental import pallas as pl
from jax.experimental.pallas import tpu as pltpu
from jax.sharding import PartitionSpec as P

X = 1024
Y = 1536
Z = 16
HALF_X = X // 2
HALF_Y = Y // 2
KZ = Z // 2

step_size = 0.5

f32 = jnp.float32
bf16 = jnp.bfloat16

FORWARD_ORDER = (0, 1, 2)
BACK_ORDER = (2, 0, 1)


def params(megabytes=56, **extra):
    return pltpu.CompilerParams(vmem_limit_bytes=megabytes * 1024 * 1024, **extra)


def cost(flops, nbytes):
    return pl.CostEstimate(flops=int(flops), bytes_accessed=int(nbytes), transcendentals=0)


def trig(first, second, length):
    angle = (np.outer(first, second) % length) * (2.0 * math.pi / length)
    return np.cos(angle), np.sin(angle)


def y_tables(blocks):
    cosine, sine = trig(np.arange(HALF_Y), np.arange(Y), Y)
    both = np.stack([cosine.reshape(blocks, -1, Y), sine.reshape(blocks, -1, Y)], 1).reshape(Y, Y)
    both = both.astype(ml_dtypes.bfloat16)
    return both, np.ascontiguousarray(both.T)


def x_tables():
    cosine, sine = trig(np.arange(X), np.arange(HALF_X), X)
    both = np.concatenate([cosine, sine], 1).astype(ml_dtypes.bfloat16)
    return both, np.ascontiguousarray(both.T)


def slope_matrix(size):
    return ((np.eye(size, k=-1) - np.eye(size, k=1)) * 0.5).astype(ml_dtypes.bfloat16)


def combine(terms):
    total = None
    for factor, value in terms:
        if abs(factor) < 1e-12:
            continue
        if abs(factor - 1.0) < 1e-12:
            part = value
        elif abs(factor + 1.0) < 1e-12:
            part = -value
        else:
            part = value * factor
        total = part if total is None else total + part
    return total


def depth_forward(values):
    even = [values[0]] + [values[n] + values[Z - n] for n in range(1, 8)] + [values[8]]
    odd = [None] + [values[n] - values[Z - n] for n in range(1, 8)]
    even_sum = [even[n] + even[8 - n] for n in range(4)] + [even[4]]
    even_dif = [even[n] - even[8 - n] for n in range(4)]
    odd_sum = [None] + [odd[n] + odd[8 - n] for n in range(1, 4)] + [odd[4]]
    odd_dif = [None] + [odd[n] - odd[8 - n] for n in range(1, 4)]
    result = []
    for k in range(KZ):
        folded = even_sum if k % 2 == 0 else even_dif
        cos_part = combine([(math.cos(math.pi * k * n / 8), folded[n]) for n in range(len(folded))])
        folded = odd_dif if k % 2 == 0 else odd_sum
        sin_part = combine(
            [(math.sin(math.pi * k * n / 8), folded[n]) for n in range(1, len(folded))]
        )
        result.append((cos_part, sin_part))
    return result


def depth_inverse(cos_parts, sin_parts):
    layers = [None] * Z
    cos_sum, sin_sum = [None] * 9, [None] * 9
    for n in range(5):
        evens = combine([(math.cos(math.pi * k * n / 8), cos_parts[k]) for k in range(0, KZ, 2)])
        odds = combine([(math.cos(math.pi * k * n / 8), cos_parts[k]) for k in range(1, KZ, 2)])
        if n == 4:
            cos_sum[4] = evens
        else:
            cos_sum[n] = evens + odds
            cos_sum[8 - n] = evens - odds
    for n in range(1, 5):
        evens = combine([(math.sin(math.pi * k * n / 8), sin_parts[k]) for k in range(0, KZ, 2)])
        odds = combine([(math.sin(math.pi * k * n / 8), sin_parts[k]) for k in range(1, KZ, 2)])
        if n == 4:
            sin_sum[4] = odds
        else:
            sin_sum[n] = odds + evens
            sin_sum[8 - n] = odds - evens
    layers[0], layers[8] = cos_sum[0], cos_sum[8]
    for n in range(1, 8):
        layers[n] = cos_sum[n] + sin_sum[n]
        layers[Z - n] = cos_sum[n] - sin_sum[n]
    return layers


ROWS = 32


def depth_forward_kernel(values_ref, planes_ref):
    height = values_ref.shape[2]
    rows = min(16, height)
    for start in range(0, height, rows):
        part = pl.ds(start, rows)
        spectrum = depth_forward([values_ref[0, n, part, :] for n in range(Z)])
        for k, (cos_part, sin_part) in enumerate(spectrum):
            planes_ref[2 * k, part, :] = cos_part.astype(bf16)
            if sin_part is None:
                sin_part = jnp.zeros_like(cos_part)
            planes_ref[2 * k + 1, part, :] = sin_part.astype(bf16)


def depth_transform(values, component):
    _, _, height, width = values.shape
    return pl.pallas_call(
        depth_forward_kernel,
        grid=(height // ROWS,),
        in_specs=[pl.BlockSpec((1, Z, ROWS, width), lambda j: (component, 0, j, 0))],
        out_specs=pl.BlockSpec((Z, ROWS, width), lambda j: (0, j, 0)),
        out_shape=jax.ShapeDtypeStruct((Z, height, width), bf16),
        compiler_params=params(),
        cost_estimate=cost(6 * Z * height * width, 6 * Z * height * width),
        name="depth_transform",
    )(values)


def y_transform(me, table, columns, blocks, halves):
    _, planes, _, width = columns.shape
    modes = HALF_Y // (blocks * halves)
    rows = Y // blocks
    shape = (halves, planes, 2, modes, width)

    def kernel(me_ref, table_ref, columns_ref, *outs):
        shift = pl.program_id(0)
        for plane in range(planes):
            column = columns_ref[:, plane].reshape(Y, width)
            part = jnp.dot(table_ref[...], column, preferred_element_type=f32).astype(bf16)
            part = part.reshape(halves, 2, modes, width)
            for s, out in enumerate(outs):

                @pl.when(shift == s)
                def _(out=out, part=part, plane=plane):
                    out[:, plane] = part

    return pl.pallas_call(
        kernel,
        grid_spec=pltpu.PrefetchScalarGridSpec(
            num_scalar_prefetch=1,
            grid=(blocks,),
            in_specs=[
                pl.BlockSpec((rows, Y), lambda j, me: (lax.rem(me[0] + j, blocks), 0)),
                pl.BlockSpec(columns.shape, lambda j, me: (0, 0, 0, 0)),
            ],
            out_specs=[pl.BlockSpec(shape, lambda j, me: (0, 0, 0, 0, 0))] * blocks,
        ),
        out_shape=[jax.ShapeDtypeStruct(shape, bf16)] * blocks,
        compiler_params=params(),
        cost_estimate=cost(2 * planes * Y * Y * width, 2 * Y * Y + 4 * planes * Y * width),
        name="y_transform",
    )(me, table, columns)


def y_inverse(me, table, modes, size_y):
    blocks = len(modes)
    halves, planes, _, _, width = modes[0].shape
    height = Y // size_y
    count = max(1, 384 // height)
    rows = Y // blocks

    def kernel(me_ref, table_ref, *refs):
        parts, rows_ref, held = refs[:blocks], refs[blocks], refs[blocks + 1]

        @pl.when(pl.program_id(0) == 0)
        def _():
            for s, part in enumerate(parts):
                source = lax.rem(me_ref[0] + blocks - s, blocks)
                place = pl.ds(pl.multiple_of(source * rows, rows), rows)
                for plane in range(planes):
                    held[plane, place, :] = part[:, plane].reshape(rows, width)

        for plane in range(planes):
            out = jnp.dot(table_ref[...], held[plane], preferred_element_type=f32)
            rows_ref[:, plane] = out.astype(bf16).reshape(count, height, width)

    return pl.pallas_call(
        kernel,
        grid=(size_y // count,),
        in_specs=[
            pl.BlockSpec(memory_space=pltpu.SMEM),
            pl.BlockSpec((count * height, Y), lambda j: (j, 0)),
        ]
        + [pl.BlockSpec(modes[0].shape, lambda j: (0, 0, 0, 0, 0))] * blocks,
        out_specs=pl.BlockSpec((count, planes, height, width), lambda j: (j, 0, 0, 0)),
        out_shape=jax.ShapeDtypeStruct((size_y, planes, height, width), bf16),
        scratch_shapes=[pltpu.VMEM((planes, Y, width), bf16)],
        compiler_params=params(),
        cost_estimate=cost(2 * planes * Y * Y * width, 2 * Y * Y + 4 * planes * Y * width),
        name="y_inverse",
    )(me, table, *modes)


def x_transform(me, table, modes, after):
    blocks = len(modes)
    _, _, count, width = modes[0].shape

    def kernel(me_ref, table_ref, *refs):
        parts, spectrum_ref, held = refs[:blocks], refs[-2], refs[-1]
        for s, part in enumerate(parts):
            source = lax.rem(me_ref[0] + blocks - s, blocks)
            place = pl.ds(pl.multiple_of(source * width, width), width)
            held[:, place] = part[0].reshape(2 * count, width)
        spectrum = jnp.dot(held[...], table_ref[...], preferred_element_type=f32)
        spectrum_ref[0] = spectrum.reshape(2, count, X)

    return pl.pallas_call(
        kernel,
        grid=(2,),
        in_specs=[
            pl.BlockSpec(memory_space=pltpu.SMEM),
            pl.BlockSpec((X, X), lambda j: (0, 0)),
        ]
        + [pl.BlockSpec((1, 2, count, width), lambda j: (j, 0, 0, 0))] * blocks
        + [pl.BlockSpec(memory_space=pl.ANY)] * len(after),
        out_specs=pl.BlockSpec((1, 2, count, X), lambda j: (j, 0, 0, 0)),
        out_shape=jax.ShapeDtypeStruct((2, 2, count, X), f32),
        scratch_shapes=[pltpu.VMEM((2 * count, X), bf16)],
        compiler_params=params(),
        cost_estimate=cost(8 * count * X * X, 2 * X * X + 24 * count * X),
        name="x_transform",
    )(me, table, *modes, *after)


def turned(field, axis, tz, ty, tx, wave):
    index = [tz, ty, tx]
    sign = 1.0 if index[axis] == 0 else -1.0
    index[axis] = 1 - index[axis]
    value = field[index[0], index[1], :, index[2] * HALF_X : (index[2] + 1) * HALF_X]
    return value * (wave * sign)


CURL = {
    0: ((1, 2), (0, 1)),
    1: ((0, 0), (2, 2)),
    2: ((2, 1), (1, 0)),
}


def curl_kernel(axes, where_ref, table_ref, plus_ref, minus_ref, *outs):
    blocks = len(outs)
    _, _, count, width = outs[0].shape
    base = where_ref[0] + pl.program_id(0) * count
    depth = where_ref[1]
    mode_y = lax.broadcasted_iota(jnp.int32, (count, HALF_X), 0) + base
    mode_x = lax.broadcasted_iota(jnp.int32, (count, HALF_X), 1)
    wave_y = mode_y.astype(f32) * (2.0 * math.pi / Y)
    wave_x = mode_x.astype(f32) * (2.0 * math.pi / X)
    wave_z = jnp.full((count, HALF_X), depth, jnp.int32).astype(f32) * (2.0 * math.pi / Z)
    square = wave_x * wave_x + wave_y * wave_y + wave_z * wave_z
    doubling = (
        jnp.where(mode_x == 0, 1.0, 2.0)
        * jnp.where(mode_y == 0, 1.0, 2.0)
        * jnp.where(wave_z == 0.0, 1.0, 2.0)
    )
    weight = jnp.where(square > 0, doubling / jnp.where(square > 0, square, 1.0), 0.0)
    waves = [wave_z * weight, wave_y * weight, wave_x * weight]
    rows = []
    for tz in range(2):
        for ty in range(2):
            parts = []
            for tx in range(2):
                parts.append(
                    (
                        turned(plus_ref, axes[0], tz, ty, tx, waves[axes[0]])
                        - turned(minus_ref, axes[1], tz, ty, tx, waves[axes[1]])
                    ).astype(bf16)
                )
            rows.append(jnp.concatenate(parts, axis=1))
    rows = jnp.concatenate(rows, axis=0)
    for s, out in enumerate(outs):
        target = lax.rem(where_ref[2] + s, blocks)
        place = pl.ds(pl.multiple_of(target * width, width), width)
        back = jnp.dot(rows, table_ref[:, place], preferred_element_type=f32)
        out[...] = back.astype(bf16).reshape(2, 2, count, width)


def curl_inverse(where, table, spectra, component, blocks):
    (plus_axis, plus), (minus_axis, minus) = CURL[component]
    total = spectra[plus].shape[2]
    width = X // blocks
    count = 96 if total % 96 == 0 else total
    spec = pl.BlockSpec((2, 2, count, X), lambda j: (0, 0, j, 0))

    def kernel(*refs):
        curl_kernel((plus_axis, minus_axis), *refs)

    return pl.pallas_call(
        kernel,
        grid=(total // count,),
        in_specs=[
            pl.BlockSpec(memory_space=pltpu.SMEM),
            pl.BlockSpec((X, X), lambda j: (0, 0)),
            spec,
            spec,
        ],
        out_specs=[pl.BlockSpec((2, 2, count, width), lambda j: (0, 0, j, 0))] * blocks,
        out_shape=[jax.ShapeDtypeStruct((2, 2, total, width), bf16)] * blocks,
        compiler_params=params(),
        cost_estimate=cost(8 * total * X * X, 2 * X * X + 40 * total * X),
        name="curl_inverse",
    )(where, table, spectra[plus], spectra[minus])


def side_columns(planes):
    width = planes[0].shape[1]
    row = lax.broadcasted_iota(jnp.int32, (2 * Z, width), 0)
    lane = lax.broadcasted_iota(jnp.int32, (2 * Z, width), 1)
    total = None
    for n in range(Z):
        pick = ((row == n) & (lane == 0)) | ((row == n + Z) & (lane == width - 1))
        part = lax.dot_general(
            pick.astype(f32).astype(bf16),
            planes[n],
            (((1,), (1,)), ((), ())),
            preferred_element_type=f32,
        )
        total = part if total is None else total + part
    return total[:Z].astype(bf16), total[Z:].astype(bf16)


def spread_columns(low, high, first, layers, width):
    row = lax.broadcasted_iota(jnp.int32, (2 * Z, layers * width), 0)
    column = lax.broadcasted_iota(jnp.int32, (2 * Z, layers * width), 1)
    place = jnp.zeros((2 * Z, layers * width), f32)
    for n in range(layers):
        place = place + jnp.where((row == first + n) & (column == n * width), -0.5, 0.0)
        place = place + jnp.where(
            (row == first + n + Z) & (column == (n + 1) * width - 1), 0.5, 0.0
        )
    both = jnp.concatenate([low, high], axis=0).astype(bf16)
    spread = lax.dot_general(
        both, place.astype(bf16), (((0,), (0,)), ((), ())), preferred_element_type=f32
    )
    return [spread[:, n * width : (n + 1) * width] for n in range(layers)]


def edges_kernel(field_ref, first_column_ref, last_column_ref):
    first, last = side_columns([field_ref[0, n] for n in range(Z)])
    first_column_ref[0] = first
    last_column_ref[0] = last


def edge_columns(field, components):
    _, _, height, width = field.shape
    shape = jax.ShapeDtypeStruct((components, Z, height), bf16)
    spec = pl.BlockSpec((1, Z, height), lambda i: (i, 0, 0))
    return pl.pallas_call(
        edges_kernel,
        grid=(components,),
        in_specs=[pl.BlockSpec((1, Z, height, width), lambda i: (i, 0, 0, 0))],
        out_specs=[spec, spec],
        out_shape=[shape, shape],
        compiler_params=params(),
        cost_estimate=cost(
            components * 64 * Z * height * width, 2 * components * Z * height * width
        ),
        name="edge_columns",
    )(field)


def exchange(first, last, axis):
    count = lax.axis_size(axis)
    up = [(i, (i + 1) % count) for i in range(count)]
    down = [((i + 1) % count, i) for i in range(count)]
    return lax.ppermute(last, axis, up), lax.ppermute(first, axis, down)


def adjoint_kernel(planes_ref, cotangent_ref, *refs):
    adjoint_ref, first_x, last_x, first_y, last_y = refs[-5:]
    height = planes_ref.shape[1]
    scale = 1.0 / (X * Y * Z)
    rows = 16
    for start in range(0, height, rows):
        part = pl.ds(start, rows)
        layers = depth_inverse(
            [planes_ref[2 * k, part, :].astype(f32) for k in range(KZ)],
            [planes_ref[2 * k + 1, part, :].astype(f32) for k in range(KZ)],
        )
        for n in range(Z):
            adjoint_ref[n, part, :] = cotangent_ref[0, n, part, :] + layers[n] * scale
    first, last = side_columns([adjoint_ref[n].astype(bf16) for n in range(Z)])
    first_x[...] = first
    last_x[...] = last
    first_y[...] = jnp.concatenate([adjoint_ref[n, 0:1, :] for n in range(Z)], 0).astype(bf16)
    last_y[...] = jnp.concatenate(
        [adjoint_ref[n, height - 1 : height, :] for n in range(Z)], 0
    ).astype(bf16)


def make_adjoint(planes, cotangent, component, after):
    _, height, width = planes.shape
    column = jax.ShapeDtypeStruct((Z, height), bf16)
    row = jax.ShapeDtypeStruct((Z, width), bf16)
    column_spec = pl.BlockSpec((Z, height), lambda j: (0, 0))
    row_spec = pl.BlockSpec((Z, width), lambda j: (0, 0))
    return pl.pallas_call(
        adjoint_kernel,
        grid=(1,),
        in_specs=[
            pl.BlockSpec((Z, height, width), lambda j: (0, 0, 0)),
            pl.BlockSpec((1, Z, height, width), lambda j: (component, 0, 0, 0)),
        ]
        + [pl.BlockSpec(memory_space=pl.ANY)] * len(after),
        out_specs=[
            pl.BlockSpec((Z, height, width), lambda j: (0, 0, 0)),
            column_spec,
            column_spec,
            row_spec,
            row_spec,
        ],
        out_shape=[
            jax.ShapeDtypeStruct((Z, height, width), f32),
            column,
            column,
            row,
            row,
        ],
        compiler_params=params(),
        cost_estimate=cost(70 * Z * height * width, 10 * Z * height * width),
        name="make_adjoint",
    )(planes, cotangent, *after)


def pick_row(rows, n):
    index = lax.broadcasted_iota(jnp.int32, rows.shape, 0)
    return jnp.sum(jnp.where(index == n, rows.astype(f32), 0.0), axis=0, keepdims=True)


def end_rows(low, high, height):
    row = lax.broadcasted_iota(jnp.int32, (height, low.shape[1]), 0)
    return jnp.where(row == 0, low * -0.5, 0.0) + jnp.where(row == height - 1, high * 0.5, 0.0)


LAYERS = 4


def grad_vort_kernel(
    component, slope_x, slope_y, velocity, adjoint, low_x, high_x, low_y, high_y, *refs
):
    before, after = refs if len(refs) == 2 else (None, refs[0])
    height, width = velocity.shape[2], velocity.shape[3]
    first = pl.program_id(0) * LAYERS
    ends = spread_columns(low_x[0], high_x[0], first, LAYERS, width)
    layers = velocity[0, pl.ds(first, LAYERS)]
    stacked = layers.reshape(LAYERS * height, width)
    inner = jnp.dot(stacked, slope_x[...], preferred_element_type=f32)
    for k in range(LAYERS):
        n = first + k
        above = lax.rem(n + 1, Z)
        below = lax.rem(n + Z - 1, Z)
        value = adjoint[k]
        half = value * step_size
        along_x = inner[k * height : (k + 1) * height] + ends[k]
        along_y = jnp.dot(slope_y[...], layers[k], preferred_element_type=f32)
        along_y = along_y + end_rows(pick_row(low_y[0], n), pick_row(high_y[0], n), height)
        along_z = (velocity[0, above].astype(f32) - velocity[0, below].astype(f32)) * 0.5
        for j, slope in enumerate((along_x, along_y, along_z)):
            term = half * slope
            if j == component:
                term = term + value
            if before is not None:
                term = before[j, k] + term
            after[j, k] = term


def add_grad_vort(component, slopes, velocity, adjoint, halos, before):
    _, _, height, width = velocity.shape
    slope_x, slope_y = slopes
    whole = lambda shape: pl.BlockSpec(shape, lambda n: (0,) * len(shape))
    column = pl.BlockSpec((1, Z, height), lambda n: (component, 0, 0))
    row = pl.BlockSpec((1, Z, width), lambda n: (component, 0, 0))
    sums = pl.BlockSpec((3, LAYERS, height, width), lambda n: (0, n, 0, 0))
    operands = [slope_x, slope_y, velocity, adjoint, *halos]
    in_specs = [
        whole((width, width)),
        whole((height, height)),
        pl.BlockSpec((1, Z, height, width), lambda n: (component, 0, 0, 0)),
        pl.BlockSpec((LAYERS, height, width), lambda n: (n, 0, 0)),
        column,
        column,
        row,
        row,
    ]
    aliases = {}
    if before is not None:
        aliases = {len(operands): 0}
        operands.append(before)
        in_specs.append(sums)

    def kernel(*refs):
        grad_vort_kernel(component, *refs)

    return pl.pallas_call(
        kernel,
        grid=(Z // LAYERS,),
        in_specs=in_specs,
        out_specs=sums,
        out_shape=jax.ShapeDtypeStruct((3, Z, height, width), f32),
        input_output_aliases=aliases,
        compiler_params=params(),
        cost_estimate=cost(
            2 * Z * height * width * (width + height), Z * height * width * (18 + 12 * len(aliases))
        ),
        name="add_grad_vort",
    )(*operands)


def grad_vel_kernel(slope_x, vorticity, vorticity_above, vorticity_below, adjoint, *refs):
    vort_low_x, vort_high_x, vort_low_y, vort_high_y, low_x, high_x, low_y, high_y = refs[:8]
    after, padded = refs[-2:]
    _, _, height, width = vorticity.shape
    first = pl.program_id(0) * LAYERS

    def times(one, other):
        return one.astype(f32) * other.astype(f32)

    ends = spread_columns(
        times(vort_low_x[...], low_x[...]),
        times(vort_high_x[...], high_x[...]),
        first,
        LAYERS,
        width,
    )
    values = adjoint[pl.ds(first, LAYERS)]
    product = (vorticity[0].astype(f32) * values).reshape(LAYERS * height, width)
    coarse = product.astype(bf16)
    fine = (product - coarse.astype(f32)).astype(bf16)
    inner = jnp.dot(coarse, slope_x[...], preferred_element_type=f32)
    inner = inner + jnp.dot(fine, slope_x[...], preferred_element_type=f32)
    up = adjoint[lax.rem(first + LAYERS, Z)] * vorticity_above[0, 0].astype(f32)
    down = adjoint[lax.rem(first + Z - 1, Z)] * vorticity_below[0, 0].astype(f32)
    deep = [down] + [vorticity[2, k].astype(f32) * values[k] for k in range(LAYERS)] + [up]
    for k in range(LAYERS):
        n = first + k
        padded[k, 8 : 8 + height, :] = vorticity[1, k].astype(f32) * values[k]
        padded[k, 7:8, :] = pick_row(vort_low_y[...], n) * pick_row(low_y[...], n)
        padded[k, 8 + height : 9 + height, :] = pick_row(vort_high_y[...], n) * pick_row(
            high_y[...], n
        )
        total = (padded[k, 9 : 9 + height, :] - padded[k, 7 : 7 + height, :]) + (
            deep[k + 2] - deep[k]
        )
        total = total * 0.5 + inner[k * height : (k + 1) * height] + ends[k]
        after[0, k] = total * -step_size


def write_grad_vel(component, slope_x, vorticity, adjoint, vort_halos, halos, before):
    _, _, height, width = vorticity.shape
    whole = lambda shape: pl.BlockSpec(shape, lambda n: (0,) * len(shape))
    column = whole((Z, height))
    row = whole((Z, width))
    operands = [slope_x, vorticity, vorticity, vorticity, adjoint, *vort_halos, *halos]
    in_specs = [
        whole((width, width)),
        pl.BlockSpec((3, LAYERS, height, width), lambda n: (0, n, 0, 0)),
        pl.BlockSpec((1, 1, height, width), lambda n: (2, lax.rem((n + 1) * LAYERS, Z), 0, 0)),
        pl.BlockSpec((1, 1, height, width), lambda n: (2, lax.rem(n * LAYERS + Z - 1, Z), 0, 0)),
        whole((Z, height, width)),
        column,
        column,
        row,
        row,
        column,
        column,
        row,
        row,
    ]
    aliases = {}
    if before is not None:
        aliases = {len(operands): 0}
        operands.append(before)
        in_specs.append(pl.BlockSpec(memory_space=pl.ANY))
    return pl.pallas_call(
        grad_vel_kernel,
        grid=(Z // LAYERS,),
        in_specs=in_specs,
        out_specs=pl.BlockSpec((1, LAYERS, height, width), lambda n: (component, n, 0, 0)),
        out_shape=jax.ShapeDtypeStruct((3, Z, height, width), f32),
        input_output_aliases=aliases,
        scratch_shapes=[pltpu.VMEM((LAYERS, height + 16, width), f32)],
        compiler_params=params(),
        cost_estimate=cost(4 * Z * height * width * width, Z * height * width * 16),
        name="write_grad_vel",
    )(*operands)


def pair_exchange(parts, axis, mine):
    count = lax.axis_size(axis)
    kept = lax.dynamic_index_in_dim(parts, mine, 0, keepdims=False)
    sent = lax.dynamic_index_in_dim(parts, 1 - mine, 0, keepdims=False)
    got = lax.ppermute(sent, axis, [(i, i ^ 1) for i in range(count)])
    return jnp.where(mine == 0, jnp.stack([kept, got]), jnp.stack([got, kept]))


def shifted(parts, axis):
    count = lax.axis_size(axis)
    return [parts[0]] + [
        lax.ppermute(parts[s], axis, [(i, (i + s) % count) for i in range(count)])
        for s in range(1, count)
    ]


def local(cot_vort, cot_vel, vorticity, velocity):
    size_x = lax.axis_size("gx")
    size_y = lax.axis_size("gy")
    planes = Z // size_y
    halves = size_y // KZ
    _, _, height, width = cot_vel.shape
    modes = HALF_Y // (size_x * halves)
    place_x = lax.axis_index("gx")
    place_y = lax.axis_index("gy")
    half = lax.rem(place_y, halves)
    me = place_x.astype(jnp.int32).reshape(1)
    where = jnp.stack(
        [(place_x * halves + half) * modes, place_y // halves, place_x]
    ).astype(jnp.int32)

    y_table, y_back_table = y_tables(size_x * halves)
    x_table, x_back_table = x_tables()
    slope_x = slope_matrix(width)
    slope_y = np.ascontiguousarray(slope_matrix(height).T)

    velocity_first, velocity_last = edge_columns(velocity, 3)
    vorticity_first, vorticity_last = edge_columns(vorticity, 1)
    low_x, high_x = exchange(
        jnp.concatenate([velocity_first, vorticity_first]),
        jnp.concatenate([velocity_last, vorticity_last]),
        "gx",
    )
    low_y, high_y = exchange(
        jnp.concatenate([velocity[:, :, 0], vorticity[1:2, :, 0]]),
        jnp.concatenate([velocity[:, :, height - 1], vorticity[1:2, :, height - 1]]),
        "gy",
    )
    velocity_halos = (low_x, high_x, low_y, high_y)
    vorticity_halos = (low_x[3], high_x[3], low_y[3], high_y[3])

    spectra = {}
    for component in FORWARD_ORDER:
        layers = depth_transform(cot_vel, component)
        columns = lax.all_to_all(
            layers.reshape(size_y, planes, height, width), "gy", 0, 0, tiled=True
        )
        parts = y_transform(me, y_table, columns, size_x, halves)
        if halves == 1:
            parts = [part[0] for part in parts]
        else:
            parts = [pair_exchange(part[:, 0], "gy", half) for part in parts]
        first = component == FORWARD_ORDER[0]
        spectra[component] = x_transform(
            me, x_table, shifted(parts, "gx"), velocity_halos if first else ()
        )

    grad_vort = None
    grad_vel = None
    for component in BACK_ORDER:
        parts = curl_inverse(where, x_back_table, spectra, component, size_x)
        parts = shifted(parts, "gx")
        if halves == 1:
            parts = [part[None] for part in parts]
        else:
            parts = [pair_exchange(part, "gy", half)[:, None] for part in parts]
        rows = y_inverse(me, y_back_table, parts, size_y)
        layers = lax.all_to_all(rows, "gy", 0, 0, tiled=True)
        adjoint, first_x, last_x, first_y, last_y = make_adjoint(
            layers.reshape(Z, height, width),
            cot_vort,
            component,
            () if grad_vort is None else (grad_vort, grad_vel),
        )
        halos = exchange(first_x, last_x, "gx") + exchange(first_y, last_y, "gy")
        grad_vort = add_grad_vort(
            component, (slope_x, slope_y), velocity, adjoint, velocity_halos, grad_vort
        )
        grad_vel = write_grad_vel(
            component, slope_x, vorticity, adjoint, vorticity_halos, halos, grad_vel
        )
    return grad_vort, grad_vel


def solution(mesh):
    spec = P(None, None, "gy", "gx")
    return jax.shard_map(
        local,
        mesh=mesh,
        in_specs=(spec, spec, spec, spec),
        out_specs=(spec, spec),
        check_vma=False,
    )
```

```python
import math

import jax
import jax.numpy as jnp
import ml_dtypes
import numpy as np
from jax import lax
from jax.experimental import pallas as pl
from jax.experimental.pallas import tpu as pltpu
from jax.sharding import PartitionSpec as P

X = 1024
Y = 1536
Z = 16
HALF_X = X // 2
HALF_Y = Y // 2
KZ = Z // 2

step_size = 0.5

f32 = jnp.float32
bf16 = jnp.bfloat16

FORWARD_ORDER = (0, 1, 2)
BACK_ORDER = (2, 0, 1)


def params(megabytes=56):
    return pltpu.CompilerParams(vmem_limit_bytes=megabytes * 1024 * 1024)


def cost(flops, nbytes):
    return pl.CostEstimate(flops=int(flops), bytes_accessed=int(nbytes), transcendentals=0)


def tied(after):
    return [pl.BlockSpec(memory_space=pl.ANY)] * len(after)


def trig(first, second, length):
    angle = (np.outer(first, second) % length) * (2.0 * math.pi / length)
    return np.cos(angle), np.sin(angle)


def y_tables(blocks):
    cosine, sine = trig(np.arange(HALF_Y), np.arange(Y), Y)
    both = np.stack([cosine.reshape(blocks, -1, Y), sine.reshape(blocks, -1, Y)], 1).reshape(Y, Y)
    both = both.astype(ml_dtypes.bfloat16)
    return both, np.ascontiguousarray(both.T)


def x_tables():
    cosine, sine = trig(np.arange(X), np.arange(HALF_X), X)
    both = np.concatenate([cosine, sine], 1).astype(ml_dtypes.bfloat16)
    return both, np.ascontiguousarray(both.T)


def slope_matrix(size):
    return ((np.eye(size, k=-1) - np.eye(size, k=1)) * 0.5).astype(ml_dtypes.bfloat16)


def combine(terms):
    total = None
    for factor, value in terms:
        if abs(factor) < 1e-12:
            continue
        if abs(factor - 1.0) < 1e-12:
            part = value
        elif abs(factor + 1.0) < 1e-12:
            part = -value
        else:
            part = value * factor
        total = part if total is None else total + part
    return total


def depth_forward(values):
    even = [values[0]] + [values[n] + values[Z - n] for n in range(1, 8)] + [values[8]]
    odd = [None] + [values[n] - values[Z - n] for n in range(1, 8)]
    even_sum = [even[n] + even[8 - n] for n in range(4)] + [even[4]]
    even_dif = [even[n] - even[8 - n] for n in range(4)]
    odd_sum = [None] + [odd[n] + odd[8 - n] for n in range(1, 4)] + [odd[4]]
    odd_dif = [None] + [odd[n] - odd[8 - n] for n in range(1, 4)]
    result = []
    for k in range(KZ):
        folded = even_sum if k % 2 == 0 else even_dif
        cos_part = combine([(math.cos(math.pi * k * n / 8), folded[n]) for n in range(len(folded))])
        folded = odd_dif if k % 2 == 0 else odd_sum
        sin_part = combine(
            [(math.sin(math.pi * k * n / 8), folded[n]) for n in range(1, len(folded))]
        )
        result.append((cos_part, sin_part))
    return result


def depth_inverse(cos_parts, sin_parts):
    layers = [None] * Z
    cos_sum, sin_sum = [None] * 9, [None] * 9
    for n in range(5):
        evens = combine([(math.cos(math.pi * k * n / 8), cos_parts[k]) for k in range(0, KZ, 2)])
        odds = combine([(math.cos(math.pi * k * n / 8), cos_parts[k]) for k in range(1, KZ, 2)])
        if n == 4:
            cos_sum[4] = evens
        else:
            cos_sum[n] = evens + odds
            cos_sum[8 - n] = evens - odds
    for n in range(1, 5):
        evens = combine([(math.sin(math.pi * k * n / 8), sin_parts[k]) for k in range(0, KZ, 2)])
        odds = combine([(math.sin(math.pi * k * n / 8), sin_parts[k]) for k in range(1, KZ, 2)])
        if n == 4:
            sin_sum[4] = odds
        else:
            sin_sum[n] = odds + evens
            sin_sum[8 - n] = odds - evens
    layers[0], layers[8] = cos_sum[0], cos_sum[8]
    for n in range(1, 8):
        layers[n] = cos_sum[n] + sin_sum[n]
        layers[Z - n] = cos_sum[n] - sin_sum[n]
    return layers


ROWS = 96


def tiles(height, width):
    for row in range(0, height, 16):
        for column in range(0, width, 128):
            yield row, pl.ds(row, 16), pl.ds(column, 128)


def depth_forward_kernel(values_ref, planes_ref):
    _, _, height, width = values_ref.shape
    for _, rows, columns in tiles(height, width):
        spectrum = depth_forward([values_ref[0, n, rows, columns] for n in range(Z)])
        for k, (cos_part, sin_part) in enumerate(spectrum):
            planes_ref[2 * k, rows, columns] = cos_part.astype(bf16)
            if sin_part is None:
                sin_part = jnp.zeros_like(cos_part)
            planes_ref[2 * k + 1, rows, columns] = sin_part.astype(bf16)


def depth_transform(values, component):
    _, _, height, width = values.shape
    return pl.pallas_call(
        depth_forward_kernel,
        grid=(height // ROWS,),
        in_specs=[pl.BlockSpec((1, Z, ROWS, width), lambda j: (component, 0, j, 0))],
        out_specs=pl.BlockSpec((Z, ROWS, width), lambda j: (0, j, 0)),
        out_shape=jax.ShapeDtypeStruct((Z, height, width), bf16),
        compiler_params=params(),
        cost_estimate=cost(6 * Z * height * width, 6 * Z * height * width),
        name="depth_transform",
    )(values)


def y_transform(me, table, columns, blocks, halves, after):
    _, planes, _, width = columns.shape
    modes = HALF_Y // (blocks * halves)
    rows = Y // blocks
    shape = (halves, planes, 2, modes, width)

    def kernel(me_ref, table_ref, columns_ref, *refs):
        outs = refs[len(after) :]
        shift = pl.program_id(0)
        for plane in range(planes):
            column = columns_ref[:, plane].reshape(Y, width)
            part = jnp.dot(table_ref[...], column, preferred_element_type=f32).astype(bf16)
            part = part.reshape(halves, 2, modes, width)
            for s, out in enumerate(outs):

                @pl.when(shift == s)
                def _(out=out, part=part, plane=plane):
                    out[:, plane] = part

    return pl.pallas_call(
        kernel,
        grid_spec=pltpu.PrefetchScalarGridSpec(
            num_scalar_prefetch=1,
            grid=(blocks,),
            in_specs=[
                pl.BlockSpec((rows, Y), lambda j, me: (lax.rem(me[0] + j, blocks), 0)),
                pl.BlockSpec(columns.shape, lambda j, me: (0, 0, 0, 0)),
            ]
            + tied(after),
            out_specs=[pl.BlockSpec(shape, lambda j, me: (0, 0, 0, 0, 0))] * blocks,
        ),
        out_shape=[jax.ShapeDtypeStruct(shape, bf16)] * blocks,
        compiler_params=params(24),
        cost_estimate=cost(2 * planes * Y * Y * width, 2 * Y * Y + 4 * planes * Y * width),
        name="y_transform",
    )(me, table, columns, *after)


def y_inverse(me, table, modes, size_y, after):
    blocks = len(modes)
    halves, planes, _, _, width = modes[0].shape
    height = Y // size_y
    count = max(1, 384 // height)
    rows = Y // blocks

    def kernel(me_ref, table_ref, *refs):
        parts, rows_ref, held = refs[:blocks], refs[-2], refs[-1]

        @pl.when(pl.program_id(0) == 0)
        def _():
            for s, part in enumerate(parts):
                source = lax.rem(me_ref[0] + blocks - s, blocks)
                place = pl.ds(pl.multiple_of(source * rows, rows), rows)
                for plane in range(planes):
                    held[plane, place, :] = part[:, plane].reshape(rows, width)

        for plane in range(planes):
            out = jnp.dot(table_ref[...], held[plane], preferred_element_type=f32)
            rows_ref[:, plane] = out.astype(bf16).reshape(count, height, width)

    return pl.pallas_call(
        kernel,
        grid=(size_y // count,),
        in_specs=[
            pl.BlockSpec(memory_space=pltpu.SMEM),
            pl.BlockSpec((count * height, Y), lambda j: (j, 0)),
        ]
        + [pl.BlockSpec(modes[0].shape, lambda j: (0, 0, 0, 0, 0))] * blocks
        + tied(after),
        out_specs=pl.BlockSpec((count, planes, height, width), lambda j: (j, 0, 0, 0)),
        out_shape=jax.ShapeDtypeStruct((size_y, planes, height, width), bf16),
        scratch_shapes=[pltpu.VMEM((planes, Y, width), bf16)],
        compiler_params=params(24),
        cost_estimate=cost(2 * planes * Y * Y * width, 2 * Y * Y + 4 * planes * Y * width),
        name="y_inverse",
    )(me, table, *modes, *after)


def x_transform(me, table, modes, after):
    blocks = len(modes)
    _, _, count, width = modes[0].shape

    def kernel(me_ref, table_ref, *refs):
        parts, spectrum_ref, held = refs[:blocks], refs[-2], refs[-1]
        for s, part in enumerate(parts):
            source = lax.rem(me_ref[0] + blocks - s, blocks)
            place = pl.ds(pl.multiple_of(source * width, width), width)
            held[:, place] = part[0].reshape(2 * count, width)
        spectrum = jnp.dot(held[...], table_ref[...], preferred_element_type=f32)
        spectrum_ref[0] = spectrum.reshape(2, count, X)

    return pl.pallas_call(
        kernel,
        grid=(2,),
        in_specs=[
            pl.BlockSpec(memory_space=pltpu.SMEM),
            pl.BlockSpec((X, X), lambda j: (0, 0)),
        ]
        + [pl.BlockSpec((1, 2, count, width), lambda j: (j, 0, 0, 0))] * blocks
        + tied(after),
        out_specs=pl.BlockSpec((1, 2, count, X), lambda j: (j, 0, 0, 0)),
        out_shape=jax.ShapeDtypeStruct((2, 2, count, X), f32),
        scratch_shapes=[pltpu.VMEM((2 * count, X), bf16)],
        compiler_params=params(24),
        cost_estimate=cost(8 * count * X * X, 2 * X * X + 24 * count * X),
        name="x_transform",
    )(me, table, *modes, *after)


def turned(field, axis, tz, ty, tx, wave):
    index = [tz, ty, tx]
    sign = 1.0 if index[axis] == 0 else -1.0
    index[axis] = 1 - index[axis]
    value = field[index[0], index[1], :, index[2] * HALF_X : (index[2] + 1) * HALF_X]
    return value * (wave * sign)


CURL = {
    0: ((1, 2), (0, 1)),
    1: ((0, 0), (2, 2)),
    2: ((2, 1), (1, 0)),
}


def curl_kernel(axes, where_ref, table_ref, plus_ref, minus_ref, *outs):
    blocks = len(outs)
    _, _, count, width = outs[0].shape
    base = where_ref[0] + pl.program_id(0) * count
    depth = where_ref[1]
    mode_y = lax.broadcasted_iota(jnp.int32, (count, HALF_X), 0) + base
    mode_x = lax.broadcasted_iota(jnp.int32, (count, HALF_X), 1)
    wave_y = mode_y.astype(f32) * (2.0 * math.pi / Y)
    wave_x = mode_x.astype(f32) * (2.0 * math.pi / X)
    wave_z = jnp.full((count, HALF_X), depth, jnp.int32).astype(f32) * (2.0 * math.pi / Z)
    square = wave_x * wave_x + wave_y * wave_y + wave_z * wave_z
    doubling = (
        jnp.where(mode_x == 0, 1.0, 2.0)
        * jnp.where(mode_y == 0, 1.0, 2.0)
        * jnp.where(wave_z == 0.0, 1.0, 2.0)
    )
    weight = jnp.where(square > 0, doubling / jnp.where(square > 0, square, 1.0), 0.0)
    waves = [wave_z * weight, wave_y * weight, wave_x * weight]
    rows = []
    for tz in range(2):
        for ty in range(2):
            parts = []
            for tx in range(2):
                parts.append(
                    (
                        turned(plus_ref, axes[0], tz, ty, tx, waves[axes[0]])
                        - turned(minus_ref, axes[1], tz, ty, tx, waves[axes[1]])
                    ).astype(bf16)
                )
            rows.append(jnp.concatenate(parts, axis=1))
    rows = jnp.concatenate(rows, axis=0)
    for s, out in enumerate(outs):
        target = lax.rem(where_ref[2] + s, blocks)
        place = pl.ds(pl.multiple_of(target * width, width), width)
        back = jnp.dot(rows, table_ref[:, place], preferred_element_type=f32)
        out[...] = back.astype(bf16).reshape(2, 2, count, width)


def curl_inverse(where, table, spectra, component, blocks, after):
    (plus_axis, plus), (minus_axis, minus) = CURL[component]
    total = spectra[plus].shape[2]
    width = X // blocks
    count = 96 if total % 96 == 0 else total
    spec = pl.BlockSpec((2, 2, count, X), lambda j: (0, 0, j, 0))

    def kernel(*refs):
        curl_kernel((plus_axis, minus_axis), *refs[:4], *refs[4 + len(after) :])

    return pl.pallas_call(
        kernel,
        grid=(total // count,),
        in_specs=[
            pl.BlockSpec(memory_space=pltpu.SMEM),
            pl.BlockSpec((X, X), lambda j: (0, 0)),
            spec,
            spec,
        ]
        + tied(after),
        out_specs=[pl.BlockSpec((2, 2, count, width), lambda j: (0, 0, j, 0))] * blocks,
        out_shape=[jax.ShapeDtypeStruct((2, 2, total, width), bf16)] * blocks,
        compiler_params=params(24),
        cost_estimate=cost(8 * total * X * X, 2 * X * X + 40 * total * X),
        name="curl_inverse",
    )(where, table, spectra[plus], spectra[minus], *after)


def side_columns(planes):
    width = planes[0].shape[1]
    row = lax.broadcasted_iota(jnp.int32, (2 * Z, width), 0)
    lane = lax.broadcasted_iota(jnp.int32, (2 * Z, width), 1)
    total = None
    for n in range(Z):
        pick = ((row == n) & (lane == 0)) | ((row == n + Z) & (lane == width - 1))
        part = lax.dot_general(
            pick.astype(f32).astype(bf16),
            planes[n],
            (((1,), (1,)), ((), ())),
            preferred_element_type=f32,
        )
        total = part if total is None else total + part
    return total[:Z].astype(bf16), total[Z:].astype(bf16)


def spread_columns(low, high, first, layers, width):
    row = lax.broadcasted_iota(jnp.int32, (2 * Z, layers * width), 0)
    column = lax.broadcasted_iota(jnp.int32, (2 * Z, layers * width), 1)
    place = jnp.zeros((2 * Z, layers * width), f32)
    for n in range(layers):
        place = place + jnp.where((row == first + n) & (column == n * width), -0.5, 0.0)
        place = place + jnp.where(
            (row == first + n + Z) & (column == (n + 1) * width - 1), 0.5, 0.0
        )
    both = jnp.concatenate([low, high], axis=0).astype(bf16)
    spread = lax.dot_general(
        both, place.astype(bf16), (((0,), (0,)), ((), ())), preferred_element_type=f32
    )
    return [spread[:, n * width : (n + 1) * width] for n in range(layers)]


def edges_kernel(field_ref, first_column_ref, last_column_ref):
    first, last = side_columns([field_ref[0, n] for n in range(Z)])
    first_column_ref[0] = first
    last_column_ref[0] = last


def edge_columns(field, components):
    _, _, height, width = field.shape
    shape = jax.ShapeDtypeStruct((components, Z, height), bf16)
    spec = pl.BlockSpec((1, Z, height), lambda i: (i, 0, 0))
    return pl.pallas_call(
        edges_kernel,
        grid=(components,),
        in_specs=[pl.BlockSpec((1, Z, height, width), lambda i: (i, 0, 0, 0))],
        out_specs=[spec, spec],
        out_shape=[shape, shape],
        compiler_params=params(),
        cost_estimate=cost(
            components * 64 * Z * height * width, 2 * components * Z * height * width
        ),
        name="edge_columns",
    )(field)


def exchange(first, last, axis):
    count = lax.axis_size(axis)
    up = [(i, (i + 1) % count) for i in range(count)]
    down = [((i + 1) % count, i) for i in range(count)]
    return lax.ppermute(last, axis, up), lax.ppermute(first, axis, down)


def adjoint_kernel(planes_ref, cotangent_ref, *refs):
    adjoint_ref, first_x, last_x, first_y, last_y, held = refs[-6:]
    _, height, width = held.shape
    scale = 1.0 / (X * Y * Z)
    base = pl.program_id(0) * ROWS
    for row, rows, columns in tiles(ROWS, width):
        place = pl.ds(pl.multiple_of(base + row, 16), 16)
        layers = depth_inverse(
            [planes_ref[2 * k, rows, columns].astype(f32) for k in range(KZ)],
            [planes_ref[2 * k + 1, rows, columns].astype(f32) for k in range(KZ)],
        )
        for n in range(Z):
            value = cotangent_ref[0, n, rows, columns] + layers[n] * scale
            adjoint_ref[n, rows, columns] = value
            held[n, place, columns] = value.astype(bf16)

    @pl.when(pl.program_id(0) == pl.num_programs(0) - 1)
    def _():
        first, last = side_columns([held[n] for n in range(Z)])
        first_x[...] = first
        last_x[...] = last
        top = [held[n, 0:16, :].astype(f32)[0:1] for n in range(Z)]
        bottom = [held[n, height - 16 : height, :].astype(f32)[15:16] for n in range(Z)]
        first_y[...] = jnp.concatenate(top, 0).astype(bf16)
        last_y[...] = jnp.concatenate(bottom, 0).astype(bf16)


def make_adjoint(planes, cotangent, component, after):
    _, height, width = planes.shape
    column = jax.ShapeDtypeStruct((Z, height), bf16)
    row = jax.ShapeDtypeStruct((Z, width), bf16)
    column_spec = pl.BlockSpec((Z, height), lambda j: (0, 0))
    row_spec = pl.BlockSpec((Z, width), lambda j: (0, 0))
    return pl.pallas_call(
        adjoint_kernel,
        grid=(height // ROWS,),
        in_specs=[
            pl.BlockSpec((Z, ROWS, width), lambda j: (0, j, 0)),
            pl.BlockSpec((1, Z, ROWS, width), lambda j: (component, 0, j, 0)),
        ]
        + tied(after),
        out_specs=[
            pl.BlockSpec((Z, ROWS, width), lambda j: (0, j, 0)),
            column_spec,
            column_spec,
            row_spec,
            row_spec,
        ],
        out_shape=[
            jax.ShapeDtypeStruct((Z, height, width), f32),
            column,
            column,
            row,
            row,
        ],
        scratch_shapes=[pltpu.VMEM((Z, height, width), bf16)],
        compiler_params=params(),
        cost_estimate=cost(70 * Z * height * width, 10 * Z * height * width),
        name="make_adjoint",
    )(planes, cotangent, *after)


def pick_row(rows, n):
    index = lax.broadcasted_iota(jnp.int32, rows.shape, 0)
    return jnp.sum(jnp.where(index == n, rows.astype(f32), 0.0), axis=0, keepdims=True)


def end_rows(low, high, height):
    row = lax.broadcasted_iota(jnp.int32, (height, low.shape[1]), 0)
    return jnp.where(row == 0, low * -0.5, 0.0) + jnp.where(row == height - 1, high * 0.5, 0.0)


LAYERS = 4


def grad_vort_kernel(
    component, slope_x, slope_y, velocity, adjoint, low_x, high_x, low_y, high_y, *refs
):
    before, after = refs
    height, width = velocity.shape[2], velocity.shape[3]
    first = pl.program_id(0) * LAYERS
    ends = spread_columns(low_x[0], high_x[0], first, LAYERS, width)
    layers = velocity[0, pl.ds(first, LAYERS)]
    stacked = layers.reshape(LAYERS * height, width)
    inner = jnp.dot(stacked, slope_x[...], preferred_element_type=f32)
    for k in range(LAYERS):
        n = first + k
        above = lax.rem(n + 1, Z)
        below = lax.rem(n + Z - 1, Z)
        value = adjoint[k]
        half = value * step_size
        along_x = inner[k * height : (k + 1) * height] + ends[k]
        along_y = jnp.dot(slope_y[...], layers[k], preferred_element_type=f32)
        along_y = along_y + end_rows(pick_row(low_y[0], n), pick_row(high_y[0], n), height)
        along_z = (velocity[0, above].astype(f32) - velocity[0, below].astype(f32)) * 0.5
        for j, slope in enumerate((along_x, along_y, along_z)):
            term = half * slope
            if j == component:
                term = term + value
            if before is not None:
                term = before[j, k] + term
            after[j, k] = term


def add_grad_vort(component, slopes, velocity, adjoint, halos, before, after):
    _, _, height, width = velocity.shape
    slope_x, slope_y = slopes
    whole = lambda shape: pl.BlockSpec(shape, lambda n: (0,) * len(shape))
    column = pl.BlockSpec((1, Z, height), lambda n: (component, 0, 0))
    row = pl.BlockSpec((1, Z, width), lambda n: (component, 0, 0))
    sums = pl.BlockSpec((3, LAYERS, height, width), lambda n: (0, n, 0, 0))
    sums_before = pl.BlockSpec((3, LAYERS, height, width), lambda n: (0, n, 0, 0))
    operands = [slope_x, slope_y, velocity, adjoint, *halos]
    in_specs = [
        whole((width, width)),
        whole((height, height)),
        pl.BlockSpec((1, Z, height, width), lambda n: (component, 0, 0, 0)),
        pl.BlockSpec((LAYERS, height, width), lambda n: (n, 0, 0)),
        column,
        column,
        row,
        row,
    ]
    aliases = {}
    if before is not None:
        aliases = {len(operands): 0}
        operands.append(before)
        in_specs.append(sums_before)

    def kernel(*refs):
        grad_vort_kernel(component, *refs[:8], None if before is None else refs[8], refs[-1])

    return pl.pallas_call(
        kernel,
        grid=(Z // LAYERS,),
        in_specs=in_specs + tied(after),
        out_specs=sums,
        out_shape=jax.ShapeDtypeStruct((3, Z, height, width), f32),
        input_output_aliases=aliases,
        compiler_params=params(),
        cost_estimate=cost(
            2 * Z * height * width * (width + height), Z * height * width * (18 + 12 * len(aliases))
        ),
        name="add_grad_vort",
    )(*operands, *after)


def grad_vel_kernel(slope_x, vorticity, vorticity_above, vorticity_below, adjoint, *refs):
    vort_low_x, vort_high_x, vort_low_y, vort_high_y, low_x, high_x, low_y, high_y = refs[:8]
    after, padded = refs[-2:]
    _, _, height, width = vorticity.shape
    first = pl.program_id(0) * LAYERS

    def times(one, other):
        return one.astype(f32) * other.astype(f32)

    ends = spread_columns(
        times(vort_low_x[0], low_x[...]),
        times(vort_high_x[0], high_x[...]),
        first,
        LAYERS,
        width,
    )
    values = adjoint[pl.ds(first, LAYERS)]
    product = (vorticity[0].astype(f32) * values).reshape(LAYERS * height, width)
    coarse = product.astype(bf16)
    fine = (product - coarse.astype(f32)).astype(bf16)
    inner = jnp.dot(coarse, slope_x[...], preferred_element_type=f32)
    inner = inner + jnp.dot(fine, slope_x[...], preferred_element_type=f32)
    up = adjoint[lax.rem(first + LAYERS, Z)] * vorticity_above[0, 0].astype(f32)
    down = adjoint[lax.rem(first + Z - 1, Z)] * vorticity_below[0, 0].astype(f32)
    deep = [down] + [vorticity[2, k].astype(f32) * values[k] for k in range(LAYERS)] + [up]
    for k in range(LAYERS):
        n = first + k
        padded[k, 8 : 8 + height, :] = vorticity[1, k].astype(f32) * values[k]
        padded[k, 7:8, :] = pick_row(vort_low_y[0], n) * pick_row(low_y[...], n)
        padded[k, 8 + height : 9 + height, :] = pick_row(vort_high_y[0], n) * pick_row(
            high_y[...], n
        )
        total = (padded[k, 9 : 9 + height, :] - padded[k, 7 : 7 + height, :]) + (
            deep[k + 2] - deep[k]
        )
        total = total * 0.5 + inner[k * height : (k + 1) * height] + ends[k]
        after[0, k] = total * -step_size


def write_grad_vel(component, slope_x, vorticity, adjoint, saved_halos, halos, before, after):
    _, _, height, width = vorticity.shape
    whole = lambda shape: pl.BlockSpec(shape, lambda n: (0,) * len(shape))
    column = whole((Z, height))
    row = whole((Z, width))
    saved_column = pl.BlockSpec((1, Z, height), lambda n: (3, 0, 0))
    saved_row = pl.BlockSpec((1, Z, width), lambda n: (3, 0, 0))
    operands = [slope_x, vorticity, vorticity, vorticity, adjoint, *saved_halos, *halos]
    in_specs = [
        whole((width, width)),
        pl.BlockSpec((3, LAYERS, height, width), lambda n: (0, n, 0, 0)),
        pl.BlockSpec((1, 1, height, width), lambda n: (2, lax.rem((n + 1) * LAYERS, Z), 0, 0)),
        pl.BlockSpec((1, 1, height, width), lambda n: (2, lax.rem(n * LAYERS + Z - 1, Z), 0, 0)),
        whole((Z, height, width)),
        saved_column,
        saved_column,
        saved_row,
        saved_row,
        column,
        column,
        row,
        row,
    ]
    aliases = {}
    if before is not None:
        aliases = {len(operands): 0}
        operands.append(before)
        in_specs.append(pl.BlockSpec(memory_space=pl.ANY))
    return pl.pallas_call(
        grad_vel_kernel,
        grid=(Z // LAYERS,),
        in_specs=in_specs + tied(after),
        out_specs=pl.BlockSpec((1, LAYERS, height, width), lambda n: (component, n, 0, 0)),
        out_shape=jax.ShapeDtypeStruct((3, Z, height, width), f32),
        input_output_aliases=aliases,
        scratch_shapes=[pltpu.VMEM((LAYERS, height + 16, width), f32)],
        compiler_params=params(),
        cost_estimate=cost(4 * Z * height * width * width, Z * height * width * 16),
        name="write_grad_vel",
    )(*operands, *after)


def pair_exchange(parts, axis, mine):
    count = lax.axis_size(axis)
    kept = lax.dynamic_index_in_dim(parts, mine, 0, keepdims=False)
    sent = lax.dynamic_index_in_dim(parts, 1 - mine, 0, keepdims=False)
    got = lax.ppermute(sent, axis, [(i, i ^ 1) for i in range(count)])
    return jnp.where(mine == 0, jnp.stack([kept, got]), jnp.stack([got, kept]))


def shifted(parts, axis):
    count = lax.axis_size(axis)
    return [parts[0]] + [
        lax.ppermute(parts[s], axis, [(i, (i + s) % count) for i in range(count)])
        for s in range(1, count)
    ]


def local(cot_vort, cot_vel, vorticity, velocity):
    size_x = lax.axis_size("gx")
    size_y = lax.axis_size("gy")
    planes = Z // size_y
    halves = size_y // KZ
    _, _, height, width = cot_vel.shape
    modes = HALF_Y // (size_x * halves)
    place_x = lax.axis_index("gx")
    place_y = lax.axis_index("gy")
    half = lax.rem(place_y, halves)
    me = place_x.astype(jnp.int32).reshape(1)
    where = jnp.stack(
        [(place_x * halves + half) * modes, place_y // halves, place_x]
    ).astype(jnp.int32)

    y_table, y_back_table = y_tables(size_x * halves)
    x_table, x_back_table = x_tables()
    slope_x = slope_matrix(width)
    slope_y = np.ascontiguousarray(slope_matrix(height).T)

    velocity_first, velocity_last = edge_columns(velocity, 3)
    vorticity_first, vorticity_last = edge_columns(vorticity, 1)
    low_x, high_x = exchange(
        jnp.concatenate([velocity_first, vorticity_first]),
        jnp.concatenate([velocity_last, vorticity_last]),
        "gx",
    )
    low_y, high_y = exchange(
        jnp.concatenate([velocity[:, :, 0], vorticity[1:2, :, 0]]),
        jnp.concatenate([velocity[:, :, height - 1], vorticity[1:2, :, height - 1]]),
        "gy",
    )
    saved_halos = (low_x, high_x, low_y, high_y)
    edges = (velocity_first, vorticity_first)

    sent = {}
    for place, component in enumerate(FORWARD_ORDER):
        layers = depth_transform(cot_vel, component)
        columns = lax.all_to_all(
            layers.reshape(size_y, planes, height, width), "gy", 0, 0, tiled=True
        )
        parts = y_transform(
            me, y_table, columns, size_x, halves, edges if place == 1 else ()
        )
        if halves == 1:
            parts = [part[0] for part in parts]
        else:
            parts = [pair_exchange(part[:, 0], "gy", half) for part in parts]
        sent[component] = parts
    spectra = {}
    for place, component in enumerate(FORWARD_ORDER):
        after = ((sent[FORWARD_ORDER[2]][0],), saved_halos, ())[place]
        spectra[component] = x_transform(me, x_table, shifted(sent[component], "gx"), after)

    returned = {}
    after = ()
    for component in BACK_ORDER:
        parts = curl_inverse(where, x_back_table, spectra, component, size_x, after)
        after = (parts[0],)
        parts = shifted(parts, "gx")
        if halves == 1:
            parts = [part[None] for part in parts]
        else:
            parts = [pair_exchange(part, "gy", half)[:, None] for part in parts]
        returned[component] = parts

    def rows_of(component, after):
        return y_inverse(me, y_back_table, returned[component], size_y, after)

    def adjoint_of(component, rows, after):
        layers = lax.all_to_all(rows, "gy", 0, 0, tiled=True)
        adjoint, first_x, last_x, first_y, last_y = make_adjoint(
            layers.reshape(Z, height, width), cot_vort, component, after
        )
        return adjoint, exchange(first_x, last_x, "gx") + exchange(first_y, last_y, "gy")

    def vort_of(component, adjoint, before, after):
        return add_grad_vort(
            component, (slope_x, slope_y), velocity, adjoint, saved_halos, before, after
        )

    def vel_of(component, adjoint, halos, before, after):
        return write_grad_vel(
            component, slope_x, vorticity, adjoint, saved_halos, halos, before, after
        )

    one, two, three = BACK_ORDER
    rows_one = rows_of(one, ())
    rows_two = rows_of(two, (rows_one,))
    adjoint_one, halos_one = adjoint_of(one, rows_one, (rows_two,))
    grad_vort = vort_of(one, adjoint_one, None, ())
    adjoint_two, halos_two = adjoint_of(two, rows_two, (grad_vort,))
    rows_three = rows_of(three, (adjoint_two,) + halos_two)
    grad_vel = vel_of(one, adjoint_one, halos_one, None, (rows_three,))
    grad_vort = vort_of(two, adjoint_two, grad_vort, (rows_three,))
    grad_vel = vel_of(two, adjoint_two, halos_two, grad_vel, ())
    adjoint_three, halos_three = adjoint_of(three, rows_three, (grad_vort, grad_vel))
    grad_vort = vort_of(three, adjoint_three, grad_vort, ())
    grad_vel = vel_of(three, adjoint_three, halos_three, grad_vel, (grad_vort,))
    return grad_vort, grad_vel


def solution(mesh):
    spec = P(None, None, "gy", "gx")
    return jax.shard_map(
        local,
        mesh=mesh,
        in_specs=(spec, spec, spec, spec),
        out_specs=(spec, spec),
        check_vma=False,
    )
```

```python
import math

import jax
import jax.numpy as jnp
import ml_dtypes
import numpy as np
from jax import lax
from jax.experimental import pallas as pl
from jax.experimental.pallas import tpu as pltpu
from jax.sharding import PartitionSpec as P

X = 1024
Y = 1536
Z = 16
HALF_X = X // 2
HALF_Y = Y // 2
KZ = Z // 2

step_size = 0.5

f32 = jnp.float32
bf16 = jnp.bfloat16

FORWARD_ORDER = (0, 1, 2)
BACK_ORDER = (2, 0, 1)


def params(megabytes=56):
    return pltpu.CompilerParams(vmem_limit_bytes=megabytes * 1024 * 1024)


SMALL = pl.CostEstimate(flops=1, bytes_accessed=1, transcendentals=0)


def tied(after):
    return [pl.BlockSpec(memory_space=pl.ANY)] * len(after)


def trig(first, second, length):
    angle = (np.outer(first, second) % length) * (2.0 * math.pi / length)
    return np.cos(angle), np.sin(angle)


def y_tables(blocks):
    cosine, sine = trig(np.arange(HALF_Y), np.arange(Y), Y)
    both = np.stack([cosine.reshape(blocks, -1, Y), sine.reshape(blocks, -1, Y)], 1).reshape(Y, Y)
    both = both.astype(ml_dtypes.bfloat16)
    return both, np.ascontiguousarray(both.T)


def x_tables():
    cosine, sine = trig(np.arange(X), np.arange(HALF_X), X)
    both = np.concatenate([cosine, sine], 1).astype(ml_dtypes.bfloat16)
    return both, np.ascontiguousarray(both.T)


def slope_matrix(size):
    return ((np.eye(size, k=-1) - np.eye(size, k=1)) * 0.5).astype(ml_dtypes.bfloat16)


def combine(terms):
    total = None
    for factor, value in terms:
        if abs(factor) < 1e-12:
            continue
        if abs(factor - 1.0) < 1e-12:
            part = value
        elif abs(factor + 1.0) < 1e-12:
            part = -value
        else:
            part = value * factor
        total = part if total is None else total + part
    return total


def depth_forward(values):
    even = [values[0]] + [values[n] + values[Z - n] for n in range(1, 8)] + [values[8]]
    odd = [None] + [values[n] - values[Z - n] for n in range(1, 8)]
    even_sum = [even[n] + even[8 - n] for n in range(4)] + [even[4]]
    even_dif = [even[n] - even[8 - n] for n in range(4)]
    odd_sum = [None] + [odd[n] + odd[8 - n] for n in range(1, 4)] + [odd[4]]
    odd_dif = [None] + [odd[n] - odd[8 - n] for n in range(1, 4)]
    result = []
    for k in range(KZ):
        folded = even_sum if k % 2 == 0 else even_dif
        cos_part = combine([(math.cos(math.pi * k * n / 8), folded[n]) for n in range(len(folded))])
        folded = odd_dif if k % 2 == 0 else odd_sum
        sin_part = combine(
            [(math.sin(math.pi * k * n / 8), folded[n]) for n in range(1, len(folded))]
        )
        result.append((cos_part, sin_part))
    return result


def depth_inverse(cos_parts, sin_parts):
    layers = [None] * Z
    cos_sum, sin_sum = [None] * 9, [None] * 9
    for n in range(5):
        evens = combine([(math.cos(math.pi * k * n / 8), cos_parts[k]) for k in range(0, KZ, 2)])
        odds = combine([(math.cos(math.pi * k * n / 8), cos_parts[k]) for k in range(1, KZ, 2)])
        if n == 4:
            cos_sum[4] = evens
        else:
            cos_sum[n] = evens + odds
            cos_sum[8 - n] = evens - odds
    for n in range(1, 5):
        evens = combine([(math.sin(math.pi * k * n / 8), sin_parts[k]) for k in range(0, KZ, 2)])
        odds = combine([(math.sin(math.pi * k * n / 8), sin_parts[k]) for k in range(1, KZ, 2)])
        if n == 4:
            sin_sum[4] = odds
        else:
            sin_sum[n] = odds + evens
            sin_sum[8 - n] = odds - evens
    layers[0], layers[8] = cos_sum[0], cos_sum[8]
    for n in range(1, 8):
        layers[n] = cos_sum[n] + sin_sum[n]
        layers[Z - n] = cos_sum[n] - sin_sum[n]
    return layers


ROWS = 96


def tiles(height, width):
    for row in range(0, height, 16):
        for column in range(0, width, 128):
            yield row, pl.ds(row, 16), pl.ds(column, 128)


def depth_forward_kernel(values_ref, planes_ref):
    _, _, height, width = values_ref.shape
    for _, rows, columns in tiles(height, width):
        spectrum = depth_forward([values_ref[0, n, rows, columns] for n in range(Z)])
        for k, (cos_part, sin_part) in enumerate(spectrum):
            planes_ref[2 * k, rows, columns] = cos_part.astype(bf16)
            if sin_part is None:
                sin_part = jnp.zeros_like(cos_part)
            planes_ref[2 * k + 1, rows, columns] = sin_part.astype(bf16)


def depth_transform(values, component):
    _, _, height, width = values.shape
    return pl.pallas_call(
        depth_forward_kernel,
        grid=(height // ROWS,),
        in_specs=[pl.BlockSpec((1, Z, ROWS, width), lambda j: (component, 0, j, 0))],
        out_specs=pl.BlockSpec((Z, ROWS, width), lambda j: (0, j, 0)),
        out_shape=jax.ShapeDtypeStruct((Z, height, width), bf16),
        compiler_params=params(),
        cost_estimate=SMALL,
        name="depth_transform",
    )(values)


def y_transform(me, table, columns, blocks, halves, after):
    _, planes, _, width = columns.shape
    modes = HALF_Y // (blocks * halves)
    rows = Y // blocks
    shape = (halves, planes, 2, modes, width)

    def kernel(me_ref, table_ref, columns_ref, *refs):
        outs, held, arrived = refs[len(after) : len(after) + blocks], refs[-2], refs[-1]
        copies = []
        for s in range(blocks):
            target = lax.rem(me_ref[0] + s, blocks)
            place = pl.ds(pl.multiple_of(target * rows, rows), rows)
            copies.append(pltpu.make_async_copy(table_ref.at[place], held.at[s], arrived.at[s]))
            copies[s].start()
        for s, out in enumerate(outs):
            copies[s].wait()
            for plane in range(planes):
                column = columns_ref[:, plane].reshape(Y, width)
                part = jnp.dot(held[s], column, preferred_element_type=f32)
                out[:, plane] = part.astype(bf16).reshape(halves, 2, modes, width)

    vmem = pl.BlockSpec(memory_space=pltpu.VMEM)
    return pl.pallas_call(
        kernel,
        in_specs=[
            pl.BlockSpec(memory_space=pltpu.SMEM),
            pl.BlockSpec(memory_space=pl.ANY),
            vmem,
        ]
        + tied(after),
        out_specs=[vmem] * blocks,
        out_shape=[jax.ShapeDtypeStruct(shape, bf16)] * blocks,
        scratch_shapes=[
            pltpu.VMEM((blocks, rows, Y), bf16),
            pltpu.SemaphoreType.DMA((blocks,)),
        ],
        compiler_params=params(),
        cost_estimate=SMALL,
        name="y_transform",
    )(me, table, columns, *after)


def y_inverse(me, table, modes, size_y, after):
    blocks = len(modes)
    halves, planes, _, _, width = modes[0].shape
    height = Y // size_y
    count = max(1, 384 // height)
    rows = Y // blocks

    def kernel(me_ref, table_ref, *refs):
        parts, rows_ref, held = refs[:blocks], refs[-2], refs[-1]

        @pl.when(pl.program_id(0) == 0)
        def _():
            for s, part in enumerate(parts):
                source = lax.rem(me_ref[0] + blocks - s, blocks)
                place = pl.ds(pl.multiple_of(source * rows, rows), rows)
                for plane in range(planes):
                    held[plane, place, :] = part[:, plane].reshape(rows, width)

        for plane in range(planes):
            out = jnp.dot(table_ref[...], held[plane], preferred_element_type=f32)
            rows_ref[:, plane] = out.astype(bf16).reshape(count, height, width)

    return pl.pallas_call(
        kernel,
        grid=(size_y // count,),
        in_specs=[
            pl.BlockSpec(memory_space=pltpu.SMEM),
            pl.BlockSpec((count * height, Y), lambda j: (j, 0)),
        ]
        + [pl.BlockSpec(modes[0].shape, lambda j: (0, 0, 0, 0, 0))] * blocks
        + tied(after),
        out_specs=pl.BlockSpec((count, planes, height, width), lambda j: (j, 0, 0, 0)),
        out_shape=jax.ShapeDtypeStruct((size_y, planes, height, width), bf16),
        scratch_shapes=[pltpu.VMEM((planes, Y, width), bf16)],
        compiler_params=params(24),
        cost_estimate=SMALL,
        name="y_inverse",
    )(me, table, *modes, *after)


def x_transform(me, table, modes, after):
    blocks = len(modes)
    _, _, count, width = modes[0].shape

    def kernel(me_ref, table_ref, *refs):
        parts, spectrum_ref, held = refs[:blocks], refs[-2], refs[-1]
        for s, part in enumerate(parts):
            source = lax.rem(me_ref[0] + blocks - s, blocks)
            place = pl.ds(pl.multiple_of(source * width, width), width)
            held[:, place] = part[0].reshape(2 * count, width)
        spectrum = jnp.dot(held[...], table_ref[...], preferred_element_type=f32)
        spectrum_ref[0] = spectrum.reshape(2, count, X)

    return pl.pallas_call(
        kernel,
        grid=(2,),
        in_specs=[
            pl.BlockSpec(memory_space=pltpu.SMEM),
            pl.BlockSpec((X, X), lambda j: (0, 0)),
        ]
        + [pl.BlockSpec((1, 2, count, width), lambda j: (j, 0, 0, 0))] * blocks
        + tied(after),
        out_specs=pl.BlockSpec((1, 2, count, X), lambda j: (j, 0, 0, 0)),
        out_shape=jax.ShapeDtypeStruct((2, 2, count, X), f32),
        scratch_shapes=[pltpu.VMEM((2 * count, X), bf16)],
        compiler_params=params(24),
        cost_estimate=SMALL,
        name="x_transform",
    )(me, table, *modes, *after)


def turned(field, axis, tz, ty, tx, wave):
    index = [tz, ty, tx]
    sign = 1.0 if index[axis] == 0 else -1.0
    index[axis] = 1 - index[axis]
    value = field[index[0], index[1], :, index[2] * HALF_X : (index[2] + 1) * HALF_X]
    return value * (wave * sign)


CURL = {
    0: ((1, 2), (0, 1)),
    1: ((0, 0), (2, 2)),
    2: ((2, 1), (1, 0)),
}


def curl_kernel(axes, where_ref, table_ref, plus_ref, minus_ref, *outs):
    blocks = len(outs)
    _, _, count, width = outs[0].shape
    base = where_ref[0] + pl.program_id(0) * count
    depth = where_ref[1]
    mode_y = lax.broadcasted_iota(jnp.int32, (count, HALF_X), 0) + base
    mode_x = lax.broadcasted_iota(jnp.int32, (count, HALF_X), 1)
    wave_y = mode_y.astype(f32) * (2.0 * math.pi / Y)
    wave_x = mode_x.astype(f32) * (2.0 * math.pi / X)
    wave_z = jnp.full((count, HALF_X), depth, jnp.int32).astype(f32) * (2.0 * math.pi / Z)
    square = wave_x * wave_x + wave_y * wave_y + wave_z * wave_z
    doubling = (
        jnp.where(mode_x == 0, 1.0, 2.0)
        * jnp.where(mode_y == 0, 1.0, 2.0)
        * jnp.where(wave_z == 0.0, 1.0, 2.0)
    )
    weight = jnp.where(square > 0, doubling / jnp.where(square > 0, square, 1.0), 0.0)
    waves = [wave_z * weight, wave_y * weight, wave_x * weight]
    rows = []
    for tz in range(2):
        for ty in range(2):
            parts = []
            for tx in range(2):
                parts.append(
                    (
                        turned(plus_ref, axes[0], tz, ty, tx, waves[axes[0]])
                        - turned(minus_ref, axes[1], tz, ty, tx, waves[axes[1]])
                    ).astype(bf16)
                )
            rows.append(jnp.concatenate(parts, axis=1))
    rows = jnp.concatenate(rows, axis=0)
    for s, out in enumerate(outs):
        target = lax.rem(where_ref[2] + s, blocks)
        place = pl.ds(pl.multiple_of(target * width, width), width)
        back = jnp.dot(rows, table_ref[:, place], preferred_element_type=f32)
        out[...] = back.astype(bf16).reshape(2, 2, count, width)


def curl_inverse(where, table, spectra, component, blocks, after):
    (plus_axis, plus), (minus_axis, minus) = CURL[component]
    total = spectra[plus].shape[2]
    width = X // blocks
    count = 96 if total % 96 == 0 else total
    spec = pl.BlockSpec((2, 2, count, X), lambda j: (0, 0, j, 0))

    def kernel(*refs):
        curl_kernel((plus_axis, minus_axis), *refs[:4], *refs[4 + len(after) :])

    return pl.pallas_call(
        kernel,
        grid=(total // count,),
        in_specs=[
            pl.BlockSpec(memory_space=pltpu.SMEM),
            pl.BlockSpec((X, X), lambda j: (0, 0)),
            spec,
            spec,
        ]
        + tied(after),
        out_specs=[pl.BlockSpec((2, 2, count, width), lambda j: (0, 0, j, 0))] * blocks,
        out_shape=[jax.ShapeDtypeStruct((2, 2, total, width), bf16)] * blocks,
        compiler_params=params(24),
        cost_estimate=SMALL,
        name="curl_inverse",
    )(where, table, spectra[plus], spectra[minus], *after)


def side_columns(planes):
    width = planes[0].shape[1]
    row = lax.broadcasted_iota(jnp.int32, (2 * Z, width), 0)
    lane = lax.broadcasted_iota(jnp.int32, (2 * Z, width), 1)
    total = None
    for n in range(Z):
        pick = ((row == n) & (lane == 0)) | ((row == n + Z) & (lane == width - 1))
        part = lax.dot_general(
            pick.astype(f32).astype(bf16),
            planes[n],
            (((1,), (1,)), ((), ())),
            preferred_element_type=f32,
        )
        total = part if total is None else total + part
    return total[:Z].astype(bf16), total[Z:].astype(bf16)


def spread_columns(low, high, first, layers, width):
    row = lax.broadcasted_iota(jnp.int32, (2 * Z, layers * width), 0)
    column = lax.broadcasted_iota(jnp.int32, (2 * Z, layers * width), 1)
    place = jnp.zeros((2 * Z, layers * width), f32)
    for n in range(layers):
        place = place + jnp.where((row == first + n) & (column == n * width), -0.5, 0.0)
        place = place + jnp.where(
            (row == first + n + Z) & (column == (n + 1) * width - 1), 0.5, 0.0
        )
    both = jnp.concatenate([low, high], axis=0).astype(bf16)
    spread = lax.dot_general(
        both, place.astype(bf16), (((0,), (0,)), ((), ())), preferred_element_type=f32
    )
    return [spread[:, n * width : (n + 1) * width] for n in range(layers)]


def edges_kernel(field_ref, *refs):
    first_column_ref, last_column_ref = refs[-2:]
    first, last = side_columns([field_ref[0, n] for n in range(Z)])
    first_column_ref[0] = first
    last_column_ref[0] = last


def edge_columns(field, components, after):
    _, _, height, width = field.shape
    shape = jax.ShapeDtypeStruct((components, Z, height), bf16)
    spec = pl.BlockSpec((1, Z, height), lambda i: (i, 0, 0))
    return pl.pallas_call(
        edges_kernel,
        grid=(components,),
        in_specs=[pl.BlockSpec((1, Z, height, width), lambda i: (i, 0, 0, 0))] + tied(after),
        out_specs=[spec, spec],
        out_shape=[shape, shape],
        compiler_params=params(),
        cost_estimate=SMALL,
        name="edge_columns",
    )(field, *after)


def exchange(first, last, axis):
    count = lax.axis_size(axis)
    up = [(i, (i + 1) % count) for i in range(count)]
    down = [((i + 1) % count, i) for i in range(count)]
    return lax.ppermute(last, axis, up), lax.ppermute(first, axis, down)


def adjoint_kernel(planes_ref, cotangent_ref, *refs):
    adjoint_ref, first_x, last_x, first_y, last_y, held = refs[-6:]
    _, height, width = held.shape
    scale = 1.0 / (X * Y * Z)
    base = pl.program_id(0) * ROWS
    for row, rows, columns in tiles(ROWS, width):
        place = pl.ds(pl.multiple_of(base + row, 16), 16)
        layers = depth_inverse(
            [planes_ref[2 * k, rows, columns].astype(f32) for k in range(KZ)],
            [planes_ref[2 * k + 1, rows, columns].astype(f32) for k in range(KZ)],
        )
        for n in range(Z):
            value = cotangent_ref[0, n, rows, columns] + layers[n] * scale
            adjoint_ref[n, rows, columns] = value
            held[n, place, columns] = value.astype(bf16)

    @pl.when(pl.program_id(0) == pl.num_programs(0) - 1)
    def _():
        first, last = side_columns([held[n] for n in range(Z)])
        first_x[...] = first
        last_x[...] = last
        top = [held[n, 0:16, :].astype(f32)[0:1] for n in range(Z)]
        bottom = [held[n, height - 16 : height, :].astype(f32)[15:16] for n in range(Z)]
        first_y[...] = jnp.concatenate(top, 0).astype(bf16)
        last_y[...] = jnp.concatenate(bottom, 0).astype(bf16)


def make_adjoint(planes, cotangent, component, after):
    _, height, width = planes.shape
    column = jax.ShapeDtypeStruct((Z, height), bf16)
    row = jax.ShapeDtypeStruct((Z, width), bf16)
    column_spec = pl.BlockSpec((Z, height), lambda j: (0, 0))
    row_spec = pl.BlockSpec((Z, width), lambda j: (0, 0))
    return pl.pallas_call(
        adjoint_kernel,
        grid=(height // ROWS,),
        in_specs=[
            pl.BlockSpec((Z, ROWS, width), lambda j: (0, j, 0)),
            pl.BlockSpec((1, Z, ROWS, width), lambda j: (component, 0, j, 0)),
        ]
        + tied(after),
        out_specs=[
            pl.BlockSpec((Z, ROWS, width), lambda j: (0, j, 0)),
            column_spec,
            column_spec,
            row_spec,
            row_spec,
        ],
        out_shape=[
            jax.ShapeDtypeStruct((Z, height, width), f32),
            column,
            column,
            row,
            row,
        ],
        scratch_shapes=[pltpu.VMEM((Z, height, width), bf16)],
        compiler_params=params(),
        cost_estimate=SMALL,
        name="make_adjoint",
    )(planes, cotangent, *after)


def pick_row(rows, n):
    index = lax.broadcasted_iota(jnp.int32, rows.shape, 0)
    return jnp.sum(jnp.where(index == n, rows.astype(f32), 0.0), axis=0, keepdims=True)


def end_rows(low, high, height):
    row = lax.broadcasted_iota(jnp.int32, (height, low.shape[1]), 0)
    return jnp.where(row == 0, low * -0.5, 0.0) + jnp.where(row == height - 1, high * 0.5, 0.0)


LAYERS = 4


def grad_vort_kernel(
    component, slope_x, slope_y, velocity, adjoint, low_x, high_x, low_y, high_y, *refs
):
    before, after = refs
    height, width = velocity.shape[2], velocity.shape[3]
    first = pl.program_id(0) * LAYERS
    ends = spread_columns(low_x[0], high_x[0], first, LAYERS, width)
    layers = velocity[0, pl.ds(first, LAYERS)]
    stacked = layers.reshape(LAYERS * height, width)
    inner = jnp.dot(stacked, slope_x[...], preferred_element_type=f32)
    for k in range(LAYERS):
        n = first + k
        above = lax.rem(n + 1, Z)
        below = lax.rem(n + Z - 1, Z)
        value = adjoint[k]
        half = value * step_size
        along_x = inner[k * height : (k + 1) * height] + ends[k]
        along_y = jnp.dot(slope_y[...], layers[k], preferred_element_type=f32)
        along_y = along_y + end_rows(pick_row(low_y[0], n), pick_row(high_y[0], n), height)
        along_z = (velocity[0, above].astype(f32) - velocity[0, below].astype(f32)) * 0.5
        for j, slope in enumerate((along_x, along_y, along_z)):
            term = half * slope
            if j == component:
                term = term + value
            if before is not None:
                term = before[j, k] + term
            after[j, k] = term


def add_grad_vort(component, slopes, velocity, adjoint, halos, before, after):
    _, _, height, width = velocity.shape
    slope_x, slope_y = slopes
    whole = lambda shape: pl.BlockSpec(shape, lambda n: (0,) * len(shape))
    column = pl.BlockSpec((1, Z, height), lambda n: (component, 0, 0))
    row = pl.BlockSpec((1, Z, width), lambda n: (component, 0, 0))
    sums = pl.BlockSpec((3, LAYERS, height, width), lambda n: (0, n, 0, 0))
    sums_before = pl.BlockSpec((3, LAYERS, height, width), lambda n: (0, n, 0, 0))
    operands = [slope_x, slope_y, velocity, adjoint, *halos]
    in_specs = [
        whole((width, width)),
        whole((height, height)),
        pl.BlockSpec((1, Z, height, width), lambda n: (component, 0, 0, 0)),
        pl.BlockSpec((LAYERS, height, width), lambda n: (n, 0, 0)),
        column,
        column,
        row,
        row,
    ]
    aliases = {}
    if before is not None:
        aliases = {len(operands): 0}
        operands.append(before)
        in_specs.append(sums_before)

    def kernel(*refs):
        grad_vort_kernel(component, *refs[:8], None if before is None else refs[8], refs[-1])

    return pl.pallas_call(
        kernel,
        grid=(Z // LAYERS,),
        in_specs=in_specs + tied(after),
        out_specs=sums,
        out_shape=jax.ShapeDtypeStruct((3, Z, height, width), f32),
        input_output_aliases=aliases,
        compiler_params=params(),
        cost_estimate=SMALL,
        name="add_grad_vort",
    )(*operands, *after)


def grad_vel_kernel(slope_x, vorticity, vorticity_above, vorticity_below, adjoint, *refs):
    vort_low_x, vort_high_x, vort_low_y, vort_high_y, low_x, high_x, low_y, high_y = refs[:8]
    after, padded = refs[-2:]
    _, _, height, width = vorticity.shape
    first = pl.program_id(0) * LAYERS

    def times(one, other):
        return one.astype(f32) * other.astype(f32)

    ends = spread_columns(
        times(vort_low_x[0], low_x[...]),
        times(vort_high_x[0], high_x[...]),
        first,
        LAYERS,
        width,
    )
    values = adjoint[pl.ds(first, LAYERS)]
    product = (vorticity[0].astype(f32) * values).astype(bf16).reshape(LAYERS * height, width)
    inner = jnp.dot(product, slope_x[...], preferred_element_type=f32)
    up = adjoint[lax.rem(first + LAYERS, Z)] * vorticity_above[0, 0].astype(f32)
    down = adjoint[lax.rem(first + Z - 1, Z)] * vorticity_below[0, 0].astype(f32)
    deep = [down] + [vorticity[2, k].astype(f32) * values[k] for k in range(LAYERS)] + [up]
    for k in range(LAYERS):
        n = first + k
        padded[k, 8 : 8 + height, :] = vorticity[1, k].astype(f32) * values[k]
        padded[k, 7:8, :] = pick_row(vort_low_y[0], n) * pick_row(low_y[...], n)
        padded[k, 8 + height : 9 + height, :] = pick_row(vort_high_y[0], n) * pick_row(
            high_y[...], n
        )
        total = (padded[k, 9 : 9 + height, :] - padded[k, 7 : 7 + height, :]) + (
            deep[k + 2] - deep[k]
        )
        total = total * 0.5 + inner[k * height : (k + 1) * height] + ends[k]
        after[0, k] = total * -step_size


def write_grad_vel(component, slope_x, vorticity, adjoint, saved_halos, halos, before, after):
    _, _, height, width = vorticity.shape
    whole = lambda shape: pl.BlockSpec(shape, lambda n: (0,) * len(shape))
    column = whole((Z, height))
    row = whole((Z, width))
    saved_column = pl.BlockSpec((1, Z, height), lambda n: (3, 0, 0))
    saved_row = pl.BlockSpec((1, Z, width), lambda n: (3, 0, 0))
    operands = [slope_x, vorticity, vorticity, vorticity, adjoint, *saved_halos, *halos]
    in_specs = [
        whole((width, width)),
        pl.BlockSpec((3, LAYERS, height, width), lambda n: (0, n, 0, 0)),
        pl.BlockSpec((1, 1, height, width), lambda n: (2, lax.rem((n + 1) * LAYERS, Z), 0, 0)),
        pl.BlockSpec((1, 1, height, width), lambda n: (2, lax.rem(n * LAYERS + Z - 1, Z), 0, 0)),
        whole((Z, height, width)),
        saved_column,
        saved_column,
        saved_row,
        saved_row,
        column,
        column,
        row,
        row,
    ]
    aliases = {}
    if before is not None:
        aliases = {len(operands): 0}
        operands.append(before)
        in_specs.append(pl.BlockSpec(memory_space=pl.ANY))
    return pl.pallas_call(
        grad_vel_kernel,
        grid=(Z // LAYERS,),
        in_specs=in_specs + tied(after),
        out_specs=pl.BlockSpec((1, LAYERS, height, width), lambda n: (component, n, 0, 0)),
        out_shape=jax.ShapeDtypeStruct((3, Z, height, width), f32),
        input_output_aliases=aliases,
        scratch_shapes=[pltpu.VMEM((LAYERS, height + 16, width), f32)],
        compiler_params=params(),
        cost_estimate=SMALL,
        name="write_grad_vel",
    )(*operands, *after)


def pair_exchange(parts, axis, mine):
    count = lax.axis_size(axis)
    kept = lax.dynamic_index_in_dim(parts, mine, 0, keepdims=False)
    sent = lax.dynamic_index_in_dim(parts, 1 - mine, 0, keepdims=False)
    got = lax.ppermute(sent, axis, [(i, i ^ 1) for i in range(count)])
    return jnp.where(mine == 0, jnp.stack([kept, got]), jnp.stack([got, kept]))


def shifted(parts, axis):
    count = lax.axis_size(axis)
    return [parts[0]] + [
        lax.ppermute(parts[s], axis, [(i, (i + s) % count) for i in range(count)])
        for s in range(1, count)
    ]


def local(cot_vort, cot_vel, vorticity, velocity):
    size_x = lax.axis_size("gx")
    size_y = lax.axis_size("gy")
    planes = Z // size_y
    halves = size_y // KZ
    _, _, height, width = cot_vel.shape
    modes = HALF_Y // (size_x * halves)
    place_x = lax.axis_index("gx")
    place_y = lax.axis_index("gy")
    half = lax.rem(place_y, halves)
    me = place_x.astype(jnp.int32).reshape(1)
    where = jnp.stack(
        [(place_x * halves + half) * modes, place_y // halves, place_x]
    ).astype(jnp.int32)

    y_table, y_back_table = y_tables(size_x * halves)
    x_table, x_back_table = x_tables()
    slope_x = slope_matrix(width)
    slope_y = np.ascontiguousarray(slope_matrix(height).T)

    layers = [depth_transform(cot_vel, component) for component in FORWARD_ORDER]

    velocity_first, velocity_last = edge_columns(velocity, 3, (layers[1],))
    vorticity_first, vorticity_last = edge_columns(vorticity, 1, (layers[1],))
    low_x, high_x = exchange(
        jnp.concatenate([velocity_first, vorticity_first]),
        jnp.concatenate([velocity_last, vorticity_last]),
        "gx",
    )
    low_y, high_y = exchange(
        jnp.concatenate([velocity[:, :, 0], vorticity[1:2, :, 0]]),
        jnp.concatenate([velocity[:, :, height - 1], vorticity[1:2, :, height - 1]]),
        "gy",
    )
    saved_halos = (low_x, high_x, low_y, high_y)
    edges = (velocity_first, vorticity_first)

    sent = []
    for place in range(3):
        columns = lax.all_to_all(
            layers[place].reshape(size_y, planes, height, width), "gy", 0, 0, tiled=True
        )
        parts = y_transform(me, y_table, columns, size_x, halves, edges if place == 0 else ())
        if halves == 1:
            parts = [part[0] for part in parts]
        else:
            parts = [pair_exchange(part[:, 0], "gy", half) for part in parts]
        sent.append(parts)
    spectra = {}
    for place, component in enumerate(FORWARD_ORDER):
        after = (sent[2][0],) + saved_halos if place == 0 else ()
        spectra[component] = x_transform(me, x_table, shifted(sent[place], "gx"), after)

    returned = {}
    after = (spectra[FORWARD_ORDER[2]],)
    for component in BACK_ORDER:
        parts = curl_inverse(where, x_back_table, spectra, component, size_x, after)
        after = (parts[0],)
        parts = shifted(parts, "gx")
        if halves == 1:
            parts = [part[None] for part in parts]
        else:
            parts = [pair_exchange(part, "gy", half)[:, None] for part in parts]
        returned[component] = parts
    last_curl = after

    def rows_of(component, after):
        return y_inverse(me, y_back_table, returned[component], size_y, after)

    def adjoint_of(component, rows, after):
        layers = lax.all_to_all(rows, "gy", 0, 0, tiled=True)
        adjoint, first_x, last_x, first_y, last_y = make_adjoint(
            layers.reshape(Z, height, width), cot_vort, component, after
        )
        return adjoint, exchange(first_x, last_x, "gx") + exchange(first_y, last_y, "gy")

    def vort_of(component, adjoint, before, after):
        return add_grad_vort(
            component, (slope_x, slope_y), velocity, adjoint, saved_halos, before, after
        )

    def vel_of(component, adjoint, halos, before, after):
        return write_grad_vel(
            component, slope_x, vorticity, adjoint, saved_halos, halos, before, after
        )

    one, two, three = BACK_ORDER
    rows_one = rows_of(one, last_curl)
    adjoint_one, halos_one = adjoint_of(one, rows_one, ())
    rows_two = rows_of(two, (adjoint_one,))
    grad_vort = vort_of(one, adjoint_one, None, (rows_two,))
    grad_vel = vel_of(one, adjoint_one, halos_one, None, (grad_vort,))
    adjoint_two, halos_two = adjoint_of(two, rows_two, (grad_vel,))
    rows_three = rows_of(three, (adjoint_two,))
    grad_vort = vort_of(two, adjoint_two, grad_vort, (rows_three,))
    grad_vel = vel_of(two, adjoint_two, halos_two, grad_vel, (grad_vort,))
    adjoint_three, halos_three = adjoint_of(three, rows_three, (grad_vel,))
    grad_vort = vort_of(three, adjoint_three, grad_vort, ())
    grad_vel = vel_of(three, adjoint_three, halos_three, grad_vel, (grad_vort,))
    return grad_vort, grad_vel


def solution(mesh):
    spec = P(None, None, "gy", "gx")
    return jax.shard_map(
        local,
        mesh=mesh,
        in_specs=(spec, spec, spec, spec),
        out_specs=(spec, spec),
        check_vma=False,
    )
```

```python
import math

import jax
import jax.numpy as jnp
import ml_dtypes
import numpy as np
from jax import lax
from jax.experimental import pallas as pl
from jax.experimental.pallas import tpu as pltpu
from jax.sharding import PartitionSpec as P

X = 1024
Y = 1536
Z = 16
HALF_X = X // 2
HALF_Y = Y // 2
KZ = Z // 2

step_size = 0.5

f32 = jnp.float32
bf16 = jnp.bfloat16

FORWARD_ORDER = (0, 1, 2)
BACK_ORDER = (2, 0, 1)


def params(megabytes=56):
    return pltpu.CompilerParams(vmem_limit_bytes=megabytes * 1024 * 1024)


def takes(microseconds):
    return pl.CostEstimate(flops=1, bytes_accessed=int(microseconds * 3.0e6), transcendentals=0)


def tied(after):
    return [pl.BlockSpec(memory_space=pl.ANY)] * len(after)


def trig(first, second, length):
    angle = (np.outer(first, second) % length) * (2.0 * math.pi / length)
    return np.cos(angle), np.sin(angle)


def y_tables(blocks):
    cosine, sine = trig(np.arange(HALF_Y), np.arange(Y), Y)
    both = np.stack([cosine.reshape(blocks, -1, Y), sine.reshape(blocks, -1, Y)], 1).reshape(Y, Y)
    both = both.astype(ml_dtypes.bfloat16)
    return both, np.ascontiguousarray(both.T)


def x_tables():
    cosine, sine = trig(np.arange(X), np.arange(HALF_X), X)
    both = np.concatenate([cosine, sine], 1).astype(ml_dtypes.bfloat16)
    return both, np.ascontiguousarray(both.T)


def slope_matrix(size):
    return ((np.eye(size, k=-1) - np.eye(size, k=1)) * 0.5).astype(ml_dtypes.bfloat16)


def combine(terms):
    total = None
    for factor, value in terms:
        if abs(factor) < 1e-12:
            continue
        if abs(factor - 1.0) < 1e-12:
            part = value
        elif abs(factor + 1.0) < 1e-12:
            part = -value
        else:
            part = value * factor
        total = part if total is None else total + part
    return total


def depth_forward(values):
    even = [values[0]] + [values[n] + values[Z - n] for n in range(1, 8)] + [values[8]]
    odd = [None] + [values[n] - values[Z - n] for n in range(1, 8)]
    even_sum = [even[n] + even[8 - n] for n in range(4)] + [even[4]]
    even_dif = [even[n] - even[8 - n] for n in range(4)]
    odd_sum = [None] + [odd[n] + odd[8 - n] for n in range(1, 4)] + [odd[4]]
    odd_dif = [None] + [odd[n] - odd[8 - n] for n in range(1, 4)]
    result = []
    for k in range(KZ):
        folded = even_sum if k % 2 == 0 else even_dif
        cos_part = combine([(math.cos(math.pi * k * n / 8), folded[n]) for n in range(len(folded))])
        folded = odd_dif if k % 2 == 0 else odd_sum
        sin_part = combine(
            [(math.sin(math.pi * k * n / 8), folded[n]) for n in range(1, len(folded))]
        )
        result.append((cos_part, sin_part))
    return result


def depth_inverse(cos_parts, sin_parts):
    layers = [None] * Z
    cos_sum, sin_sum = [None] * 9, [None] * 9
    for n in range(5):
        evens = combine([(math.cos(math.pi * k * n / 8), cos_parts[k]) for k in range(0, KZ, 2)])
        odds = combine([(math.cos(math.pi * k * n / 8), cos_parts[k]) for k in range(1, KZ, 2)])
        if n == 4:
            cos_sum[4] = evens
        else:
            cos_sum[n] = evens + odds
            cos_sum[8 - n] = evens - odds
    for n in range(1, 5):
        evens = combine([(math.sin(math.pi * k * n / 8), sin_parts[k]) for k in range(0, KZ, 2)])
        odds = combine([(math.sin(math.pi * k * n / 8), sin_parts[k]) for k in range(1, KZ, 2)])
        if n == 4:
            sin_sum[4] = odds
        else:
            sin_sum[n] = odds + evens
            sin_sum[8 - n] = odds - evens
    layers[0], layers[8] = cos_sum[0], cos_sum[8]
    for n in range(1, 8):
        layers[n] = cos_sum[n] + sin_sum[n]
        layers[Z - n] = cos_sum[n] - sin_sum[n]
    return layers


ROWS = 96


def tiles(height, width):
    for row in range(0, height, 16):
        for column in range(0, width, 128):
            yield row, pl.ds(row, 16), pl.ds(column, 128)


def depth_forward_kernel(values_ref, planes_ref):
    _, _, height, width = values_ref.shape
    for _, rows, columns in tiles(height, width):
        spectrum = depth_forward([values_ref[0, n, rows, columns] for n in range(Z)])
        for k, (cos_part, sin_part) in enumerate(spectrum):
            planes_ref[2 * k, rows, columns] = cos_part.astype(bf16)
            if sin_part is None:
                sin_part = jnp.zeros_like(cos_part)
            planes_ref[2 * k + 1, rows, columns] = sin_part.astype(bf16)


def depth_transform(values, component, me=None, size_y=1, after=()):
    _, _, height, width = values.shape
    planes = Z // size_y
    shifted_out = me is not None

    def kernel(*refs):
        if not shifted_out:
            depth_forward_kernel(*refs)
            return
        me_ref, values_ref, outs, held = refs[0], refs[1], refs[2 + len(after) : -1], refs[-1]
        depth_forward_kernel(values_ref, held)
        for s, out in enumerate(outs):
            target = lax.rem(me_ref[0] + s, size_y)
            out[...] = held[pl.ds(target * planes, planes)]

    block = (Z // size_y, ROWS, width)
    out_spec = pl.BlockSpec(block, lambda j: (0, j, 0))
    out_shape = jax.ShapeDtypeStruct((planes, height, width), bf16)
    smem = pl.BlockSpec(memory_space=pltpu.SMEM)
    return pl.pallas_call(
        kernel,
        grid=(height // ROWS,),
        in_specs=([smem] if shifted_out else [])
        + [pl.BlockSpec((1, Z, ROWS, width), lambda j: (component, 0, j, 0))]
        + tied(after),
        out_specs=[out_spec] * size_y if shifted_out else out_spec,
        out_shape=[out_shape] * size_y if shifted_out else out_shape,
        scratch_shapes=[pltpu.VMEM((Z, ROWS, width), bf16)] if shifted_out else [],
        compiler_params=params(),
        cost_estimate=takes(3),
        name="depth_transform",
    )(*(([me] if shifted_out else []) + [values, *after]))


def fetch_blocks(table_ref, held, arrived, order):
    count, rows, _ = held.shape
    copies = []
    for s in range(count):
        place = pl.ds(pl.multiple_of(order(s) * rows, rows), rows)
        copies.append(pltpu.make_async_copy(table_ref.at[place], held.at[s], arrived.at[s]))
        copies[s].start()
    return copies


def y_transform(me, table, columns, blocks, halves, after):
    whole = len(columns) == 1
    size_y = columns[0].shape[0] if whole else len(columns)
    planes, height, width = columns[0].shape[-3:]
    modes = HALF_Y // (blocks * halves)
    rows = Y // blocks

    def kernel(me_ref, table_ref, *refs):
        parts = refs[: len(columns)]
        out, held, arrived, lines = refs[-4:]
        copies = fetch_blocks(table_ref, held, arrived, lambda s: s)
        for s in range(size_y):
            source = lax.rem(me_ref[0] + size_y - s, size_y)
            for plane in range(planes):
                if whole:
                    lines[plane, s * height : (s + 1) * height, :] = parts[0][s, plane]
                else:
                    place = pl.ds(pl.multiple_of(source * height, height), height)
                    lines[plane, place, :] = parts[s][plane]
        for s in range(blocks):
            copies[s].wait()
            for plane in range(planes):
                part = jnp.dot(held[s], lines[plane], preferred_element_type=f32)
                out[s, :, plane] = part.astype(bf16).reshape(halves, 2, modes, width)

    vmem = pl.BlockSpec(memory_space=pltpu.VMEM)
    return pl.pallas_call(
        kernel,
        in_specs=[pl.BlockSpec(memory_space=pltpu.SMEM), pl.BlockSpec(memory_space=pl.ANY)]
        + [vmem] * len(columns)
        + tied(after),
        out_specs=vmem,
        out_shape=jax.ShapeDtypeStruct((blocks, halves, planes, 2, modes, width), bf16),
        scratch_shapes=[
            pltpu.VMEM((blocks, rows, Y), bf16),
            pltpu.SemaphoreType.DMA((blocks,)),
            pltpu.VMEM((planes, Y, width), bf16),
        ],
        compiler_params=params(),
        cost_estimate=takes(5),
        name="y_transform",
    )(me, table, *columns, *after)


def y_inverse(me, table, modes, size_y, split, after):
    planes, width = modes.shape[2], modes.shape[5]
    height = Y // size_y
    shape = (planes, height, width)

    def kernel(me_ref, table_ref, modes_ref, *refs):
        outs, held, arrived = refs[len(after) : -2], refs[-2], refs[-1]
        copies = fetch_blocks(
            table_ref, held, arrived, lambda s: lax.rem(me_ref[0] + s, size_y) if split else s
        )
        lines = [modes_ref[:, :, plane].reshape(Y, width) for plane in range(planes)]
        for s in range(size_y):
            copies[s].wait()
            for plane in range(planes):
                rows = jnp.dot(held[s], lines[plane], preferred_element_type=f32).astype(bf16)
                if split:
                    outs[s][plane] = rows
                else:
                    outs[0][s, plane] = rows

    vmem = pl.BlockSpec(memory_space=pltpu.VMEM)
    if split:
        out_shape = [jax.ShapeDtypeStruct(shape, bf16)] * size_y
    else:
        out_shape = [jax.ShapeDtypeStruct((size_y,) + shape, bf16)]
    return pl.pallas_call(
        kernel,
        in_specs=[
            pl.BlockSpec(memory_space=pltpu.SMEM),
            pl.BlockSpec(memory_space=pl.ANY),
            vmem,
        ]
        + tied(after),
        out_specs=[vmem] * len(out_shape),
        out_shape=out_shape,
        scratch_shapes=[
            pltpu.VMEM((size_y, height, Y), bf16),
            pltpu.SemaphoreType.DMA((size_y,)),
        ],
        compiler_params=params(),
        cost_estimate=takes(4),
        name="y_inverse",
    )(me, table, modes, *after)


def x_transform(table, modes, after):
    blocks, _, _, count, width = modes.shape

    def kernel(table_ref, modes_ref, *refs):
        spectrum_ref = refs[-1]
        rows = jnp.concatenate(
            [modes_ref[block, 0].reshape(2 * count, width) for block in range(blocks)], axis=1
        )
        spectrum = jnp.dot(rows, table_ref[...], preferred_element_type=f32)
        spectrum_ref[0] = spectrum.reshape(2, count, X)

    return pl.pallas_call(
        kernel,
        grid=(2,),
        in_specs=[
            pl.BlockSpec((X, X), lambda j: (0, 0)),
            pl.BlockSpec((blocks, 1, 2, count, width), lambda j: (0, j, 0, 0, 0)),
        ]
        + tied(after),
        out_specs=pl.BlockSpec((1, 2, count, X), lambda j: (j, 0, 0, 0)),
        out_shape=jax.ShapeDtypeStruct((2, 2, count, X), f32),
        compiler_params=params(24),
        cost_estimate=takes(3),
        name="x_transform",
    )(table, modes, *after)


def turned(field, axis, tz, ty, tx, wave):
    index = [tz, ty, tx]
    sign = 1.0 if index[axis] == 0 else -1.0
    index[axis] = 1 - index[axis]
    value = field[index[0], index[1], :, index[2] * HALF_X : (index[2] + 1) * HALF_X]
    return value * (wave * sign)


CURL = {
    0: ((1, 2), (0, 1)),
    1: ((0, 0), (2, 2)),
    2: ((2, 1), (1, 0)),
}


def curl_kernel(axes, where_ref, table_ref, plus_ref, minus_ref, back_ref):
    blocks, _, _, count, width = back_ref.shape
    base = where_ref[0] + pl.program_id(0) * count
    depth = where_ref[1]
    mode_y = lax.broadcasted_iota(jnp.int32, (count, HALF_X), 0) + base
    mode_x = lax.broadcasted_iota(jnp.int32, (count, HALF_X), 1)
    wave_y = mode_y.astype(f32) * (2.0 * math.pi / Y)
    wave_x = mode_x.astype(f32) * (2.0 * math.pi / X)
    wave_z = jnp.full((count, HALF_X), depth, jnp.int32).astype(f32) * (2.0 * math.pi / Z)
    square = wave_x * wave_x + wave_y * wave_y + wave_z * wave_z
    doubling = (
        jnp.where(mode_x == 0, 1.0, 2.0)
        * jnp.where(mode_y == 0, 1.0, 2.0)
        * jnp.where(wave_z == 0.0, 1.0, 2.0)
    )
    weight = jnp.where(square > 0, doubling / jnp.where(square > 0, square, 1.0), 0.0)
    waves = [wave_z * weight, wave_y * weight, wave_x * weight]
    rows = []
    for tz in range(2):
        for ty in range(2):
            parts = []
            for tx in range(2):
                parts.append(
                    (
                        turned(plus_ref, axes[0], tz, ty, tx, waves[axes[0]])
                        - turned(minus_ref, axes[1], tz, ty, tx, waves[axes[1]])
                    ).astype(bf16)
                )
            rows.append(jnp.concatenate(parts, axis=1))
    rows = jnp.concatenate(rows, axis=0)
    back = jnp.dot(rows, table_ref[...], preferred_element_type=f32).astype(bf16)
    for block in range(blocks):
        back_ref[block] = back[:, block * width : (block + 1) * width].reshape(2, 2, count, width)


def curl_inverse(where, table, spectra, component, blocks, after):
    (plus_axis, plus), (minus_axis, minus) = CURL[component]
    total = spectra[plus].shape[2]
    width = X // blocks
    count = 96 if total % 96 == 0 else total
    spec = pl.BlockSpec((2, 2, count, X), lambda j: (0, 0, j, 0))

    def kernel(*refs):
        curl_kernel((plus_axis, minus_axis), *refs[:4], refs[-1])

    return pl.pallas_call(
        kernel,
        grid=(total // count,),
        in_specs=[
            pl.BlockSpec(memory_space=pltpu.SMEM),
            pl.BlockSpec((X, X), lambda j: (0, 0)),
            spec,
            spec,
        ]
        + tied(after),
        out_specs=pl.BlockSpec((blocks, 2, 2, count, width), lambda j: (0, 0, 0, j, 0)),
        out_shape=jax.ShapeDtypeStruct((blocks, 2, 2, total, width), bf16),
        compiler_params=params(24),
        cost_estimate=takes(4),
        name="curl_inverse",
    )(where, table, spectra[plus], spectra[minus], *after)


def side_columns(planes):
    width = planes[0].shape[1]
    row = lax.broadcasted_iota(jnp.int32, (2 * Z, width), 0)
    lane = lax.broadcasted_iota(jnp.int32, (2 * Z, width), 1)
    total = None
    for n in range(Z):
        pick = ((row == n) & (lane == 0)) | ((row == n + Z) & (lane == width - 1))
        part = lax.dot_general(
            pick.astype(f32).astype(bf16),
            planes[n],
            (((1,), (1,)), ((), ())),
            preferred_element_type=f32,
        )
        total = part if total is None else total + part
    return total[:Z].astype(bf16), total[Z:].astype(bf16)


def spread_columns(low, high, first, layers, width):
    row = lax.broadcasted_iota(jnp.int32, (2 * Z, layers * width), 0)
    column = lax.broadcasted_iota(jnp.int32, (2 * Z, layers * width), 1)
    place = jnp.zeros((2 * Z, layers * width), f32)
    for n in range(layers):
        place = place + jnp.where((row == first + n) & (column == n * width), -0.5, 0.0)
        place = place + jnp.where(
            (row == first + n + Z) & (column == (n + 1) * width - 1), 0.5, 0.0
        )
    both = jnp.concatenate([low, high], axis=0).astype(bf16)
    spread = lax.dot_general(
        both, place.astype(bf16), (((0,), (0,)), ((), ())), preferred_element_type=f32
    )
    return [spread[:, n * width : (n + 1) * width] for n in range(layers)]


def edges_kernel(field_ref, *refs):
    first_column_ref, last_column_ref = refs[-2:]
    first, last = side_columns([field_ref[0, n] for n in range(Z)])
    first_column_ref[0] = first
    last_column_ref[0] = last


def edge_columns(field, components, after):
    _, _, height, width = field.shape
    shape = jax.ShapeDtypeStruct((components, Z, height), bf16)
    spec = pl.BlockSpec((1, Z, height), lambda i: (i, 0, 0))
    return pl.pallas_call(
        edges_kernel,
        grid=(components,),
        in_specs=[pl.BlockSpec((1, Z, height, width), lambda i: (i, 0, 0, 0))] + tied(after),
        out_specs=[spec, spec],
        out_shape=[shape, shape],
        compiler_params=params(),
        cost_estimate=takes(4),
        name="edge_columns",
    )(field, *after)


def exchange(first, last, axis):
    count = lax.axis_size(axis)
    up = [(i, (i + 1) % count) for i in range(count)]
    down = [((i + 1) % count, i) for i in range(count)]
    return lax.ppermute(last, axis, up), lax.ppermute(first, axis, down)


def adjoint_kernel(planes_ref, cotangent_ref, *refs):
    adjoint_ref, first_x, last_x, first_y, last_y, held = refs
    _, height, width = held.shape
    scale = 1.0 / (X * Y * Z)
    base = pl.program_id(0) * ROWS
    for row, rows, columns in tiles(ROWS, width):
        place = pl.ds(pl.multiple_of(base + row, 16), 16)
        layers = depth_inverse(
            [planes_ref[2 * k, rows, columns].astype(f32) for k in range(KZ)],
            [planes_ref[2 * k + 1, rows, columns].astype(f32) for k in range(KZ)],
        )
        for n in range(Z):
            value = cotangent_ref[0, n, rows, columns] + layers[n] * scale
            adjoint_ref[n, rows, columns] = value
            held[n, place, columns] = value.astype(bf16)

    @pl.when(pl.program_id(0) == pl.num_programs(0) - 1)
    def _():
        first, last = side_columns([held[n] for n in range(Z)])
        first_x[...] = first
        last_x[...] = last
        top = [held[n, 0:16, :].astype(f32)[0:1] for n in range(Z)]
        bottom = [held[n, height - 16 : height, :].astype(f32)[15:16] for n in range(Z)]
        first_y[...] = jnp.concatenate(top, 0).astype(bf16)
        last_y[...] = jnp.concatenate(bottom, 0).astype(bf16)


def make_adjoint(me, parts, cotangent, component, after):
    whole = len(parts) == 1
    planes, height, width = parts[0].shape
    column = jax.ShapeDtypeStruct((Z, height), bf16)
    row = jax.ShapeDtypeStruct((Z, width), bf16)
    column_spec = pl.BlockSpec((Z, height), lambda j: (0, 0))
    row_spec = pl.BlockSpec((Z, width), lambda j: (0, 0))

    def kernel(me_ref, *refs):
        part_refs, cotangent_ref = refs[: len(parts)], refs[len(parts)]
        outs, held, spectrum = refs[-7:-2], refs[-2], refs[-1]
        if whole:
            spectrum = part_refs[0]
        else:
            for s, part in enumerate(part_refs):
                source = lax.rem(me_ref[0] + len(parts) - s, len(parts))
                spectrum[pl.ds(source * planes, planes)] = part[...]
        adjoint_kernel(spectrum, cotangent_ref, *outs, held)

    return pl.pallas_call(
        kernel,
        grid=(height // ROWS,),
        in_specs=[pl.BlockSpec(memory_space=pltpu.SMEM)]
        + [pl.BlockSpec((planes, ROWS, width), lambda j: (0, j, 0))] * len(parts)
        + [pl.BlockSpec((1, Z, ROWS, width), lambda j: (component, 0, j, 0))]
        + tied(after),
        out_specs=[
            pl.BlockSpec((Z, ROWS, width), lambda j: (0, j, 0)),
            column_spec,
            column_spec,
            row_spec,
            row_spec,
        ],
        out_shape=[
            jax.ShapeDtypeStruct((Z, height, width), f32),
            column,
            column,
            row,
            row,
        ],
        scratch_shapes=[
            pltpu.VMEM((Z, height, width), bf16),
            pltpu.VMEM((Z, ROWS, width), bf16),
        ],
        compiler_params=params(),
        cost_estimate=takes(5),
        name="make_adjoint",
    )(me, *parts, cotangent, *after)


def pick_row(rows, n):
    index = lax.broadcasted_iota(jnp.int32, rows.shape, 0)
    return jnp.sum(jnp.where(index == n, rows.astype(f32), 0.0), axis=0, keepdims=True)


def end_rows(low, high, height):
    row = lax.broadcasted_iota(jnp.int32, (height, low.shape[1]), 0)
    return jnp.where(row == 0, low * -0.5, 0.0) + jnp.where(row == height - 1, high * 0.5, 0.0)


LAYERS = 4


def grad_vort_kernel(
    component, slope_x, slope_y, velocity, adjoint, low_x, high_x, low_y, high_y, *refs
):
    before, after = refs
    height, width = velocity.shape[2], velocity.shape[3]
    first = pl.program_id(0) * LAYERS
    ends = spread_columns(low_x[0], high_x[0], first, LAYERS, width)
    layers = velocity[0, pl.ds(first, LAYERS)]
    stacked = layers.reshape(LAYERS * height, width)
    inner = jnp.dot(stacked, slope_x[...], preferred_element_type=f32)
    for k in range(LAYERS):
        n = first + k
        above = lax.rem(n + 1, Z)
        below = lax.rem(n + Z - 1, Z)
        value = adjoint[k]
        half = value * step_size
        along_x = inner[k * height : (k + 1) * height] + ends[k]
        along_y = jnp.dot(slope_y[...], layers[k], preferred_element_type=f32)
        along_y = along_y + end_rows(pick_row(low_y[0], n), pick_row(high_y[0], n), height)
        along_z = (velocity[0, above].astype(f32) - velocity[0, below].astype(f32)) * 0.5
        for j, slope in enumerate((along_x, along_y, along_z)):
            term = half * slope
            if j == component:
                term = term + value
            if before is not None:
                term = before[j, k] + term
            after[j, k] = term


def add_grad_vort(component, slopes, velocity, adjoint, halos, before, after):
    _, _, height, width = velocity.shape
    slope_x, slope_y = slopes
    whole = lambda shape: pl.BlockSpec(shape, lambda n: (0,) * len(shape))
    column = pl.BlockSpec((1, Z, height), lambda n: (component, 0, 0))
    row = pl.BlockSpec((1, Z, width), lambda n: (component, 0, 0))
    sums = pl.BlockSpec((3, LAYERS, height, width), lambda n: (0, n, 0, 0))
    sums_before = pl.BlockSpec((3, LAYERS, height, width), lambda n: (0, n, 0, 0))
    operands = [slope_x, slope_y, velocity, adjoint, *halos]
    in_specs = [
        whole((width, width)),
        whole((height, height)),
        pl.BlockSpec((1, Z, height, width), lambda n: (component, 0, 0, 0)),
        pl.BlockSpec((LAYERS, height, width), lambda n: (n, 0, 0)),
        column,
        column,
        row,
        row,
    ]
    aliases = {}
    if before is not None:
        aliases = {len(operands): 0}
        operands.append(before)
        in_specs.append(sums_before)

    def kernel(*refs):
        grad_vort_kernel(component, *refs[:8], None if before is None else refs[8], refs[-1])

    return pl.pallas_call(
        kernel,
        grid=(Z // LAYERS,),
        in_specs=in_specs + tied(after),
        out_specs=sums,
        out_shape=jax.ShapeDtypeStruct((3, Z, height, width), f32),
        input_output_aliases=aliases,
        compiler_params=params(),
        cost_estimate=takes(9),
        name="add_grad_vort",
    )(*operands, *after)


def grad_vel_kernel(slope_x, vorticity, vorticity_above, vorticity_below, adjoint, *refs):
    vort_low_x, vort_high_x, vort_low_y, vort_high_y, low_x, high_x, low_y, high_y = refs[:8]
    after, padded = refs[-2:]
    _, _, height, width = vorticity.shape
    first = pl.program_id(0) * LAYERS

    def times(one, other):
        return one.astype(f32) * other.astype(f32)

    ends = spread_columns(
        times(vort_low_x[0], low_x[...]),
        times(vort_high_x[0], high_x[...]),
        first,
        LAYERS,
        width,
    )
    values = adjoint[pl.ds(first, LAYERS)]
    product = (vorticity[0].astype(f32) * values).astype(bf16).reshape(LAYERS * height, width)
    inner = jnp.dot(product, slope_x[...], preferred_element_type=f32)
    up = adjoint[lax.rem(first + LAYERS, Z)] * vorticity_above[0, 0].astype(f32)
    down = adjoint[lax.rem(first + Z - 1, Z)] * vorticity_below[0, 0].astype(f32)
    deep = [down] + [vorticity[2, k].astype(f32) * values[k] for k in range(LAYERS)] + [up]
    for k in range(LAYERS):
        n = first + k
        padded[k, 8 : 8 + height, :] = vorticity[1, k].astype(f32) * values[k]
        padded[k, 7:8, :] = pick_row(vort_low_y[0], n) * pick_row(low_y[...], n)
        padded[k, 8 + height : 9 + height, :] = pick_row(vort_high_y[0], n) * pick_row(
            high_y[...], n
        )
        total = (padded[k, 9 : 9 + height, :] - padded[k, 7 : 7 + height, :]) + (
            deep[k + 2] - deep[k]
        )
        total = total * 0.5 + inner[k * height : (k + 1) * height] + ends[k]
        after[0, k] = total * -step_size


def write_grad_vel(component, slope_x, vorticity, adjoint, saved_halos, halos, before, after):
    _, _, height, width = vorticity.shape
    whole = lambda shape: pl.BlockSpec(shape, lambda n: (0,) * len(shape))
    column = whole((Z, height))
    row = whole((Z, width))
    saved_column = pl.BlockSpec((1, Z, height), lambda n: (3, 0, 0))
    saved_row = pl.BlockSpec((1, Z, width), lambda n: (3, 0, 0))
    operands = [slope_x, vorticity, vorticity, vorticity, adjoint, *saved_halos, *halos]
    in_specs = [
        whole((width, width)),
        pl.BlockSpec((3, LAYERS, height, width), lambda n: (0, n, 0, 0)),
        pl.BlockSpec((1, 1, height, width), lambda n: (2, lax.rem((n + 1) * LAYERS, Z), 0, 0)),
        pl.BlockSpec((1, 1, height, width), lambda n: (2, lax.rem(n * LAYERS + Z - 1, Z), 0, 0)),
        whole((Z, height, width)),
        saved_column,
        saved_column,
        saved_row,
        saved_row,
        column,
        column,
        row,
        row,
    ]
    aliases = {}
    if before is not None:
        aliases = {len(operands): 0}
        operands.append(before)
        in_specs.append(pl.BlockSpec(memory_space=pl.ANY))
    return pl.pallas_call(
        grad_vel_kernel,
        grid=(Z // LAYERS,),
        in_specs=in_specs + tied(after),
        out_specs=pl.BlockSpec((1, LAYERS, height, width), lambda n: (component, n, 0, 0)),
        out_shape=jax.ShapeDtypeStruct((3, Z, height, width), f32),
        input_output_aliases=aliases,
        scratch_shapes=[pltpu.VMEM((LAYERS, height + 16, width), f32)],
        compiler_params=params(),
        cost_estimate=takes(7),
        name="write_grad_vel",
    )(*operands, *after)


def pair_exchange(parts, axis, mine):
    count = lax.axis_size(axis)
    kept = lax.dynamic_index_in_dim(parts, mine, 1, keepdims=False)
    sent = lax.dynamic_index_in_dim(parts, 1 - mine, 1, keepdims=False)
    got = lax.ppermute(sent, axis, [(i, i ^ 1) for i in range(count)])
    return jnp.where(mine == 0, jnp.stack([kept, got], 1), jnp.stack([got, kept], 1))


def shifted(parts, axis):
    count = lax.axis_size(axis)
    return [parts[0]] + [
        lax.ppermute(parts[s], axis, [(i, (i + s) % count) for i in range(count)])
        for s in range(1, count)
    ]


def local(cot_vort, cot_vel, vorticity, velocity):
    size_x = lax.axis_size("gx")
    size_y = lax.axis_size("gy")
    planes = Z // size_y
    halves = size_y // KZ
    _, _, height, width = cot_vel.shape
    modes = HALF_Y // (size_x * halves)
    place_x = lax.axis_index("gx")
    place_y = lax.axis_index("gy")
    half = lax.rem(place_y, halves)
    me = place_y.astype(jnp.int32).reshape(1)
    where = jnp.stack([(place_x * halves + half) * modes, place_y // halves]).astype(jnp.int32)

    y_table, y_back_table = y_tables(size_x * halves)
    x_table, x_back_table = x_tables()
    slope_x = slope_matrix(width)
    slope_y = np.ascontiguousarray(slope_matrix(height).T)

    layers = [depth_transform(cot_vel, FORWARD_ORDER[0])]
    layers.append(depth_transform(cot_vel, FORWARD_ORDER[1], me, size_y, (layers[0],)))
    layers.append(depth_transform(cot_vel, FORWARD_ORDER[2], me, size_y, (layers[1][0],)))

    velocity_first, velocity_last = edge_columns(velocity, 3, (layers[0],))
    vorticity_first, vorticity_last = edge_columns(vorticity, 1, (layers[0],))
    low_x, high_x = exchange(
        jnp.concatenate([velocity_first, vorticity_first]),
        jnp.concatenate([velocity_last, vorticity_last]),
        "gx",
    )
    low_y, high_y = exchange(
        jnp.concatenate([velocity[:, :, 0], vorticity[1:2, :, 0]]),
        jnp.concatenate([velocity[:, :, height - 1], vorticity[1:2, :, height - 1]]),
        "gy",
    )
    saved_halos = (low_x, high_x, low_y, high_y)
    edges = (velocity_first, vorticity_first)

    sent = []
    for place in range(3):
        if place == 0:
            columns = layers[0].reshape(size_y, planes, height, width)
            columns = [lax.all_to_all(columns, "gy", 0, 0, tiled=True)]
        else:
            columns = shifted(layers[place], "gy")
        parts = y_transform(me, y_table, columns, size_x, halves, edges if place == 0 else ())
        parts = parts.reshape(size_x, 2, 2, modes, width)
        sent.append(parts if halves == 1 else pair_exchange(parts, "gy", half))
    spectra = {}
    for place, component in enumerate(FORWARD_ORDER):
        lines = lax.all_to_all(sent[place], "gx", 0, 0, tiled=True)
        spectra[component] = x_transform(x_table, lines, saved_halos if place == 1 else ())

    returned = {}
    after = (sent[2],)
    for component in BACK_ORDER:
        parts = curl_inverse(where, x_back_table, spectra, component, size_x, after)
        after = (parts,)
        parts = lax.all_to_all(parts, "gx", 0, 0, tiled=True)
        if halves == 2:
            parts = pair_exchange(parts, "gy", half)
        returned[component] = parts.reshape(size_x, halves, planes, 2, modes, width)

    def rows_of(component, after):
        split = component != BACK_ORDER[2]
        return y_inverse(me, y_back_table, returned[component], size_y, split, after)

    def adjoint_of(component, rows, after):
        if len(rows) == 1:
            parts = [lax.all_to_all(rows[0], "gy", 0, 0, tiled=True).reshape(Z, height, width)]
        else:
            parts = shifted(rows, "gy")
        adjoint, first_x, last_x, first_y, last_y = make_adjoint(
            me, parts, cot_vort, component, after
        )
        return adjoint, exchange(first_x, last_x, "gx") + exchange(first_y, last_y, "gy")

    def vort_of(component, adjoint, before, after):
        return add_grad_vort(
            component, (slope_x, slope_y), velocity, adjoint, saved_halos, before, after
        )

    def vel_of(component, adjoint, halos, before, after):
        return write_grad_vel(
            component, slope_x, vorticity, adjoint, saved_halos, halos, before, after
        )

    one, two, three = BACK_ORDER
    rows_one = rows_of(one, ())
    adjoint_one, halos_one = adjoint_of(one, rows_one, ())
    rows_two = rows_of(two, ())
    grad_vort = vort_of(one, adjoint_one, None, (rows_two[0],))
    adjoint_two, halos_two = adjoint_of(two, rows_two, (grad_vort,))
    rows_three = rows_of(three, (adjoint_two,))
    grad_vel = vel_of(one, adjoint_one, halos_one, None, (rows_three[0],))
    grad_vort = vort_of(two, adjoint_two, grad_vort, (grad_vel,))
    grad_vel = vel_of(two, adjoint_two, halos_two, grad_vel, (grad_vort,))
    adjoint_three, halos_three = adjoint_of(three, rows_three, (grad_vel,))
    grad_vort = vort_of(three, adjoint_three, grad_vort, ())
    grad_vel = vel_of(three, adjoint_three, halos_three, grad_vel, (grad_vort,))
    return grad_vort, grad_vel


def solution(mesh):
    spec = P(None, None, "gy", "gx")
    return jax.shard_map(
        local,
        mesh=mesh,
        in_specs=(spec, spec, spec, spec),
        out_specs=(spec, spec),
        check_vma=False,
    )
```

```python
import math

import jax
import jax.numpy as jnp
import ml_dtypes
import numpy as np
from jax import lax
from jax.experimental import pallas as pl
from jax.experimental.pallas import tpu as pltpu
from jax.sharding import PartitionSpec as P

X = 1024
Y = 1536
Z = 16
HALF_X = X // 2
HALF_Y = Y // 2
KZ = Z // 2

step_size = 0.5

f32 = jnp.float32
bf16 = jnp.bfloat16

FORWARD_ORDER = (0, 1, 2)
BACK_ORDER = (2, 0, 1)


def params(megabytes=56):
    return pltpu.CompilerParams(vmem_limit_bytes=megabytes * 1024 * 1024)


def takes(microseconds):
    return pl.CostEstimate(flops=1, bytes_accessed=int(microseconds * 3.0e6), transcendentals=0)


def tied(after):
    return [pl.BlockSpec(memory_space=pl.ANY)] * len(after)


def trig(first, second, length):
    angle = (np.outer(first, second) % length) * (2.0 * math.pi / length)
    return np.cos(angle), np.sin(angle)


def y_tables(blocks):
    cosine, sine = trig(np.arange(HALF_Y), np.arange(Y), Y)
    both = np.stack([cosine.reshape(blocks, -1, Y), sine.reshape(blocks, -1, Y)], 1).reshape(Y, Y)
    both = both.astype(ml_dtypes.bfloat16)
    return both, np.ascontiguousarray(both.T)


def x_tables():
    cosine, sine = trig(np.arange(X), np.arange(HALF_X), X)
    both = np.concatenate([cosine, sine], 1).astype(ml_dtypes.bfloat16)
    return both, np.ascontiguousarray(both.T)


def slope_matrix(size):
    return ((np.eye(size, k=-1) - np.eye(size, k=1)) * 0.5).astype(ml_dtypes.bfloat16)


def combine(terms):
    total = None
    for factor, value in terms:
        if abs(factor) < 1e-12:
            continue
        if abs(factor - 1.0) < 1e-12:
            part = value
        elif abs(factor + 1.0) < 1e-12:
            part = -value
        else:
            part = value * factor
        total = part if total is None else total + part
    return total


def depth_forward(values):
    even = [values[0]] + [values[n] + values[Z - n] for n in range(1, 8)] + [values[8]]
    odd = [None] + [values[n] - values[Z - n] for n in range(1, 8)]
    even_sum = [even[n] + even[8 - n] for n in range(4)] + [even[4]]
    even_dif = [even[n] - even[8 - n] for n in range(4)]
    odd_sum = [None] + [odd[n] + odd[8 - n] for n in range(1, 4)] + [odd[4]]
    odd_dif = [None] + [odd[n] - odd[8 - n] for n in range(1, 4)]
    result = []
    for k in range(KZ):
        folded = even_sum if k % 2 == 0 else even_dif
        cos_part = combine([(math.cos(math.pi * k * n / 8), folded[n]) for n in range(len(folded))])
        folded = odd_dif if k % 2 == 0 else odd_sum
        sin_part = combine(
            [(math.sin(math.pi * k * n / 8), folded[n]) for n in range(1, len(folded))]
        )
        result.append((cos_part, sin_part))
    return result


def depth_inverse(cos_parts, sin_parts):
    layers = [None] * Z
    cos_sum, sin_sum = [None] * 9, [None] * 9
    for n in range(5):
        evens = combine([(math.cos(math.pi * k * n / 8), cos_parts[k]) for k in range(0, KZ, 2)])
        odds = combine([(math.cos(math.pi * k * n / 8), cos_parts[k]) for k in range(1, KZ, 2)])
        if n == 4:
            cos_sum[4] = evens
        else:
            cos_sum[n] = evens + odds
            cos_sum[8 - n] = evens - odds
    for n in range(1, 5):
        evens = combine([(math.sin(math.pi * k * n / 8), sin_parts[k]) for k in range(0, KZ, 2)])
        odds = combine([(math.sin(math.pi * k * n / 8), sin_parts[k]) for k in range(1, KZ, 2)])
        if n == 4:
            sin_sum[4] = odds
        else:
            sin_sum[n] = odds + evens
            sin_sum[8 - n] = odds - evens
    layers[0], layers[8] = cos_sum[0], cos_sum[8]
    for n in range(1, 8):
        layers[n] = cos_sum[n] + sin_sum[n]
        layers[Z - n] = cos_sum[n] - sin_sum[n]
    return layers


ROWS = 96


def tiles(height, width):
    for row in range(0, height, 16):
        for column in range(0, width, 128):
            yield row, pl.ds(row, 16), pl.ds(column, 128)


def depth_forward_kernel(values_ref, planes_ref):
    _, _, height, width = values_ref.shape
    for _, rows, columns in tiles(height, width):
        spectrum = depth_forward([values_ref[0, n, rows, columns] for n in range(Z)])
        for k, (cos_part, sin_part) in enumerate(spectrum):
            planes_ref[2 * k, rows, columns] = cos_part.astype(bf16)
            if sin_part is None:
                sin_part = jnp.zeros_like(cos_part)
            planes_ref[2 * k + 1, rows, columns] = sin_part.astype(bf16)


def depth_transform(values, component, me=None, size_y=1, after=()):
    _, _, height, width = values.shape
    planes = Z // size_y
    shifted_out = me is not None

    def kernel(*refs):
        if not shifted_out:
            depth_forward_kernel(*refs)
            return
        me_ref, values_ref, outs, held = refs[0], refs[1], refs[2 + len(after) : -1], refs[-1]
        depth_forward_kernel(values_ref, held)
        for s, out in enumerate(outs):
            target = lax.rem(me_ref[0] + s, size_y)
            out[...] = held[pl.ds(target * planes, planes)]

    block = (Z // size_y, ROWS, width)
    out_spec = pl.BlockSpec(block, lambda j: (0, j, 0))
    out_shape = jax.ShapeDtypeStruct((planes, height, width), bf16)
    smem = pl.BlockSpec(memory_space=pltpu.SMEM)
    return pl.pallas_call(
        kernel,
        grid=(height // ROWS,),
        in_specs=([smem] if shifted_out else [])
        + [pl.BlockSpec((1, Z, ROWS, width), lambda j: (component, 0, j, 0))]
        + tied(after),
        out_specs=[out_spec] * size_y if shifted_out else out_spec,
        out_shape=[out_shape] * size_y if shifted_out else out_shape,
        scratch_shapes=[pltpu.VMEM((Z, ROWS, width), bf16)] if shifted_out else [],
        compiler_params=params(),
        cost_estimate=takes(3),
        name="depth_transform",
    )(*(([me] if shifted_out else []) + [values, *after]))


def fetch_blocks(table_ref, held, arrived, order):
    count, rows, _ = held.shape
    copies = []
    for s in range(count):
        place = pl.ds(pl.multiple_of(order(s) * rows, rows), rows)
        copies.append(pltpu.make_async_copy(table_ref.at[place], held.at[s], arrived.at[s]))
        copies[s].start()
    return copies


def y_transform(me, table, columns, blocks, halves, after):
    whole = len(columns) == 1
    size_y = columns[0].shape[0] if whole else len(columns)
    planes, height, width = columns[0].shape[-3:]
    modes = HALF_Y // (blocks * halves)
    rows = Y // blocks

    def kernel(me_ref, table_ref, *refs):
        parts = refs[: len(columns)]
        out, held, arrived, lines = refs[-4:]
        copies = fetch_blocks(table_ref, held, arrived, lambda s: s)
        for s in range(size_y):
            source = lax.rem(me_ref[0] + size_y - s, size_y)
            for plane in range(planes):
                if whole:
                    lines[plane, s * height : (s + 1) * height, :] = parts[0][s, plane]
                else:
                    place = pl.ds(pl.multiple_of(source * height, height), height)
                    lines[plane, place, :] = parts[s][plane]
        for s in range(blocks):
            copies[s].wait()
            for plane in range(planes):
                part = jnp.dot(held[s], lines[plane], preferred_element_type=f32)
                out[s, :, plane] = part.astype(bf16).reshape(halves, 2, modes, width)

    vmem = pl.BlockSpec(memory_space=pltpu.VMEM)
    return pl.pallas_call(
        kernel,
        in_specs=[pl.BlockSpec(memory_space=pltpu.SMEM), pl.BlockSpec(memory_space=pl.ANY)]
        + [vmem] * len(columns)
        + tied(after),
        out_specs=vmem,
        out_shape=jax.ShapeDtypeStruct((blocks, halves, planes, 2, modes, width), bf16),
        scratch_shapes=[
            pltpu.VMEM((blocks, rows, Y), bf16),
            pltpu.SemaphoreType.DMA((blocks,)),
            pltpu.VMEM((planes, Y, width), bf16),
        ],
        compiler_params=params(),
        cost_estimate=takes(5),
        name="y_transform",
    )(me, table, *columns, *after)


def y_inverse(me, table, modes, size_y, split, after):
    planes, width = modes.shape[2], modes.shape[5]
    height = Y // size_y
    shape = (planes, height, width)

    def kernel(me_ref, table_ref, modes_ref, *refs):
        outs, held, arrived = refs[len(after) : -2], refs[-2], refs[-1]
        copies = fetch_blocks(
            table_ref, held, arrived, lambda s: lax.rem(me_ref[0] + s, size_y) if split else s
        )
        lines = [modes_ref[:, :, plane].reshape(Y, width) for plane in range(planes)]
        for s in range(size_y):
            copies[s].wait()
            for plane in range(planes):
                rows = jnp.dot(held[s], lines[plane], preferred_element_type=f32).astype(bf16)
                if split:
                    outs[s][plane] = rows
                else:
                    outs[0][s, plane] = rows

    vmem = pl.BlockSpec(memory_space=pltpu.VMEM)
    if split:
        out_shape = [jax.ShapeDtypeStruct(shape, bf16)] * size_y
    else:
        out_shape = [jax.ShapeDtypeStruct((size_y,) + shape, bf16)]
    return pl.pallas_call(
        kernel,
        in_specs=[
            pl.BlockSpec(memory_space=pltpu.SMEM),
            pl.BlockSpec(memory_space=pl.ANY),
            vmem,
        ]
        + tied(after),
        out_specs=[vmem] * len(out_shape),
        out_shape=out_shape,
        scratch_shapes=[
            pltpu.VMEM((size_y, height, Y), bf16),
            pltpu.SemaphoreType.DMA((size_y,)),
        ],
        compiler_params=params(),
        cost_estimate=takes(4),
        name="y_inverse",
    )(me, table, modes, *after)


def x_transform(table, modes, after):
    blocks, _, _, count, width = modes.shape

    def kernel(table_ref, modes_ref, *refs):
        spectrum_ref = refs[-1]
        rows = jnp.concatenate(
            [modes_ref[block, 0].reshape(2 * count, width) for block in range(blocks)], axis=1
        )
        spectrum = jnp.dot(rows, table_ref[...], preferred_element_type=f32)
        spectrum_ref[0] = spectrum.reshape(2, count, X)

    return pl.pallas_call(
        kernel,
        grid=(2,),
        in_specs=[
            pl.BlockSpec((X, X), lambda j: (0, 0)),
            pl.BlockSpec((blocks, 1, 2, count, width), lambda j: (0, j, 0, 0, 0)),
        ]
        + tied(after),
        out_specs=pl.BlockSpec((1, 2, count, X), lambda j: (j, 0, 0, 0)),
        out_shape=jax.ShapeDtypeStruct((2, 2, count, X), f32),
        compiler_params=params(24),
        cost_estimate=takes(3),
        name="x_transform",
    )(table, modes, *after)


def turned(field, axis, tz, ty, tx, wave):
    index = [tz, ty, tx]
    sign = 1.0 if index[axis] == 0 else -1.0
    index[axis] = 1 - index[axis]
    value = field[index[0], index[1], :, index[2] * HALF_X : (index[2] + 1) * HALF_X]
    return value * (wave * sign)


CURL = {
    0: ((1, 2), (0, 1)),
    1: ((0, 0), (2, 2)),
    2: ((2, 1), (1, 0)),
}


def curl_kernel(axes, where_ref, table_ref, plus_ref, minus_ref, back_ref):
    blocks, _, _, count, width = back_ref.shape
    base = where_ref[0] + pl.program_id(0) * count
    depth = where_ref[1]
    mode_y = lax.broadcasted_iota(jnp.int32, (count, HALF_X), 0) + base
    mode_x = lax.broadcasted_iota(jnp.int32, (count, HALF_X), 1)
    wave_y = mode_y.astype(f32) * (2.0 * math.pi / Y)
    wave_x = mode_x.astype(f32) * (2.0 * math.pi / X)
    wave_z = jnp.full((count, HALF_X), depth, jnp.int32).astype(f32) * (2.0 * math.pi / Z)
    square = wave_x * wave_x + wave_y * wave_y + wave_z * wave_z
    doubling = (
        jnp.where(mode_x == 0, 1.0, 2.0)
        * jnp.where(mode_y == 0, 1.0, 2.0)
        * jnp.where(wave_z == 0.0, 1.0, 2.0)
    )
    weight = jnp.where(square > 0, doubling / jnp.where(square > 0, square, 1.0), 0.0)
    waves = [wave_z * weight, wave_y * weight, wave_x * weight]
    rows = []
    for tz in range(2):
        for ty in range(2):
            parts = []
            for tx in range(2):
                parts.append(
                    (
                        turned(plus_ref, axes[0], tz, ty, tx, waves[axes[0]])
                        - turned(minus_ref, axes[1], tz, ty, tx, waves[axes[1]])
                    ).astype(bf16)
                )
            rows.append(jnp.concatenate(parts, axis=1))
    rows = jnp.concatenate(rows, axis=0)
    back = jnp.dot(rows, table_ref[...], preferred_element_type=f32).astype(bf16)
    for block in range(blocks):
        back_ref[block] = back[:, block * width : (block + 1) * width].reshape(2, 2, count, width)


def curl_inverse(where, table, spectra, component, blocks, after):
    (plus_axis, plus), (minus_axis, minus) = CURL[component]
    total = spectra[plus].shape[2]
    width = X // blocks
    count = 96 if total % 96 == 0 else total
    spec = pl.BlockSpec((2, 2, count, X), lambda j: (0, 0, j, 0))

    def kernel(*refs):
        curl_kernel((plus_axis, minus_axis), *refs[:4], refs[-1])

    return pl.pallas_call(
        kernel,
        grid=(total // count,),
        in_specs=[
            pl.BlockSpec(memory_space=pltpu.SMEM),
            pl.BlockSpec((X, X), lambda j: (0, 0)),
            spec,
            spec,
        ]
        + tied(after),
        out_specs=pl.BlockSpec((blocks, 2, 2, count, width), lambda j: (0, 0, 0, j, 0)),
        out_shape=jax.ShapeDtypeStruct((blocks, 2, 2, total, width), bf16),
        compiler_params=params(24),
        cost_estimate=takes(4),
        name="curl_inverse",
    )(where, table, spectra[plus], spectra[minus], *after)


def side_columns(planes):
    width = planes[0].shape[1]
    row = lax.broadcasted_iota(jnp.int32, (2 * Z, width), 0)
    lane = lax.broadcasted_iota(jnp.int32, (2 * Z, width), 1)
    total = None
    for n in range(Z):
        pick = ((row == n) & (lane == 0)) | ((row == n + Z) & (lane == width - 1))
        part = lax.dot_general(
            pick.astype(f32).astype(bf16),
            planes[n],
            (((1,), (1,)), ((), ())),
            preferred_element_type=f32,
        )
        total = part if total is None else total + part
    return total[:Z].astype(bf16), total[Z:].astype(bf16)


def spread_columns(low, high, first, layers, width):
    row = lax.broadcasted_iota(jnp.int32, (2 * Z, layers * width), 0)
    column = lax.broadcasted_iota(jnp.int32, (2 * Z, layers * width), 1)
    place = jnp.zeros((2 * Z, layers * width), f32)
    for n in range(layers):
        place = place + jnp.where((row == first + n) & (column == n * width), -0.5, 0.0)
        place = place + jnp.where(
            (row == first + n + Z) & (column == (n + 1) * width - 1), 0.5, 0.0
        )
    both = jnp.concatenate([low, high], axis=0).astype(bf16)
    spread = lax.dot_general(
        both, place.astype(bf16), (((0,), (0,)), ((), ())), preferred_element_type=f32
    )
    return [spread[:, n * width : (n + 1) * width] for n in range(layers)]


def edges_kernel(field_ref, *refs):
    first_column_ref, last_column_ref = refs[-2:]
    first, last = side_columns([field_ref[0, n] for n in range(Z)])
    first_column_ref[0] = first
    last_column_ref[0] = last


def edge_columns(field, components, after):
    _, _, height, width = field.shape
    shape = jax.ShapeDtypeStruct((components, Z, height), bf16)
    spec = pl.BlockSpec((1, Z, height), lambda i: (i, 0, 0))
    return pl.pallas_call(
        edges_kernel,
        grid=(components,),
        in_specs=[pl.BlockSpec((1, Z, height, width), lambda i: (i, 0, 0, 0))] + tied(after),
        out_specs=[spec, spec],
        out_shape=[shape, shape],
        compiler_params=params(),
        cost_estimate=takes(4),
        name="edge_columns",
    )(field, *after)


def exchange(first, last, axis):
    count = lax.axis_size(axis)
    up = [(i, (i + 1) % count) for i in range(count)]
    down = [((i + 1) % count, i) for i in range(count)]
    return lax.ppermute(last, axis, up), lax.ppermute(first, axis, down)


def adjoint_kernel(planes_ref, cotangent_ref, *refs):
    adjoint_ref, first_x, last_x, first_y, last_y, held = refs
    _, height, width = held.shape
    scale = 1.0 / (X * Y * Z)
    base = pl.program_id(0) * ROWS
    for row, rows, columns in tiles(ROWS, width):
        place = pl.ds(pl.multiple_of(base + row, 16), 16)
        layers = depth_inverse(
            [planes_ref[2 * k, rows, columns].astype(f32) for k in range(KZ)],
            [planes_ref[2 * k + 1, rows, columns].astype(f32) for k in range(KZ)],
        )
        for n in range(Z):
            value = cotangent_ref[0, n, rows, columns] + layers[n] * scale
            adjoint_ref[n, rows, columns] = value
            held[n, place, columns] = value.astype(bf16)

    @pl.when(pl.program_id(0) == pl.num_programs(0) - 1)
    def _():
        first, last = side_columns([held[n] for n in range(Z)])
        first_x[...] = first
        last_x[...] = last
        top = [held[n, 0:16, :].astype(f32)[0:1] for n in range(Z)]
        bottom = [held[n, height - 16 : height, :].astype(f32)[15:16] for n in range(Z)]
        first_y[...] = jnp.concatenate(top, 0).astype(bf16)
        last_y[...] = jnp.concatenate(bottom, 0).astype(bf16)


def make_adjoint(me, parts, cotangent, component, after):
    whole = len(parts) == 1
    planes, height, width = parts[0].shape
    column = jax.ShapeDtypeStruct((Z, height), bf16)
    row = jax.ShapeDtypeStruct((Z, width), bf16)
    column_spec = pl.BlockSpec((Z, height), lambda j: (0, 0))
    row_spec = pl.BlockSpec((Z, width), lambda j: (0, 0))

    def kernel(me_ref, *refs):
        part_refs, cotangent_ref = refs[: len(parts)], refs[len(parts)]
        outs, held, spectrum = refs[-7:-2], refs[-2], refs[-1]
        if whole:
            spectrum = part_refs[0]
        else:
            for s, part in enumerate(part_refs):
                source = lax.rem(me_ref[0] + len(parts) - s, len(parts))
                spectrum[pl.ds(source * planes, planes)] = part[...]
        adjoint_kernel(spectrum, cotangent_ref, *outs, held)

    return pl.pallas_call(
        kernel,
        grid=(height // ROWS,),
        in_specs=[pl.BlockSpec(memory_space=pltpu.SMEM)]
        + [pl.BlockSpec((planes, ROWS, width), lambda j: (0, j, 0))] * len(parts)
        + [pl.BlockSpec((1, Z, ROWS, width), lambda j: (component, 0, j, 0))]
        + tied(after),
        out_specs=[
            pl.BlockSpec((Z, ROWS, width), lambda j: (0, j, 0)),
            column_spec,
            column_spec,
            row_spec,
            row_spec,
        ],
        out_shape=[
            jax.ShapeDtypeStruct((Z, height, width), f32),
            column,
            column,
            row,
            row,
        ],
        scratch_shapes=[
            pltpu.VMEM((Z, height, width), bf16),
            pltpu.VMEM((Z, ROWS, width), bf16),
        ],
        compiler_params=params(),
        cost_estimate=takes(5),
        name="make_adjoint",
    )(me, *parts, cotangent, *after)


def pick_row(rows, n):
    index = lax.broadcasted_iota(jnp.int32, rows.shape, 0)
    return jnp.sum(jnp.where(index == n, rows.astype(f32), 0.0), axis=0, keepdims=True)


def end_rows(low, high, height):
    row = lax.broadcasted_iota(jnp.int32, (height, low.shape[1]), 0)
    return jnp.where(row == 0, low * -0.5, 0.0) + jnp.where(row == height - 1, high * 0.5, 0.0)


LAYERS = 4


def grad_vort_kernel(
    component, slope_x, slope_y, velocity, adjoint, low_x, high_x, low_y, high_y, *refs
):
    before, after = refs
    height, width = velocity.shape[2], velocity.shape[3]
    first = pl.program_id(0) * LAYERS
    ends = spread_columns(low_x[0], high_x[0], first, LAYERS, width)
    layers = velocity[0, pl.ds(first, LAYERS)]
    stacked = layers.reshape(LAYERS * height, width)
    inner = jnp.dot(stacked, slope_x[...], preferred_element_type=f32)
    for k in range(LAYERS):
        n = first + k
        above = lax.rem(n + 1, Z)
        below = lax.rem(n + Z - 1, Z)
        value = adjoint[k]
        half = value * step_size
        along_x = inner[k * height : (k + 1) * height] + ends[k]
        along_y = jnp.dot(slope_y[...], layers[k], preferred_element_type=f32)
        along_y = along_y + end_rows(pick_row(low_y[0], n), pick_row(high_y[0], n), height)
        along_z = (velocity[0, above].astype(f32) - velocity[0, below].astype(f32)) * 0.5
        for j, slope in enumerate((along_x, along_y, along_z)):
            term = half * slope
            if j == component:
                term = term + value
            if before is not None:
                term = before[j, k] + term
            after[j, k] = term


def add_grad_vort(component, slopes, velocity, adjoint, halos, before, after):
    _, _, height, width = velocity.shape
    slope_x, slope_y = slopes
    whole = lambda shape: pl.BlockSpec(shape, lambda n: (0,) * len(shape))
    column = pl.BlockSpec((1, Z, height), lambda n: (component, 0, 0))
    row = pl.BlockSpec((1, Z, width), lambda n: (component, 0, 0))
    sums = pl.BlockSpec((3, LAYERS, height, width), lambda n: (0, n, 0, 0))
    sums_before = pl.BlockSpec((3, LAYERS, height, width), lambda n: (0, n, 0, 0))
    operands = [slope_x, slope_y, velocity, adjoint, *halos]
    in_specs = [
        whole((width, width)),
        whole((height, height)),
        pl.BlockSpec((1, Z, height, width), lambda n: (component, 0, 0, 0)),
        pl.BlockSpec((LAYERS, height, width), lambda n: (n, 0, 0)),
        column,
        column,
        row,
        row,
    ]
    aliases = {}
    if before is not None:
        aliases = {len(operands): 0}
        operands.append(before)
        in_specs.append(sums_before)

    def kernel(*refs):
        grad_vort_kernel(component, *refs[:8], None if before is None else refs[8], refs[-1])

    return pl.pallas_call(
        kernel,
        grid=(Z // LAYERS,),
        in_specs=in_specs + tied(after),
        out_specs=sums,
        out_shape=jax.ShapeDtypeStruct((3, Z, height, width), f32),
        input_output_aliases=aliases,
        compiler_params=params(),
        cost_estimate=takes(9),
        name="add_grad_vort",
    )(*operands, *after)


def grad_vel_kernel(count, slope_x, vorticity, vorticity_above, vorticity_below, *refs):
    adjoints, saved, halos = refs[: 3 * count], refs[3 * count :], refs[3 * count + 4 :]
    vort_low_x, vort_high_x, vort_low_y, vort_high_y = saved[:4]
    after, padded = refs[-2:]
    _, _, height, width = vorticity.shape
    first = pl.program_id(0) * LAYERS

    def times(one, other):
        return one.astype(f32) * other.astype(f32)

    for c in range(count):
        here, above, below = adjoints[3 * c : 3 * c + 3]
        low_x, high_x, low_y, high_y = halos[4 * c : 4 * c + 4]
        ends = spread_columns(
            times(vort_low_x[0], low_x[...]),
            times(vort_high_x[0], high_x[...]),
            first,
            LAYERS,
            width,
        )
        product = [times(vorticity[0, k], here[k]).astype(bf16) for k in range(LAYERS)]
        inner = jnp.dot(
            jnp.concatenate(product, axis=0), slope_x[...], preferred_element_type=f32
        )
        deep = [times(vorticity_below[0, 0], below[0])]
        deep = deep + [times(vorticity[2, k], here[k]) for k in range(LAYERS)]
        deep = deep + [times(vorticity_above[0, 0], above[0])]
        for k in range(LAYERS):
            n = first + k
            padded[k, 8 : 8 + height, :] = times(vorticity[1, k], here[k])
            padded[k, 7:8, :] = pick_row(vort_low_y[0], n) * pick_row(low_y[...], n)
            padded[k, 8 + height : 9 + height, :] = pick_row(vort_high_y[0], n) * pick_row(
                high_y[...], n
            )
            total = (padded[k, 9 : 9 + height, :] - padded[k, 7 : 7 + height, :]) + (
                deep[k + 2] - deep[k]
            )
            total = total * 0.5 + inner[k * height : (k + 1) * height] + ends[k]
            after[c, k] = total * -step_size


def write_grad_vel(components, slope_x, vorticity, adjoints, saved_halos, halos, before, after):
    _, _, height, width = vorticity.shape
    count = len(components)
    start = components[0] // count
    whole = lambda shape: pl.BlockSpec(shape, lambda n: (0,) * len(shape))
    saved_column = pl.BlockSpec((1, Z, height), lambda n: (3, 0, 0))
    saved_row = pl.BlockSpec((1, Z, width), lambda n: (3, 0, 0))
    layer_above = lambda n: lax.rem((n + 1) * LAYERS, Z)
    layer_below = lambda n: lax.rem(n * LAYERS + Z - 1, Z)
    operands = [slope_x, vorticity, vorticity, vorticity]
    in_specs = [
        whole((width, width)),
        pl.BlockSpec((3, LAYERS, height, width), lambda n: (0, n, 0, 0)),
        pl.BlockSpec((1, 1, height, width), lambda n: (2, layer_above(n), 0, 0)),
        pl.BlockSpec((1, 1, height, width), lambda n: (2, layer_below(n), 0, 0)),
    ]
    for adjoint in adjoints:
        operands = operands + [adjoint] * 3
        in_specs = in_specs + [
            pl.BlockSpec((LAYERS, height, width), lambda n: (n, 0, 0)),
            pl.BlockSpec((1, height, width), lambda n: (layer_above(n), 0, 0)),
            pl.BlockSpec((1, height, width), lambda n: (layer_below(n), 0, 0)),
        ]
    operands = operands + list(saved_halos)
    in_specs = in_specs + [saved_column, saved_column, saved_row, saved_row]
    for edge in halos:
        operands = operands + list(edge)
        in_specs = in_specs + [whole((Z, height))] * 2 + [whole((Z, width))] * 2
    aliases = {}
    if before is not None:
        aliases = {len(operands): 0}
        operands.append(before)
        in_specs.append(pl.BlockSpec(memory_space=pl.ANY))

    def kernel(*refs):
        grad_vel_kernel(count, *refs)

    return pl.pallas_call(
        kernel,
        grid=(Z // LAYERS,),
        in_specs=in_specs + tied(after),
        out_specs=pl.BlockSpec((count, LAYERS, height, width), lambda n: (start, n, 0, 0)),
        out_shape=jax.ShapeDtypeStruct((3, Z, height, width), f32),
        input_output_aliases=aliases,
        scratch_shapes=[pltpu.VMEM((LAYERS, height + 16, width), f32)],
        compiler_params=params(),
        cost_estimate=takes(6 * count),
        name="write_grad_vel",
    )(*operands, *after)


def pair_exchange(parts, axis, mine):
    count = lax.axis_size(axis)
    kept = lax.dynamic_index_in_dim(parts, mine, 1, keepdims=False)
    sent = lax.dynamic_index_in_dim(parts, 1 - mine, 1, keepdims=False)
    got = lax.ppermute(sent, axis, [(i, i ^ 1) for i in range(count)])
    return jnp.where(mine == 0, jnp.stack([kept, got], 1), jnp.stack([got, kept], 1))


def shifted(parts, axis):
    count = lax.axis_size(axis)
    return [parts[0]] + [
        lax.ppermute(parts[s], axis, [(i, (i + s) % count) for i in range(count)])
        for s in range(1, count)
    ]


def local(cot_vort, cot_vel, vorticity, velocity):
    size_x = lax.axis_size("gx")
    size_y = lax.axis_size("gy")
    planes = Z // size_y
    halves = size_y // KZ
    _, _, height, width = cot_vel.shape
    modes = HALF_Y // (size_x * halves)
    place_x = lax.axis_index("gx")
    place_y = lax.axis_index("gy")
    half = lax.rem(place_y, halves)
    me = place_y.astype(jnp.int32).reshape(1)
    where = jnp.stack([(place_x * halves + half) * modes, place_y // halves]).astype(jnp.int32)

    y_table, y_back_table = y_tables(size_x * halves)
    x_table, x_back_table = x_tables()
    slope_x = slope_matrix(width)
    slope_y = np.ascontiguousarray(slope_matrix(height).T)

    layers = depth_transform(cot_vel, FORWARD_ORDER[0])

    velocity_first, velocity_last = edge_columns(velocity, 3, (layers,))
    vorticity_first, vorticity_last = edge_columns(vorticity, 1, (layers,))
    low_x, high_x = exchange(
        jnp.concatenate([velocity_first, vorticity_first]),
        jnp.concatenate([velocity_last, vorticity_last]),
        "gx",
    )
    low_y, high_y = exchange(
        jnp.concatenate([velocity[:, :, 0], vorticity[1:2, :, 0]]),
        jnp.concatenate([velocity[:, :, height - 1], vorticity[1:2, :, height - 1]]),
        "gy",
    )
    saved_halos = (low_x, high_x, low_y, high_y)
    edges = (velocity_first, vorticity_first)

    columns = layers.reshape(size_y, planes, height, width)
    columns = [lax.all_to_all(columns, "gy", 0, 0, tiled=True)]
    sent = []
    for place in range(3):
        if place > 0:
            layers = depth_transform(cot_vel, FORWARD_ORDER[place], me, size_y, (sent[-1],))
            columns = shifted(layers, "gy")
        parts = y_transform(me, y_table, columns, size_x, halves, edges if place == 0 else ())
        parts = parts.reshape(size_x, 2, 2, modes, width)
        sent.append(parts if halves == 1 else pair_exchange(parts, "gy", half))

    def spectrum(place, after):
        lines = lax.all_to_all(sent[place], "gx", 0, 0, tiled=True)
        return x_transform(x_table, lines, after)

    def curl(component, after):
        return curl_inverse(where, x_back_table, spectra, component, size_x, after)

    def back(filtered):
        parts = lax.all_to_all(filtered, "gx", 0, 0, tiled=True)
        if halves == 2:
            parts = pair_exchange(parts, "gy", half)
        return parts.reshape(size_x, halves, planes, 2, modes, width)

    one, two, three = BACK_ORDER
    spectra = {FORWARD_ORDER[0]: spectrum(0, (sent[1],))}
    spectra[FORWARD_ORDER[1]] = spectrum(1, (sent[2],) + saved_halos)
    curl_one = curl(one, ())
    spectra[FORWARD_ORDER[2]] = spectrum(2, (curl_one,))
    curl_two = curl(two, ())
    curl_three = curl(three, (curl_two,))
    returned = {one: back(curl_one), two: back(curl_two), three: back(curl_three)}

    def rows_of(component, after):
        split = component != BACK_ORDER[2]
        return y_inverse(me, y_back_table, returned[component], size_y, split, after)

    def adjoint_of(component, rows, after):
        if len(rows) == 1:
            parts = [lax.all_to_all(rows[0], "gy", 0, 0, tiled=True).reshape(Z, height, width)]
        else:
            parts = shifted(rows, "gy")
        adjoint, first_x, last_x, first_y, last_y = make_adjoint(
            me, parts, cot_vort, component, after
        )
        return adjoint, exchange(first_x, last_x, "gx") + exchange(first_y, last_y, "gy")

    def vort_of(component, adjoint, before, after):
        return add_grad_vort(
            component, (slope_x, slope_y), velocity, adjoint, saved_halos, before, after
        )

    def vel_of(components, adjoints, halos, before, after):
        return write_grad_vel(
            components, slope_x, vorticity, adjoints, saved_halos, halos, before, after
        )

    rows_one = rows_of(one, (curl_three,))
    adjoint_one, halos_one = adjoint_of(one, rows_one, ())
    rows_two = rows_of(two, (adjoint_one,))
    grad_vort = vort_of(one, adjoint_one, None, (rows_two[0],))
    adjoint_two, halos_two = adjoint_of(two, rows_two, (grad_vort,))
    rows_three = rows_of(three, (adjoint_two,) + halos_one)
    grad_vel = vel_of((one,), [adjoint_one], [halos_one], None, (rows_three[0],))
    grad_vort = vort_of(two, adjoint_two, grad_vort, (grad_vel,))
    adjoint_three, halos_three = adjoint_of(three, rows_three, (grad_vort,))
    grad_vort = vort_of(three, adjoint_three, grad_vort, ())
    grad_vel = vel_of(
        (two, three), [adjoint_two, adjoint_three], [halos_two, halos_three], grad_vel, (grad_vort,)
    )
    return grad_vort, grad_vel


def solution(mesh):
    spec = P(None, None, "gy", "gx")
    return jax.shard_map(
        local,
        mesh=mesh,
        in_specs=(spec, spec, spec, spec),
        out_specs=(spec, spec),
        check_vma=False,
    )
```

```python
import math

import jax
import jax.numpy as jnp
import ml_dtypes
import numpy as np
from jax import lax
from jax.experimental import pallas as pl
from jax.experimental.pallas import tpu as pltpu
from jax.sharding import PartitionSpec as P

X = 1024
Y = 1536
Z = 16
HALF_X = X // 2
HALF_Y = Y // 2
KZ = Z // 2

step_size = 0.5

f32 = jnp.float32
bf16 = jnp.bfloat16

FORWARD_ORDER = (0, 1, 2)
BACK_ORDER = (2, 0, 1)


def params(megabytes=56):
    return pltpu.CompilerParams(vmem_limit_bytes=megabytes * 1024 * 1024)


def takes(microseconds):
    return pl.CostEstimate(flops=1, bytes_accessed=int(microseconds * 3.0e6), transcendentals=0)


def tied(after):
    return [pl.BlockSpec(memory_space=pl.ANY)] * len(after)


def trig(first, second, length):
    angle = (np.outer(first, second) % length) * (2.0 * math.pi / length)
    return np.cos(angle), np.sin(angle)


def y_tables(blocks):
    cosine, sine = trig(np.arange(HALF_Y), np.arange(Y), Y)
    both = np.stack([cosine.reshape(blocks, -1, Y), sine.reshape(blocks, -1, Y)], 1).reshape(Y, Y)
    both = both.astype(ml_dtypes.bfloat16)
    return both, np.ascontiguousarray(both.T)


def x_tables():
    cosine, sine = trig(np.arange(X), np.arange(HALF_X), X)
    both = np.concatenate([cosine, sine], 1).astype(ml_dtypes.bfloat16)
    return both, np.ascontiguousarray(both.T)


def slope_matrix(size):
    return ((np.eye(size, k=-1) - np.eye(size, k=1)) * 0.5).astype(ml_dtypes.bfloat16)


def combine(terms):
    total = None
    for factor, value in terms:
        if abs(factor) < 1e-12:
            continue
        if abs(factor - 1.0) < 1e-12:
            part = value
        elif abs(factor + 1.0) < 1e-12:
            part = -value
        else:
            part = value * factor
        total = part if total is None else total + part
    return total


def depth_forward(values):
    even = [values[0]] + [values[n] + values[Z - n] for n in range(1, 8)] + [values[8]]
    odd = [None] + [values[n] - values[Z - n] for n in range(1, 8)]
    even_sum = [even[n] + even[8 - n] for n in range(4)] + [even[4]]
    even_dif = [even[n] - even[8 - n] for n in range(4)]
    odd_sum = [None] + [odd[n] + odd[8 - n] for n in range(1, 4)] + [odd[4]]
    odd_dif = [None] + [odd[n] - odd[8 - n] for n in range(1, 4)]
    result = []
    for k in range(KZ):
        folded = even_sum if k % 2 == 0 else even_dif
        cos_part = combine([(math.cos(math.pi * k * n / 8), folded[n]) for n in range(len(folded))])
        folded = odd_dif if k % 2 == 0 else odd_sum
        sin_part = combine(
            [(math.sin(math.pi * k * n / 8), folded[n]) for n in range(1, len(folded))]
        )
        result.append((cos_part, sin_part))
    return result


def depth_inverse(cos_parts, sin_parts):
    layers = [None] * Z
    cos_sum, sin_sum = [None] * 9, [None] * 9
    for n in range(5):
        evens = combine([(math.cos(math.pi * k * n / 8), cos_parts[k]) for k in range(0, KZ, 2)])
        odds = combine([(math.cos(math.pi * k * n / 8), cos_parts[k]) for k in range(1, KZ, 2)])
        if n == 4:
            cos_sum[4] = evens
        else:
            cos_sum[n] = evens + odds
            cos_sum[8 - n] = evens - odds
    for n in range(1, 5):
        evens = combine([(math.sin(math.pi * k * n / 8), sin_parts[k]) for k in range(0, KZ, 2)])
        odds = combine([(math.sin(math.pi * k * n / 8), sin_parts[k]) for k in range(1, KZ, 2)])
        if n == 4:
            sin_sum[4] = odds
        else:
            sin_sum[n] = odds + evens
            sin_sum[8 - n] = odds - evens
    layers[0], layers[8] = cos_sum[0], cos_sum[8]
    for n in range(1, 8):
        layers[n] = cos_sum[n] + sin_sum[n]
        layers[Z - n] = cos_sum[n] - sin_sum[n]
    return layers


ROWS = 96


def tiles(height, width):
    for row in range(0, height, 16):
        for column in range(0, width, 128):
            yield row, pl.ds(row, 16), pl.ds(column, 128)


def depth_forward_kernel(values_ref, planes_ref):
    _, _, height, width = values_ref.shape
    for _, rows, columns in tiles(height, width):
        spectrum = depth_forward([values_ref[0, n, rows, columns] for n in range(Z)])
        for k, (cos_part, sin_part) in enumerate(spectrum):
            planes_ref[2 * k, rows, columns] = cos_part.astype(bf16)
            if sin_part is None:
                sin_part = jnp.zeros_like(cos_part)
            planes_ref[2 * k + 1, rows, columns] = sin_part.astype(bf16)


def depth_transform(values, component, me=None, size_y=1, after=()):
    _, _, height, width = values.shape
    planes = Z // size_y
    shifted_out = me is not None

    def kernel(*refs):
        if not shifted_out:
            depth_forward_kernel(*refs)
            return
        me_ref, values_ref, outs, held = refs[0], refs[1], refs[2 + len(after) : -1], refs[-1]
        depth_forward_kernel(values_ref, held)
        for s, out in enumerate(outs):
            target = lax.rem(me_ref[0] + s, size_y)
            out[...] = held[pl.ds(target * planes, planes)]

    block = (Z // size_y, ROWS, width)
    out_spec = pl.BlockSpec(block, lambda j: (0, j, 0))
    out_shape = jax.ShapeDtypeStruct((planes, height, width), bf16)
    smem = pl.BlockSpec(memory_space=pltpu.SMEM)
    return pl.pallas_call(
        kernel,
        grid=(height // ROWS,),
        in_specs=([smem] if shifted_out else [])
        + [pl.BlockSpec((1, Z, ROWS, width), lambda j: (component, 0, j, 0))]
        + tied(after),
        out_specs=[out_spec] * size_y if shifted_out else out_spec,
        out_shape=[out_shape] * size_y if shifted_out else out_shape,
        scratch_shapes=[pltpu.VMEM((Z, ROWS, width), bf16)] if shifted_out else [],
        compiler_params=params(),
        cost_estimate=takes(3),
        name="depth_transform",
    )(*(([me] if shifted_out else []) + [values, *after]))


def fetch_blocks(table_ref, held, arrived, order):
    count, rows, _ = held.shape
    copies = []
    for s in range(count):
        place = pl.ds(pl.multiple_of(order(s) * rows, rows), rows)
        copies.append(pltpu.make_async_copy(table_ref.at[place], held.at[s], arrived.at[s]))
        copies[s].start()
    return copies


def y_transform(me, table, columns, blocks, halves, after):
    whole = len(columns) == 1
    size_y = columns[0].shape[0] if whole else len(columns)
    planes, height, width = columns[0].shape[-3:]
    modes = HALF_Y // (blocks * halves)
    rows = Y // blocks

    def kernel(me_ref, table_ref, *refs):
        parts = refs[: len(columns)]
        out, held, arrived, lines = refs[-4:]
        copies = fetch_blocks(table_ref, held, arrived, lambda s: s)
        for s in range(size_y):
            source = lax.rem(me_ref[0] + size_y - s, size_y)
            for plane in range(planes):
                if whole:
                    lines[plane, s * height : (s + 1) * height, :] = parts[0][s, plane]
                else:
                    place = pl.ds(pl.multiple_of(source * height, height), height)
                    lines[plane, place, :] = parts[s][plane]
        for s in range(blocks):
            copies[s].wait()
            for plane in range(planes):
                part = jnp.dot(held[s], lines[plane], preferred_element_type=f32)
                out[s, :, plane] = part.astype(bf16).reshape(halves, 2, modes, width)

    vmem = pl.BlockSpec(memory_space=pltpu.VMEM)
    return pl.pallas_call(
        kernel,
        in_specs=[pl.BlockSpec(memory_space=pltpu.SMEM), pl.BlockSpec(memory_space=pl.ANY)]
        + [vmem] * len(columns)
        + tied(after),
        out_specs=vmem,
        out_shape=jax.ShapeDtypeStruct((blocks, halves, planes, 2, modes, width), bf16),
        scratch_shapes=[
            pltpu.VMEM((blocks, rows, Y), bf16),
            pltpu.SemaphoreType.DMA((blocks,)),
            pltpu.VMEM((planes, Y, width), bf16),
        ],
        compiler_params=params(),
        cost_estimate=takes(5),
        name="y_transform",
    )(me, table, *columns, *after)


def y_inverse(me, table, modes, size_y, split, after):
    planes, width = modes.shape[2], modes.shape[5]
    height = Y // size_y
    shape = (planes, height, width)

    def kernel(me_ref, table_ref, modes_ref, *refs):
        outs, held, arrived = refs[len(after) : -2], refs[-2], refs[-1]
        copies = fetch_blocks(
            table_ref, held, arrived, lambda s: lax.rem(me_ref[0] + s, size_y) if split else s
        )
        lines = [modes_ref[:, :, plane].reshape(Y, width) for plane in range(planes)]
        for s in range(size_y):
            copies[s].wait()
            for plane in range(planes):
                rows = jnp.dot(held[s], lines[plane], preferred_element_type=f32).astype(bf16)
                if split:
                    outs[s][plane] = rows
                else:
                    outs[0][s, plane] = rows

    vmem = pl.BlockSpec(memory_space=pltpu.VMEM)
    if split:
        out_shape = [jax.ShapeDtypeStruct(shape, bf16)] * size_y
    else:
        out_shape = [jax.ShapeDtypeStruct((size_y,) + shape, bf16)]
    return pl.pallas_call(
        kernel,
        in_specs=[
            pl.BlockSpec(memory_space=pltpu.SMEM),
            pl.BlockSpec(memory_space=pl.ANY),
            vmem,
        ]
        + tied(after),
        out_specs=[vmem] * len(out_shape),
        out_shape=out_shape,
        scratch_shapes=[
            pltpu.VMEM((size_y, height, Y), bf16),
            pltpu.SemaphoreType.DMA((size_y,)),
        ],
        compiler_params=params(),
        cost_estimate=takes(4),
        name="y_inverse",
    )(me, table, modes, *after)


def x_transform(table, modes, after):
    blocks, _, _, count, width = modes.shape

    def kernel(table_ref, modes_ref, *refs):
        spectrum_ref = refs[-1]
        rows = jnp.concatenate(
            [modes_ref[block, 0].reshape(2 * count, width) for block in range(blocks)], axis=1
        )
        spectrum = jnp.dot(rows, table_ref[...], preferred_element_type=f32)
        spectrum_ref[0] = spectrum.reshape(2, count, X)

    return pl.pallas_call(
        kernel,
        grid=(2,),
        in_specs=[
            pl.BlockSpec((X, X), lambda j: (0, 0)),
            pl.BlockSpec((blocks, 1, 2, count, width), lambda j: (0, j, 0, 0, 0)),
        ]
        + tied(after),
        out_specs=pl.BlockSpec((1, 2, count, X), lambda j: (j, 0, 0, 0)),
        out_shape=jax.ShapeDtypeStruct((2, 2, count, X), f32),
        compiler_params=params(24),
        cost_estimate=takes(3),
        name="x_transform",
    )(table, modes, *after)


def turned(field, axis, tz, ty, tx, wave):
    index = [tz, ty, tx]
    sign = 1.0 if index[axis] == 0 else -1.0
    index[axis] = 1 - index[axis]
    value = field[index[0], index[1], :, index[2] * HALF_X : (index[2] + 1) * HALF_X]
    return value * (wave * sign)


CURL = {
    0: ((1, 2), (0, 1)),
    1: ((0, 0), (2, 2)),
    2: ((2, 1), (1, 0)),
}


def curl_kernel(axes, where_ref, table_ref, plus_ref, minus_ref, back_ref):
    blocks, _, _, count, width = back_ref.shape
    base = where_ref[0] + pl.program_id(0) * count
    depth = where_ref[1]
    mode_y = lax.broadcasted_iota(jnp.int32, (count, HALF_X), 0) + base
    mode_x = lax.broadcasted_iota(jnp.int32, (count, HALF_X), 1)
    wave_y = mode_y.astype(f32) * (2.0 * math.pi / Y)
    wave_x = mode_x.astype(f32) * (2.0 * math.pi / X)
    wave_z = jnp.full((count, HALF_X), depth, jnp.int32).astype(f32) * (2.0 * math.pi / Z)
    square = wave_x * wave_x + wave_y * wave_y + wave_z * wave_z
    doubling = (
        jnp.where(mode_x == 0, 1.0, 2.0)
        * jnp.where(mode_y == 0, 1.0, 2.0)
        * jnp.where(wave_z == 0.0, 1.0, 2.0)
    )
    weight = jnp.where(square > 0, doubling / jnp.where(square > 0, square, 1.0), 0.0)
    waves = [wave_z * weight, wave_y * weight, wave_x * weight]
    rows = []
    for tz in range(2):
        for ty in range(2):
            parts = []
            for tx in range(2):
                parts.append(
                    (
                        turned(plus_ref, axes[0], tz, ty, tx, waves[axes[0]])
                        - turned(minus_ref, axes[1], tz, ty, tx, waves[axes[1]])
                    ).astype(bf16)
                )
            rows.append(jnp.concatenate(parts, axis=1))
    rows = jnp.concatenate(rows, axis=0)
    back = jnp.dot(rows, table_ref[...], preferred_element_type=f32).astype(bf16)
    for block in range(blocks):
        back_ref[block] = back[:, block * width : (block + 1) * width].reshape(2, 2, count, width)


def curl_inverse(where, table, spectra, component, blocks, after):
    (plus_axis, plus), (minus_axis, minus) = CURL[component]
    total = spectra[plus].shape[2]
    width = X // blocks
    count = 96 if total % 96 == 0 else total
    spec = pl.BlockSpec((2, 2, count, X), lambda j: (0, 0, j, 0))

    def kernel(*refs):
        curl_kernel((plus_axis, minus_axis), *refs[:4], refs[-1])

    return pl.pallas_call(
        kernel,
        grid=(total // count,),
        in_specs=[
            pl.BlockSpec(memory_space=pltpu.SMEM),
            pl.BlockSpec((X, X), lambda j: (0, 0)),
            spec,
            spec,
        ]
        + tied(after),
        out_specs=pl.BlockSpec((blocks, 2, 2, count, width), lambda j: (0, 0, 0, j, 0)),
        out_shape=jax.ShapeDtypeStruct((blocks, 2, 2, total, width), bf16),
        compiler_params=params(24),
        cost_estimate=takes(4),
        name="curl_inverse",
    )(where, table, spectra[plus], spectra[minus], *after)


def side_columns(planes):
    width = planes[0].shape[1]
    row = lax.broadcasted_iota(jnp.int32, (2 * Z, width), 0)
    lane = lax.broadcasted_iota(jnp.int32, (2 * Z, width), 1)
    total = None
    for n in range(Z):
        pick = ((row == n) & (lane == 0)) | ((row == n + Z) & (lane == width - 1))
        part = lax.dot_general(
            pick.astype(f32).astype(bf16),
            planes[n],
            (((1,), (1,)), ((), ())),
            preferred_element_type=f32,
        )
        total = part if total is None else total + part
    return total[:Z].astype(bf16), total[Z:].astype(bf16)


def spread_columns(low, high, first, layers, width):
    row = lax.broadcasted_iota(jnp.int32, (2 * Z, layers * width), 0)
    column = lax.broadcasted_iota(jnp.int32, (2 * Z, layers * width), 1)
    place = jnp.zeros((2 * Z, layers * width), f32)
    for n in range(layers):
        place = place + jnp.where((row == first + n) & (column == n * width), -0.5, 0.0)
        place = place + jnp.where(
            (row == first + n + Z) & (column == (n + 1) * width - 1), 0.5, 0.0
        )
    both = jnp.concatenate([low, high], axis=0).astype(bf16)
    spread = lax.dot_general(
        both, place.astype(bf16), (((0,), (0,)), ((), ())), preferred_element_type=f32
    )
    return [spread[:, n * width : (n + 1) * width] for n in range(layers)]


def edges_kernel(field_ref, *refs):
    first_column_ref, last_column_ref = refs[-2:]
    first, last = side_columns([field_ref[0, n] for n in range(Z)])
    first_column_ref[0] = first
    last_column_ref[0] = last


def edge_columns(field, components, after):
    _, _, height, width = field.shape
    shape = jax.ShapeDtypeStruct((components, Z, height), bf16)
    spec = pl.BlockSpec((1, Z, height), lambda i: (i, 0, 0))
    return pl.pallas_call(
        edges_kernel,
        grid=(components,),
        in_specs=[pl.BlockSpec((1, Z, height, width), lambda i: (i, 0, 0, 0))] + tied(after),
        out_specs=[spec, spec],
        out_shape=[shape, shape],
        compiler_params=params(),
        cost_estimate=takes(4),
        name="edge_columns",
    )(field, *after)


def exchange(first, last, axis):
    count = lax.axis_size(axis)
    up = [(i, (i + 1) % count) for i in range(count)]
    down = [((i + 1) % count, i) for i in range(count)]
    return lax.ppermute(last, axis, up), lax.ppermute(first, axis, down)


def adjoint_kernel(planes_ref, cotangent_ref, *refs):
    adjoint_ref, first_x, last_x, first_y, last_y, held = refs
    _, height, width = held.shape
    scale = 1.0 / (X * Y * Z)
    base = pl.program_id(0) * ROWS
    for row, rows, columns in tiles(ROWS, width):
        place = pl.ds(pl.multiple_of(base + row, 16), 16)
        layers = depth_inverse(
            [planes_ref[2 * k, rows, columns].astype(f32) for k in range(KZ)],
            [planes_ref[2 * k + 1, rows, columns].astype(f32) for k in range(KZ)],
        )
        for n in range(Z):
            value = cotangent_ref[0, n, rows, columns] + layers[n] * scale
            adjoint_ref[n, rows, columns] = value
            held[n, place, columns] = value.astype(bf16)

    @pl.when(pl.program_id(0) == pl.num_programs(0) - 1)
    def _():
        first, last = side_columns([held[n] for n in range(Z)])
        first_x[...] = first
        last_x[...] = last
        top = [held[n, 0:16, :].astype(f32)[0:1] for n in range(Z)]
        bottom = [held[n, height - 16 : height, :].astype(f32)[15:16] for n in range(Z)]
        first_y[...] = jnp.concatenate(top, 0).astype(bf16)
        last_y[...] = jnp.concatenate(bottom, 0).astype(bf16)


def make_adjoint(me, parts, cotangent, component, after):
    whole = len(parts) == 1
    planes, height, width = parts[0].shape
    column = jax.ShapeDtypeStruct((Z, height), bf16)
    row = jax.ShapeDtypeStruct((Z, width), bf16)
    column_spec = pl.BlockSpec((Z, height), lambda j: (0, 0))
    row_spec = pl.BlockSpec((Z, width), lambda j: (0, 0))

    def kernel(me_ref, *refs):
        part_refs, cotangent_ref = refs[: len(parts)], refs[len(parts)]
        outs, held, spectrum = refs[-7:-2], refs[-2], refs[-1]
        if whole:
            spectrum = part_refs[0]
        else:
            for s, part in enumerate(part_refs):
                source = lax.rem(me_ref[0] + len(parts) - s, len(parts))
                spectrum[pl.ds(source * planes, planes)] = part[...]
        adjoint_kernel(spectrum, cotangent_ref, *outs, held)

    return pl.pallas_call(
        kernel,
        grid=(height // ROWS,),
        in_specs=[pl.BlockSpec(memory_space=pltpu.SMEM)]
        + [pl.BlockSpec((planes, ROWS, width), lambda j: (0, j, 0))] * len(parts)
        + [pl.BlockSpec((1, Z, ROWS, width), lambda j: (component, 0, j, 0))]
        + tied(after),
        out_specs=[
            pl.BlockSpec((Z, ROWS, width), lambda j: (0, j, 0)),
            column_spec,
            column_spec,
            row_spec,
            row_spec,
        ],
        out_shape=[
            jax.ShapeDtypeStruct((Z, height, width), f32),
            column,
            column,
            row,
            row,
        ],
        scratch_shapes=[
            pltpu.VMEM((Z, height, width), bf16),
            pltpu.VMEM((Z, ROWS, width), bf16),
        ],
        compiler_params=params(),
        cost_estimate=takes(5),
        name="make_adjoint",
    )(me, *parts, cotangent, *after)


def pick_row(rows, n):
    index = lax.broadcasted_iota(jnp.int32, rows.shape, 0)
    return jnp.sum(jnp.where(index == n, rows.astype(f32), 0.0), axis=0, keepdims=True)


def end_rows(low, high, height):
    row = lax.broadcasted_iota(jnp.int32, (height, low.shape[1]), 0)
    return jnp.where(row == 0, low * -0.5, 0.0) + jnp.where(row == height - 1, high * 0.5, 0.0)


LAYERS = 4


def grad_vort_kernel(
    component, slope_x, slope_y, velocity, adjoint, low_x, high_x, low_y, high_y, *refs
):
    before, after = refs
    height, width = velocity.shape[2], velocity.shape[3]
    first = pl.program_id(0) * LAYERS
    ends = spread_columns(low_x[0], high_x[0], first, LAYERS, width)
    layers = velocity[0, pl.ds(first, LAYERS)]
    stacked = layers.reshape(LAYERS * height, width)
    inner = jnp.dot(stacked, slope_x[...], preferred_element_type=f32)
    for k in range(LAYERS):
        n = first + k
        above = lax.rem(n + 1, Z)
        below = lax.rem(n + Z - 1, Z)
        value = adjoint[k]
        half = value * step_size
        along_x = inner[k * height : (k + 1) * height] + ends[k]
        along_y = jnp.dot(slope_y[...], layers[k], preferred_element_type=f32)
        along_y = along_y + end_rows(pick_row(low_y[0], n), pick_row(high_y[0], n), height)
        along_z = (velocity[0, above].astype(f32) - velocity[0, below].astype(f32)) * 0.5
        for j, slope in enumerate((along_x, along_y, along_z)):
            term = half * slope
            if j == component:
                term = term + value
            if before is not None:
                term = before[j, k] + term
            after[j, k] = term


def add_grad_vort(component, slopes, velocity, adjoint, halos, before, after):
    _, _, height, width = velocity.shape
    slope_x, slope_y = slopes
    whole = lambda shape: pl.BlockSpec(shape, lambda n: (0,) * len(shape))
    column = pl.BlockSpec((1, Z, height), lambda n: (component, 0, 0))
    row = pl.BlockSpec((1, Z, width), lambda n: (component, 0, 0))
    sums = pl.BlockSpec((3, LAYERS, height, width), lambda n: (0, n, 0, 0))
    operands = [slope_x, slope_y, velocity, adjoint, *halos]
    in_specs = [
        whole((width, width)),
        whole((height, height)),
        pl.BlockSpec((1, Z, height, width), lambda n: (component, 0, 0, 0)),
        pl.BlockSpec((LAYERS, height, width), lambda n: (n, 0, 0)),
        column,
        column,
        row,
        row,
    ]
    if before is not None:
        operands.append(before)
        in_specs.append(sums)

    def kernel(*refs):
        grad_vort_kernel(component, *refs[:8], None if before is None else refs[8], refs[-1])

    return pl.pallas_call(
        kernel,
        grid=(Z // LAYERS,),
        in_specs=in_specs + tied(after),
        out_specs=sums,
        out_shape=jax.ShapeDtypeStruct((3, Z, height, width), f32),
        compiler_params=params(),
        cost_estimate=takes(9),
        name="add_grad_vort",
    )(*operands, *after)


def grad_vel_kernel(count, slope_x, vorticity, vorticity_above, vorticity_below, *refs):
    adjoints, saved, halos = refs[: 3 * count], refs[3 * count :], refs[3 * count + 4 :]
    vort_low_x, vort_high_x, vort_low_y, vort_high_y = saved[:4]
    after, padded = refs[-2:]
    _, _, height, width = vorticity.shape
    first = pl.program_id(0) * LAYERS

    def times(one, other):
        return one.astype(f32) * other.astype(f32)

    for c in range(count):
        here, above, below = adjoints[3 * c : 3 * c + 3]
        low_x, high_x, low_y, high_y = halos[4 * c : 4 * c + 4]
        ends = spread_columns(
            times(vort_low_x[0], low_x[...]),
            times(vort_high_x[0], high_x[...]),
            first,
            LAYERS,
            width,
        )
        product = [times(vorticity[0, k], here[k]).astype(bf16) for k in range(LAYERS)]
        inner = jnp.dot(
            jnp.concatenate(product, axis=0), slope_x[...], preferred_element_type=f32
        )
        deep = [times(vorticity_below[0, 0], below[0])]
        deep = deep + [times(vorticity[2, k], here[k]) for k in range(LAYERS)]
        deep = deep + [times(vorticity_above[0, 0], above[0])]
        for k in range(LAYERS):
            n = first + k
            padded[k, 8 : 8 + height, :] = times(vorticity[1, k], here[k])
            padded[k, 7:8, :] = pick_row(vort_low_y[0], n) * pick_row(low_y[...], n)
            padded[k, 8 + height : 9 + height, :] = pick_row(vort_high_y[0], n) * pick_row(
                high_y[...], n
            )
            total = (padded[k, 9 : 9 + height, :] - padded[k, 7 : 7 + height, :]) + (
                deep[k + 2] - deep[k]
            )
            total = total * 0.5 + inner[k * height : (k + 1) * height] + ends[k]
            after[c, k] = total * -step_size


def write_grad_vel(components, slope_x, vorticity, adjoints, saved_halos, halos, before, after):
    _, _, height, width = vorticity.shape
    count = len(components)
    start = components[0] // count
    whole = lambda shape: pl.BlockSpec(shape, lambda n: (0,) * len(shape))
    saved_column = pl.BlockSpec((1, Z, height), lambda n: (3, 0, 0))
    saved_row = pl.BlockSpec((1, Z, width), lambda n: (3, 0, 0))
    layer_above = lambda n: lax.rem((n + 1) * LAYERS, Z)
    layer_below = lambda n: lax.rem(n * LAYERS + Z - 1, Z)
    operands = [slope_x, vorticity, vorticity, vorticity]
    in_specs = [
        whole((width, width)),
        pl.BlockSpec((3, LAYERS, height, width), lambda n: (0, n, 0, 0)),
        pl.BlockSpec((1, 1, height, width), lambda n: (2, layer_above(n), 0, 0)),
        pl.BlockSpec((1, 1, height, width), lambda n: (2, layer_below(n), 0, 0)),
    ]
    for adjoint in adjoints:
        operands = operands + [adjoint] * 3
        in_specs = in_specs + [
            pl.BlockSpec((LAYERS, height, width), lambda n: (n, 0, 0)),
            pl.BlockSpec((1, height, width), lambda n: (layer_above(n), 0, 0)),
            pl.BlockSpec((1, height, width), lambda n: (layer_below(n), 0, 0)),
        ]
    operands = operands + list(saved_halos)
    in_specs = in_specs + [saved_column, saved_column, saved_row, saved_row]
    for edge in halos:
        operands = operands + list(edge)
        in_specs = in_specs + [whole((Z, height))] * 2 + [whole((Z, width))] * 2
    aliases = {}
    if before is not None:
        aliases = {len(operands): 0}
        operands.append(before)
        in_specs.append(pl.BlockSpec(memory_space=pl.ANY))

    def kernel(*refs):
        grad_vel_kernel(count, *refs)

    return pl.pallas_call(
        kernel,
        grid=(Z // LAYERS,),
        in_specs=in_specs + tied(after),
        out_specs=pl.BlockSpec((count, LAYERS, height, width), lambda n: (start, n, 0, 0)),
        out_shape=jax.ShapeDtypeStruct((3, Z, height, width), f32),
        input_output_aliases=aliases,
        scratch_shapes=[pltpu.VMEM((LAYERS, height + 16, width), f32)],
        compiler_params=params(),
        cost_estimate=takes(6 * count),
        name="write_grad_vel",
    )(*operands, *after)


def pair_exchange(parts, axis, mine):
    count = lax.axis_size(axis)
    kept = lax.dynamic_index_in_dim(parts, mine, 1, keepdims=False)
    sent = lax.dynamic_index_in_dim(parts, 1 - mine, 1, keepdims=False)
    got = lax.ppermute(sent, axis, [(i, i ^ 1) for i in range(count)])
    return jnp.where(mine == 0, jnp.stack([kept, got], 1), jnp.stack([got, kept], 1))


def shifted(parts, axis):
    count = lax.axis_size(axis)
    return [parts[0]] + [
        lax.ppermute(parts[s], axis, [(i, (i + s) % count) for i in range(count)])
        for s in range(1, count)
    ]


def local(cot_vort, cot_vel, vorticity, velocity):
    size_x = lax.axis_size("gx")
    size_y = lax.axis_size("gy")
    planes = Z // size_y
    halves = size_y // KZ
    _, _, height, width = cot_vel.shape
    modes = HALF_Y // (size_x * halves)
    place_x = lax.axis_index("gx")
    place_y = lax.axis_index("gy")
    half = lax.rem(place_y, halves)
    me = place_y.astype(jnp.int32).reshape(1)
    where = jnp.stack([(place_x * halves + half) * modes, place_y // halves]).astype(jnp.int32)

    y_table, y_back_table = y_tables(size_x * halves)
    x_table, x_back_table = x_tables()
    slope_x = slope_matrix(width)
    slope_y = np.ascontiguousarray(slope_matrix(height).T)

    layers = depth_transform(cot_vel, FORWARD_ORDER[0])

    velocity_first, velocity_last = edge_columns(velocity, 3, (layers,))
    vorticity_first, vorticity_last = edge_columns(vorticity, 1, (layers,))
    low_x, high_x = exchange(
        jnp.concatenate([velocity_first, vorticity_first]),
        jnp.concatenate([velocity_last, vorticity_last]),
        "gx",
    )
    low_y, high_y = exchange(
        jnp.concatenate([velocity[:, :, 0], vorticity[1:2, :, 0]]),
        jnp.concatenate([velocity[:, :, height - 1], vorticity[1:2, :, height - 1]]),
        "gy",
    )
    saved_halos = (low_x, high_x, low_y, high_y)
    edges = (velocity_first, vorticity_first)

    columns = layers.reshape(size_y, planes, height, width)
    columns = [lax.all_to_all(columns, "gy", 0, 0, tiled=True)]
    sent = []
    for place in range(3):
        if place > 0:
            layers = depth_transform(cot_vel, FORWARD_ORDER[place], me, size_y, (sent[-1],))
            columns = shifted(layers, "gy")
        parts = y_transform(me, y_table, columns, size_x, halves, edges if place == 0 else ())
        parts = parts.reshape(size_x, 2, 2, modes, width)
        sent.append(parts if halves == 1 else pair_exchange(parts, "gy", half))

    def spectrum(place, after):
        lines = lax.all_to_all(sent[place], "gx", 0, 0, tiled=True)
        return x_transform(x_table, lines, after)

    def curl(component, after):
        return curl_inverse(where, x_back_table, spectra, component, size_x, after)

    def back(filtered):
        parts = lax.all_to_all(filtered, "gx", 0, 0, tiled=True)
        if halves == 2:
            parts = pair_exchange(parts, "gy", half)
        return parts.reshape(size_x, halves, planes, 2, modes, width)

    def rows_of(component, modes_back, after):
        split = component != BACK_ORDER[2]
        return y_inverse(me, y_back_table, modes_back, size_y, split, after)

    def layers_of(rows):
        if len(rows) == 1:
            return [lax.all_to_all(rows[0], "gy", 0, 0, tiled=True).reshape(Z, height, width)]
        return shifted(rows, "gy")

    one, two, three = BACK_ORDER
    spectra = {FORWARD_ORDER[0]: spectrum(0, (sent[1],))}
    spectra[FORWARD_ORDER[1]] = spectrum(1, (sent[2],) + saved_halos)
    curl_one = curl(one, ())
    spectra[FORWARD_ORDER[2]] = spectrum(2, (curl_one,))
    curl_two = curl(two, ())
    rows_one = rows_of(one, back(curl_one), (curl_two,))
    layers_one = layers_of(rows_one)
    curl_three = curl(three, tuple(layers_one))

    def adjoint_of(component, parts, after):
        adjoint, first_x, last_x, first_y, last_y = make_adjoint(
            me, parts, cot_vort, component, after
        )
        return adjoint, exchange(first_x, last_x, "gx") + exchange(first_y, last_y, "gy")

    def vort_of(component, adjoint, before, after):
        return add_grad_vort(
            component, (slope_x, slope_y), velocity, adjoint, saved_halos, before, after
        )

    def vel_of(components, adjoints, halos, before, after):
        return write_grad_vel(
            components, slope_x, vorticity, adjoints, saved_halos, halos, before, after
        )

    adjoint_one, halos_one = adjoint_of(one, layers_one, ())
    rows_two = rows_of(two, back(curl_two), (adjoint_one,))
    grad_vort = vort_of(one, adjoint_one, None, (rows_two[0],))
    adjoint_two, halos_two = adjoint_of(two, layers_of(rows_two), (grad_vort,))
    rows_three = rows_of(three, back(curl_three), (adjoint_two,) + halos_one)
    grad_vel = vel_of((one,), [adjoint_one], [halos_one], None, (rows_three[0],))
    grad_vort = vort_of(two, adjoint_two, grad_vort, (grad_vel,))
    adjoint_three, halos_three = adjoint_of(three, layers_of(rows_three), (grad_vort,))
    grad_vort = vort_of(three, adjoint_three, grad_vort, ())
    grad_vel = vel_of(
        (two, three), [adjoint_two, adjoint_three], [halos_two, halos_three], grad_vel, (grad_vort,)
    )
    return grad_vort, grad_vel


def solution(mesh):
    spec = P(None, None, "gy", "gx")
    return jax.shard_map(
        local,
        mesh=mesh,
        in_specs=(spec, spec, spec, spec),
        out_specs=(spec, spec),
        check_vma=False,
    )
```

```python
import math

import jax
import jax.numpy as jnp
import ml_dtypes
import numpy as np
from jax import lax
from jax.experimental import pallas as pl
from jax.experimental.pallas import tpu as pltpu
from jax.sharding import PartitionSpec as P

X = 1024
Y = 1536
Z = 16
HALF_X = X // 2
HALF_Y = Y // 2
KZ = Z // 2

step_size = 0.5

f32 = jnp.float32
bf16 = jnp.bfloat16

FORWARD_ORDER = (0, 1, 2)
BACK_ORDER = (2, 0, 1)


def params(megabytes=56):
    return pltpu.CompilerParams(vmem_limit_bytes=megabytes * 1024 * 1024)


def takes(microseconds):
    return pl.CostEstimate(flops=1, bytes_accessed=int(microseconds * 3.0e6), transcendentals=0)


def tied(after):
    return [pl.BlockSpec(memory_space=pl.ANY)] * len(after)


def trig(first, second, length):
    angle = (np.outer(first, second) % length) * (2.0 * math.pi / length)
    return np.cos(angle), np.sin(angle)


def y_tables(blocks):
    cosine, sine = trig(np.arange(HALF_Y), np.arange(Y), Y)
    both = np.stack([cosine.reshape(blocks, -1, Y), sine.reshape(blocks, -1, Y)], 1).reshape(Y, Y)
    both = both.astype(ml_dtypes.bfloat16)
    return both, np.ascontiguousarray(both.T)


def x_tables():
    cosine, sine = trig(np.arange(X), np.arange(HALF_X), X)
    both = np.concatenate([cosine, sine], 1).astype(ml_dtypes.bfloat16)
    return both, np.ascontiguousarray(both.T)


def slope_matrix(size):
    return ((np.eye(size, k=-1) - np.eye(size, k=1)) * 0.5).astype(ml_dtypes.bfloat16)


def combine(terms):
    total = None
    for factor, value in terms:
        if abs(factor) < 1e-12:
            continue
        if abs(factor - 1.0) < 1e-12:
            part = value
        elif abs(factor + 1.0) < 1e-12:
            part = -value
        else:
            part = value * factor
        total = part if total is None else total + part
    return total


def depth_forward(values):
    even = [values[0]] + [values[n] + values[Z - n] for n in range(1, 8)] + [values[8]]
    odd = [None] + [values[n] - values[Z - n] for n in range(1, 8)]
    even_sum = [even[n] + even[8 - n] for n in range(4)] + [even[4]]
    even_dif = [even[n] - even[8 - n] for n in range(4)]
    odd_sum = [None] + [odd[n] + odd[8 - n] for n in range(1, 4)] + [odd[4]]
    odd_dif = [None] + [odd[n] - odd[8 - n] for n in range(1, 4)]
    result = []
    for k in range(KZ):
        folded = even_sum if k % 2 == 0 else even_dif
        cos_part = combine([(math.cos(math.pi * k * n / 8), folded[n]) for n in range(len(folded))])
        folded = odd_dif if k % 2 == 0 else odd_sum
        sin_part = combine(
            [(math.sin(math.pi * k * n / 8), folded[n]) for n in range(1, len(folded))]
        )
        result.append((cos_part, sin_part))
    return result


def depth_inverse(cos_parts, sin_parts):
    layers = [None] * Z
    cos_sum, sin_sum = [None] * 9, [None] * 9
    for n in range(5):
        evens = combine([(math.cos(math.pi * k * n / 8), cos_parts[k]) for k in range(0, KZ, 2)])
        odds = combine([(math.cos(math.pi * k * n / 8), cos_parts[k]) for k in range(1, KZ, 2)])
        if n == 4:
            cos_sum[4] = evens
        else:
            cos_sum[n] = evens + odds
            cos_sum[8 - n] = evens - odds
    for n in range(1, 5):
        evens = combine([(math.sin(math.pi * k * n / 8), sin_parts[k]) for k in range(0, KZ, 2)])
        odds = combine([(math.sin(math.pi * k * n / 8), sin_parts[k]) for k in range(1, KZ, 2)])
        if n == 4:
            sin_sum[4] = odds
        else:
            sin_sum[n] = odds + evens
            sin_sum[8 - n] = odds - evens
    layers[0], layers[8] = cos_sum[0], cos_sum[8]
    for n in range(1, 8):
        layers[n] = cos_sum[n] + sin_sum[n]
        layers[Z - n] = cos_sum[n] - sin_sum[n]
    return layers


ROWS = 96


def tiles(height, width):
    for row in range(0, height, 16):
        for column in range(0, width, 128):
            yield row, pl.ds(row, 16), pl.ds(column, 128)


def depth_forward_kernel(values_ref, planes_ref):
    _, _, height, width = values_ref.shape
    for _, rows, columns in tiles(height, width):
        spectrum = depth_forward([values_ref[0, n, rows, columns] for n in range(Z)])
        for k, (cos_part, sin_part) in enumerate(spectrum):
            planes_ref[2 * k, rows, columns] = cos_part.astype(bf16)
            if sin_part is None:
                sin_part = jnp.zeros_like(cos_part)
            planes_ref[2 * k + 1, rows, columns] = sin_part.astype(bf16)


def depth_transform(values, component, me=None, size_y=1, after=()):
    _, _, height, width = values.shape
    planes = Z // size_y
    shifted_out = me is not None

    def kernel(*refs):
        if not shifted_out:
            depth_forward_kernel(*refs)
            return
        me_ref, values_ref, outs, held = refs[0], refs[1], refs[2 + len(after) : -1], refs[-1]
        depth_forward_kernel(values_ref, held)
        for s, out in enumerate(outs):
            target = lax.rem(me_ref[0] + s, size_y)
            out[...] = held[pl.ds(target * planes, planes)]

    block = (Z // size_y, ROWS, width)
    out_spec = pl.BlockSpec(block, lambda j: (0, j, 0))
    out_shape = jax.ShapeDtypeStruct((planes, height, width), bf16)
    smem = pl.BlockSpec(memory_space=pltpu.SMEM)
    return pl.pallas_call(
        kernel,
        grid=(height // ROWS,),
        in_specs=([smem] if shifted_out else [])
        + [pl.BlockSpec((1, Z, ROWS, width), lambda j: (component, 0, j, 0))]
        + tied(after),
        out_specs=[out_spec] * size_y if shifted_out else out_spec,
        out_shape=[out_shape] * size_y if shifted_out else out_shape,
        scratch_shapes=[pltpu.VMEM((Z, ROWS, width), bf16)] if shifted_out else [],
        compiler_params=params(),
        cost_estimate=takes(3),
        name="depth_transform",
    )(*(([me] if shifted_out else []) + [values, *after]))


def fetch_blocks(table_ref, held, arrived, order):
    count, rows, _ = held.shape
    copies = []
    for s in range(count):
        place = pl.ds(pl.multiple_of(order(s) * rows, rows), rows)
        copies.append(pltpu.make_async_copy(table_ref.at[place], held.at[s], arrived.at[s]))
        copies[s].start()
    return copies


def y_transform(me, table, columns, blocks, halves, after):
    whole = len(columns) == 1
    size_y = columns[0].shape[0] if whole else len(columns)
    planes, height, width = columns[0].shape[-3:]
    modes = HALF_Y // (blocks * halves)
    rows = Y // blocks
    shape = (blocks, halves, planes, 2, modes, width)

    def kernel(me_ref, table_ref, *refs):
        parts = refs[: len(columns)]
        out, held, lines, ready, table_in, lines_in, ready_out = refs[-7:]
        copies = []
        for s in range(size_y):
            source = s if whole else lax.rem(me_ref[0] + size_y - s, size_y)
            place = pl.ds(pl.multiple_of(source * height, height), height)
            for plane in range(planes):
                part = parts[0].at[s, plane] if whole else parts[s].at[plane]
                copies.append(
                    pltpu.make_async_copy(
                        part, lines.at[plane, place], lines_in.at[s * planes + plane]
                    )
                )
                copies[-1].start()
        tables = fetch_blocks(table_ref, held, table_in, lambda s: s)
        for copy in copies:
            copy.wait()
        results = []
        for s in range(blocks):
            tables[s].wait()
            for plane in range(planes):
                part = jnp.dot(held[s], lines[plane], preferred_element_type=f32)
                ready[s, :, plane] = part.astype(bf16).reshape(halves, 2, modes, width)
            results.append(pltpu.make_async_copy(ready.at[s], out.at[s], ready_out.at[s]))
            results[s].start()
        for result in results:
            result.wait()

    anywhere = pl.BlockSpec(memory_space=pl.ANY)
    return pl.pallas_call(
        kernel,
        in_specs=[pl.BlockSpec(memory_space=pltpu.SMEM), anywhere]
        + [anywhere] * len(columns)
        + tied(after),
        out_specs=anywhere,
        out_shape=jax.ShapeDtypeStruct(shape, bf16),
        scratch_shapes=[
            pltpu.VMEM((blocks, rows, Y), bf16),
            pltpu.VMEM((planes, Y, width), bf16),
            pltpu.VMEM(shape, bf16),
            pltpu.SemaphoreType.DMA((blocks,)),
            pltpu.SemaphoreType.DMA((size_y * planes,)),
            pltpu.SemaphoreType.DMA((blocks,)),
        ],
        compiler_params=params(),
        cost_estimate=takes(5),
        name="y_transform",
    )(me, table, *columns, *after)


def y_inverse(me, table, modes, size_y, split, after):
    blocks, halves, planes, _, count, width = modes.shape
    height = Y // size_y
    shape = (planes, height, width)

    def kernel(me_ref, table_ref, modes_ref, *refs):
        outs = refs[len(after) : -6]
        held, lines, ready, table_in, lines_in, ready_out = refs[-6:]
        copies = []
        for block in range(blocks):
            for h in range(halves):
                for plane in range(planes):
                    copies.append(
                        pltpu.make_async_copy(
                            modes_ref.at[block, h, plane],
                            lines.at[plane, block, h],
                            lines_in.at[(block * halves + h) * planes + plane],
                        )
                    )
                    copies[-1].start()
        tables = fetch_blocks(
            table_ref, held, table_in, lambda s: lax.rem(me_ref[0] + s, size_y) if split else s
        )
        for copy in copies:
            copy.wait()
        results = []
        for s in range(size_y):
            tables[s].wait()
            for plane in range(planes):
                columns = lines[plane].reshape(Y, width)
                rows = jnp.dot(held[s], columns, preferred_element_type=f32)
                ready[s, plane] = rows.astype(bf16)
            out = outs[s] if split else outs[0].at[s]
            results.append(pltpu.make_async_copy(ready.at[s], out, ready_out.at[s]))
            results[s].start()
        for result in results:
            result.wait()

    anywhere = pl.BlockSpec(memory_space=pl.ANY)
    if split:
        out_shape = [jax.ShapeDtypeStruct(shape, bf16)] * size_y
    else:
        out_shape = [jax.ShapeDtypeStruct((size_y,) + shape, bf16)]
    return pl.pallas_call(
        kernel,
        in_specs=[pl.BlockSpec(memory_space=pltpu.SMEM), anywhere, anywhere] + tied(after),
        out_specs=[anywhere] * len(out_shape),
        out_shape=out_shape,
        scratch_shapes=[
            pltpu.VMEM((size_y, height, Y), bf16),
            pltpu.VMEM((planes, blocks, halves, 2, count, width), bf16),
            pltpu.VMEM((size_y,) + shape, bf16),
            pltpu.SemaphoreType.DMA((size_y,)),
            pltpu.SemaphoreType.DMA((blocks * halves * planes,)),
            pltpu.SemaphoreType.DMA((size_y,)),
        ],
        compiler_params=params(),
        cost_estimate=takes(4),
        name="y_inverse",
    )(me, table, modes, *after)


def x_transform(table, modes, after):
    blocks, _, _, count, width = modes.shape

    def kernel(table_ref, modes_ref, *refs):
        spectrum_ref = refs[-1]
        rows = jnp.concatenate(
            [modes_ref[block, 0].reshape(2 * count, width) for block in range(blocks)], axis=1
        )
        spectrum = jnp.dot(rows, table_ref[...], preferred_element_type=f32)
        spectrum_ref[0] = spectrum.reshape(2, count, X)

    return pl.pallas_call(
        kernel,
        grid=(2,),
        in_specs=[
            pl.BlockSpec((X, X), lambda j: (0, 0)),
            pl.BlockSpec((blocks, 1, 2, count, width), lambda j: (0, j, 0, 0, 0)),
        ]
        + tied(after),
        out_specs=pl.BlockSpec((1, 2, count, X), lambda j: (j, 0, 0, 0)),
        out_shape=jax.ShapeDtypeStruct((2, 2, count, X), f32),
        compiler_params=params(24),
        cost_estimate=takes(3),
        name="x_transform",
    )(table, modes, *after)


def turned(field, axis, tz, ty, tx, wave):
    index = [tz, ty, tx]
    sign = 1.0 if index[axis] == 0 else -1.0
    index[axis] = 1 - index[axis]
    value = field[index[0], index[1], :, index[2] * HALF_X : (index[2] + 1) * HALF_X]
    return value * (wave * sign)


CURL = {
    0: ((1, 2), (0, 1)),
    1: ((0, 0), (2, 2)),
    2: ((2, 1), (1, 0)),
}


def curl_kernel(axes, where_ref, table_ref, plus_ref, minus_ref, back_ref):
    blocks, _, _, count, width = back_ref.shape
    base = where_ref[0] + pl.program_id(0) * count
    depth = where_ref[1]
    mode_y = lax.broadcasted_iota(jnp.int32, (count, HALF_X), 0) + base
    mode_x = lax.broadcasted_iota(jnp.int32, (count, HALF_X), 1)
    wave_y = mode_y.astype(f32) * (2.0 * math.pi / Y)
    wave_x = mode_x.astype(f32) * (2.0 * math.pi / X)
    wave_z = jnp.full((count, HALF_X), depth, jnp.int32).astype(f32) * (2.0 * math.pi / Z)
    square = wave_x * wave_x + wave_y * wave_y + wave_z * wave_z
    doubling = (
        jnp.where(mode_x == 0, 1.0, 2.0)
        * jnp.where(mode_y == 0, 1.0, 2.0)
        * jnp.where(wave_z == 0.0, 1.0, 2.0)
    )
    weight = jnp.where(square > 0, doubling / jnp.where(square > 0, square, 1.0), 0.0)
    waves = [wave_z * weight, wave_y * weight, wave_x * weight]
    rows = []
    for tz in range(2):
        for ty in range(2):
            parts = []
            for tx in range(2):
                parts.append(
                    (
                        turned(plus_ref, axes[0], tz, ty, tx, waves[axes[0]])
                        - turned(minus_ref, axes[1], tz, ty, tx, waves[axes[1]])
                    ).astype(bf16)
                )
            rows.append(jnp.concatenate(parts, axis=1))
    rows = jnp.concatenate(rows, axis=0)
    back = jnp.dot(rows, table_ref[...], preferred_element_type=f32).astype(bf16)
    for block in range(blocks):
        back_ref[block] = back[:, block * width : (block + 1) * width].reshape(2, 2, count, width)


def curl_inverse(where, table, spectra, component, blocks, after):
    (plus_axis, plus), (minus_axis, minus) = CURL[component]
    total = spectra[plus].shape[2]
    width = X // blocks
    count = 96 if total % 96 == 0 else total
    spec = pl.BlockSpec((2, 2, count, X), lambda j: (0, 0, j, 0))

    def kernel(*refs):
        curl_kernel((plus_axis, minus_axis), *refs[:4], refs[-1])

    return pl.pallas_call(
        kernel,
        grid=(total // count,),
        in_specs=[
            pl.BlockSpec(memory_space=pltpu.SMEM),
            pl.BlockSpec((X, X), lambda j: (0, 0)),
            spec,
            spec,
        ]
        + tied(after),
        out_specs=pl.BlockSpec((blocks, 2, 2, count, width), lambda j: (0, 0, 0, j, 0)),
        out_shape=jax.ShapeDtypeStruct((blocks, 2, 2, total, width), bf16),
        compiler_params=params(24),
        cost_estimate=takes(4),
        name="curl_inverse",
    )(where, table, spectra[plus], spectra[minus], *after)


def side_columns(planes):
    width = planes[0].shape[1]
    row = lax.broadcasted_iota(jnp.int32, (2 * Z, width), 0)
    lane = lax.broadcasted_iota(jnp.int32, (2 * Z, width), 1)
    total = None
    for n in range(Z):
        pick = ((row == n) & (lane == 0)) | ((row == n + Z) & (lane == width - 1))
        part = lax.dot_general(
            pick.astype(f32).astype(bf16),
            planes[n],
            (((1,), (1,)), ((), ())),
            preferred_element_type=f32,
        )
        total = part if total is None else total + part
    return total[:Z].astype(bf16), total[Z:].astype(bf16)


def spread_columns(low, high, first, layers, width):
    row = lax.broadcasted_iota(jnp.int32, (2 * Z, layers * width), 0)
    column = lax.broadcasted_iota(jnp.int32, (2 * Z, layers * width), 1)
    place = jnp.zeros((2 * Z, layers * width), f32)
    for n in range(layers):
        place = place + jnp.where((row == first + n) & (column == n * width), -0.5, 0.0)
        place = place + jnp.where(
            (row == first + n + Z) & (column == (n + 1) * width - 1), 0.5, 0.0
        )
    both = jnp.concatenate([low, high], axis=0).astype(bf16)
    spread = lax.dot_general(
        both, place.astype(bf16), (((0,), (0,)), ((), ())), preferred_element_type=f32
    )
    return [spread[:, n * width : (n + 1) * width] for n in range(layers)]


def edges_kernel(field_ref, *refs):
    first_column_ref, last_column_ref = refs[-2:]
    first, last = side_columns([field_ref[0, n] for n in range(Z)])
    first_column_ref[0] = first
    last_column_ref[0] = last


def edge_columns(field, components, after):
    _, _, height, width = field.shape
    shape = jax.ShapeDtypeStruct((components, Z, height), bf16)
    spec = pl.BlockSpec((1, Z, height), lambda i: (i, 0, 0))
    return pl.pallas_call(
        edges_kernel,
        grid=(components,),
        in_specs=[pl.BlockSpec((1, Z, height, width), lambda i: (i, 0, 0, 0))] + tied(after),
        out_specs=[spec, spec],
        out_shape=[shape, shape],
        compiler_params=params(),
        cost_estimate=takes(4),
        name="edge_columns",
    )(field, *after)


def exchange(first, last, axis):
    count = lax.axis_size(axis)
    up = [(i, (i + 1) % count) for i in range(count)]
    down = [((i + 1) % count, i) for i in range(count)]
    return lax.ppermute(last, axis, up), lax.ppermute(first, axis, down)


def adjoint_kernel(planes_ref, cotangent_ref, *refs):
    adjoint_ref, short_ref, first_x, last_x, first_y, last_y, held = refs
    _, height, width = held.shape
    scale = 1.0 / (X * Y * Z)
    base = pl.program_id(0) * ROWS
    for row, rows, columns in tiles(ROWS, width):
        place = pl.ds(pl.multiple_of(base + row, 16), 16)
        layers = depth_inverse(
            [planes_ref[2 * k, rows, columns].astype(f32) for k in range(KZ)],
            [planes_ref[2 * k + 1, rows, columns].astype(f32) for k in range(KZ)],
        )
        for n in range(Z):
            value = cotangent_ref[0, n, rows, columns] + layers[n] * scale
            adjoint_ref[n, rows, columns] = value
            short_ref[n, rows, columns] = value.astype(bf16)
            held[n, place, columns] = value.astype(bf16)

    @pl.when(pl.program_id(0) == pl.num_programs(0) - 1)
    def _():
        first, last = side_columns([held[n] for n in range(Z)])
        first_x[...] = first
        last_x[...] = last
        top = [held[n, 0:16, :].astype(f32)[0:1] for n in range(Z)]
        bottom = [held[n, height - 16 : height, :].astype(f32)[15:16] for n in range(Z)]
        first_y[...] = jnp.concatenate(top, 0).astype(bf16)
        last_y[...] = jnp.concatenate(bottom, 0).astype(bf16)


def make_adjoint(me, parts, cotangent, component, after):
    whole = len(parts) == 1
    planes, height, width = parts[0].shape
    column = jax.ShapeDtypeStruct((Z, height), bf16)
    row = jax.ShapeDtypeStruct((Z, width), bf16)
    column_spec = pl.BlockSpec((Z, height), lambda j: (0, 0))
    row_spec = pl.BlockSpec((Z, width), lambda j: (0, 0))

    def kernel(me_ref, *refs):
        part_refs, cotangent_ref = refs[: len(parts)], refs[len(parts)]
        outs, held, spectrum = refs[-8:-2], refs[-2], refs[-1]
        if whole:
            spectrum = part_refs[0]
        else:
            for s, part in enumerate(part_refs):
                source = lax.rem(me_ref[0] + len(parts) - s, len(parts))
                spectrum[pl.ds(source * planes, planes)] = part[...]
        adjoint_kernel(spectrum, cotangent_ref, *outs, held)

    return pl.pallas_call(
        kernel,
        grid=(height // ROWS,),
        in_specs=[pl.BlockSpec(memory_space=pltpu.SMEM)]
        + [pl.BlockSpec((planes, ROWS, width), lambda j: (0, j, 0))] * len(parts)
        + [pl.BlockSpec((1, Z, ROWS, width), lambda j: (component, 0, j, 0))]
        + tied(after),
        out_specs=[
            pl.BlockSpec((Z, ROWS, width), lambda j: (0, j, 0)),
            pl.BlockSpec((Z, ROWS, width), lambda j: (0, j, 0)),
            column_spec,
            column_spec,
            row_spec,
            row_spec,
        ],
        out_shape=[
            jax.ShapeDtypeStruct((Z, height, width), f32),
            jax.ShapeDtypeStruct((Z, height, width), bf16),
            column,
            column,
            row,
            row,
        ],
        scratch_shapes=[
            pltpu.VMEM((Z, height, width), bf16),
            pltpu.VMEM((Z, ROWS, width), bf16),
        ],
        compiler_params=params(),
        cost_estimate=takes(5),
        name="make_adjoint",
    )(me, *parts, cotangent, *after)


def pick_row(rows, n):
    index = lax.broadcasted_iota(jnp.int32, rows.shape, 0)
    return jnp.sum(jnp.where(index == n, rows.astype(f32), 0.0), axis=0, keepdims=True)


def end_rows(low, high, height):
    row = lax.broadcasted_iota(jnp.int32, (height, low.shape[1]), 0)
    return jnp.where(row == 0, low * -0.5, 0.0) + jnp.where(row == height - 1, high * 0.5, 0.0)


LAYERS = 4


def grad_vort_kernel(
    component, slope_x, slope_y, velocity, adjoint, low_x, high_x, low_y, high_y, *refs
):
    before, after = refs
    height, width = velocity.shape[2], velocity.shape[3]
    first = pl.program_id(0) * LAYERS
    ends = spread_columns(low_x[0], high_x[0], first, LAYERS, width)
    layers = velocity[0, pl.ds(first, LAYERS)]
    stacked = layers.reshape(LAYERS * height, width)
    inner = jnp.dot(stacked, slope_x[...], preferred_element_type=f32)
    for k in range(LAYERS):
        n = first + k
        above = lax.rem(n + 1, Z)
        below = lax.rem(n + Z - 1, Z)
        value = adjoint[k]
        half = value * step_size
        along_x = inner[k * height : (k + 1) * height] + ends[k]
        along_y = jnp.dot(slope_y[...], layers[k], preferred_element_type=f32)
        along_y = along_y + end_rows(pick_row(low_y[0], n), pick_row(high_y[0], n), height)
        along_z = (velocity[0, above].astype(f32) - velocity[0, below].astype(f32)) * 0.5
        for j, slope in enumerate((along_x, along_y, along_z)):
            term = half * slope
            if j == component:
                term = term + value
            if before is not None:
                term = before[j, k].astype(f32) + term
            after[j, k] = term.astype(after.dtype)


def add_grad_vort(component, slopes, velocity, adjoint, halos, before, after, kind):
    _, _, height, width = velocity.shape
    slope_x, slope_y = slopes
    whole = lambda shape: pl.BlockSpec(shape, lambda n: (0,) * len(shape))
    column = pl.BlockSpec((1, Z, height), lambda n: (component, 0, 0))
    row = pl.BlockSpec((1, Z, width), lambda n: (component, 0, 0))
    sums = pl.BlockSpec((3, LAYERS, height, width), lambda n: (0, n, 0, 0))
    operands = [slope_x, slope_y, velocity, adjoint, *halos]
    in_specs = [
        whole((width, width)),
        whole((height, height)),
        pl.BlockSpec((1, Z, height, width), lambda n: (component, 0, 0, 0)),
        pl.BlockSpec((LAYERS, height, width), lambda n: (n, 0, 0)),
        column,
        column,
        row,
        row,
    ]
    if before is not None:
        operands.append(before)
        in_specs.append(sums)

    def kernel(*refs):
        grad_vort_kernel(component, *refs[:8], None if before is None else refs[8], refs[-1])

    return pl.pallas_call(
        kernel,
        grid=(Z // LAYERS,),
        in_specs=in_specs + tied(after),
        out_specs=sums,
        out_shape=jax.ShapeDtypeStruct((3, Z, height, width), kind),
        compiler_params=params(),
        cost_estimate=takes(9),
        name="add_grad_vort",
    )(*operands, *after)


def grad_vel_kernel(count, slope_x, vorticity, vorticity_above, vorticity_below, *refs):
    adjoints, saved, halos = refs[: 3 * count], refs[3 * count :], refs[3 * count + 4 :]
    vort_low_x, vort_high_x, vort_low_y, vort_high_y = saved[:4]
    after, padded = refs[-2:]
    _, _, height, width = vorticity.shape
    first = pl.program_id(0) * LAYERS

    def times(one, other):
        return one.astype(f32) * other.astype(f32)

    for c in range(count):
        here, above, below = adjoints[3 * c : 3 * c + 3]
        low_x, high_x, low_y, high_y = halos[4 * c : 4 * c + 4]
        ends = spread_columns(
            times(vort_low_x[0], low_x[...]),
            times(vort_high_x[0], high_x[...]),
            first,
            LAYERS,
            width,
        )
        product = [times(vorticity[0, k], here[k]).astype(bf16) for k in range(LAYERS)]
        inner = jnp.dot(
            jnp.concatenate(product, axis=0), slope_x[...], preferred_element_type=f32
        )
        deep = [times(vorticity_below[0, 0], below[0])]
        deep = deep + [times(vorticity[2, k], here[k]) for k in range(LAYERS)]
        deep = deep + [times(vorticity_above[0, 0], above[0])]
        for k in range(LAYERS):
            n = first + k
            padded[k, 8 : 8 + height, :] = times(vorticity[1, k], here[k])
            padded[k, 7:8, :] = pick_row(vort_low_y[0], n) * pick_row(low_y[...], n)
            padded[k, 8 + height : 9 + height, :] = pick_row(vort_high_y[0], n) * pick_row(
                high_y[...], n
            )
            total = (padded[k, 9 : 9 + height, :] - padded[k, 7 : 7 + height, :]) + (
                deep[k + 2] - deep[k]
            )
            total = total * 0.5 + inner[k * height : (k + 1) * height] + ends[k]
            after[c, k] = total * -step_size


def write_grad_vel(components, slope_x, vorticity, adjoints, saved_halos, halos, before, after):
    _, _, height, width = vorticity.shape
    count = len(components)
    start = components[0] // count
    whole = lambda shape: pl.BlockSpec(shape, lambda n: (0,) * len(shape))
    saved_column = pl.BlockSpec((1, Z, height), lambda n: (3, 0, 0))
    saved_row = pl.BlockSpec((1, Z, width), lambda n: (3, 0, 0))
    layer_above = lambda n: lax.rem((n + 1) * LAYERS, Z)
    layer_below = lambda n: lax.rem(n * LAYERS + Z - 1, Z)
    operands = [slope_x, vorticity, vorticity, vorticity]
    in_specs = [
        whole((width, width)),
        pl.BlockSpec((3, LAYERS, height, width), lambda n: (0, n, 0, 0)),
        pl.BlockSpec((1, 1, height, width), lambda n: (2, layer_above(n), 0, 0)),
        pl.BlockSpec((1, 1, height, width), lambda n: (2, layer_below(n), 0, 0)),
    ]
    for adjoint in adjoints:
        operands = operands + [adjoint] * 3
        in_specs = in_specs + [
            pl.BlockSpec((LAYERS, height, width), lambda n: (n, 0, 0)),
            pl.BlockSpec((1, height, width), lambda n: (layer_above(n), 0, 0)),
            pl.BlockSpec((1, height, width), lambda n: (layer_below(n), 0, 0)),
        ]
    operands = operands + list(saved_halos)
    in_specs = in_specs + [saved_column, saved_column, saved_row, saved_row]
    for edge in halos:
        operands = operands + list(edge)
        in_specs = in_specs + [whole((Z, height))] * 2 + [whole((Z, width))] * 2
    aliases = {}
    if before is not None:
        aliases = {len(operands): 0}
        operands.append(before)
        in_specs.append(pl.BlockSpec(memory_space=pl.ANY))

    def kernel(*refs):
        grad_vel_kernel(count, *refs)

    return pl.pallas_call(
        kernel,
        grid=(Z // LAYERS,),
        in_specs=in_specs + tied(after),
        out_specs=pl.BlockSpec((count, LAYERS, height, width), lambda n: (start, n, 0, 0)),
        out_shape=jax.ShapeDtypeStruct((3, Z, height, width), f32),
        input_output_aliases=aliases,
        scratch_shapes=[pltpu.VMEM((LAYERS, height + 16, width), f32)],
        compiler_params=params(),
        cost_estimate=takes(6 * count),
        name="write_grad_vel",
    )(*operands, *after)


def pair_exchange(parts, axis, mine):
    count = lax.axis_size(axis)
    kept = lax.dynamic_index_in_dim(parts, mine, 1, keepdims=False)
    sent = lax.dynamic_index_in_dim(parts, 1 - mine, 1, keepdims=False)
    got = lax.ppermute(sent, axis, [(i, i ^ 1) for i in range(count)])
    return jnp.where(mine == 0, jnp.stack([kept, got], 1), jnp.stack([got, kept], 1))


def shifted(parts, axis):
    count = lax.axis_size(axis)
    return [parts[0]] + [
        lax.ppermute(parts[s], axis, [(i, (i + s) % count) for i in range(count)])
        for s in range(1, count)
    ]


def local(cot_vort, cot_vel, vorticity, velocity):
    size_x = lax.axis_size("gx")
    size_y = lax.axis_size("gy")
    planes = Z // size_y
    halves = size_y // KZ
    _, _, height, width = cot_vel.shape
    modes = HALF_Y // (size_x * halves)
    place_x = lax.axis_index("gx")
    place_y = lax.axis_index("gy")
    half = lax.rem(place_y, halves)
    me = place_y.astype(jnp.int32).reshape(1)
    where = jnp.stack([(place_x * halves + half) * modes, place_y // halves]).astype(jnp.int32)

    y_table, y_back_table = y_tables(size_x * halves)
    x_table, x_back_table = x_tables()
    slope_x = slope_matrix(width)
    slope_y = np.ascontiguousarray(slope_matrix(height).T)

    layers = depth_transform(cot_vel, FORWARD_ORDER[0])

    velocity_first, velocity_last = edge_columns(velocity, 3, (layers,))
    vorticity_first, vorticity_last = edge_columns(vorticity, 1, (layers,))
    low_x, high_x = exchange(
        jnp.concatenate([velocity_first, vorticity_first]),
        jnp.concatenate([velocity_last, vorticity_last]),
        "gx",
    )
    low_y, high_y = exchange(
        jnp.concatenate([velocity[:, :, 0], vorticity[1:2, :, 0]]),
        jnp.concatenate([velocity[:, :, height - 1], vorticity[1:2, :, height - 1]]),
        "gy",
    )
    saved_halos = (low_x, high_x, low_y, high_y)
    early = ((low_x, high_x), (low_y, high_y), ())

    columns = layers.reshape(size_y, planes, height, width)
    columns = [lax.all_to_all(columns, "gy", 0, 0, tiled=True)]
    sent = []
    for place in range(3):
        if place > 0:
            layers = depth_transform(cot_vel, FORWARD_ORDER[place], me, size_y, (sent[-1],))
            columns = shifted(layers, "gy")
        parts = y_transform(me, y_table, columns, size_x, halves, early[place])
        parts = parts.reshape(size_x, 2, 2, modes, width)
        sent.append(parts if halves == 1 else pair_exchange(parts, "gy", half))

    def spectrum(place, after):
        lines = lax.all_to_all(sent[place], "gx", 0, 0, tiled=True)
        return x_transform(x_table, lines, after)

    def curl(component, after):
        return curl_inverse(where, x_back_table, spectra, component, size_x, after)

    def back(filtered):
        parts = lax.all_to_all(filtered, "gx", 0, 0, tiled=True)
        if halves == 2:
            parts = pair_exchange(parts, "gy", half)
        return parts.reshape(size_x, halves, planes, 2, modes, width)

    def rows_of(component, modes_back, after):
        split = component != BACK_ORDER[2]
        return y_inverse(me, y_back_table, modes_back, size_y, split, after)

    def layers_of(rows):
        if len(rows) == 1:
            return [lax.all_to_all(rows[0], "gy", 0, 0, tiled=True).reshape(Z, height, width)]
        return shifted(rows, "gy")

    one, two, three = BACK_ORDER
    spectra = {FORWARD_ORDER[0]: spectrum(0, (sent[1],))}
    spectra[FORWARD_ORDER[1]] = spectrum(1, (sent[2],))
    curl_one = curl(one, ())
    spectra[FORWARD_ORDER[2]] = spectrum(2, (curl_one,))
    curl_two = curl(two, ())
    rows_one = rows_of(one, back(curl_one), (curl_two,))
    layers_one = layers_of(rows_one)
    curl_three = curl(three, tuple(layers_one))

    def adjoint_of(component, parts, after):
        adjoint, short, first_x, last_x, first_y, last_y = make_adjoint(
            me, parts, cot_vort, component, after
        )
        return adjoint, short, exchange(first_x, last_x, "gx") + exchange(first_y, last_y, "gy")

    def vort_of(component, adjoint, before, after):
        kind = f32 if component == three else bf16
        return add_grad_vort(
            component, (slope_x, slope_y), velocity, adjoint, saved_halos, before, after, kind
        )

    def vel_of(components, adjoints, halos, before, after):
        return write_grad_vel(
            components, slope_x, vorticity, adjoints, saved_halos, halos, before, after
        )

    adjoint_one, short_one, halos_one = adjoint_of(one, layers_one, ())
    rows_two = rows_of(two, back(curl_two), (adjoint_one,))
    layers_two = layers_of(rows_two)
    rows_three = rows_of(three, back(curl_three), tuple(layers_two) + halos_one)
    grad_vort = vort_of(one, adjoint_one, None, (rows_three[0],))
    adjoint_two, short_two, halos_two = adjoint_of(two, layers_two, (grad_vort,))
    grad_vel = vel_of((one,), [short_one], [halos_one], None, (grad_vort,))
    grad_vort = vort_of(two, adjoint_two, grad_vort, (grad_vel,))
    adjoint_three, short_three, halos_three = adjoint_of(
        three, layers_of(rows_three), (grad_vort,)
    )
    grad_vort = vort_of(three, adjoint_three, grad_vort, ())
    grad_vel = vel_of(
        (two, three), [short_two, short_three], [halos_two, halos_three], grad_vel, (grad_vort,)
    )
    return grad_vort, grad_vel


def solution(mesh):
    spec = P(None, None, "gy", "gx")
    return jax.shard_map(
        local,
        mesh=mesh,
        in_specs=(spec, spec, spec, spec),
        out_specs=(spec, spec),
        check_vma=False,
    )
```

```python
import math

import jax
import jax.numpy as jnp
import ml_dtypes
import numpy as np
from jax import lax
from jax.experimental import pallas as pl
from jax.experimental.pallas import tpu as pltpu
from jax.sharding import PartitionSpec as P

X = 1024
Y = 1536
Z = 16
HALF_X = X // 2
HALF_Y = Y // 2
KZ = Z // 2

step_size = 0.5

f32 = jnp.float32
bf16 = jnp.bfloat16

FORWARD_ORDER = (0, 1, 2)
BACK_ORDER = (2, 0, 1)


def params(megabytes=56):
    return pltpu.CompilerParams(vmem_limit_bytes=megabytes * 1024 * 1024)


def takes(microseconds):
    return pl.CostEstimate(flops=1, bytes_accessed=int(microseconds * 3.0e6), transcendentals=0)


def tied(after):
    return [pl.BlockSpec(memory_space=pl.ANY)] * len(after)


def trig(first, second, length):
    angle = (np.outer(first, second) % length) * (2.0 * math.pi / length)
    return np.cos(angle), np.sin(angle)


def y_tables(blocks):
    cosine, sine = trig(np.arange(HALF_Y), np.arange(Y), Y)
    both = np.stack([cosine.reshape(blocks, -1, Y), sine.reshape(blocks, -1, Y)], 1).reshape(Y, Y)
    both = both.astype(ml_dtypes.bfloat16)
    return both, np.ascontiguousarray(both.T)


def x_tables():
    cosine, sine = trig(np.arange(X), np.arange(HALF_X), X)
    both = np.concatenate([cosine, sine], 1).astype(ml_dtypes.bfloat16)
    return both, np.ascontiguousarray(both.T)


def slope_matrix(size):
    return ((np.eye(size, k=-1) - np.eye(size, k=1)) * 0.5).astype(ml_dtypes.bfloat16)


def combine(terms):
    total = None
    for factor, value in terms:
        if abs(factor) < 1e-12:
            continue
        if abs(factor - 1.0) < 1e-12:
            part = value
        elif abs(factor + 1.0) < 1e-12:
            part = -value
        else:
            part = value * factor
        total = part if total is None else total + part
    return total


def depth_forward(values):
    even = [values[0]] + [values[n] + values[Z - n] for n in range(1, 8)] + [values[8]]
    odd = [None] + [values[n] - values[Z - n] for n in range(1, 8)]
    even_sum = [even[n] + even[8 - n] for n in range(4)] + [even[4]]
    even_dif = [even[n] - even[8 - n] for n in range(4)]
    odd_sum = [None] + [odd[n] + odd[8 - n] for n in range(1, 4)] + [odd[4]]
    odd_dif = [None] + [odd[n] - odd[8 - n] for n in range(1, 4)]
    result = []
    for k in range(KZ):
        folded = even_sum if k % 2 == 0 else even_dif
        cos_part = combine([(math.cos(math.pi * k * n / 8), folded[n]) for n in range(len(folded))])
        folded = odd_dif if k % 2 == 0 else odd_sum
        sin_part = combine(
            [(math.sin(math.pi * k * n / 8), folded[n]) for n in range(1, len(folded))]
        )
        result.append((cos_part, sin_part))
    return result


def depth_inverse(cos_parts, sin_parts):
    layers = [None] * Z
    cos_sum, sin_sum = [None] * 9, [None] * 9
    for n in range(5):
        evens = combine([(math.cos(math.pi * k * n / 8), cos_parts[k]) for k in range(0, KZ, 2)])
        odds = combine([(math.cos(math.pi * k * n / 8), cos_parts[k]) for k in range(1, KZ, 2)])
        if n == 4:
            cos_sum[4] = evens
        else:
            cos_sum[n] = evens + odds
            cos_sum[8 - n] = evens - odds
    for n in range(1, 5):
        evens = combine([(math.sin(math.pi * k * n / 8), sin_parts[k]) for k in range(0, KZ, 2)])
        odds = combine([(math.sin(math.pi * k * n / 8), sin_parts[k]) for k in range(1, KZ, 2)])
        if n == 4:
            sin_sum[4] = odds
        else:
            sin_sum[n] = odds + evens
            sin_sum[8 - n] = odds - evens
    layers[0], layers[8] = cos_sum[0], cos_sum[8]
    for n in range(1, 8):
        layers[n] = cos_sum[n] + sin_sum[n]
        layers[Z - n] = cos_sum[n] - sin_sum[n]
    return layers


ROWS = 96


def tiles(height, width):
    for row in range(0, height, 16):
        for column in range(0, width, 128):
            yield row, pl.ds(row, 16), pl.ds(column, 128)


def depth_forward_kernel(values_ref, planes_ref):
    _, _, height, width = values_ref.shape
    for _, rows, columns in tiles(height, width):
        spectrum = depth_forward([values_ref[0, n, rows, columns] for n in range(Z)])
        for k, (cos_part, sin_part) in enumerate(spectrum):
            planes_ref[2 * k, rows, columns] = cos_part.astype(bf16)
            if sin_part is None:
                sin_part = jnp.zeros_like(cos_part)
            planes_ref[2 * k + 1, rows, columns] = sin_part.astype(bf16)


def depth_transform(values, component, me=None, size_y=1, after=()):
    _, _, height, width = values.shape
    planes = Z // size_y
    shifted_out = me is not None

    def kernel(*refs):
        if not shifted_out:
            depth_forward_kernel(*refs)
            return
        me_ref, values_ref, outs, held = refs[0], refs[1], refs[2 + len(after) : -1], refs[-1]
        depth_forward_kernel(values_ref, held)
        for s, out in enumerate(outs):
            target = lax.rem(me_ref[0] + s, size_y)
            out[...] = held[pl.ds(target * planes, planes)]

    block = (Z // size_y, ROWS, width)
    out_spec = pl.BlockSpec(block, lambda j: (0, j, 0))
    out_shape = jax.ShapeDtypeStruct((planes, height, width), bf16)
    smem = pl.BlockSpec(memory_space=pltpu.SMEM)
    return pl.pallas_call(
        kernel,
        grid=(height // ROWS,),
        in_specs=([smem] if shifted_out else [])
        + [pl.BlockSpec((1, Z, ROWS, width), lambda j: (component, 0, j, 0))]
        + tied(after),
        out_specs=[out_spec] * size_y if shifted_out else out_spec,
        out_shape=[out_shape] * size_y if shifted_out else out_shape,
        scratch_shapes=[pltpu.VMEM((Z, ROWS, width), bf16)] if shifted_out else [],
        compiler_params=params(),
        cost_estimate=takes(3),
        name="depth_transform",
    )(*(([me] if shifted_out else []) + [values, *after]))


def fetch_blocks(table_ref, held, arrived, order):
    count, rows, _ = held.shape
    copies = []
    for s in range(count):
        place = pl.ds(pl.multiple_of(order(s) * rows, rows), rows)
        copies.append(pltpu.make_async_copy(table_ref.at[place], held.at[s], arrived.at[s]))
        copies[s].start()
    return copies


def y_transform(me, table, columns, blocks, halves, after):
    whole = len(columns) == 1
    size_y = columns[0].shape[0] if whole else len(columns)
    planes, height, width = columns[0].shape[-3:]
    modes = HALF_Y // (blocks * halves)
    rows = Y // blocks
    shape = (blocks, halves, planes, 2, modes, width)

    def kernel(me_ref, table_ref, *refs):
        parts = refs[: len(columns)]
        out, held, lines, ready, table_in, lines_in, ready_out = refs[-7:]
        copies = []
        for s in range(size_y):
            source = s if whole else lax.rem(me_ref[0] + size_y - s, size_y)
            place = pl.ds(pl.multiple_of(source * height, height), height)
            for plane in range(planes):
                part = parts[0].at[s, plane] if whole else parts[s].at[plane]
                copies.append(
                    pltpu.make_async_copy(
                        part, lines.at[plane, place], lines_in.at[s * planes + plane]
                    )
                )
                copies[-1].start()
        tables = fetch_blocks(table_ref, held, table_in, lambda s: s)
        for copy in copies:
            copy.wait()
        results = []
        for s in range(blocks):
            tables[s].wait()
            for plane in range(planes):
                part = jnp.dot(held[s], lines[plane], preferred_element_type=f32)
                ready[s, :, plane] = part.astype(bf16).reshape(halves, 2, modes, width)
            results.append(pltpu.make_async_copy(ready.at[s], out.at[s], ready_out.at[s]))
            results[s].start()
        for result in results:
            result.wait()

    anywhere = pl.BlockSpec(memory_space=pl.ANY)
    return pl.pallas_call(
        kernel,
        in_specs=[pl.BlockSpec(memory_space=pltpu.SMEM), anywhere]
        + [anywhere] * len(columns)
        + tied(after),
        out_specs=anywhere,
        out_shape=jax.ShapeDtypeStruct(shape, bf16),
        scratch_shapes=[
            pltpu.VMEM((blocks, rows, Y), bf16),
            pltpu.VMEM((planes, Y, width), bf16),
            pltpu.VMEM(shape, bf16),
            pltpu.SemaphoreType.DMA((blocks,)),
            pltpu.SemaphoreType.DMA((size_y * planes,)),
            pltpu.SemaphoreType.DMA((blocks,)),
        ],
        compiler_params=params(),
        cost_estimate=takes(5),
        name="y_transform",
    )(me, table, *columns, *after)


def y_inverse(me, table, modes, size_y, split, after):
    blocks, halves, planes, _, count, width = modes.shape
    height = Y // size_y
    shape = (planes, height, width)

    def kernel(me_ref, table_ref, modes_ref, *refs):
        outs = refs[len(after) : -6]
        held, lines, ready, table_in, lines_in, ready_out = refs[-6:]
        copies = []
        for block in range(blocks):
            for h in range(halves):
                for plane in range(planes):
                    copies.append(
                        pltpu.make_async_copy(
                            modes_ref.at[block, h, plane],
                            lines.at[plane, block, h],
                            lines_in.at[(block * halves + h) * planes + plane],
                        )
                    )
                    copies[-1].start()
        tables = fetch_blocks(
            table_ref, held, table_in, lambda s: lax.rem(me_ref[0] + s, size_y) if split else s
        )
        for copy in copies:
            copy.wait()
        results = []
        for s in range(size_y):
            tables[s].wait()
            for plane in range(planes):
                columns = lines[plane].reshape(Y, width)
                rows = jnp.dot(held[s], columns, preferred_element_type=f32)
                ready[s, plane] = rows.astype(bf16)
            out = outs[s] if split else outs[0].at[s]
            results.append(pltpu.make_async_copy(ready.at[s], out, ready_out.at[s]))
            results[s].start()
        for result in results:
            result.wait()

    anywhere = pl.BlockSpec(memory_space=pl.ANY)
    if split:
        out_shape = [jax.ShapeDtypeStruct(shape, bf16)] * size_y
    else:
        out_shape = [jax.ShapeDtypeStruct((size_y,) + shape, bf16)]
    return pl.pallas_call(
        kernel,
        in_specs=[pl.BlockSpec(memory_space=pltpu.SMEM), anywhere, anywhere] + tied(after),
        out_specs=[anywhere] * len(out_shape),
        out_shape=out_shape,
        scratch_shapes=[
            pltpu.VMEM((size_y, height, Y), bf16),
            pltpu.VMEM((planes, blocks, halves, 2, count, width), bf16),
            pltpu.VMEM((size_y,) + shape, bf16),
            pltpu.SemaphoreType.DMA((size_y,)),
            pltpu.SemaphoreType.DMA((blocks * halves * planes,)),
            pltpu.SemaphoreType.DMA((size_y,)),
        ],
        compiler_params=params(),
        cost_estimate=takes(4),
        name="y_inverse",
    )(me, table, modes, *after)


def x_transform(table, modes, after):
    blocks, _, _, count, width = modes.shape

    def kernel(table_ref, modes_ref, *refs):
        spectrum_ref = refs[-1]
        rows = jnp.concatenate(
            [modes_ref[block, 0].reshape(2 * count, width) for block in range(blocks)], axis=1
        )
        spectrum = jnp.dot(rows, table_ref[...], preferred_element_type=f32)
        spectrum_ref[0] = spectrum.reshape(2, count, X)

    return pl.pallas_call(
        kernel,
        grid=(2,),
        in_specs=[
            pl.BlockSpec((X, X), lambda j: (0, 0)),
            pl.BlockSpec((blocks, 1, 2, count, width), lambda j: (0, j, 0, 0, 0)),
        ]
        + tied(after),
        out_specs=pl.BlockSpec((1, 2, count, X), lambda j: (j, 0, 0, 0)),
        out_shape=jax.ShapeDtypeStruct((2, 2, count, X), f32),
        compiler_params=params(24),
        cost_estimate=takes(3),
        name="x_transform",
    )(table, modes, *after)


def turned(field, axis, tz, ty, tx, wave):
    index = [tz, ty, tx]
    sign = 1.0 if index[axis] == 0 else -1.0
    index[axis] = 1 - index[axis]
    value = field[index[0], index[1], :, index[2] * HALF_X : (index[2] + 1) * HALF_X]
    return value * (wave * sign)


CURL = {
    0: ((1, 2), (0, 1)),
    1: ((0, 0), (2, 2)),
    2: ((2, 1), (1, 0)),
}


def curl_kernel(axes, where_ref, table_ref, plus_ref, minus_ref, back_ref):
    blocks, _, _, count, width = back_ref.shape
    base = where_ref[0] + pl.program_id(0) * count
    depth = where_ref[1]
    mode_y = lax.broadcasted_iota(jnp.int32, (count, HALF_X), 0) + base
    mode_x = lax.broadcasted_iota(jnp.int32, (count, HALF_X), 1)
    wave_y = mode_y.astype(f32) * (2.0 * math.pi / Y)
    wave_x = mode_x.astype(f32) * (2.0 * math.pi / X)
    wave_z = jnp.full((count, HALF_X), depth, jnp.int32).astype(f32) * (2.0 * math.pi / Z)
    square = wave_x * wave_x + wave_y * wave_y + wave_z * wave_z
    doubling = (
        jnp.where(mode_x == 0, 1.0, 2.0)
        * jnp.where(mode_y == 0, 1.0, 2.0)
        * jnp.where(wave_z == 0.0, 1.0, 2.0)
    )
    weight = jnp.where(square > 0, doubling / jnp.where(square > 0, square, 1.0), 0.0)
    waves = [wave_z * weight, wave_y * weight, wave_x * weight]
    rows = []
    for tz in range(2):
        for ty in range(2):
            parts = []
            for tx in range(2):
                parts.append(
                    (
                        turned(plus_ref, axes[0], tz, ty, tx, waves[axes[0]])
                        - turned(minus_ref, axes[1], tz, ty, tx, waves[axes[1]])
                    ).astype(bf16)
                )
            rows.append(jnp.concatenate(parts, axis=1))
    rows = jnp.concatenate(rows, axis=0)
    back = jnp.dot(rows, table_ref[...], preferred_element_type=f32).astype(bf16)
    for block in range(blocks):
        back_ref[block] = back[:, block * width : (block + 1) * width].reshape(2, 2, count, width)


def curl_inverse(where, table, spectra, component, blocks, after):
    (plus_axis, plus), (minus_axis, minus) = CURL[component]
    total = spectra[plus].shape[2]
    width = X // blocks
    count = 96 if total % 96 == 0 else total
    spec = pl.BlockSpec((2, 2, count, X), lambda j: (0, 0, j, 0))

    def kernel(*refs):
        curl_kernel((plus_axis, minus_axis), *refs[:4], refs[-1])

    return pl.pallas_call(
        kernel,
        grid=(total // count,),
        in_specs=[
            pl.BlockSpec(memory_space=pltpu.SMEM),
            pl.BlockSpec((X, X), lambda j: (0, 0)),
            spec,
            spec,
        ]
        + tied(after),
        out_specs=pl.BlockSpec((blocks, 2, 2, count, width), lambda j: (0, 0, 0, j, 0)),
        out_shape=jax.ShapeDtypeStruct((blocks, 2, 2, total, width), bf16),
        compiler_params=params(24),
        cost_estimate=takes(4),
        name="curl_inverse",
    )(where, table, spectra[plus], spectra[minus], *after)


def side_columns(planes):
    width = planes[0].shape[1]
    row = lax.broadcasted_iota(jnp.int32, (2 * Z, width), 0)
    lane = lax.broadcasted_iota(jnp.int32, (2 * Z, width), 1)
    total = None
    for n in range(Z):
        pick = ((row == n) & (lane == 0)) | ((row == n + Z) & (lane == width - 1))
        part = lax.dot_general(
            pick.astype(f32).astype(bf16),
            planes[n],
            (((1,), (1,)), ((), ())),
            preferred_element_type=f32,
        )
        total = part if total is None else total + part
    return total[:Z].astype(bf16), total[Z:].astype(bf16)


def spread_columns(low, high, first, layers, width):
    row = lax.broadcasted_iota(jnp.int32, (2 * Z, layers * width), 0)
    column = lax.broadcasted_iota(jnp.int32, (2 * Z, layers * width), 1)
    place = jnp.zeros((2 * Z, layers * width), f32)
    for n in range(layers):
        place = place + jnp.where((row == first + n) & (column == n * width), -0.5, 0.0)
        place = place + jnp.where(
            (row == first + n + Z) & (column == (n + 1) * width - 1), 0.5, 0.0
        )
    both = jnp.concatenate([low, high], axis=0).astype(bf16)
    spread = lax.dot_general(
        both, place.astype(bf16), (((0,), (0,)), ((), ())), preferred_element_type=f32
    )
    return [spread[:, n * width : (n + 1) * width] for n in range(layers)]


def edges_kernel(field_ref, *refs):
    first_column_ref, last_column_ref = refs[-2:]
    first, last = side_columns([field_ref[0, n] for n in range(Z)])
    first_column_ref[0] = first
    last_column_ref[0] = last


def edge_columns(field, components, after):
    _, _, height, width = field.shape
    shape = jax.ShapeDtypeStruct((components, Z, height), bf16)
    spec = pl.BlockSpec((1, Z, height), lambda i: (i, 0, 0))
    return pl.pallas_call(
        edges_kernel,
        grid=(components,),
        in_specs=[pl.BlockSpec((1, Z, height, width), lambda i: (i, 0, 0, 0))] + tied(after),
        out_specs=[spec, spec],
        out_shape=[shape, shape],
        compiler_params=params(),
        cost_estimate=takes(4),
        name="edge_columns",
    )(field, *after)


def exchange(first, last, axis):
    count = lax.axis_size(axis)
    up = [(i, (i + 1) % count) for i in range(count)]
    down = [((i + 1) % count, i) for i in range(count)]
    return lax.ppermute(last, axis, up), lax.ppermute(first, axis, down)


def adjoint_kernel(planes_ref, cotangent_ref, *refs):
    adjoint_ref, short_ref, first_x, last_x, first_y, last_y, held = refs
    _, height, width = held.shape
    scale = 1.0 / (X * Y * Z)
    base = pl.program_id(0) * ROWS
    for row, rows, columns in tiles(ROWS, width):
        place = pl.ds(pl.multiple_of(base + row, 16), 16)
        layers = depth_inverse(
            [planes_ref[2 * k, rows, columns].astype(f32) for k in range(KZ)],
            [planes_ref[2 * k + 1, rows, columns].astype(f32) for k in range(KZ)],
        )
        for n in range(Z):
            value = cotangent_ref[0, n, rows, columns] + layers[n] * scale
            adjoint_ref[n, rows, columns] = value
            short_ref[n, rows, columns] = value.astype(bf16)
            held[n, place, columns] = value.astype(bf16)

    @pl.when(pl.program_id(0) == pl.num_programs(0) - 1)
    def _():
        first, last = side_columns([held[n] for n in range(Z)])
        first_x[0] = first
        last_x[0] = last
        top = [held[n, 0:16, :].astype(f32)[0:1] for n in range(Z)]
        bottom = [held[n, height - 16 : height, :].astype(f32)[15:16] for n in range(Z)]
        first_y[0] = jnp.concatenate(top, 0).astype(bf16)
        last_y[0] = jnp.concatenate(bottom, 0).astype(bf16)


def make_adjoint(me, parts, cotangent, component, edges, after):
    whole = len(parts) == 1
    planes, height, width = parts[0].shape
    column = jax.ShapeDtypeStruct((3, Z, height), bf16)
    row = jax.ShapeDtypeStruct((3, Z, width), bf16)
    column_spec = pl.BlockSpec((1, Z, height), lambda j: (component, 0, 0))
    row_spec = pl.BlockSpec((1, Z, width), lambda j: (component, 0, 0))
    first_edge = 2 + len(parts)

    def kernel(me_ref, *refs):
        part_refs, cotangent_ref = refs[: len(parts)], refs[len(parts)]
        outs, held, spectrum = refs[-8:-2], refs[-2], refs[-1]
        if whole:
            spectrum = part_refs[0]
        else:
            for s, part in enumerate(part_refs):
                source = lax.rem(me_ref[0] + len(parts) - s, len(parts))
                spectrum[pl.ds(source * planes, planes)] = part[...]
        adjoint_kernel(spectrum, cotangent_ref, *outs, held)

    return pl.pallas_call(
        kernel,
        grid=(height // ROWS,),
        in_specs=[pl.BlockSpec(memory_space=pltpu.SMEM)]
        + [pl.BlockSpec((planes, ROWS, width), lambda j: (0, j, 0))] * len(parts)
        + [pl.BlockSpec((1, Z, ROWS, width), lambda j: (component, 0, j, 0))]
        + tied(edges)
        + tied(after),
        out_specs=[
            pl.BlockSpec((Z, ROWS, width), lambda j: (0, j, 0)),
            pl.BlockSpec((Z, ROWS, width), lambda j: (0, j, 0)),
            column_spec,
            column_spec,
            row_spec,
            row_spec,
        ],
        out_shape=[
            jax.ShapeDtypeStruct((Z, height, width), f32),
            jax.ShapeDtypeStruct((Z, height, width), bf16),
            column,
            column,
            row,
            row,
        ],
        input_output_aliases={first_edge + n: 2 + n for n in range(len(edges))},
        scratch_shapes=[
            pltpu.VMEM((Z, height, width), bf16),
            pltpu.VMEM((Z, ROWS, width), bf16),
        ],
        compiler_params=params(),
        cost_estimate=takes(5),
        name="make_adjoint",
    )(me, *parts, cotangent, *edges, *after)


def pick_row(rows, n):
    index = lax.broadcasted_iota(jnp.int32, rows.shape, 0)
    return jnp.sum(jnp.where(index == n, rows.astype(f32), 0.0), axis=0, keepdims=True)


def end_rows(low, high, height):
    row = lax.broadcasted_iota(jnp.int32, (height, low.shape[1]), 0)
    return jnp.where(row == 0, low * -0.5, 0.0) + jnp.where(row == height - 1, high * 0.5, 0.0)


LAYERS = 2


def grad_vort_kernel(
    component, slope_x, slope_y, velocity, adjoint, low_x, high_x, low_y, high_y, *refs
):
    before, after = refs
    height, width = velocity.shape[2], velocity.shape[3]
    first = pl.program_id(0) * LAYERS
    ends = spread_columns(low_x[0], high_x[0], first, LAYERS, width)
    layers = velocity[0, pl.ds(first, LAYERS)]
    stacked = layers.reshape(LAYERS * height, width)
    inner = jnp.dot(stacked, slope_x[...], preferred_element_type=f32)
    for k in range(LAYERS):
        n = first + k
        above = lax.rem(n + 1, Z)
        below = lax.rem(n + Z - 1, Z)
        value = adjoint[k]
        half = value * step_size
        along_x = inner[k * height : (k + 1) * height] + ends[k]
        along_y = jnp.dot(slope_y[...], layers[k], preferred_element_type=f32)
        along_y = along_y + end_rows(pick_row(low_y[0], n), pick_row(high_y[0], n), height)
        along_z = (velocity[0, above].astype(f32) - velocity[0, below].astype(f32)) * 0.5
        for j, slope in enumerate((along_x, along_y, along_z)):
            term = half * slope
            if j == component:
                term = term + value
            if before is not None:
                term = before[j, k].astype(f32) + term
            after[j, k] = term.astype(after.dtype)


def add_grad_vort(component, slopes, velocity, adjoint, halos, before, after, kind):
    _, _, height, width = velocity.shape
    slope_x, slope_y = slopes
    whole = lambda shape: pl.BlockSpec(shape, lambda n: (0,) * len(shape))
    column = pl.BlockSpec((1, Z, height), lambda n: (component, 0, 0))
    row = pl.BlockSpec((1, Z, width), lambda n: (component, 0, 0))
    sums = pl.BlockSpec((3, LAYERS, height, width), lambda n: (0, n, 0, 0))
    operands = [slope_x, slope_y, velocity, adjoint, *halos]
    in_specs = [
        whole((width, width)),
        whole((height, height)),
        pl.BlockSpec((1, Z, height, width), lambda n: (component, 0, 0, 0)),
        pl.BlockSpec((LAYERS, height, width), lambda n: (n, 0, 0)),
        column,
        column,
        row,
        row,
    ]
    if before is not None:
        operands.append(before)
        in_specs.append(sums)

    def kernel(*refs):
        grad_vort_kernel(component, *refs[:8], None if before is None else refs[8], refs[-1])

    return pl.pallas_call(
        kernel,
        grid=(Z // LAYERS,),
        in_specs=in_specs + tied(after),
        out_specs=sums,
        out_shape=jax.ShapeDtypeStruct((3, Z, height, width), kind),
        compiler_params=params(),
        cost_estimate=takes(9),
        name="add_grad_vort",
    )(*operands, *after)


def grad_vel_kernel(count, slope_x, vorticity, vorticity_above, vorticity_below, *refs):
    adjoints, edges = refs[: 3 * count], refs[3 * count :]
    vort_low_x, vort_high_x, vort_low_y, vort_high_y, low_x, high_x, low_y, high_y = edges[:8]
    after, padded = refs[-2:]
    _, _, height, width = vorticity.shape
    first = pl.program_id(0) * LAYERS

    def times(one, other):
        return one.astype(f32) * other.astype(f32)

    for c in range(count):
        here, above, below = adjoints[3 * c : 3 * c + 3]
        ends = spread_columns(
            times(vort_low_x[0], low_x[c]),
            times(vort_high_x[0], high_x[c]),
            first,
            LAYERS,
            width,
        )
        product = [times(vorticity[0, k], here[k]).astype(bf16) for k in range(LAYERS)]
        inner = jnp.dot(
            jnp.concatenate(product, axis=0), slope_x[...], preferred_element_type=f32
        )
        deep = [times(vorticity_below[0, 0], below[0])]
        deep = deep + [times(vorticity[2, k], here[k]) for k in range(LAYERS)]
        deep = deep + [times(vorticity_above[0, 0], above[0])]
        for k in range(LAYERS):
            n = first + k
            padded[k, 8 : 8 + height, :] = times(vorticity[1, k], here[k])
            padded[k, 7:8, :] = pick_row(vort_low_y[0], n) * pick_row(low_y[c], n)
            padded[k, 8 + height : 9 + height, :] = pick_row(vort_high_y[0], n) * pick_row(
                high_y[c], n
            )
            total = (padded[k, 9 : 9 + height, :] - padded[k, 7 : 7 + height, :]) + (
                deep[k + 2] - deep[k]
            )
            total = total * 0.5 + inner[k * height : (k + 1) * height] + ends[k]
            after[c, k] = total * -step_size


def write_grad_vel(slope_x, vorticity, adjoints, saved_halos, halos, after):
    _, _, height, width = vorticity.shape
    count = len(adjoints)
    whole = lambda shape: pl.BlockSpec(shape, lambda n: (0,) * len(shape))
    saved_column = pl.BlockSpec((1, Z, height), lambda n: (3, 0, 0))
    saved_row = pl.BlockSpec((1, Z, width), lambda n: (3, 0, 0))
    layer_above = lambda n: lax.rem((n + 1) * LAYERS, Z)
    layer_below = lambda n: lax.rem(n * LAYERS + Z - 1, Z)
    operands = [slope_x, vorticity, vorticity, vorticity]
    in_specs = [
        whole((width, width)),
        pl.BlockSpec((3, LAYERS, height, width), lambda n: (0, n, 0, 0)),
        pl.BlockSpec((1, 1, height, width), lambda n: (2, layer_above(n), 0, 0)),
        pl.BlockSpec((1, 1, height, width), lambda n: (2, layer_below(n), 0, 0)),
    ]
    for adjoint in adjoints:
        operands = operands + [adjoint] * 3
        in_specs = in_specs + [
            pl.BlockSpec((LAYERS, height, width), lambda n: (n, 0, 0)),
            pl.BlockSpec((1, height, width), lambda n: (layer_above(n), 0, 0)),
            pl.BlockSpec((1, height, width), lambda n: (layer_below(n), 0, 0)),
        ]
    operands = operands + list(saved_halos) + list(halos)
    in_specs = in_specs + [saved_column, saved_column, saved_row, saved_row]
    in_specs = in_specs + [whole((count, Z, height))] * 2 + [whole((count, Z, width))] * 2

    def kernel(*refs):
        grad_vel_kernel(count, *refs)

    return pl.pallas_call(
        kernel,
        grid=(Z // LAYERS,),
        in_specs=in_specs + tied(after),
        out_specs=pl.BlockSpec((count, LAYERS, height, width), lambda n: (0, n, 0, 0)),
        out_shape=jax.ShapeDtypeStruct((count, Z, height, width), f32),
        scratch_shapes=[pltpu.VMEM((LAYERS, height + 16, width), f32)],
        compiler_params=params(),
        cost_estimate=takes(12),
        name="write_grad_vel",
    )(*operands, *after)


def pair_exchange(parts, axis, mine):
    count = lax.axis_size(axis)
    kept = lax.dynamic_index_in_dim(parts, mine, 1, keepdims=False)
    sent = lax.dynamic_index_in_dim(parts, 1 - mine, 1, keepdims=False)
    got = lax.ppermute(sent, axis, [(i, i ^ 1) for i in range(count)])
    return jnp.where(mine == 0, jnp.stack([kept, got], 1), jnp.stack([got, kept], 1))


def shifted(parts, axis):
    count = lax.axis_size(axis)
    return [parts[0]] + [
        lax.ppermute(parts[s], axis, [(i, (i + s) % count) for i in range(count)])
        for s in range(1, count)
    ]


def local(cot_vort, cot_vel, vorticity, velocity):
    size_x = lax.axis_size("gx")
    size_y = lax.axis_size("gy")
    planes = Z // size_y
    halves = size_y // KZ
    _, _, height, width = cot_vel.shape
    modes = HALF_Y // (size_x * halves)
    place_x = lax.axis_index("gx")
    place_y = lax.axis_index("gy")
    half = lax.rem(place_y, halves)
    me = place_y.astype(jnp.int32).reshape(1)
    where = jnp.stack([(place_x * halves + half) * modes, place_y // halves]).astype(jnp.int32)

    y_table, y_back_table = y_tables(size_x * halves)
    x_table, x_back_table = x_tables()
    slope_x = slope_matrix(width)
    slope_y = np.ascontiguousarray(slope_matrix(height).T)

    layers = depth_transform(cot_vel, FORWARD_ORDER[0])

    velocity_first, velocity_last = edge_columns(velocity, 3, (layers,))
    vorticity_first, vorticity_last = edge_columns(vorticity, 1, (layers,))
    low_x, high_x = exchange(
        jnp.concatenate([velocity_first, vorticity_first]),
        jnp.concatenate([velocity_last, vorticity_last]),
        "gx",
    )
    low_y, high_y = exchange(
        jnp.concatenate([velocity[:, :, 0], vorticity[1:2, :, 0]]),
        jnp.concatenate([velocity[:, :, height - 1], vorticity[1:2, :, height - 1]]),
        "gy",
    )
    saved_halos = (low_x, high_x, low_y, high_y)
    early = ((low_x, high_x), (low_y, high_y), ())

    columns = layers.reshape(size_y, planes, height, width)
    columns = [lax.all_to_all(columns, "gy", 0, 0, tiled=True)]
    sent = []
    for place in range(3):
        if place > 0:
            layers = depth_transform(cot_vel, FORWARD_ORDER[place], me, size_y, (sent[-1],))
            columns = shifted(layers, "gy")
        parts = y_transform(me, y_table, columns, size_x, halves, early[place])
        parts = parts.reshape(size_x, 2, 2, modes, width)
        sent.append(parts if halves == 1 else pair_exchange(parts, "gy", half))

    def spectrum(place, after):
        lines = lax.all_to_all(sent[place], "gx", 0, 0, tiled=True)
        return x_transform(x_table, lines, after)

    def curl(component, after):
        return curl_inverse(where, x_back_table, spectra, component, size_x, after)

    def back(filtered):
        parts = lax.all_to_all(filtered, "gx", 0, 0, tiled=True)
        if halves == 2:
            parts = pair_exchange(parts, "gy", half)
        return parts.reshape(size_x, halves, planes, 2, modes, width)

    def rows_of(component, modes_back, after):
        split = component != BACK_ORDER[2]
        return y_inverse(me, y_back_table, modes_back, size_y, split, after)

    def layers_of(rows):
        if len(rows) == 1:
            return [lax.all_to_all(rows[0], "gy", 0, 0, tiled=True).reshape(Z, height, width)]
        return shifted(rows, "gy")

    one, two, three = BACK_ORDER
    spectra = {FORWARD_ORDER[0]: spectrum(0, (sent[1],))}
    spectra[FORWARD_ORDER[1]] = spectrum(1, (sent[2],))
    curl_one = curl(one, ())
    spectra[FORWARD_ORDER[2]] = spectrum(2, (curl_one,))
    curl_two = curl(two, ())
    rows_one = rows_of(one, back(curl_one), (curl_two,))
    layers_one = layers_of(rows_one)
    curl_three = curl(three, tuple(layers_one))

    def vort_of(component, adjoint, before, after):
        kind = f32 if component == three else bf16
        return add_grad_vort(
            component, (slope_x, slope_y), velocity, adjoint, saved_halos, before, after, kind
        )

    adjoint_one, short_one, *edges = make_adjoint(me, layers_one, cot_vort, one, [], ())
    rows_two = rows_of(two, back(curl_two), (adjoint_one,))
    layers_two = layers_of(rows_two)
    grad_vort = vort_of(one, adjoint_one, None, (rows_two[0],))
    rows_three = rows_of(three, back(curl_three), tuple(layers_two) + (grad_vort,))
    adjoint_two, short_two, *edges = make_adjoint(
        me, layers_two, cot_vort, two, edges, (rows_three[0],)
    )
    grad_vort = vort_of(two, adjoint_two, grad_vort, ())
    adjoint_three, short_three, *edges = make_adjoint(
        me, layers_of(rows_three), cot_vort, three, edges, (grad_vort,)
    )
    halos = exchange(edges[0], edges[1], "gx") + exchange(edges[2], edges[3], "gy")
    grad_vort = vort_of(three, adjoint_three, grad_vort, ())
    shorts = {one: short_one, two: short_two, three: short_three}
    grad_vel = write_grad_vel(
        slope_x, vorticity, [shorts[i] for i in range(3)], saved_halos, halos, (grad_vort,)
    )
    return grad_vort, grad_vel


def solution(mesh):
    spec = P(None, None, "gy", "gx")
    return jax.shard_map(
        local,
        mesh=mesh,
        in_specs=(spec, spec, spec, spec),
        out_specs=(spec, spec),
        check_vma=False,
    )
```

```python
import math

import jax
import jax.numpy as jnp
import ml_dtypes
import numpy as np
from jax import lax
from jax.experimental import pallas as pl
from jax.experimental.pallas import tpu as pltpu
from jax.sharding import PartitionSpec as P

X = 1024
Y = 1536
Z = 16
HALF_X = X // 2
HALF_Y = Y // 2
KZ = Z // 2

step_size = 0.5

f32 = jnp.float32
bf16 = jnp.bfloat16

FORWARD_ORDER = (0, 1, 2)
BACK_ORDER = (2, 0, 1)


def params(megabytes=56):
    return pltpu.CompilerParams(vmem_limit_bytes=megabytes * 1024 * 1024)


def takes(microseconds):
    return pl.CostEstimate(flops=1, bytes_accessed=int(microseconds * 3.0e6), transcendentals=0)


def tied(after):
    return [pl.BlockSpec(memory_space=pl.ANY)] * len(after)


def trig(first, second, length):
    angle = (np.outer(first, second) % length) * (2.0 * math.pi / length)
    return np.cos(angle), np.sin(angle)


def y_tables(blocks):
    cosine, sine = trig(np.arange(HALF_Y), np.arange(Y), Y)
    both = np.stack([cosine.reshape(blocks, -1, Y), sine.reshape(blocks, -1, Y)], 1).reshape(Y, Y)
    both = both.astype(ml_dtypes.bfloat16)
    return both, np.ascontiguousarray(both.T)


def x_tables():
    cosine, sine = trig(np.arange(X), np.arange(HALF_X), X)
    both = np.concatenate([cosine, sine], 1).astype(ml_dtypes.bfloat16)
    return both, np.ascontiguousarray(both.T)


def slope_matrix(size):
    return ((np.eye(size, k=-1) - np.eye(size, k=1)) * 0.5).astype(ml_dtypes.bfloat16)


def combine(terms):
    total = None
    for factor, value in terms:
        if abs(factor) < 1e-12:
            continue
        if abs(factor - 1.0) < 1e-12:
            part = value
        elif abs(factor + 1.0) < 1e-12:
            part = -value
        else:
            part = value * factor
        total = part if total is None else total + part
    return total


def depth_forward(values):
    even = [values[0]] + [values[n] + values[Z - n] for n in range(1, 8)] + [values[8]]
    odd = [None] + [values[n] - values[Z - n] for n in range(1, 8)]
    even_sum = [even[n] + even[8 - n] for n in range(4)] + [even[4]]
    even_dif = [even[n] - even[8 - n] for n in range(4)]
    odd_sum = [None] + [odd[n] + odd[8 - n] for n in range(1, 4)] + [odd[4]]
    odd_dif = [None] + [odd[n] - odd[8 - n] for n in range(1, 4)]
    result = []
    for k in range(KZ):
        folded = even_sum if k % 2 == 0 else even_dif
        cos_part = combine([(math.cos(math.pi * k * n / 8), folded[n]) for n in range(len(folded))])
        folded = odd_dif if k % 2 == 0 else odd_sum
        sin_part = combine(
            [(math.sin(math.pi * k * n / 8), folded[n]) for n in range(1, len(folded))]
        )
        result.append((cos_part, sin_part))
    return result


def depth_inverse(cos_parts, sin_parts):
    layers = [None] * Z
    cos_sum, sin_sum = [None] * 9, [None] * 9
    for n in range(5):
        evens = combine([(math.cos(math.pi * k * n / 8), cos_parts[k]) for k in range(0, KZ, 2)])
        odds = combine([(math.cos(math.pi * k * n / 8), cos_parts[k]) for k in range(1, KZ, 2)])
        if n == 4:
            cos_sum[4] = evens
        else:
            cos_sum[n] = evens + odds
            cos_sum[8 - n] = evens - odds
    for n in range(1, 5):
        evens = combine([(math.sin(math.pi * k * n / 8), sin_parts[k]) for k in range(0, KZ, 2)])
        odds = combine([(math.sin(math.pi * k * n / 8), sin_parts[k]) for k in range(1, KZ, 2)])
        if n == 4:
            sin_sum[4] = odds
        else:
            sin_sum[n] = odds + evens
            sin_sum[8 - n] = odds - evens
    layers[0], layers[8] = cos_sum[0], cos_sum[8]
    for n in range(1, 8):
        layers[n] = cos_sum[n] + sin_sum[n]
        layers[Z - n] = cos_sum[n] - sin_sum[n]
    return layers


ROWS = 96


def tiles(height, width):
    for row in range(0, height, 16):
        for column in range(0, width, 128):
            yield row, pl.ds(row, 16), pl.ds(column, 128)


def depth_forward_kernel(values_ref, planes_ref):
    _, _, height, width = values_ref.shape
    for _, rows, columns in tiles(height, width):
        spectrum = depth_forward([values_ref[0, n, rows, columns] for n in range(Z)])
        for k, (cos_part, sin_part) in enumerate(spectrum):
            planes_ref[2 * k, rows, columns] = cos_part.astype(bf16)
            if sin_part is None:
                sin_part = jnp.zeros_like(cos_part)
            planes_ref[2 * k + 1, rows, columns] = sin_part.astype(bf16)


def depth_transform(values, component, me=None, size_y=1, after=()):
    _, _, height, width = values.shape
    planes = Z // size_y
    shifted_out = me is not None

    def kernel(*refs):
        if not shifted_out:
            depth_forward_kernel(*refs)
            return
        me_ref, values_ref, outs, held = refs[0], refs[1], refs[2 + len(after) : -1], refs[-1]
        depth_forward_kernel(values_ref, held)
        for s, out in enumerate(outs):
            target = lax.rem(me_ref[0] + s, size_y)
            out[...] = held[pl.ds(target * planes, planes)]

    block = (Z // size_y, ROWS, width)
    out_spec = pl.BlockSpec(block, lambda j: (0, j, 0))
    out_shape = jax.ShapeDtypeStruct((planes, height, width), bf16)
    smem = pl.BlockSpec(memory_space=pltpu.SMEM)
    return pl.pallas_call(
        kernel,
        grid=(height // ROWS,),
        in_specs=([smem] if shifted_out else [])
        + [pl.BlockSpec((1, Z, ROWS, width), lambda j: (component, 0, j, 0))]
        + tied(after),
        out_specs=[out_spec] * size_y if shifted_out else out_spec,
        out_shape=[out_shape] * size_y if shifted_out else out_shape,
        scratch_shapes=[pltpu.VMEM((Z, ROWS, width), bf16)] if shifted_out else [],
        compiler_params=params(),
        cost_estimate=takes(3),
        name="depth_transform",
    )(*(([me] if shifted_out else []) + [values, *after]))


def fetch_blocks(table_ref, held, arrived, order):
    count, rows, _ = held.shape
    copies = []
    for s in range(count):
        place = pl.ds(pl.multiple_of(order(s) * rows, rows), rows)
        copies.append(pltpu.make_async_copy(table_ref.at[place], held.at[s], arrived.at[s]))
        copies[s].start()
    return copies


def y_transform(me, table, columns, blocks, halves, after):
    whole = len(columns) == 1
    size_y = columns[0].shape[0] if whole else len(columns)
    planes, height, width = columns[0].shape[-3:]
    modes = HALF_Y // (blocks * halves)
    rows = Y // blocks
    shape = (blocks, halves, planes, 2, modes, width)

    def kernel(me_ref, table_ref, *refs):
        parts = refs[: len(columns)]
        out, held, lines, ready, table_in, lines_in, ready_out = refs[-7:]
        copies = []
        for s in range(size_y):
            source = s if whole else lax.rem(me_ref[0] + size_y - s, size_y)
            place = pl.ds(pl.multiple_of(source * height, height), height)
            for plane in range(planes):
                part = parts[0].at[s, plane] if whole else parts[s].at[plane]
                copies.append(
                    pltpu.make_async_copy(
                        part, lines.at[plane, place], lines_in.at[s * planes + plane]
                    )
                )
                copies[-1].start()
        tables = fetch_blocks(table_ref, held, table_in, lambda s: s)
        for copy in copies:
            copy.wait()
        results = []
        for s in range(blocks):
            tables[s].wait()
            for plane in range(planes):
                part = jnp.dot(held[s], lines[plane], preferred_element_type=f32)
                ready[s, :, plane] = part.astype(bf16).reshape(halves, 2, modes, width)
            results.append(pltpu.make_async_copy(ready.at[s], out.at[s], ready_out.at[s]))
            results[s].start()
        for result in results:
            result.wait()

    anywhere = pl.BlockSpec(memory_space=pl.ANY)
    return pl.pallas_call(
        kernel,
        in_specs=[pl.BlockSpec(memory_space=pltpu.SMEM), anywhere]
        + [anywhere] * len(columns)
        + tied(after),
        out_specs=anywhere,
        out_shape=jax.ShapeDtypeStruct(shape, bf16),
        scratch_shapes=[
            pltpu.VMEM((blocks, rows, Y), bf16),
            pltpu.VMEM((planes, Y, width), bf16),
            pltpu.VMEM(shape, bf16),
            pltpu.SemaphoreType.DMA((blocks,)),
            pltpu.SemaphoreType.DMA((size_y * planes,)),
            pltpu.SemaphoreType.DMA((blocks,)),
        ],
        compiler_params=params(24),
        cost_estimate=takes(5),
        name="y_transform",
    )(me, table, *columns, *after)


def y_inverse(me, table, modes, size_y, split, after):
    blocks, halves, planes, _, count, width = modes.shape
    height = Y // size_y
    shape = (planes, height, width)

    def kernel(me_ref, table_ref, modes_ref, *refs):
        outs = refs[len(after) : -6]
        held, lines, ready, table_in, lines_in, ready_out = refs[-6:]
        copies = []
        for block in range(blocks):
            for h in range(halves):
                for plane in range(planes):
                    copies.append(
                        pltpu.make_async_copy(
                            modes_ref.at[block, h, plane],
                            lines.at[plane, block, h],
                            lines_in.at[(block * halves + h) * planes + plane],
                        )
                    )
                    copies[-1].start()
        tables = fetch_blocks(
            table_ref, held, table_in, lambda s: lax.rem(me_ref[0] + s, size_y) if split else s
        )
        for copy in copies:
            copy.wait()
        results = []
        for s in range(size_y):
            tables[s].wait()
            for plane in range(planes):
                columns = lines[plane].reshape(Y, width)
                rows = jnp.dot(held[s], columns, preferred_element_type=f32)
                ready[s, plane] = rows.astype(bf16)
            out = outs[s] if split else outs[0].at[s]
            results.append(pltpu.make_async_copy(ready.at[s], out, ready_out.at[s]))
            results[s].start()
        for result in results:
            result.wait()

    anywhere = pl.BlockSpec(memory_space=pl.ANY)
    if split:
        out_shape = [jax.ShapeDtypeStruct(shape, bf16)] * size_y
    else:
        out_shape = [jax.ShapeDtypeStruct((size_y,) + shape, bf16)]
    return pl.pallas_call(
        kernel,
        in_specs=[pl.BlockSpec(memory_space=pltpu.SMEM), anywhere, anywhere] + tied(after),
        out_specs=[anywhere] * len(out_shape),
        out_shape=out_shape,
        scratch_shapes=[
            pltpu.VMEM((size_y, height, Y), bf16),
            pltpu.VMEM((planes, blocks, halves, 2, count, width), bf16),
            pltpu.VMEM((size_y,) + shape, bf16),
            pltpu.SemaphoreType.DMA((size_y,)),
            pltpu.SemaphoreType.DMA((blocks * halves * planes,)),
            pltpu.SemaphoreType.DMA((size_y,)),
        ],
        compiler_params=params(24),
        cost_estimate=takes(4),
        name="y_inverse",
    )(me, table, modes, *after)


def x_transform(table, modes, after):
    blocks, _, _, count, width = modes.shape

    def kernel(table_ref, modes_ref, *refs):
        spectrum_ref = refs[-1]
        rows = jnp.concatenate(
            [modes_ref[block, 0].reshape(2 * count, width) for block in range(blocks)], axis=1
        )
        spectrum = jnp.dot(rows, table_ref[...], preferred_element_type=f32)
        spectrum_ref[0] = spectrum.reshape(2, count, X)

    return pl.pallas_call(
        kernel,
        grid=(2,),
        in_specs=[
            pl.BlockSpec((X, X), lambda j: (0, 0)),
            pl.BlockSpec((blocks, 1, 2, count, width), lambda j: (0, j, 0, 0, 0)),
        ]
        + tied(after),
        out_specs=pl.BlockSpec((1, 2, count, X), lambda j: (j, 0, 0, 0)),
        out_shape=jax.ShapeDtypeStruct((2, 2, count, X), f32),
        compiler_params=params(24),
        cost_estimate=takes(3),
        name="x_transform",
    )(table, modes, *after)


def turned(field, axis, tz, ty, tx, wave):
    index = [tz, ty, tx]
    sign = 1.0 if index[axis] == 0 else -1.0
    index[axis] = 1 - index[axis]
    value = field[index[0], index[1], :, index[2] * HALF_X : (index[2] + 1) * HALF_X]
    return value * (wave * sign)


CURL = {
    0: ((1, 2), (0, 1)),
    1: ((0, 0), (2, 2)),
    2: ((2, 1), (1, 0)),
}


def curl_kernel(axes, where_ref, table_ref, plus_ref, minus_ref, back_ref):
    blocks, _, _, count, width = back_ref.shape
    base = where_ref[0] + pl.program_id(0) * count
    depth = where_ref[1]
    mode_y = lax.broadcasted_iota(jnp.int32, (count, HALF_X), 0) + base
    mode_x = lax.broadcasted_iota(jnp.int32, (count, HALF_X), 1)
    wave_y = mode_y.astype(f32) * (2.0 * math.pi / Y)
    wave_x = mode_x.astype(f32) * (2.0 * math.pi / X)
    wave_z = jnp.full((count, HALF_X), depth, jnp.int32).astype(f32) * (2.0 * math.pi / Z)
    square = wave_x * wave_x + wave_y * wave_y + wave_z * wave_z
    doubling = (
        jnp.where(mode_x == 0, 1.0, 2.0)
        * jnp.where(mode_y == 0, 1.0, 2.0)
        * jnp.where(wave_z == 0.0, 1.0, 2.0)
    )
    weight = jnp.where(square > 0, doubling / jnp.where(square > 0, square, 1.0), 0.0)
    waves = [wave_z * weight, wave_y * weight, wave_x * weight]
    rows = []
    for tz in range(2):
        for ty in range(2):
            parts = []
            for tx in range(2):
                parts.append(
                    (
                        turned(plus_ref, axes[0], tz, ty, tx, waves[axes[0]])
                        - turned(minus_ref, axes[1], tz, ty, tx, waves[axes[1]])
                    ).astype(bf16)
                )
            rows.append(jnp.concatenate(parts, axis=1))
    rows = jnp.concatenate(rows, axis=0)
    back = jnp.dot(rows, table_ref[...], preferred_element_type=f32).astype(bf16)
    for block in range(blocks):
        back_ref[block] = back[:, block * width : (block + 1) * width].reshape(2, 2, count, width)


def curl_inverse(where, table, spectra, component, blocks, after):
    (plus_axis, plus), (minus_axis, minus) = CURL[component]
    total = spectra[plus].shape[2]
    width = X // blocks
    count = 96 if total % 96 == 0 else total
    spec = pl.BlockSpec((2, 2, count, X), lambda j: (0, 0, j, 0))

    def kernel(*refs):
        curl_kernel((plus_axis, minus_axis), *refs[:4], refs[-1])

    return pl.pallas_call(
        kernel,
        grid=(total // count,),
        in_specs=[
            pl.BlockSpec(memory_space=pltpu.SMEM),
            pl.BlockSpec((X, X), lambda j: (0, 0)),
            spec,
            spec,
        ]
        + tied(after),
        out_specs=pl.BlockSpec((blocks, 2, 2, count, width), lambda j: (0, 0, 0, j, 0)),
        out_shape=jax.ShapeDtypeStruct((blocks, 2, 2, total, width), bf16),
        compiler_params=params(24),
        cost_estimate=takes(4),
        name="curl_inverse",
    )(where, table, spectra[plus], spectra[minus], *after)


def side_columns(planes):
    width = planes[0].shape[1]
    row = lax.broadcasted_iota(jnp.int32, (2 * Z, width), 0)
    lane = lax.broadcasted_iota(jnp.int32, (2 * Z, width), 1)
    total = None
    for n in range(Z):
        pick = ((row == n) & (lane == 0)) | ((row == n + Z) & (lane == width - 1))
        part = lax.dot_general(
            pick.astype(f32).astype(bf16),
            planes[n],
            (((1,), (1,)), ((), ())),
            preferred_element_type=f32,
        )
        total = part if total is None else total + part
    return total[:Z].astype(bf16), total[Z:].astype(bf16)


def spread_columns(low, high, first, layers, width):
    row = lax.broadcasted_iota(jnp.int32, (2 * Z, layers * width), 0)
    column = lax.broadcasted_iota(jnp.int32, (2 * Z, layers * width), 1)
    place = jnp.zeros((2 * Z, layers * width), f32)
    for n in range(layers):
        place = place + jnp.where((row == first + n) & (column == n * width), -0.5, 0.0)
        place = place + jnp.where(
            (row == first + n + Z) & (column == (n + 1) * width - 1), 0.5, 0.0
        )
    both = jnp.concatenate([low, high], axis=0).astype(bf16)
    spread = lax.dot_general(
        both, place.astype(bf16), (((0,), (0,)), ((), ())), preferred_element_type=f32
    )
    return [spread[:, n * width : (n + 1) * width] for n in range(layers)]


def edges_kernel(field_ref, *refs):
    first_column_ref, last_column_ref = refs[-2:]
    first, last = side_columns([field_ref[0, n] for n in range(Z)])
    first_column_ref[0] = first
    last_column_ref[0] = last


def edge_columns(field, components, after):
    _, _, height, width = field.shape
    shape = jax.ShapeDtypeStruct((components, Z, height), bf16)
    spec = pl.BlockSpec((1, Z, height), lambda i: (i, 0, 0))
    return pl.pallas_call(
        edges_kernel,
        grid=(components,),
        in_specs=[pl.BlockSpec((1, Z, height, width), lambda i: (i, 0, 0, 0))] + tied(after),
        out_specs=[spec, spec],
        out_shape=[shape, shape],
        compiler_params=params(),
        cost_estimate=takes(4),
        name="edge_columns",
    )(field, *after)


def exchange(first, last, axis):
    count = lax.axis_size(axis)
    up = [(i, (i + 1) % count) for i in range(count)]
    down = [((i + 1) % count, i) for i in range(count)]
    return lax.ppermute(last, axis, up), lax.ppermute(first, axis, down)


def adjoint_kernel(planes_ref, cotangent_ref, *refs):
    adjoint_ref, short_ref, first_x, last_x, first_y, last_y, held = refs
    _, height, width = held.shape
    scale = 1.0 / (X * Y * Z)
    base = pl.program_id(0) * ROWS
    for row, rows, columns in tiles(ROWS, width):
        place = pl.ds(pl.multiple_of(base + row, 16), 16)
        layers = depth_inverse(
            [planes_ref[2 * k, rows, columns].astype(f32) for k in range(KZ)],
            [planes_ref[2 * k + 1, rows, columns].astype(f32) for k in range(KZ)],
        )
        for n in range(Z):
            value = cotangent_ref[0, n, rows, columns] + layers[n] * scale
            adjoint_ref[n, rows, columns] = value
            short_ref[n, rows, columns] = value.astype(bf16)
            held[n, place, columns] = value.astype(bf16)

    @pl.when(pl.program_id(0) == pl.num_programs(0) - 1)
    def _():
        first, last = side_columns([held[n] for n in range(Z)])
        first_x[0] = first
        last_x[0] = last
        top = [held[n, 0:16, :].astype(f32)[0:1] for n in range(Z)]
        bottom = [held[n, height - 16 : height, :].astype(f32)[15:16] for n in range(Z)]
        first_y[0] = jnp.concatenate(top, 0).astype(bf16)
        last_y[0] = jnp.concatenate(bottom, 0).astype(bf16)


def make_adjoint(me, parts, cotangent, component, edges, after):
    whole = len(parts) == 1
    planes, height, width = parts[0].shape
    column = jax.ShapeDtypeStruct((3, Z, height), bf16)
    row = jax.ShapeDtypeStruct((3, Z, width), bf16)
    column_spec = pl.BlockSpec((1, Z, height), lambda j: (component, 0, 0))
    row_spec = pl.BlockSpec((1, Z, width), lambda j: (component, 0, 0))
    first_edge = 2 + len(parts)

    def kernel(me_ref, *refs):
        part_refs, cotangent_ref = refs[: len(parts)], refs[len(parts)]
        outs, held, spectrum = refs[-8:-2], refs[-2], refs[-1]
        if whole:
            spectrum = part_refs[0]
        else:
            for s, part in enumerate(part_refs):
                source = lax.rem(me_ref[0] + len(parts) - s, len(parts))
                spectrum[pl.ds(source * planes, planes)] = part[...]
        adjoint_kernel(spectrum, cotangent_ref, *outs, held)

    return pl.pallas_call(
        kernel,
        grid=(height // ROWS,),
        in_specs=[pl.BlockSpec(memory_space=pltpu.SMEM)]
        + [pl.BlockSpec((planes, ROWS, width), lambda j: (0, j, 0))] * len(parts)
        + [pl.BlockSpec((1, Z, ROWS, width), lambda j: (component, 0, j, 0))]
        + tied(edges)
        + tied(after),
        out_specs=[
            pl.BlockSpec((Z, ROWS, width), lambda j: (0, j, 0)),
            pl.BlockSpec((Z, ROWS, width), lambda j: (0, j, 0)),
            column_spec,
            column_spec,
            row_spec,
            row_spec,
        ],
        out_shape=[
            jax.ShapeDtypeStruct((Z, height, width), f32),
            jax.ShapeDtypeStruct((Z, height, width), bf16),
            column,
            column,
            row,
            row,
        ],
        input_output_aliases={first_edge + n: 2 + n for n in range(len(edges))},
        scratch_shapes=[
            pltpu.VMEM((Z, height, width), bf16),
            pltpu.VMEM((Z, ROWS, width), bf16),
        ],
        compiler_params=params(),
        cost_estimate=takes(5),
        name="make_adjoint",
    )(me, *parts, cotangent, *edges, *after)


def pick_row(rows, n):
    index = lax.broadcasted_iota(jnp.int32, rows.shape, 0)
    return jnp.sum(jnp.where(index == n, rows.astype(f32), 0.0), axis=0, keepdims=True)


def end_rows(low, high, height):
    row = lax.broadcasted_iota(jnp.int32, (height, low.shape[1]), 0)
    return jnp.where(row == 0, low * -0.5, 0.0) + jnp.where(row == height - 1, high * 0.5, 0.0)


LAYERS = 4


def grad_vort_kernel(
    component,
    slope_x,
    slope_y,
    velocity,
    velocity_above,
    velocity_below,
    adjoint,
    low_x,
    high_x,
    low_y,
    high_y,
    *refs,
):
    before, after = refs
    height, width = velocity.shape[2], velocity.shape[3]
    first = pl.program_id(0) * LAYERS
    ends = spread_columns(low_x[0], high_x[0], first, LAYERS, width)
    layers = velocity[0]
    stacked = layers.reshape(LAYERS * height, width)
    deep = [velocity_below[0, 0]] + [layers[k] for k in range(LAYERS)] + [velocity_above[0, 0]]
    inner = jnp.dot(stacked, slope_x[...], preferred_element_type=f32)
    for k in range(LAYERS):
        n = first + k
        value = adjoint[k]
        half = value * step_size
        along_x = inner[k * height : (k + 1) * height] + ends[k]
        along_y = jnp.dot(slope_y[...], layers[k], preferred_element_type=f32)
        along_y = along_y + end_rows(pick_row(low_y[0], n), pick_row(high_y[0], n), height)
        along_z = (deep[k + 2].astype(f32) - deep[k].astype(f32)) * 0.5
        for j, slope in enumerate((along_x, along_y, along_z)):
            term = half * slope
            if j == component:
                term = term + value
            if before is not None:
                term = before[j, k].astype(f32) + term
            after[j, k] = term.astype(after.dtype)


def add_grad_vort(component, slopes, velocity, adjoint, halos, before, after, kind):
    _, _, height, width = velocity.shape
    slope_x, slope_y = slopes
    whole = lambda shape: pl.BlockSpec(shape, lambda n: (0,) * len(shape))
    column = pl.BlockSpec((1, Z, height), lambda n: (component, 0, 0))
    row = pl.BlockSpec((1, Z, width), lambda n: (component, 0, 0))
    sums = pl.BlockSpec((3, LAYERS, height, width), lambda n: (0, n, 0, 0))
    layer_above = lambda n: lax.rem((n + 1) * LAYERS, Z)
    layer_below = lambda n: lax.rem(n * LAYERS + Z - 1, Z)
    operands = [slope_x, slope_y, velocity, velocity, velocity, adjoint, *halos]
    in_specs = [
        whole((width, width)),
        whole((height, height)),
        pl.BlockSpec((1, LAYERS, height, width), lambda n: (component, n, 0, 0)),
        pl.BlockSpec((1, 1, height, width), lambda n: (component, layer_above(n), 0, 0)),
        pl.BlockSpec((1, 1, height, width), lambda n: (component, layer_below(n), 0, 0)),
        pl.BlockSpec((LAYERS, height, width), lambda n: (n, 0, 0)),
        column,
        column,
        row,
        row,
    ]
    if before is not None:
        operands.append(before)
        in_specs.append(sums)

    def kernel(*refs):
        grad_vort_kernel(component, *refs[:10], None if before is None else refs[10], refs[-1])

    return pl.pallas_call(
        kernel,
        grid=(Z // LAYERS,),
        in_specs=in_specs + tied(after),
        out_specs=sums,
        out_shape=jax.ShapeDtypeStruct((3, Z, height, width), kind),
        compiler_params=params(),
        cost_estimate=takes(9),
        name="add_grad_vort",
    )(*operands, *after)


def grad_vel_kernel(count, slope_x, vorticity, vorticity_above, vorticity_below, *refs):
    adjoints, edges = refs[: 3 * count], refs[3 * count :]
    vort_low_x, vort_high_x, vort_low_y, vort_high_y, low_x, high_x, low_y, high_y = edges[:8]
    after, padded = refs[-2:]
    _, _, height, width = vorticity.shape
    first = pl.program_id(0) * LAYERS

    def times(one, other):
        return one.astype(f32) * other.astype(f32)

    for c in range(count):
        here, above, below = adjoints[3 * c : 3 * c + 3]
        ends = spread_columns(
            times(vort_low_x[0], low_x[c]),
            times(vort_high_x[0], high_x[c]),
            first,
            LAYERS,
            width,
        )
        product = [times(vorticity[0, k], here[k]).astype(bf16) for k in range(LAYERS)]
        inner = jnp.dot(
            jnp.concatenate(product, axis=0), slope_x[...], preferred_element_type=f32
        )
        deep = [times(vorticity_below[0, 0], below[0])]
        deep = deep + [times(vorticity[2, k], here[k]) for k in range(LAYERS)]
        deep = deep + [times(vorticity_above[0, 0], above[0])]
        for k in range(LAYERS):
            n = first + k
            padded[k, 8 : 8 + height, :] = times(vorticity[1, k], here[k])
            padded[k, 7:8, :] = pick_row(vort_low_y[0], n) * pick_row(low_y[c], n)
            padded[k, 8 + height : 9 + height, :] = pick_row(vort_high_y[0], n) * pick_row(
                high_y[c], n
            )
            total = (padded[k, 9 : 9 + height, :] - padded[k, 7 : 7 + height, :]) + (
                deep[k + 2] - deep[k]
            )
            total = total * 0.5 + inner[k * height : (k + 1) * height] + ends[k]
            after[c, k] = total * -step_size


def write_grad_vel(slope_x, vorticity, adjoints, saved_halos, halos, after):
    _, _, height, width = vorticity.shape
    count = len(adjoints)
    whole = lambda shape: pl.BlockSpec(shape, lambda n: (0,) * len(shape))
    saved_column = pl.BlockSpec((1, Z, height), lambda n: (3, 0, 0))
    saved_row = pl.BlockSpec((1, Z, width), lambda n: (3, 0, 0))
    layer_above = lambda n: lax.rem((n + 1) * LAYERS, Z)
    layer_below = lambda n: lax.rem(n * LAYERS + Z - 1, Z)
    operands = [slope_x, vorticity, vorticity, vorticity]
    in_specs = [
        whole((width, width)),
        pl.BlockSpec((3, LAYERS, height, width), lambda n: (0, n, 0, 0)),
        pl.BlockSpec((1, 1, height, width), lambda n: (2, layer_above(n), 0, 0)),
        pl.BlockSpec((1, 1, height, width), lambda n: (2, layer_below(n), 0, 0)),
    ]
    for adjoint in adjoints:
        operands = operands + [adjoint] * 3
        in_specs = in_specs + [
            pl.BlockSpec((LAYERS, height, width), lambda n: (n, 0, 0)),
            pl.BlockSpec((1, height, width), lambda n: (layer_above(n), 0, 0)),
            pl.BlockSpec((1, height, width), lambda n: (layer_below(n), 0, 0)),
        ]
    operands = operands + list(saved_halos) + list(halos)
    in_specs = in_specs + [saved_column, saved_column, saved_row, saved_row]
    in_specs = in_specs + [whole((count, Z, height))] * 2 + [whole((count, Z, width))] * 2

    def kernel(*refs):
        grad_vel_kernel(count, *refs)

    return pl.pallas_call(
        kernel,
        grid=(Z // LAYERS,),
        in_specs=in_specs + tied(after),
        out_specs=pl.BlockSpec((count, LAYERS, height, width), lambda n: (0, n, 0, 0)),
        out_shape=jax.ShapeDtypeStruct((count, Z, height, width), f32),
        scratch_shapes=[pltpu.VMEM((LAYERS, height + 16, width), f32)],
        compiler_params=params(),
        cost_estimate=takes(12),
        name="write_grad_vel",
    )(*operands, *after)


def pair_exchange(parts, axis, mine):
    count = lax.axis_size(axis)
    kept = lax.dynamic_index_in_dim(parts, mine, 1, keepdims=False)
    sent = lax.dynamic_index_in_dim(parts, 1 - mine, 1, keepdims=False)
    got = lax.ppermute(sent, axis, [(i, i ^ 1) for i in range(count)])
    return jnp.where(mine == 0, jnp.stack([kept, got], 1), jnp.stack([got, kept], 1))


def shifted(parts, axis):
    count = lax.axis_size(axis)
    return [parts[0]] + [
        lax.ppermute(parts[s], axis, [(i, (i + s) % count) for i in range(count)])
        for s in range(1, count)
    ]


def local(cot_vort, cot_vel, vorticity, velocity):
    size_x = lax.axis_size("gx")
    size_y = lax.axis_size("gy")
    planes = Z // size_y
    halves = size_y // KZ
    _, _, height, width = cot_vel.shape
    modes = HALF_Y // (size_x * halves)
    place_x = lax.axis_index("gx")
    place_y = lax.axis_index("gy")
    half = lax.rem(place_y, halves)
    me = place_y.astype(jnp.int32).reshape(1)
    where = jnp.stack([(place_x * halves + half) * modes, place_y // halves]).astype(jnp.int32)

    y_table, y_back_table = y_tables(size_x * halves)
    x_table, x_back_table = x_tables()
    slope_x = slope_matrix(width)
    slope_y = np.ascontiguousarray(slope_matrix(height).T)

    layers = depth_transform(cot_vel, FORWARD_ORDER[0])

    velocity_first, velocity_last = edge_columns(velocity, 3, (layers,))
    vorticity_first, vorticity_last = edge_columns(vorticity, 1, (layers,))
    low_x, high_x = exchange(
        jnp.concatenate([velocity_first, vorticity_first]),
        jnp.concatenate([velocity_last, vorticity_last]),
        "gx",
    )
    low_y, high_y = exchange(
        jnp.concatenate([velocity[:, :, 0], vorticity[1:2, :, 0]]),
        jnp.concatenate([velocity[:, :, height - 1], vorticity[1:2, :, height - 1]]),
        "gy",
    )
    saved_halos = (low_x, high_x, low_y, high_y)
    early = ((low_x, high_x), (low_y, high_y), ())

    columns = layers.reshape(size_y, planes, height, width)
    columns = [lax.all_to_all(columns, "gy", 0, 0, tiled=True)]
    sent = []
    for place in range(3):
        if place > 0:
            layers = depth_transform(cot_vel, FORWARD_ORDER[place], me, size_y, (sent[-1],))
            columns = shifted(layers, "gy")
        parts = y_transform(me, y_table, columns, size_x, halves, early[place])
        parts = parts.reshape(size_x, 2, 2, modes, width)
        sent.append(parts if halves == 1 else pair_exchange(parts, "gy", half))

    def spectrum(place, after):
        lines = lax.all_to_all(sent[place], "gx", 0, 0, tiled=True)
        return x_transform(x_table, lines, after)

    def curl(component, after):
        return curl_inverse(where, x_back_table, spectra, component, size_x, after)

    def back(filtered):
        parts = lax.all_to_all(filtered, "gx", 0, 0, tiled=True)
        if halves == 2:
            parts = pair_exchange(parts, "gy", half)
        return parts.reshape(size_x, halves, planes, 2, modes, width)

    def rows_of(component, modes_back, after):
        split = component != BACK_ORDER[2]
        return y_inverse(me, y_back_table, modes_back, size_y, split, after)

    def layers_of(rows):
        if len(rows) == 1:
            return [lax.all_to_all(rows[0], "gy", 0, 0, tiled=True).reshape(Z, height, width)]
        return shifted(rows, "gy")

    one, two, three = BACK_ORDER
    spectra = {FORWARD_ORDER[0]: spectrum(0, (sent[1],))}
    spectra[FORWARD_ORDER[1]] = spectrum(1, (sent[2],))
    curl_one = curl(one, ())
    spectra[FORWARD_ORDER[2]] = spectrum(2, (curl_one,))
    curl_two = curl(two, ())
    rows_one = rows_of(one, back(curl_one), (curl_two,))
    layers_one = layers_of(rows_one)
    curl_three = curl(three, tuple(layers_one))

    def vort_of(component, adjoint, before, after):
        kind = f32 if component == three else bf16
        return add_grad_vort(
            component, (slope_x, slope_y), velocity, adjoint, saved_halos, before, after, kind
        )

    adjoint_one, short_one, *edges = make_adjoint(me, layers_one, cot_vort, one, [], ())
    rows_two = rows_of(two, back(curl_two), (adjoint_one,))
    layers_two = layers_of(rows_two)
    rows_three = rows_of(three, back(curl_three), tuple(layers_two))
    grad_vort = vort_of(one, adjoint_one, None, (rows_two[0],))
    adjoint_two, short_two, *edges = make_adjoint(
        me, layers_two, cot_vort, two, edges, (rows_three[0],)
    )
    grad_vort = vort_of(two, adjoint_two, grad_vort, ())
    adjoint_three, short_three, *edges = make_adjoint(
        me, layers_of(rows_three), cot_vort, three, edges, (grad_vort,)
    )
    halos = exchange(edges[0], edges[1], "gx") + exchange(edges[2], edges[3], "gy")
    grad_vort = vort_of(three, adjoint_three, grad_vort, ())
    shorts = {one: short_one, two: short_two, three: short_three}
    grad_vel = write_grad_vel(
        slope_x, vorticity, [shorts[i] for i in range(3)], saved_halos, halos, (grad_vort,)
    )
    return grad_vort, grad_vel


def solution(mesh):
    spec = P(None, None, "gy", "gx")
    return jax.shard_map(
        local,
        mesh=mesh,
        in_specs=(spec, spec, spec, spec),
        out_specs=(spec, spec),
        check_vma=False,
    )
```

```python
import math

import jax
import jax.numpy as jnp
import ml_dtypes
import numpy as np
from jax import lax
from jax.experimental import pallas as pl
from jax.experimental.pallas import tpu as pltpu
from jax.sharding import PartitionSpec as P

X = 1024
Y = 1536
Z = 16
HALF_X = X // 2
HALF_Y = Y // 2
KZ = Z // 2

step_size = 0.5

f32 = jnp.float32
bf16 = jnp.bfloat16

FORWARD_ORDER = (0, 1, 2)
BACK_ORDER = (2, 0, 1)


def params(megabytes=56):
    return pltpu.CompilerParams(vmem_limit_bytes=megabytes * 1024 * 1024)


def takes(microseconds):
    return pl.CostEstimate(flops=1, bytes_accessed=int(microseconds * 3.0e6), transcendentals=0)


def tied(after):
    return [pl.BlockSpec(memory_space=pl.ANY)] * len(after)


def trig(first, second, length):
    angle = (np.outer(first, second) % length) * (2.0 * math.pi / length)
    return np.cos(angle), np.sin(angle)


def y_tables(blocks):
    cosine, sine = trig(np.arange(HALF_Y), np.arange(Y), Y)
    both = np.stack([cosine.reshape(blocks, -1, Y), sine.reshape(blocks, -1, Y)], 1).reshape(Y, Y)
    both = both.astype(ml_dtypes.bfloat16)
    return both, np.ascontiguousarray(both.T)


def x_tables():
    cosine, sine = trig(np.arange(X), np.arange(HALF_X), X)
    both = np.concatenate([cosine, sine], 1).astype(ml_dtypes.bfloat16)
    return both, np.ascontiguousarray(both.T)


def slope_matrix(size):
    return ((np.eye(size, k=-1) - np.eye(size, k=1)) * 0.5).astype(ml_dtypes.bfloat16)


def combine(terms):
    total = None
    for factor, value in terms:
        if abs(factor) < 1e-12:
            continue
        if abs(factor - 1.0) < 1e-12:
            part = value
        elif abs(factor + 1.0) < 1e-12:
            part = -value
        else:
            part = value * factor
        total = part if total is None else total + part
    return total


def depth_forward(values):
    even = [values[0]] + [values[n] + values[Z - n] for n in range(1, 8)] + [values[8]]
    odd = [None] + [values[n] - values[Z - n] for n in range(1, 8)]
    even_sum = [even[n] + even[8 - n] for n in range(4)] + [even[4]]
    even_dif = [even[n] - even[8 - n] for n in range(4)]
    odd_sum = [None] + [odd[n] + odd[8 - n] for n in range(1, 4)] + [odd[4]]
    odd_dif = [None] + [odd[n] - odd[8 - n] for n in range(1, 4)]
    result = []
    for k in range(KZ):
        folded = even_sum if k % 2 == 0 else even_dif
        cos_part = combine([(math.cos(math.pi * k * n / 8), folded[n]) for n in range(len(folded))])
        folded = odd_dif if k % 2 == 0 else odd_sum
        sin_part = combine(
            [(math.sin(math.pi * k * n / 8), folded[n]) for n in range(1, len(folded))]
        )
        result.append((cos_part, sin_part))
    return result


def depth_inverse(cos_parts, sin_parts):
    layers = [None] * Z
    cos_sum, sin_sum = [None] * 9, [None] * 9
    for n in range(5):
        evens = combine([(math.cos(math.pi * k * n / 8), cos_parts[k]) for k in range(0, KZ, 2)])
        odds = combine([(math.cos(math.pi * k * n / 8), cos_parts[k]) for k in range(1, KZ, 2)])
        if n == 4:
            cos_sum[4] = evens
        else:
            cos_sum[n] = evens + odds
            cos_sum[8 - n] = evens - odds
    for n in range(1, 5):
        evens = combine([(math.sin(math.pi * k * n / 8), sin_parts[k]) for k in range(0, KZ, 2)])
        odds = combine([(math.sin(math.pi * k * n / 8), sin_parts[k]) for k in range(1, KZ, 2)])
        if n == 4:
            sin_sum[4] = odds
        else:
            sin_sum[n] = odds + evens
            sin_sum[8 - n] = odds - evens
    layers[0], layers[8] = cos_sum[0], cos_sum[8]
    for n in range(1, 8):
        layers[n] = cos_sum[n] + sin_sum[n]
        layers[Z - n] = cos_sum[n] - sin_sum[n]
    return layers


ROWS = 96


def tiles(height, width):
    for row in range(0, height, 16):
        for column in range(0, width, 128):
            yield row, pl.ds(row, 16), pl.ds(column, 128)


def depth_forward_kernel(values_ref, planes_ref):
    _, _, height, width = values_ref.shape
    for _, rows, columns in tiles(height, width):
        spectrum = depth_forward([values_ref[0, n, rows, columns] for n in range(Z)])
        for k, (cos_part, sin_part) in enumerate(spectrum):
            planes_ref[2 * k, rows, columns] = cos_part.astype(bf16)
            if sin_part is None:
                sin_part = jnp.zeros_like(cos_part)
            planes_ref[2 * k + 1, rows, columns] = sin_part.astype(bf16)


def depth_transform(values, component, me=None, size_y=1, after=()):
    _, _, height, width = values.shape
    planes = Z // size_y
    shifted_out = me is not None

    def kernel(*refs):
        if not shifted_out:
            depth_forward_kernel(*refs)
            return
        me_ref, values_ref, outs, held = refs[0], refs[1], refs[2 + len(after) : -1], refs[-1]
        depth_forward_kernel(values_ref, held)
        for s, out in enumerate(outs):
            target = lax.rem(me_ref[0] + s, size_y)
            out[...] = held[pl.ds(target * planes, planes)]

    block = (Z // size_y, ROWS, width)
    out_spec = pl.BlockSpec(block, lambda j: (0, j, 0))
    out_shape = jax.ShapeDtypeStruct((planes, height, width), bf16)
    smem = pl.BlockSpec(memory_space=pltpu.SMEM)
    return pl.pallas_call(
        kernel,
        grid=(height // ROWS,),
        in_specs=([smem] if shifted_out else [])
        + [pl.BlockSpec((1, Z, ROWS, width), lambda j: (component, 0, j, 0))]
        + tied(after),
        out_specs=[out_spec] * size_y if shifted_out else out_spec,
        out_shape=[out_shape] * size_y if shifted_out else out_shape,
        scratch_shapes=[pltpu.VMEM((Z, ROWS, width), bf16)] if shifted_out else [],
        compiler_params=params(),
        cost_estimate=takes(3),
        name="depth_transform",
    )(*(([me] if shifted_out else []) + [values, *after]))


def fetch_blocks(table_ref, held, arrived, order):
    count, rows, _ = held.shape
    copies = []
    for s in range(count):
        place = pl.ds(pl.multiple_of(order(s) * rows, rows), rows)
        copies.append(pltpu.make_async_copy(table_ref.at[place], held.at[s], arrived.at[s]))
        copies[s].start()
    return copies


def y_transform(table, columns, blocks, halves, after):
    _, planes, _, width = columns.shape
    modes = HALF_Y // (blocks * halves)
    rows = Y // blocks

    def kernel(table_ref, columns_ref, *refs):
        out = refs[-1]
        for plane in range(planes):
            column = columns_ref[:, plane].reshape(Y, width)
            part = jnp.dot(table_ref[...], column, preferred_element_type=f32)
            out[0, :, plane] = part.astype(bf16).reshape(halves, 2, modes, width)

    return pl.pallas_call(
        kernel,
        grid=(blocks,),
        in_specs=[
            pl.BlockSpec((rows, Y), lambda j: (j, 0)),
            pl.BlockSpec(columns.shape, lambda j: (0, 0, 0, 0)),
        ]
        + tied(after),
        out_specs=pl.BlockSpec((1, halves, planes, 2, modes, width), lambda j: (j, 0, 0, 0, 0, 0)),
        out_shape=jax.ShapeDtypeStruct((blocks, halves, planes, 2, modes, width), bf16),
        compiler_params=params(24),
        cost_estimate=takes(4),
        name="y_transform",
    )(table, columns, *after)


def y_transform_parts(me, table, columns, blocks, halves, after):
    size_y = len(columns)
    planes, height, width = columns[0].shape[-3:]
    modes = HALF_Y // (blocks * halves)
    rows = Y // blocks
    shape = (blocks, halves, planes, 2, modes, width)

    def kernel(me_ref, table_ref, *refs):
        parts = refs[: len(columns)]
        out, held, lines, ready, table_in, lines_in, ready_out = refs[-7:]
        copies = []
        for s in range(size_y):
            source = lax.rem(me_ref[0] + size_y - s, size_y)
            place = pl.ds(pl.multiple_of(source * height, height), height)
            for plane in range(planes):
                copies.append(
                    pltpu.make_async_copy(
                        parts[s].at[plane],
                        lines.at[plane, place],
                        lines_in.at[s * planes + plane],
                    )
                )
                copies[-1].start()
        tables = fetch_blocks(table_ref, held, table_in, lambda s: s)
        for copy in copies:
            copy.wait()
        results = []
        for s in range(blocks):
            tables[s].wait()
            for plane in range(planes):
                part = jnp.dot(held[s], lines[plane], preferred_element_type=f32)
                ready[s, :, plane] = part.astype(bf16).reshape(halves, 2, modes, width)
            results.append(pltpu.make_async_copy(ready.at[s], out.at[s], ready_out.at[s]))
            results[s].start()
        for result in results:
            result.wait()

    anywhere = pl.BlockSpec(memory_space=pl.ANY)
    return pl.pallas_call(
        kernel,
        in_specs=[pl.BlockSpec(memory_space=pltpu.SMEM), anywhere]
        + [anywhere] * len(columns)
        + tied(after),
        out_specs=anywhere,
        out_shape=jax.ShapeDtypeStruct(shape, bf16),
        scratch_shapes=[
            pltpu.VMEM((blocks, rows, Y), bf16),
            pltpu.VMEM((planes, Y, width), bf16),
            pltpu.VMEM(shape, bf16),
            pltpu.SemaphoreType.DMA((blocks,)),
            pltpu.SemaphoreType.DMA((size_y * planes,)),
            pltpu.SemaphoreType.DMA((blocks,)),
        ],
        compiler_params=params(),
        cost_estimate=takes(5),
        name="y_transform_parts",
    )(me, table, *columns, *after)


def y_inverse(table, modes, size_y, after):
    planes, width = modes.shape[2], modes.shape[5]
    height = Y // size_y
    count = 384 // height

    def kernel(table_ref, modes_ref, *refs):
        out = refs[-1]
        for plane in range(planes):
            columns = modes_ref[:, :, plane].reshape(Y, width)
            rows = jnp.dot(table_ref[...], columns, preferred_element_type=f32)
            out[:, plane] = rows.astype(bf16).reshape(count, height, width)

    return pl.pallas_call(
        kernel,
        grid=(size_y // count,),
        in_specs=[
            pl.BlockSpec((count * height, Y), lambda j: (j, 0)),
            pl.BlockSpec(modes.shape, lambda j: (0, 0, 0, 0, 0, 0)),
        ]
        + tied(after),
        out_specs=pl.BlockSpec((count, planes, height, width), lambda j: (j, 0, 0, 0)),
        out_shape=jax.ShapeDtypeStruct((size_y, planes, height, width), bf16),
        compiler_params=params(24),
        cost_estimate=takes(4),
        name="y_inverse",
    )(table, modes, *after)


def y_inverse_parts(me, table, modes, size_y, after):
    blocks, halves, planes, _, count, width = modes.shape
    height = Y // size_y
    shape = (planes, height, width)

    def kernel(me_ref, table_ref, modes_ref, *refs):
        outs = refs[len(after) : -6]
        held, lines, ready, table_in, lines_in, ready_out = refs[-6:]
        copies = []
        for block in range(blocks):
            for h in range(halves):
                for plane in range(planes):
                    copies.append(
                        pltpu.make_async_copy(
                            modes_ref.at[block, h, plane],
                            lines.at[plane, block, h],
                            lines_in.at[(block * halves + h) * planes + plane],
                        )
                    )
                    copies[-1].start()
        tables = fetch_blocks(
            table_ref, held, table_in, lambda s: lax.rem(me_ref[0] + s, size_y)
        )
        for copy in copies:
            copy.wait()
        results = []
        for s in range(size_y):
            tables[s].wait()
            for plane in range(planes):
                columns = lines[plane].reshape(Y, width)
                rows = jnp.dot(held[s], columns, preferred_element_type=f32)
                ready[s, plane] = rows.astype(bf16)
            results.append(pltpu.make_async_copy(ready.at[s], outs[s], ready_out.at[s]))
            results[s].start()
        for result in results:
            result.wait()

    anywhere = pl.BlockSpec(memory_space=pl.ANY)
    out_shape = [jax.ShapeDtypeStruct(shape, bf16)] * size_y
    return pl.pallas_call(
        kernel,
        in_specs=[pl.BlockSpec(memory_space=pltpu.SMEM), anywhere, anywhere] + tied(after),
        out_specs=[anywhere] * len(out_shape),
        out_shape=out_shape,
        scratch_shapes=[
            pltpu.VMEM((size_y, height, Y), bf16),
            pltpu.VMEM((planes, blocks, halves, 2, count, width), bf16),
            pltpu.VMEM((size_y,) + shape, bf16),
            pltpu.SemaphoreType.DMA((size_y,)),
            pltpu.SemaphoreType.DMA((blocks * halves * planes,)),
            pltpu.SemaphoreType.DMA((size_y,)),
        ],
        compiler_params=params(),
        cost_estimate=takes(4),
        name="y_inverse_parts",
    )(me, table, modes, *after)


def x_transform(table, modes, after):
    blocks, _, _, count, width = modes.shape

    def kernel(table_ref, modes_ref, *refs):
        spectrum_ref = refs[-1]
        rows = jnp.concatenate(
            [modes_ref[block, 0].reshape(2 * count, width) for block in range(blocks)], axis=1
        )
        spectrum = jnp.dot(rows, table_ref[...], preferred_element_type=f32)
        spectrum_ref[0] = spectrum.reshape(2, count, X)

    return pl.pallas_call(
        kernel,
        grid=(2,),
        in_specs=[
            pl.BlockSpec((X, X), lambda j: (0, 0)),
            pl.BlockSpec((blocks, 1, 2, count, width), lambda j: (0, j, 0, 0, 0)),
        ]
        + tied(after),
        out_specs=pl.BlockSpec((1, 2, count, X), lambda j: (j, 0, 0, 0)),
        out_shape=jax.ShapeDtypeStruct((2, 2, count, X), f32),
        compiler_params=params(24),
        cost_estimate=takes(3),
        name="x_transform",
    )(table, modes, *after)


def turned(field, axis, tz, ty, tx, wave):
    index = [tz, ty, tx]
    sign = 1.0 if index[axis] == 0 else -1.0
    index[axis] = 1 - index[axis]
    value = field[index[0], index[1], :, index[2] * HALF_X : (index[2] + 1) * HALF_X]
    return value * (wave * sign)


CURL = {
    0: ((1, 2), (0, 1)),
    1: ((0, 0), (2, 2)),
    2: ((2, 1), (1, 0)),
}


def curl_kernel(axes, where_ref, table_ref, plus_ref, minus_ref, back_ref):
    blocks, _, _, count, width = back_ref.shape
    base = where_ref[0] + pl.program_id(0) * count
    depth = where_ref[1]
    mode_y = lax.broadcasted_iota(jnp.int32, (count, HALF_X), 0) + base
    mode_x = lax.broadcasted_iota(jnp.int32, (count, HALF_X), 1)
    wave_y = mode_y.astype(f32) * (2.0 * math.pi / Y)
    wave_x = mode_x.astype(f32) * (2.0 * math.pi / X)
    wave_z = jnp.full((count, HALF_X), depth, jnp.int32).astype(f32) * (2.0 * math.pi / Z)
    square = wave_x * wave_x + wave_y * wave_y + wave_z * wave_z
    doubling = (
        jnp.where(mode_x == 0, 1.0, 2.0)
        * jnp.where(mode_y == 0, 1.0, 2.0)
        * jnp.where(wave_z == 0.0, 1.0, 2.0)
    )
    weight = jnp.where(square > 0, doubling / jnp.where(square > 0, square, 1.0), 0.0)
    waves = [wave_z * weight, wave_y * weight, wave_x * weight]
    rows = []
    for tz in range(2):
        for ty in range(2):
            parts = []
            for tx in range(2):
                parts.append(
                    (
                        turned(plus_ref, axes[0], tz, ty, tx, waves[axes[0]])
                        - turned(minus_ref, axes[1], tz, ty, tx, waves[axes[1]])
                    ).astype(bf16)
                )
            rows.append(jnp.concatenate(parts, axis=1))
    rows = jnp.concatenate(rows, axis=0)
    back = jnp.dot(rows, table_ref[...], preferred_element_type=f32).astype(bf16)
    for block in range(blocks):
        back_ref[block] = back[:, block * width : (block + 1) * width].reshape(2, 2, count, width)


def curl_inverse(where, table, spectra, component, blocks, after):
    (plus_axis, plus), (minus_axis, minus) = CURL[component]
    total = spectra[plus].shape[2]
    width = X // blocks
    count = 96 if total % 96 == 0 else total
    spec = pl.BlockSpec((2, 2, count, X), lambda j: (0, 0, j, 0))

    def kernel(*refs):
        curl_kernel((plus_axis, minus_axis), *refs[:4], refs[-1])

    return pl.pallas_call(
        kernel,
        grid=(total // count,),
        in_specs=[
            pl.BlockSpec(memory_space=pltpu.SMEM),
            pl.BlockSpec((X, X), lambda j: (0, 0)),
            spec,
            spec,
        ]
        + tied(after),
        out_specs=pl.BlockSpec((blocks, 2, 2, count, width), lambda j: (0, 0, 0, j, 0)),
        out_shape=jax.ShapeDtypeStruct((blocks, 2, 2, total, width), bf16),
        compiler_params=params(24),
        cost_estimate=takes(4),
        name="curl_inverse",
    )(where, table, spectra[plus], spectra[minus], *after)


def side_columns(planes):
    width = planes[0].shape[1]
    row = lax.broadcasted_iota(jnp.int32, (2 * Z, width), 0)
    lane = lax.broadcasted_iota(jnp.int32, (2 * Z, width), 1)
    total = None
    for n in range(Z):
        pick = ((row == n) & (lane == 0)) | ((row == n + Z) & (lane == width - 1))
        part = lax.dot_general(
            pick.astype(f32).astype(bf16),
            planes[n],
            (((1,), (1,)), ((), ())),
            preferred_element_type=f32,
        )
        total = part if total is None else total + part
    return total[:Z].astype(bf16), total[Z:].astype(bf16)


def spread_columns(low, high, first, layers, width):
    row = lax.broadcasted_iota(jnp.int32, (2 * Z, layers * width), 0)
    column = lax.broadcasted_iota(jnp.int32, (2 * Z, layers * width), 1)
    place = jnp.zeros((2 * Z, layers * width), f32)
    for n in range(layers):
        place = place + jnp.where((row == first + n) & (column == n * width), -0.5, 0.0)
        place = place + jnp.where(
            (row == first + n + Z) & (column == (n + 1) * width - 1), 0.5, 0.0
        )
    both = jnp.concatenate([low, high], axis=0).astype(bf16)
    spread = lax.dot_general(
        both, place.astype(bf16), (((0,), (0,)), ((), ())), preferred_element_type=f32
    )
    return [spread[:, n * width : (n + 1) * width] for n in range(layers)]


def edges_kernel(field_ref, *refs):
    first_column_ref, last_column_ref = refs[-2:]
    first, last = side_columns([field_ref[0, n] for n in range(Z)])
    first_column_ref[0] = first
    last_column_ref[0] = last


def edge_columns(field, components, after):
    _, _, height, width = field.shape
    shape = jax.ShapeDtypeStruct((components, Z, height), bf16)
    spec = pl.BlockSpec((1, Z, height), lambda i: (i, 0, 0))
    return pl.pallas_call(
        edges_kernel,
        grid=(components,),
        in_specs=[pl.BlockSpec((1, Z, height, width), lambda i: (i, 0, 0, 0))] + tied(after),
        out_specs=[spec, spec],
        out_shape=[shape, shape],
        compiler_params=params(),
        cost_estimate=takes(4),
        name="edge_columns",
    )(field, *after)


def exchange(first, last, axis):
    count = lax.axis_size(axis)
    up = [(i, (i + 1) % count) for i in range(count)]
    down = [((i + 1) % count, i) for i in range(count)]
    return lax.ppermute(last, axis, up), lax.ppermute(first, axis, down)


def adjoint_kernel(planes_ref, cotangent_ref, *refs):
    adjoint_ref, short_ref, first_x, last_x, first_y, last_y, held = refs
    _, height, width = held.shape
    scale = 1.0 / (X * Y * Z)
    base = pl.program_id(0) * ROWS
    for row, rows, columns in tiles(ROWS, width):
        place = pl.ds(pl.multiple_of(base + row, 16), 16)
        layers = depth_inverse(
            [planes_ref[2 * k, rows, columns].astype(f32) for k in range(KZ)],
            [planes_ref[2 * k + 1, rows, columns].astype(f32) for k in range(KZ)],
        )
        for n in range(Z):
            value = cotangent_ref[0, n, rows, columns] + layers[n] * scale
            adjoint_ref[n, rows, columns] = value
            short_ref[n, rows, columns] = value.astype(bf16)
            held[n, place, columns] = value.astype(bf16)

    @pl.when(pl.program_id(0) == pl.num_programs(0) - 1)
    def _():
        first, last = side_columns([held[n] for n in range(Z)])
        first_x[0] = first
        last_x[0] = last
        top = [held[n, 0:16, :].astype(f32)[0:1] for n in range(Z)]
        bottom = [held[n, height - 16 : height, :].astype(f32)[15:16] for n in range(Z)]
        first_y[0] = jnp.concatenate(top, 0).astype(bf16)
        last_y[0] = jnp.concatenate(bottom, 0).astype(bf16)


def make_adjoint(me, parts, cotangent, component, edges, after):
    whole = len(parts) == 1
    planes, height, width = parts[0].shape
    column = jax.ShapeDtypeStruct((3, Z, height), bf16)
    row = jax.ShapeDtypeStruct((3, Z, width), bf16)
    column_spec = pl.BlockSpec((1, Z, height), lambda j: (component, 0, 0))
    row_spec = pl.BlockSpec((1, Z, width), lambda j: (component, 0, 0))
    first_edge = 2 + len(parts)

    def kernel(me_ref, *refs):
        part_refs, cotangent_ref = refs[: len(parts)], refs[len(parts)]
        outs, held, spectrum = refs[-8:-2], refs[-2], refs[-1]
        if whole:
            spectrum = part_refs[0]
        else:
            for s, part in enumerate(part_refs):
                source = lax.rem(me_ref[0] + len(parts) - s, len(parts))
                spectrum[pl.ds(source * planes, planes)] = part[...]
        adjoint_kernel(spectrum, cotangent_ref, *outs, held)

    return pl.pallas_call(
        kernel,
        grid=(height // ROWS,),
        in_specs=[pl.BlockSpec(memory_space=pltpu.SMEM)]
        + [pl.BlockSpec((planes, ROWS, width), lambda j: (0, j, 0))] * len(parts)
        + [pl.BlockSpec((1, Z, ROWS, width), lambda j: (component, 0, j, 0))]
        + tied(edges)
        + tied(after),
        out_specs=[
            pl.BlockSpec((Z, ROWS, width), lambda j: (0, j, 0)),
            pl.BlockSpec((Z, ROWS, width), lambda j: (0, j, 0)),
            column_spec,
            column_spec,
            row_spec,
            row_spec,
        ],
        out_shape=[
            jax.ShapeDtypeStruct((Z, height, width), f32),
            jax.ShapeDtypeStruct((Z, height, width), bf16),
            column,
            column,
            row,
            row,
        ],
        input_output_aliases={first_edge + n: 2 + n for n in range(len(edges))},
        scratch_shapes=[
            pltpu.VMEM((Z, height, width), bf16),
            pltpu.VMEM((Z, ROWS, width), bf16),
        ],
        compiler_params=params(),
        cost_estimate=takes(5),
        name="make_adjoint",
    )(me, *parts, cotangent, *edges, *after)


def pick_row(rows, n):
    index = lax.broadcasted_iota(jnp.int32, rows.shape, 0)
    return jnp.sum(jnp.where(index == n, rows.astype(f32), 0.0), axis=0, keepdims=True)


def end_rows(low, high, height):
    row = lax.broadcasted_iota(jnp.int32, (height, low.shape[1]), 0)
    return jnp.where(row == 0, low * -0.5, 0.0) + jnp.where(row == height - 1, high * 0.5, 0.0)


LAYERS = 4


def grad_vort_kernel(
    component,
    slope_x,
    slope_y,
    velocity,
    velocity_above,
    velocity_below,
    adjoint,
    low_x,
    high_x,
    low_y,
    high_y,
    *refs,
):
    before, after = refs
    height, width = velocity.shape[2], velocity.shape[3]
    first = pl.program_id(0) * LAYERS
    ends = spread_columns(low_x[0], high_x[0], first, LAYERS, width)
    layers = velocity[0]
    stacked = layers.reshape(LAYERS * height, width)
    deep = [velocity_below[0, 0]] + [layers[k] for k in range(LAYERS)] + [velocity_above[0, 0]]
    inner = jnp.dot(stacked, slope_x[...], preferred_element_type=f32)
    for k in range(LAYERS):
        n = first + k
        value = adjoint[k]
        half = value * step_size
        along_x = inner[k * height : (k + 1) * height] + ends[k]
        along_y = jnp.dot(slope_y[...], layers[k], preferred_element_type=f32)
        along_y = along_y + end_rows(pick_row(low_y[0], n), pick_row(high_y[0], n), height)
        along_z = (deep[k + 2].astype(f32) - deep[k].astype(f32)) * 0.5
        for j, slope in enumerate((along_x, along_y, along_z)):
            term = half * slope
            if j == component:
                term = term + value
            if before is not None:
                term = before[j, k].astype(f32) + term
            after[j, k] = term.astype(after.dtype)


def add_grad_vort(component, slopes, velocity, adjoint, halos, before, after, kind):
    _, _, height, width = velocity.shape
    slope_x, slope_y = slopes
    whole = lambda shape: pl.BlockSpec(shape, lambda n: (0,) * len(shape))
    column = pl.BlockSpec((1, Z, height), lambda n: (component, 0, 0))
    row = pl.BlockSpec((1, Z, width), lambda n: (component, 0, 0))
    sums = pl.BlockSpec((3, LAYERS, height, width), lambda n: (0, n, 0, 0))
    layer_above = lambda n: lax.rem((n + 1) * LAYERS, Z)
    layer_below = lambda n: lax.rem(n * LAYERS + Z - 1, Z)
    operands = [slope_x, slope_y, velocity, velocity, velocity, adjoint, *halos]
    in_specs = [
        whole((width, width)),
        whole((height, height)),
        pl.BlockSpec((1, LAYERS, height, width), lambda n: (component, n, 0, 0)),
        pl.BlockSpec((1, 1, height, width), lambda n: (component, layer_above(n), 0, 0)),
        pl.BlockSpec((1, 1, height, width), lambda n: (component, layer_below(n), 0, 0)),
        pl.BlockSpec((LAYERS, height, width), lambda n: (n, 0, 0)),
        column,
        column,
        row,
        row,
    ]
    if before is not None:
        operands.append(before)
        in_specs.append(sums)

    def kernel(*refs):
        grad_vort_kernel(component, *refs[:10], None if before is None else refs[10], refs[-1])

    return pl.pallas_call(
        kernel,
        grid=(Z // LAYERS,),
        in_specs=in_specs + tied(after),
        out_specs=sums,
        out_shape=jax.ShapeDtypeStruct((3, Z, height, width), kind),
        compiler_params=params(),
        cost_estimate=takes(9),
        name="add_grad_vort",
    )(*operands, *after)


def grad_vel_kernel(
    count, slope_x, slope_y, vorticity, vorticity_above, vorticity_below, *refs
):
    adjoints, edges = refs[: 3 * count], refs[3 * count :]
    vort_low_x, vort_high_x, vort_low_y, vort_high_y, low_x, high_x, low_y, high_y = edges[:8]
    after = refs[-1]
    _, _, height, width = vorticity.shape
    first = pl.program_id(0) * LAYERS
    factor = -0.5 * step_size

    def times(one, other):
        return one.astype(f32) * other.astype(f32)

    for c in range(count):
        here, above, below = adjoints[3 * c : 3 * c + 3]
        ends = spread_columns(
            times(vort_low_x[0], low_x[c]) * -step_size,
            times(vort_high_x[0], high_x[c]) * -step_size,
            first,
            LAYERS,
            width,
        )
        deep = [times(vorticity_below[0, 0], below[0])]
        along_x = []
        along_y = []
        for k in range(LAYERS):
            value = here[k].astype(f32)
            along_x.append((vorticity[0, k].astype(f32) * value).astype(bf16))
            along_y.append((vorticity[1, k].astype(f32) * value).astype(bf16))
            deep.append(vorticity[2, k].astype(f32) * value)
        deep.append(times(vorticity_above[0, 0], above[0]))
        along_x = jnp.dot(
            jnp.concatenate(along_x, axis=0), slope_x[...], preferred_element_type=f32
        )
        for k in range(LAYERS):
            n = first + k
            total = jnp.dot(slope_y[...], along_y[k], preferred_element_type=f32)
            total = total + along_x[k * height : (k + 1) * height] + ends[k]
            after[c, k] = total + (deep[k + 2] - deep[k]) * factor
            low = pick_row(vort_low_y[0], n) * pick_row(low_y[c], n)
            high = pick_row(vort_high_y[0], n) * pick_row(high_y[c], n)
            after[c, k, 0:1, :] = after[c, k, 0:1, :] - low * factor
            after[c, k, height - 1 : height, :] = (
                after[c, k, height - 1 : height, :] + high * factor
            )


def write_grad_vel(slopes, vorticity, adjoints, saved_halos, halos, after):
    _, _, height, width = vorticity.shape
    count = len(adjoints)
    whole = lambda shape: pl.BlockSpec(shape, lambda n: (0,) * len(shape))
    saved_column = pl.BlockSpec((1, Z, height), lambda n: (3, 0, 0))
    saved_row = pl.BlockSpec((1, Z, width), lambda n: (3, 0, 0))
    layer_above = lambda n: lax.rem((n + 1) * LAYERS, Z)
    layer_below = lambda n: lax.rem(n * LAYERS + Z - 1, Z)
    operands = [*slopes, vorticity, vorticity, vorticity]
    in_specs = [
        whole((width, width)),
        whole((height, height)),
        pl.BlockSpec((3, LAYERS, height, width), lambda n: (0, n, 0, 0)),
        pl.BlockSpec((1, 1, height, width), lambda n: (2, layer_above(n), 0, 0)),
        pl.BlockSpec((1, 1, height, width), lambda n: (2, layer_below(n), 0, 0)),
    ]
    for adjoint in adjoints:
        operands = operands + [adjoint] * 3
        in_specs = in_specs + [
            pl.BlockSpec((LAYERS, height, width), lambda n: (n, 0, 0)),
            pl.BlockSpec((1, height, width), lambda n: (layer_above(n), 0, 0)),
            pl.BlockSpec((1, height, width), lambda n: (layer_below(n), 0, 0)),
        ]
    operands = operands + list(saved_halos) + list(halos)
    in_specs = in_specs + [saved_column, saved_column, saved_row, saved_row]
    in_specs = in_specs + [whole((count, Z, height))] * 2 + [whole((count, Z, width))] * 2

    def kernel(*refs):
        grad_vel_kernel(count, *refs)

    return pl.pallas_call(
        kernel,
        grid=(Z // LAYERS,),
        in_specs=in_specs + tied(after),
        out_specs=pl.BlockSpec((count, LAYERS, height, width), lambda n: (0, n, 0, 0)),
        out_shape=jax.ShapeDtypeStruct((count, Z, height, width), f32),
        compiler_params=params(),
        cost_estimate=takes(12),
        name="write_grad_vel",
    )(*operands, *after)


def pair_exchange(parts, axis, mine):
    count = lax.axis_size(axis)
    kept = lax.dynamic_index_in_dim(parts, mine, 1, keepdims=False)
    sent = lax.dynamic_index_in_dim(parts, 1 - mine, 1, keepdims=False)
    got = lax.ppermute(sent, axis, [(i, i ^ 1) for i in range(count)])
    return jnp.where(mine == 0, jnp.stack([kept, got], 1), jnp.stack([got, kept], 1))


def shifted(parts, axis):
    count = lax.axis_size(axis)
    return [parts[0]] + [
        lax.ppermute(parts[s], axis, [(i, (i + s) % count) for i in range(count)])
        for s in range(1, count)
    ]


def local(cot_vort, cot_vel, vorticity, velocity):
    size_x = lax.axis_size("gx")
    size_y = lax.axis_size("gy")
    planes = Z // size_y
    halves = size_y // KZ
    _, _, height, width = cot_vel.shape
    modes = HALF_Y // (size_x * halves)
    place_x = lax.axis_index("gx")
    place_y = lax.axis_index("gy")
    half = lax.rem(place_y, halves)
    me = place_y.astype(jnp.int32).reshape(1)
    where = jnp.stack([(place_x * halves + half) * modes, place_y // halves]).astype(jnp.int32)

    y_table, y_back_table = y_tables(size_x * halves)
    x_table, x_back_table = x_tables()
    slope_x = slope_matrix(width)
    slope_y = np.ascontiguousarray(slope_matrix(height).T)

    layers = depth_transform(cot_vel, FORWARD_ORDER[0])

    velocity_first, velocity_last = edge_columns(velocity, 3, (layers,))
    vorticity_first, vorticity_last = edge_columns(vorticity, 1, (layers,))
    low_x, high_x = exchange(
        jnp.concatenate([velocity_first, vorticity_first]),
        jnp.concatenate([velocity_last, vorticity_last]),
        "gx",
    )
    low_y, high_y = exchange(
        jnp.concatenate([velocity[:, :, 0], vorticity[1:2, :, 0]]),
        jnp.concatenate([velocity[:, :, height - 1], vorticity[1:2, :, height - 1]]),
        "gy",
    )
    saved_halos = (low_x, high_x, low_y, high_y)
    early = ((low_x, high_x), (low_y, high_y), ())

    columns = layers.reshape(size_y, planes, height, width)
    columns = lax.all_to_all(columns, "gy", 0, 0, tiled=True)
    sent = []
    for place in range(3):
        if place > 0:
            layers = depth_transform(cot_vel, FORWARD_ORDER[place], me, size_y, (sent[-1],))
            columns = shifted(layers, "gy")
        if place == 0:
            parts = y_transform(y_table, columns, size_x, halves, early[place])
        else:
            parts = y_transform_parts(me, y_table, columns, size_x, halves, early[place])
        parts = parts.reshape(size_x, 2, 2, modes, width)
        sent.append(parts if halves == 1 else pair_exchange(parts, "gy", half))

    def spectrum(place, after):
        lines = lax.all_to_all(sent[place], "gx", 0, 0, tiled=True)
        return x_transform(x_table, lines, after)

    def curl(component, after):
        return curl_inverse(where, x_back_table, spectra, component, size_x, after)

    def back(filtered):
        parts = lax.all_to_all(filtered, "gx", 0, 0, tiled=True)
        if halves == 2:
            parts = pair_exchange(parts, "gy", half)
        return parts.reshape(size_x, halves, planes, 2, modes, width)

    def rows_of(component, modes_back, after):
        if component == BACK_ORDER[2]:
            return [y_inverse(y_back_table, modes_back, size_y, after)]
        return y_inverse_parts(me, y_back_table, modes_back, size_y, after)

    def layers_of(rows):
        if len(rows) == 1:
            return [lax.all_to_all(rows[0], "gy", 0, 0, tiled=True).reshape(Z, height, width)]
        return shifted(rows, "gy")

    one, two, three = BACK_ORDER
    spectra = {FORWARD_ORDER[0]: spectrum(0, (sent[1],))}
    spectra[FORWARD_ORDER[1]] = spectrum(1, (sent[2],))
    curl_one = curl(one, ())
    spectra[FORWARD_ORDER[2]] = spectrum(2, (curl_one,))
    curl_two = curl(two, ())
    rows_one = rows_of(one, back(curl_one), (curl_two,))
    layers_one = layers_of(rows_one)
    curl_three = curl(three, tuple(layers_one))

    def vort_of(component, adjoint, before, after):
        kind = f32 if component == three else bf16
        return add_grad_vort(
            component, (slope_x, slope_y), velocity, adjoint, saved_halos, before, after, kind
        )

    adjoint_one, short_one, *edges = make_adjoint(me, layers_one, cot_vort, one, [], ())
    rows_two = rows_of(two, back(curl_two), (adjoint_one,))
    layers_two = layers_of(rows_two)
    rows_three = rows_of(three, back(curl_three), tuple(layers_two))
    grad_vort = vort_of(one, adjoint_one, None, (rows_two[0],))
    adjoint_two, short_two, *edges = make_adjoint(
        me, layers_two, cot_vort, two, edges, (rows_three[0],)
    )
    grad_vort = vort_of(two, adjoint_two, grad_vort, ())
    adjoint_three, short_three, *edges = make_adjoint(
        me, layers_of(rows_three), cot_vort, three, edges, (grad_vort,)
    )
    halos = exchange(edges[0], edges[1], "gx") + exchange(edges[2], edges[3], "gy")
    grad_vort = vort_of(three, adjoint_three, grad_vort, ())
    shorts = {one: short_one, two: short_two, three: short_three}
    scaled = [(slope * np.float32(-step_size)).astype(slope.dtype) for slope in (slope_x, slope_y)]
    grad_vel = write_grad_vel(
        scaled, vorticity, [shorts[i] for i in range(3)], saved_halos, halos, (grad_vort,)
    )
    return grad_vort, grad_vel


def solution(mesh):
    spec = P(None, None, "gy", "gx")
    return jax.shard_map(
        local,
        mesh=mesh,
        in_specs=(spec, spec, spec, spec),
        out_specs=(spec, spec),
        check_vma=False,
    )
```

```python
import math

import jax
import jax.numpy as jnp
import ml_dtypes
import numpy as np
from jax import lax
from jax.experimental import pallas as pl
from jax.experimental.pallas import tpu as pltpu
from jax.sharding import PartitionSpec as P

X = 1024
Y = 1536
Z = 16
HALF_X = X // 2
HALF_Y = Y // 2
KZ = Z // 2

step_size = 0.5

f32 = jnp.float32
bf16 = jnp.bfloat16

FORWARD_ORDER = (0, 1, 2)
BACK_ORDER = (2, 0, 1)


def params(megabytes=56):
    return pltpu.CompilerParams(vmem_limit_bytes=megabytes * 1024 * 1024)


def takes(microseconds):
    return pl.CostEstimate(flops=1, bytes_accessed=int(microseconds * 3.0e6), transcendentals=0)


def tied(after):
    return [pl.BlockSpec(memory_space=pl.ANY)] * len(after)


def trig(first, second, length):
    angle = (np.outer(first, second) % length) * (2.0 * math.pi / length)
    return np.cos(angle), np.sin(angle)


def y_tables(blocks):
    cosine, sine = trig(np.arange(HALF_Y), np.arange(Y), Y)
    both = np.stack([cosine.reshape(blocks, -1, Y), sine.reshape(blocks, -1, Y)], 1).reshape(Y, Y)
    both = both.astype(ml_dtypes.bfloat16)
    return both, np.ascontiguousarray(both.T)


def x_tables():
    cosine, sine = trig(np.arange(X), np.arange(HALF_X), X)
    both = np.concatenate([cosine, sine], 1).astype(ml_dtypes.bfloat16)
    return both, np.ascontiguousarray(both.T)


def slope_matrix(size):
    return ((np.eye(size, k=-1) - np.eye(size, k=1)) * 0.5).astype(ml_dtypes.bfloat16)


def combine(terms):
    total = None
    for factor, value in terms:
        if abs(factor) < 1e-12:
            continue
        if abs(factor - 1.0) < 1e-12:
            part = value
        elif abs(factor + 1.0) < 1e-12:
            part = -value
        else:
            part = value * factor
        total = part if total is None else total + part
    return total


def depth_forward(values):
    even = [values[0]] + [values[n] + values[Z - n] for n in range(1, 8)] + [values[8]]
    odd = [None] + [values[n] - values[Z - n] for n in range(1, 8)]
    even_sum = [even[n] + even[8 - n] for n in range(4)] + [even[4]]
    even_dif = [even[n] - even[8 - n] for n in range(4)]
    odd_sum = [None] + [odd[n] + odd[8 - n] for n in range(1, 4)] + [odd[4]]
    odd_dif = [None] + [odd[n] - odd[8 - n] for n in range(1, 4)]
    result = []
    for k in range(KZ):
        folded = even_sum if k % 2 == 0 else even_dif
        cos_part = combine([(math.cos(math.pi * k * n / 8), folded[n]) for n in range(len(folded))])
        folded = odd_dif if k % 2 == 0 else odd_sum
        sin_part = combine(
            [(math.sin(math.pi * k * n / 8), folded[n]) for n in range(1, len(folded))]
        )
        result.append((cos_part, sin_part))
    return result


def depth_inverse(cos_parts, sin_parts):
    layers = [None] * Z
    cos_sum, sin_sum = [None] * 9, [None] * 9
    for n in range(5):
        evens = combine([(math.cos(math.pi * k * n / 8), cos_parts[k]) for k in range(0, KZ, 2)])
        odds = combine([(math.cos(math.pi * k * n / 8), cos_parts[k]) for k in range(1, KZ, 2)])
        if n == 4:
            cos_sum[4] = evens
        else:
            cos_sum[n] = evens + odds
            cos_sum[8 - n] = evens - odds
    for n in range(1, 5):
        evens = combine([(math.sin(math.pi * k * n / 8), sin_parts[k]) for k in range(0, KZ, 2)])
        odds = combine([(math.sin(math.pi * k * n / 8), sin_parts[k]) for k in range(1, KZ, 2)])
        if n == 4:
            sin_sum[4] = odds
        else:
            sin_sum[n] = odds + evens
            sin_sum[8 - n] = odds - evens
    layers[0], layers[8] = cos_sum[0], cos_sum[8]
    for n in range(1, 8):
        layers[n] = cos_sum[n] + sin_sum[n]
        layers[Z - n] = cos_sum[n] - sin_sum[n]
    return layers


ROWS = 48


def tiles(height, width):
    for row in range(0, height, 16):
        for column in range(0, width, 128):
            yield row, pl.ds(row, 16), pl.ds(column, 128)


def depth_forward_kernel(values_ref, planes_ref):
    _, _, height, width = values_ref.shape
    for _, rows, columns in tiles(height, width):
        spectrum = depth_forward([values_ref[0, n, rows, columns] for n in range(Z)])
        for k, (cos_part, sin_part) in enumerate(spectrum):
            planes_ref[2 * k, rows, columns] = cos_part.astype(bf16)
            if sin_part is None:
                sin_part = jnp.zeros_like(cos_part)
            planes_ref[2 * k + 1, rows, columns] = sin_part.astype(bf16)


def depth_transform(values, component, me=None, size_y=1, after=()):
    _, _, height, width = values.shape
    planes = Z // size_y
    shifted_out = me is not None

    def kernel(*refs):
        if not shifted_out:
            depth_forward_kernel(*refs)
            return
        me_ref, values_ref, outs, held = refs[0], refs[1], refs[2 + len(after) : -1], refs[-1]
        depth_forward_kernel(values_ref, held)
        for s, out in enumerate(outs):
            target = lax.rem(me_ref[0] + s, size_y)
            out[...] = held[pl.ds(target * planes, planes)]

    block = (Z // size_y, ROWS, width)
    out_spec = pl.BlockSpec(block, lambda j: (0, j, 0))
    out_shape = jax.ShapeDtypeStruct((planes, height, width), bf16)
    smem = pl.BlockSpec(memory_space=pltpu.SMEM)
    return pl.pallas_call(
        kernel,
        grid=(height // ROWS,),
        in_specs=([smem] if shifted_out else [])
        + [pl.BlockSpec((1, Z, ROWS, width), lambda j: (component, 0, j, 0))]
        + tied(after),
        out_specs=[out_spec] * size_y if shifted_out else out_spec,
        out_shape=[out_shape] * size_y if shifted_out else out_shape,
        scratch_shapes=[pltpu.VMEM((Z, ROWS, width), bf16)] if shifted_out else [],
        compiler_params=params(),
        cost_estimate=takes(3),
        name="depth_transform",
    )(*(([me] if shifted_out else []) + [values, *after]))


def fetch_blocks(table_ref, held, arrived, order):
    count, rows, _ = held.shape
    copies = []
    for s in range(count):
        place = pl.ds(pl.multiple_of(order(s) * rows, rows), rows)
        copies.append(pltpu.make_async_copy(table_ref.at[place], held.at[s], arrived.at[s]))
        copies[s].start()
    return copies


def y_transform(table, columns, blocks, halves, after):
    _, planes, _, width = columns.shape
    modes = HALF_Y // (blocks * halves)
    rows = Y // blocks

    def kernel(table_ref, columns_ref, *refs):
        out = refs[-1]
        for plane in range(planes):
            column = columns_ref[:, plane].reshape(Y, width)
            part = jnp.dot(table_ref[...], column, preferred_element_type=f32)
            out[0, :, plane] = part.astype(bf16).reshape(halves, 2, modes, width)

    return pl.pallas_call(
        kernel,
        grid=(blocks,),
        in_specs=[
            pl.BlockSpec((rows, Y), lambda j: (j, 0)),
            pl.BlockSpec(columns.shape, lambda j: (0, 0, 0, 0)),
        ]
        + tied(after),
        out_specs=pl.BlockSpec((1, halves, planes, 2, modes, width), lambda j: (j, 0, 0, 0, 0, 0)),
        out_shape=jax.ShapeDtypeStruct((blocks, halves, planes, 2, modes, width), bf16),
        compiler_params=params(24),
        cost_estimate=takes(4),
        name="y_transform",
    )(table, columns, *after)


def y_transform_parts(me, table, columns, blocks, halves, after):
    size_y = len(columns)
    planes, height, width = columns[0].shape[-3:]
    modes = HALF_Y // (blocks * halves)
    rows = Y // blocks
    shape = (blocks, halves, planes, 2, modes, width)

    def kernel(me_ref, table_ref, *refs):
        parts = refs[: len(columns)]
        out, held, lines, ready, table_in, lines_in, ready_out = refs[-7:]
        copies = []
        for s in range(size_y):
            source = lax.rem(me_ref[0] + size_y - s, size_y)
            place = pl.ds(pl.multiple_of(source * height, height), height)
            for plane in range(planes):
                copies.append(
                    pltpu.make_async_copy(
                        parts[s].at[plane],
                        lines.at[plane, place],
                        lines_in.at[s * planes + plane],
                    )
                )
                copies[-1].start()
        tables = fetch_blocks(table_ref, held, table_in, lambda s: s)
        for copy in copies:
            copy.wait()
        results = []
        for s in range(blocks):
            tables[s].wait()
            for plane in range(planes):
                part = jnp.dot(held[s], lines[plane], preferred_element_type=f32)
                ready[s, :, plane] = part.astype(bf16).reshape(halves, 2, modes, width)
            results.append(pltpu.make_async_copy(ready.at[s], out.at[s], ready_out.at[s]))
            results[s].start()
        for result in results:
            result.wait()

    anywhere = pl.BlockSpec(memory_space=pl.ANY)
    return pl.pallas_call(
        kernel,
        in_specs=[pl.BlockSpec(memory_space=pltpu.SMEM), anywhere]
        + [anywhere] * len(columns)
        + tied(after),
        out_specs=anywhere,
        out_shape=jax.ShapeDtypeStruct(shape, bf16),
        scratch_shapes=[
            pltpu.VMEM((blocks, rows, Y), bf16),
            pltpu.VMEM((planes, Y, width), bf16),
            pltpu.VMEM(shape, bf16),
            pltpu.SemaphoreType.DMA((blocks,)),
            pltpu.SemaphoreType.DMA((size_y * planes,)),
            pltpu.SemaphoreType.DMA((blocks,)),
        ],
        compiler_params=params(),
        cost_estimate=takes(5),
        name="y_transform_parts",
    )(me, table, *columns, *after)


def y_inverse(table, modes, size_y, after):
    planes, width = modes.shape[2], modes.shape[5]
    height = Y // size_y
    count = 384 // height

    def kernel(table_ref, modes_ref, *refs):
        out = refs[-1]
        for plane in range(planes):
            columns = modes_ref[:, :, plane].reshape(Y, width)
            rows = jnp.dot(table_ref[...], columns, preferred_element_type=f32)
            out[:, plane] = rows.astype(bf16).reshape(count, height, width)

    return pl.pallas_call(
        kernel,
        grid=(size_y // count,),
        in_specs=[
            pl.BlockSpec((count * height, Y), lambda j: (j, 0)),
            pl.BlockSpec(modes.shape, lambda j: (0, 0, 0, 0, 0, 0)),
        ]
        + tied(after),
        out_specs=pl.BlockSpec((count, planes, height, width), lambda j: (j, 0, 0, 0)),
        out_shape=jax.ShapeDtypeStruct((size_y, planes, height, width), bf16),
        compiler_params=params(24),
        cost_estimate=takes(4),
        name="y_inverse",
    )(table, modes, *after)


def y_inverse_parts(me, table, modes, size_y, after):
    blocks, halves, planes, _, count, width = modes.shape
    height = Y // size_y
    shape = (planes, height, width)

    def kernel(me_ref, table_ref, modes_ref, *refs):
        outs = refs[len(after) : -6]
        held, lines, ready, table_in, lines_in, ready_out = refs[-6:]
        copies = []
        for block in range(blocks):
            for h in range(halves):
                for plane in range(planes):
                    copies.append(
                        pltpu.make_async_copy(
                            modes_ref.at[block, h, plane],
                            lines.at[plane, block, h],
                            lines_in.at[(block * halves + h) * planes + plane],
                        )
                    )
                    copies[-1].start()
        tables = fetch_blocks(
            table_ref, held, table_in, lambda s: lax.rem(me_ref[0] + s, size_y)
        )
        for copy in copies:
            copy.wait()
        results = []
        for s in range(size_y):
            tables[s].wait()
            for plane in range(planes):
                columns = lines[plane].reshape(Y, width)
                rows = jnp.dot(held[s], columns, preferred_element_type=f32)
                ready[s, plane] = rows.astype(bf16)
            results.append(pltpu.make_async_copy(ready.at[s], outs[s], ready_out.at[s]))
            results[s].start()
        for result in results:
            result.wait()

    anywhere = pl.BlockSpec(memory_space=pl.ANY)
    out_shape = [jax.ShapeDtypeStruct(shape, bf16)] * size_y
    return pl.pallas_call(
        kernel,
        in_specs=[pl.BlockSpec(memory_space=pltpu.SMEM), anywhere, anywhere] + tied(after),
        out_specs=[anywhere] * len(out_shape),
        out_shape=out_shape,
        scratch_shapes=[
            pltpu.VMEM((size_y, height, Y), bf16),
            pltpu.VMEM((planes, blocks, halves, 2, count, width), bf16),
            pltpu.VMEM((size_y,) + shape, bf16),
            pltpu.SemaphoreType.DMA((size_y,)),
            pltpu.SemaphoreType.DMA((blocks * halves * planes,)),
            pltpu.SemaphoreType.DMA((size_y,)),
        ],
        compiler_params=params(),
        cost_estimate=takes(4),
        name="y_inverse_parts",
    )(me, table, modes, *after)


def x_transform(table, modes, after):
    blocks, _, _, count, width = modes.shape

    def kernel(table_ref, modes_ref, *refs):
        spectrum_ref = refs[-1]
        rows = jnp.concatenate(
            [modes_ref[block, 0].reshape(2 * count, width) for block in range(blocks)], axis=1
        )
        spectrum = jnp.dot(rows, table_ref[...], preferred_element_type=f32)
        spectrum_ref[0] = spectrum.reshape(2, count, X)

    return pl.pallas_call(
        kernel,
        grid=(2,),
        in_specs=[
            pl.BlockSpec((X, X), lambda j: (0, 0)),
            pl.BlockSpec((blocks, 1, 2, count, width), lambda j: (0, j, 0, 0, 0)),
        ]
        + tied(after),
        out_specs=pl.BlockSpec((1, 2, count, X), lambda j: (j, 0, 0, 0)),
        out_shape=jax.ShapeDtypeStruct((2, 2, count, X), f32),
        compiler_params=params(24),
        cost_estimate=takes(3),
        name="x_transform",
    )(table, modes, *after)


def turned(field, axis, tz, ty, tx, wave):
    index = [tz, ty, tx]
    sign = 1.0 if index[axis] == 0 else -1.0
    index[axis] = 1 - index[axis]
    value = field[index[0], index[1], :, index[2] * HALF_X : (index[2] + 1) * HALF_X]
    return value * (wave * sign)


CURL = {
    0: ((1, 2), (0, 1)),
    1: ((0, 0), (2, 2)),
    2: ((2, 1), (1, 0)),
}


def curl_kernel(axes, where_ref, table_ref, plus_ref, minus_ref, back_ref):
    blocks, _, _, count, width = back_ref.shape
    base = where_ref[0] + pl.program_id(0) * count
    depth = where_ref[1]
    mode_y = lax.broadcasted_iota(jnp.int32, (count, HALF_X), 0) + base
    mode_x = lax.broadcasted_iota(jnp.int32, (count, HALF_X), 1)
    wave_y = mode_y.astype(f32) * (2.0 * math.pi / Y)
    wave_x = mode_x.astype(f32) * (2.0 * math.pi / X)
    wave_z = jnp.full((count, HALF_X), depth, jnp.int32).astype(f32) * (2.0 * math.pi / Z)
    square = wave_x * wave_x + wave_y * wave_y + wave_z * wave_z
    doubling = (
        jnp.where(mode_x == 0, 1.0, 2.0)
        * jnp.where(mode_y == 0, 1.0, 2.0)
        * jnp.where(wave_z == 0.0, 1.0, 2.0)
    )
    weight = jnp.where(square > 0, doubling / jnp.where(square > 0, square, 1.0), 0.0)
    waves = [wave_z * weight, wave_y * weight, wave_x * weight]
    rows = []
    for tz in range(2):
        for ty in range(2):
            parts = []
            for tx in range(2):
                parts.append(
                    (
                        turned(plus_ref, axes[0], tz, ty, tx, waves[axes[0]])
                        - turned(minus_ref, axes[1], tz, ty, tx, waves[axes[1]])
                    ).astype(bf16)
                )
            rows.append(jnp.concatenate(parts, axis=1))
    rows = jnp.concatenate(rows, axis=0)
    back = jnp.dot(rows, table_ref[...], preferred_element_type=f32).astype(bf16)
    for block in range(blocks):
        back_ref[block] = back[:, block * width : (block + 1) * width].reshape(2, 2, count, width)


def curl_inverse(where, table, spectra, component, blocks, after):
    (plus_axis, plus), (minus_axis, minus) = CURL[component]
    total = spectra[plus].shape[2]
    width = X // blocks
    count = 96 if total % 96 == 0 else total
    spec = pl.BlockSpec((2, 2, count, X), lambda j: (0, 0, j, 0))

    def kernel(*refs):
        curl_kernel((plus_axis, minus_axis), *refs[:4], refs[-1])

    return pl.pallas_call(
        kernel,
        grid=(total // count,),
        in_specs=[
            pl.BlockSpec(memory_space=pltpu.SMEM),
            pl.BlockSpec((X, X), lambda j: (0, 0)),
            spec,
            spec,
        ]
        + tied(after),
        out_specs=pl.BlockSpec((blocks, 2, 2, count, width), lambda j: (0, 0, 0, j, 0)),
        out_shape=jax.ShapeDtypeStruct((blocks, 2, 2, total, width), bf16),
        compiler_params=params(24),
        cost_estimate=takes(4),
        name="curl_inverse",
    )(where, table, spectra[plus], spectra[minus], *after)


def side_columns(planes):
    width = planes[0].shape[1]
    row = lax.broadcasted_iota(jnp.int32, (2 * Z, width), 0)
    lane = lax.broadcasted_iota(jnp.int32, (2 * Z, width), 1)
    total = None
    for n in range(Z):
        pick = ((row == n) & (lane == 0)) | ((row == n + Z) & (lane == width - 1))
        part = lax.dot_general(
            pick.astype(f32).astype(bf16),
            planes[n],
            (((1,), (1,)), ((), ())),
            preferred_element_type=f32,
        )
        total = part if total is None else total + part
    return total[:Z].astype(bf16), total[Z:].astype(bf16)


def spread_columns(low, high, first, layers, width):
    row = lax.broadcasted_iota(jnp.int32, (2 * Z, layers * width), 0)
    column = lax.broadcasted_iota(jnp.int32, (2 * Z, layers * width), 1)
    place = jnp.zeros((2 * Z, layers * width), f32)
    for n in range(layers):
        place = place + jnp.where((row == first + n) & (column == n * width), -0.5, 0.0)
        place = place + jnp.where(
            (row == first + n + Z) & (column == (n + 1) * width - 1), 0.5, 0.0
        )
    both = jnp.concatenate([low, high], axis=0).astype(bf16)
    spread = lax.dot_general(
        both, place.astype(bf16), (((0,), (0,)), ((), ())), preferred_element_type=f32
    )
    return [spread[:, n * width : (n + 1) * width] for n in range(layers)]


def edges_kernel(field_ref, *refs):
    first_column_ref, last_column_ref = refs[-2:]
    first, last = side_columns([field_ref[0, n] for n in range(Z)])
    first_column_ref[0] = first
    last_column_ref[0] = last


def edge_columns(field, components, after):
    _, _, height, width = field.shape
    shape = jax.ShapeDtypeStruct((components, Z, height), bf16)
    spec = pl.BlockSpec((1, Z, height), lambda i: (i, 0, 0))
    return pl.pallas_call(
        edges_kernel,
        grid=(components,),
        in_specs=[pl.BlockSpec((1, Z, height, width), lambda i: (i, 0, 0, 0))] + tied(after),
        out_specs=[spec, spec],
        out_shape=[shape, shape],
        compiler_params=params(),
        cost_estimate=takes(4),
        name="edge_columns",
    )(field, *after)


def exchange(first, last, axis):
    count = lax.axis_size(axis)
    up = [(i, (i + 1) % count) for i in range(count)]
    down = [((i + 1) % count, i) for i in range(count)]
    return lax.ppermute(last, axis, up), lax.ppermute(first, axis, down)


def adjoint_kernel(planes_ref, cotangent_ref, *refs):
    adjoint_ref, short_ref, first_x, last_x, first_y, last_y, held = refs
    _, height, width = held.shape
    scale = 1.0 / (X * Y * Z)
    base = pl.program_id(0) * ROWS
    for row, rows, columns in tiles(ROWS, width):
        place = pl.ds(pl.multiple_of(base + row, 16), 16)
        layers = depth_inverse(
            [planes_ref[2 * k, rows, columns].astype(f32) for k in range(KZ)],
            [planes_ref[2 * k + 1, rows, columns].astype(f32) for k in range(KZ)],
        )
        for n in range(Z):
            value = cotangent_ref[0, n, rows, columns] + layers[n] * scale
            adjoint_ref[n, rows, columns] = value
            short_ref[n, rows, columns] = value.astype(bf16)
            held[n, place, columns] = value.astype(bf16)

    @pl.when(pl.program_id(0) == pl.num_programs(0) - 1)
    def _():
        first, last = side_columns([held[n] for n in range(Z)])
        first_x[0] = first
        last_x[0] = last
        top = [held[n, 0:16, :].astype(f32)[0:1] for n in range(Z)]
        bottom = [held[n, height - 16 : height, :].astype(f32)[15:16] for n in range(Z)]
        first_y[0] = jnp.concatenate(top, 0).astype(bf16)
        last_y[0] = jnp.concatenate(bottom, 0).astype(bf16)


def make_adjoint(me, parts, cotangent, component, edges, after):
    whole = len(parts) == 1
    planes, height, width = parts[0].shape
    column = jax.ShapeDtypeStruct((3, Z, height), bf16)
    row = jax.ShapeDtypeStruct((3, Z, width), bf16)
    column_spec = pl.BlockSpec((1, Z, height), lambda j: (component, 0, 0))
    row_spec = pl.BlockSpec((1, Z, width), lambda j: (component, 0, 0))
    first_edge = 2 + len(parts)

    def kernel(me_ref, *refs):
        part_refs, cotangent_ref = refs[: len(parts)], refs[len(parts)]
        outs, held, spectrum = refs[-8:-2], refs[-2], refs[-1]
        if whole:
            spectrum = part_refs[0]
        else:
            for s, part in enumerate(part_refs):
                source = lax.rem(me_ref[0] + len(parts) - s, len(parts))
                spectrum[pl.ds(source * planes, planes)] = part[...]
        adjoint_kernel(spectrum, cotangent_ref, *outs, held)

    return pl.pallas_call(
        kernel,
        grid=(height // ROWS,),
        in_specs=[pl.BlockSpec(memory_space=pltpu.SMEM)]
        + [pl.BlockSpec((planes, ROWS, width), lambda j: (0, j, 0))] * len(parts)
        + [pl.BlockSpec((1, Z, ROWS, width), lambda j: (component, 0, j, 0))]
        + tied(edges)
        + tied(after),
        out_specs=[
            pl.BlockSpec((Z, ROWS, width), lambda j: (0, j, 0)),
            pl.BlockSpec((Z, ROWS, width), lambda j: (0, j, 0)),
            column_spec,
            column_spec,
            row_spec,
            row_spec,
        ],
        out_shape=[
            jax.ShapeDtypeStruct((Z, height, width), f32),
            jax.ShapeDtypeStruct((Z, height, width), bf16),
            column,
            column,
            row,
            row,
        ],
        input_output_aliases={first_edge + n: 2 + n for n in range(len(edges))},
        scratch_shapes=[
            pltpu.VMEM((Z, height, width), bf16),
            pltpu.VMEM((Z, ROWS, width), bf16),
        ],
        compiler_params=params(),
        cost_estimate=takes(5),
        name="make_adjoint",
    )(me, *parts, cotangent, *edges, *after)


def pick_row(rows, n):
    index = lax.broadcasted_iota(jnp.int32, rows.shape, 0)
    return jnp.sum(jnp.where(index == n, rows.astype(f32), 0.0), axis=0, keepdims=True)


def with_end_rows(slope, low, high):
    height, width = slope.shape
    row = lax.broadcasted_iota(jnp.int32, (8, width), 0)
    top = slope[:8] - jnp.where(row == 0, low, 0.0)
    bottom = slope[height - 8 :] + jnp.where(row == 7, high, 0.0)
    return jnp.concatenate([top, slope[8 : height - 8], bottom], axis=0)


LAYERS = 8


def grad_vort_kernel(
    component,
    slope_x,
    slope_y,
    velocity,
    velocity_above,
    velocity_below,
    adjoint,
    low_x,
    high_x,
    low_y,
    high_y,
    *refs,
):
    before, after = refs
    height, width = velocity.shape[2], velocity.shape[3]
    factor = 0.5 * step_size
    first = pl.program_id(0) * LAYERS
    ends = spread_columns(
        low_x[0].astype(f32) * step_size, high_x[0].astype(f32) * step_size, first, LAYERS, width
    )
    layers = velocity[0]
    stacked = layers.reshape(LAYERS * height, width)
    deep = [velocity_below[0, 0]] + [layers[k] for k in range(LAYERS)] + [velocity_above[0, 0]]
    inner = jnp.dot(stacked, slope_x[...], preferred_element_type=f32)
    for k in range(LAYERS):
        n = first + k
        value = adjoint[k]
        along_x = inner[k * height : (k + 1) * height] + ends[k]
        along_y = jnp.dot(slope_y[...], layers[k], preferred_element_type=f32)
        along_y = with_end_rows(
            along_y, pick_row(low_y[0], n) * factor, pick_row(high_y[0], n) * factor
        )
        along_z = (deep[k + 2].astype(f32) - deep[k].astype(f32)) * factor
        for j, slope in enumerate((along_x, along_y, along_z)):
            term = value * slope
            if j == component:
                term = term + value
            if before is not None:
                term = before[j, k].astype(f32) + term
            after[j, k] = term.astype(after.dtype)


def add_grad_vort(component, slopes, velocity, adjoint, halos, before, after, kind):
    _, _, height, width = velocity.shape
    slope_x, slope_y = slopes
    whole = lambda shape: pl.BlockSpec(shape, lambda n: (0,) * len(shape))
    column = pl.BlockSpec((1, Z, height), lambda n: (component, 0, 0))
    row = pl.BlockSpec((1, Z, width), lambda n: (component, 0, 0))
    sums = pl.BlockSpec((3, LAYERS, height, width), lambda n: (0, n, 0, 0))
    layer_above = lambda n: lax.rem((n + 1) * LAYERS, Z)
    layer_below = lambda n: lax.rem(n * LAYERS + Z - 1, Z)
    operands = [slope_x, slope_y, velocity, velocity, velocity, adjoint, *halos]
    in_specs = [
        whole((width, width)),
        whole((height, height)),
        pl.BlockSpec((1, LAYERS, height, width), lambda n: (component, n, 0, 0)),
        pl.BlockSpec((1, 1, height, width), lambda n: (component, layer_above(n), 0, 0)),
        pl.BlockSpec((1, 1, height, width), lambda n: (component, layer_below(n), 0, 0)),
        pl.BlockSpec((LAYERS, height, width), lambda n: (n, 0, 0)),
        column,
        column,
        row,
        row,
    ]
    if before is not None:
        operands.append(before)
        in_specs.append(sums)

    def kernel(*refs):
        grad_vort_kernel(component, *refs[:10], None if before is None else refs[10], refs[-1])

    return pl.pallas_call(
        kernel,
        grid=(Z // LAYERS,),
        in_specs=in_specs + tied(after),
        out_specs=sums,
        out_shape=jax.ShapeDtypeStruct((3, Z, height, width), kind),
        compiler_params=params(),
        cost_estimate=takes(9),
        name="add_grad_vort",
    )(*operands, *after)


def grad_vel_kernel(
    count, slope_x, slope_y, vorticity, vorticity_above, vorticity_below, *refs
):
    adjoints, edges = refs[: 3 * count], refs[3 * count :]
    vort_low_x, vort_high_x, vort_low_y, vort_high_y, low_x, high_x, low_y, high_y = edges[:8]
    after = refs[-1]
    _, _, height, width = vorticity.shape
    first = pl.program_id(0) * LAYERS
    factor = -0.5 * step_size

    def times(one, other):
        return one.astype(f32) * other.astype(f32)

    for c in range(count):
        here, above, below = adjoints[3 * c : 3 * c + 3]
        ends = spread_columns(
            times(vort_low_x[0], low_x[c]) * -step_size,
            times(vort_high_x[0], high_x[c]) * -step_size,
            first,
            LAYERS,
            width,
        )
        deep = [times(vorticity_below[0, 0], below[0])]
        along_x = []
        along_y = []
        for k in range(LAYERS):
            value = here[k].astype(f32)
            along_x.append((vorticity[0, k].astype(f32) * value).astype(bf16))
            along_y.append((vorticity[1, k].astype(f32) * value).astype(bf16))
            deep.append(vorticity[2, k].astype(f32) * value)
        deep.append(times(vorticity_above[0, 0], above[0]))
        along_x = jnp.dot(
            jnp.concatenate(along_x, axis=0), slope_x[...], preferred_element_type=f32
        )
        for k in range(LAYERS):
            n = first + k
            total = jnp.dot(slope_y[...], along_y[k], preferred_element_type=f32)
            total = total + along_x[k * height : (k + 1) * height] + ends[k]
            after[c, k] = total + (deep[k + 2] - deep[k]) * factor
            low = pick_row(vort_low_y[0], n) * pick_row(low_y[c], n)
            high = pick_row(vort_high_y[0], n) * pick_row(high_y[c], n)
            after[c, k, 0:1, :] = after[c, k, 0:1, :] - low * factor
            after[c, k, height - 1 : height, :] = (
                after[c, k, height - 1 : height, :] + high * factor
            )


def write_grad_vel(slopes, vorticity, adjoints, saved_halos, halos, after):
    _, _, height, width = vorticity.shape
    count = len(adjoints)
    whole = lambda shape: pl.BlockSpec(shape, lambda n: (0,) * len(shape))
    saved_column = pl.BlockSpec((1, Z, height), lambda n: (3, 0, 0))
    saved_row = pl.BlockSpec((1, Z, width), lambda n: (3, 0, 0))
    layer_above = lambda n: lax.rem((n + 1) * LAYERS, Z)
    layer_below = lambda n: lax.rem(n * LAYERS + Z - 1, Z)
    operands = [*slopes, vorticity, vorticity, vorticity]
    in_specs = [
        whole((width, width)),
        whole((height, height)),
        pl.BlockSpec((3, LAYERS, height, width), lambda n: (0, n, 0, 0)),
        pl.BlockSpec((1, 1, height, width), lambda n: (2, layer_above(n), 0, 0)),
        pl.BlockSpec((1, 1, height, width), lambda n: (2, layer_below(n), 0, 0)),
    ]
    for adjoint in adjoints:
        operands = operands + [adjoint] * 3
        in_specs = in_specs + [
            pl.BlockSpec((LAYERS, height, width), lambda n: (n, 0, 0)),
            pl.BlockSpec((1, height, width), lambda n: (layer_above(n), 0, 0)),
            pl.BlockSpec((1, height, width), lambda n: (layer_below(n), 0, 0)),
        ]
    operands = operands + list(saved_halos) + list(halos)
    in_specs = in_specs + [saved_column, saved_column, saved_row, saved_row]
    in_specs = in_specs + [whole((count, Z, height))] * 2 + [whole((count, Z, width))] * 2

    def kernel(*refs):
        grad_vel_kernel(count, *refs)

    return pl.pallas_call(
        kernel,
        grid=(Z // LAYERS,),
        in_specs=in_specs + tied(after),
        out_specs=pl.BlockSpec((count, LAYERS, height, width), lambda n: (0, n, 0, 0)),
        out_shape=jax.ShapeDtypeStruct((count, Z, height, width), f32),
        compiler_params=params(),
        cost_estimate=takes(12),
        name="write_grad_vel",
    )(*operands, *after)


def pair_exchange(parts, axis, mine):
    count = lax.axis_size(axis)
    kept = lax.dynamic_index_in_dim(parts, mine, 1, keepdims=False)
    sent = lax.dynamic_index_in_dim(parts, 1 - mine, 1, keepdims=False)
    got = lax.ppermute(sent, axis, [(i, i ^ 1) for i in range(count)])
    return jnp.where(mine == 0, jnp.stack([kept, got], 1), jnp.stack([got, kept], 1))


def shifted(parts, axis):
    count = lax.axis_size(axis)
    return [parts[0]] + [
        lax.ppermute(parts[s], axis, [(i, (i + s) % count) for i in range(count)])
        for s in range(1, count)
    ]


def local(cot_vort, cot_vel, vorticity, velocity):
    size_x = lax.axis_size("gx")
    size_y = lax.axis_size("gy")
    planes = Z // size_y
    halves = size_y // KZ
    _, _, height, width = cot_vel.shape
    modes = HALF_Y // (size_x * halves)
    place_x = lax.axis_index("gx")
    place_y = lax.axis_index("gy")
    half = lax.rem(place_y, halves)
    me = place_y.astype(jnp.int32).reshape(1)
    where = jnp.stack([(place_x * halves + half) * modes, place_y // halves]).astype(jnp.int32)

    y_table, y_back_table = y_tables(size_x * halves)
    x_table, x_back_table = x_tables()
    slopes = [slope_matrix(width), np.ascontiguousarray(slope_matrix(height).T)]
    slopes = [(slope * np.float32(step_size)).astype(slope.dtype) for slope in slopes]

    layers = depth_transform(cot_vel, FORWARD_ORDER[0])

    velocity_first, velocity_last = edge_columns(velocity, 3, (layers,))
    vorticity_first, vorticity_last = edge_columns(vorticity, 1, (layers,))
    low_x, high_x = exchange(
        jnp.concatenate([velocity_first, vorticity_first]),
        jnp.concatenate([velocity_last, vorticity_last]),
        "gx",
    )
    low_y, high_y = exchange(
        jnp.concatenate([velocity[:, :, 0], vorticity[1:2, :, 0]]),
        jnp.concatenate([velocity[:, :, height - 1], vorticity[1:2, :, height - 1]]),
        "gy",
    )
    saved_halos = (low_x, high_x, low_y, high_y)
    early = ((low_x, high_x), (low_y, high_y), ())

    columns = layers.reshape(size_y, planes, height, width)
    columns = lax.all_to_all(columns, "gy", 0, 0, tiled=True)
    sent = []
    for place in range(3):
        if place > 0:
            layers = depth_transform(cot_vel, FORWARD_ORDER[place], me, size_y, (sent[-1],))
            columns = shifted(layers, "gy")
        if place == 0:
            parts = y_transform(y_table, columns, size_x, halves, early[place])
        else:
            parts = y_transform_parts(me, y_table, columns, size_x, halves, early[place])
        parts = parts.reshape(size_x, 2, 2, modes, width)
        sent.append(parts if halves == 1 else pair_exchange(parts, "gy", half))

    def spectrum(place, after):
        lines = lax.all_to_all(sent[place], "gx", 0, 0, tiled=True)
        return x_transform(x_table, lines, after)

    def curl(component, after):
        return curl_inverse(where, x_back_table, spectra, component, size_x, after)

    def back(filtered):
        parts = lax.all_to_all(filtered, "gx", 0, 0, tiled=True)
        if halves == 2:
            parts = pair_exchange(parts, "gy", half)
        return parts.reshape(size_x, halves, planes, 2, modes, width)

    def rows_of(component, modes_back, after):
        if component == BACK_ORDER[2]:
            return [y_inverse(y_back_table, modes_back, size_y, after)]
        return y_inverse_parts(me, y_back_table, modes_back, size_y, after)

    def layers_of(rows):
        if len(rows) == 1:
            return [lax.all_to_all(rows[0], "gy", 0, 0, tiled=True).reshape(Z, height, width)]
        return shifted(rows, "gy")

    one, two, three = BACK_ORDER
    spectra = {FORWARD_ORDER[0]: spectrum(0, (sent[1],))}
    spectra[FORWARD_ORDER[1]] = spectrum(1, (sent[2],))
    curl_one = curl(one, ())
    spectra[FORWARD_ORDER[2]] = spectrum(2, (curl_one,))
    curl_two = curl(two, ())
    rows_one = rows_of(one, back(curl_one), (curl_two,))
    layers_one = layers_of(rows_one)
    curl_three = curl(three, tuple(layers_one))

    def vort_of(component, adjoint, before, after):
        kind = f32 if component == three else bf16
        return add_grad_vort(
            component, slopes, velocity, adjoint, saved_halos, before, after, kind
        )

    adjoint_one, short_one, *edges = make_adjoint(me, layers_one, cot_vort, one, [], ())
    rows_two = rows_of(two, back(curl_two), (adjoint_one,))
    layers_two = layers_of(rows_two)
    rows_three = rows_of(three, back(curl_three), tuple(layers_two))
    grad_vort = vort_of(one, adjoint_one, None, (rows_two[0],))
    adjoint_two, short_two, *edges = make_adjoint(
        me, layers_two, cot_vort, two, edges, (rows_three[0],)
    )
    grad_vort = vort_of(two, adjoint_two, grad_vort, ())
    adjoint_three, short_three, *edges = make_adjoint(
        me, layers_of(rows_three), cot_vort, three, edges, (grad_vort,)
    )
    halos = exchange(edges[0], edges[1], "gx") + exchange(edges[2], edges[3], "gy")
    grad_vort = vort_of(three, adjoint_three, grad_vort, ())
    shorts = {one: short_one, two: short_two, three: short_three}
    grad_vel = write_grad_vel(
        [-slope for slope in slopes], vorticity, [shorts[i] for i in range(3)], saved_halos, halos, (grad_vort,)
    )
    return grad_vort, grad_vel


def solution(mesh):
    spec = P(None, None, "gy", "gx")
    return jax.shard_map(
        local,
        mesh=mesh,
        in_specs=(spec, spec, spec, spec),
        out_specs=(spec, spec),
        check_vma=False,
    )
```

```python
import math

import jax
import jax.numpy as jnp
import ml_dtypes
import numpy as np
from jax import lax
from jax.experimental import pallas as pl
from jax.experimental.pallas import tpu as pltpu
from jax.sharding import PartitionSpec as P

X = 1024
Y = 1536
Z = 16
HALF_X = X // 2
HALF_Y = Y // 2
KZ = Z // 2

step_size = 0.5

f32 = jnp.float32
bf16 = jnp.bfloat16

FORWARD_ORDER = (0, 1, 2)
BACK_ORDER = (2, 0, 1)


def params(megabytes=56):
    return pltpu.CompilerParams(vmem_limit_bytes=megabytes * 1024 * 1024)


def takes(microseconds):
    return pl.CostEstimate(flops=1, bytes_accessed=int(microseconds * 3.0e6), transcendentals=0)


def tied(after):
    return [pl.BlockSpec(memory_space=pl.ANY)] * len(after)


def trig(first, second, length):
    angle = (np.outer(first, second) % length) * (2.0 * math.pi / length)
    return np.cos(angle), np.sin(angle)


def y_tables(blocks):
    cosine, sine = trig(np.arange(HALF_Y), np.arange(Y), Y)
    both = np.stack([cosine.reshape(blocks, -1, Y), sine.reshape(blocks, -1, Y)], 1).reshape(Y, Y)
    both = both.astype(ml_dtypes.bfloat16)
    return both, np.ascontiguousarray(both.T)


def x_tables():
    cosine, sine = trig(np.arange(X), np.arange(HALF_X), X)
    both = np.concatenate([cosine, sine], 1).astype(ml_dtypes.bfloat16)
    return both, np.ascontiguousarray(both.T)


def slope_matrix(size):
    return ((np.eye(size, k=-1) - np.eye(size, k=1)) * 0.5).astype(ml_dtypes.bfloat16)


def combine(terms):
    total = None
    for factor, value in terms:
        if abs(factor) < 1e-12:
            continue
        if abs(factor - 1.0) < 1e-12:
            part = value
        elif abs(factor + 1.0) < 1e-12:
            part = -value
        else:
            part = value * factor
        total = part if total is None else total + part
    return total


def depth_forward(values):
    even = [values[0]] + [values[n] + values[Z - n] for n in range(1, 8)] + [values[8]]
    odd = [None] + [values[n] - values[Z - n] for n in range(1, 8)]
    even_sum = [even[n] + even[8 - n] for n in range(4)] + [even[4]]
    even_dif = [even[n] - even[8 - n] for n in range(4)]
    odd_sum = [None] + [odd[n] + odd[8 - n] for n in range(1, 4)] + [odd[4]]
    odd_dif = [None] + [odd[n] - odd[8 - n] for n in range(1, 4)]
    result = []
    for k in range(KZ):
        folded = even_sum if k % 2 == 0 else even_dif
        cos_part = combine([(math.cos(math.pi * k * n / 8), folded[n]) for n in range(len(folded))])
        folded = odd_dif if k % 2 == 0 else odd_sum
        sin_part = combine(
            [(math.sin(math.pi * k * n / 8), folded[n]) for n in range(1, len(folded))]
        )
        result.append((cos_part, sin_part))
    return result


def depth_inverse(cos_parts, sin_parts):
    layers = [None] * Z
    cos_sum, sin_sum = [None] * 9, [None] * 9
    for n in range(5):
        evens = combine([(math.cos(math.pi * k * n / 8), cos_parts[k]) for k in range(0, KZ, 2)])
        odds = combine([(math.cos(math.pi * k * n / 8), cos_parts[k]) for k in range(1, KZ, 2)])
        if n == 4:
            cos_sum[4] = evens
        else:
            cos_sum[n] = evens + odds
            cos_sum[8 - n] = evens - odds
    for n in range(1, 5):
        evens = combine([(math.sin(math.pi * k * n / 8), sin_parts[k]) for k in range(0, KZ, 2)])
        odds = combine([(math.sin(math.pi * k * n / 8), sin_parts[k]) for k in range(1, KZ, 2)])
        if n == 4:
            sin_sum[4] = odds
        else:
            sin_sum[n] = odds + evens
            sin_sum[8 - n] = odds - evens
    layers[0], layers[8] = cos_sum[0], cos_sum[8]
    for n in range(1, 8):
        layers[n] = cos_sum[n] + sin_sum[n]
        layers[Z - n] = cos_sum[n] - sin_sum[n]
    return layers


ROWS = 96


def tiles(height, width):
    for row in range(0, height, 16):
        for column in range(0, width, 128):
            yield row, pl.ds(row, 16), pl.ds(column, 128)


def depth_forward_kernel(values_ref, planes_ref):
    _, _, height, width = values_ref.shape
    for _, rows, columns in tiles(height, width):
        spectrum = depth_forward([values_ref[0, n, rows, columns] for n in range(Z)])
        for k, (cos_part, sin_part) in enumerate(spectrum):
            planes_ref[2 * k, rows, columns] = cos_part.astype(bf16)
            if sin_part is None:
                sin_part = jnp.zeros_like(cos_part)
            planes_ref[2 * k + 1, rows, columns] = sin_part.astype(bf16)


def depth_transform(values, component, me=None, size_y=1, after=()):
    _, _, height, width = values.shape
    planes = Z // size_y
    shifted_out = me is not None

    def kernel(*refs):
        if not shifted_out:
            depth_forward_kernel(*refs)
            return
        me_ref, values_ref, outs, held = refs[0], refs[1], refs[2 + len(after) : -1], refs[-1]
        depth_forward_kernel(values_ref, held)
        for s, out in enumerate(outs):
            target = lax.rem(me_ref[0] + s, size_y)
            out[...] = held[pl.ds(target * planes, planes)]

    block = (Z // size_y, ROWS, width)
    out_spec = pl.BlockSpec(block, lambda j: (0, j, 0))
    out_shape = jax.ShapeDtypeStruct((planes, height, width), bf16)
    smem = pl.BlockSpec(memory_space=pltpu.SMEM)
    return pl.pallas_call(
        kernel,
        grid=(height // ROWS,),
        in_specs=([smem] if shifted_out else [])
        + [pl.BlockSpec((1, Z, ROWS, width), lambda j: (component, 0, j, 0))]
        + tied(after),
        out_specs=[out_spec] * size_y if shifted_out else out_spec,
        out_shape=[out_shape] * size_y if shifted_out else out_shape,
        scratch_shapes=[pltpu.VMEM((Z, ROWS, width), bf16)] if shifted_out else [],
        compiler_params=params(),
        cost_estimate=takes(3),
        name="depth_transform",
    )(*(([me] if shifted_out else []) + [values, *after]))


def fetch_blocks(table_ref, held, arrived, order):
    count, rows, _ = held.shape
    copies = []
    for s in range(count):
        place = pl.ds(pl.multiple_of(order(s) * rows, rows), rows)
        copies.append(pltpu.make_async_copy(table_ref.at[place], held.at[s], arrived.at[s]))
        copies[s].start()
    return copies


def y_transform(table, columns, blocks, halves, after):
    _, planes, _, width = columns.shape
    modes = HALF_Y // (blocks * halves)
    rows = Y // blocks

    def kernel(table_ref, columns_ref, *refs):
        out = refs[-1]
        for plane in range(planes):
            column = columns_ref[:, plane].reshape(Y, width)
            part = jnp.dot(table_ref[...], column, preferred_element_type=f32)
            out[0, :, plane] = part.astype(bf16).reshape(halves, 2, modes, width)

    return pl.pallas_call(
        kernel,
        grid=(blocks,),
        in_specs=[
            pl.BlockSpec((rows, Y), lambda j: (j, 0)),
            pl.BlockSpec(columns.shape, lambda j: (0, 0, 0, 0)),
        ]
        + tied(after),
        out_specs=pl.BlockSpec((1, halves, planes, 2, modes, width), lambda j: (j, 0, 0, 0, 0, 0)),
        out_shape=jax.ShapeDtypeStruct((blocks, halves, planes, 2, modes, width), bf16),
        compiler_params=params(24),
        cost_estimate=takes(4),
        name="y_transform",
    )(table, columns, *after)


def y_transform_parts(me, table, columns, blocks, halves, after):
    size_y = len(columns)
    planes, height, width = columns[0].shape[-3:]
    modes = HALF_Y // (blocks * halves)
    rows = Y // blocks
    shape = (blocks, halves, planes, 2, modes, width)

    def kernel(me_ref, table_ref, *refs):
        parts = refs[: len(columns)]
        out, held, lines, ready, table_in, lines_in, ready_out = refs[-7:]
        copies = []
        for s in range(size_y):
            source = lax.rem(me_ref[0] + size_y - s, size_y)
            place = pl.ds(pl.multiple_of(source * height, height), height)
            for plane in range(planes):
                copies.append(
                    pltpu.make_async_copy(
                        parts[s].at[plane],
                        lines.at[plane, place],
                        lines_in.at[s * planes + plane],
                    )
                )
                copies[-1].start()
        tables = fetch_blocks(table_ref, held, table_in, lambda s: s)
        for copy in copies:
            copy.wait()
        results = []
        for s in range(blocks):
            tables[s].wait()
            for plane in range(planes):
                part = jnp.dot(held[s], lines[plane], preferred_element_type=f32)
                ready[s, :, plane] = part.astype(bf16).reshape(halves, 2, modes, width)
            results.append(pltpu.make_async_copy(ready.at[s], out.at[s], ready_out.at[s]))
            results[s].start()
        for result in results:
            result.wait()

    anywhere = pl.BlockSpec(memory_space=pl.ANY)
    return pl.pallas_call(
        kernel,
        in_specs=[pl.BlockSpec(memory_space=pltpu.SMEM), anywhere]
        + [anywhere] * len(columns)
        + tied(after),
        out_specs=anywhere,
        out_shape=jax.ShapeDtypeStruct(shape, bf16),
        scratch_shapes=[
            pltpu.VMEM((blocks, rows, Y), bf16),
            pltpu.VMEM((planes, Y, width), bf16),
            pltpu.VMEM(shape, bf16),
            pltpu.SemaphoreType.DMA((blocks,)),
            pltpu.SemaphoreType.DMA((size_y * planes,)),
            pltpu.SemaphoreType.DMA((blocks,)),
        ],
        compiler_params=params(),
        cost_estimate=takes(5),
        name="y_transform_parts",
    )(me, table, *columns, *after)


def y_inverse(table, modes, size_y, after):
    planes, width = modes.shape[2], modes.shape[5]
    height = Y // size_y
    count = 384 // height

    def kernel(table_ref, modes_ref, *refs):
        out = refs[-1]
        for plane in range(planes):
            columns = modes_ref[:, :, plane].reshape(Y, width)
            rows = jnp.dot(table_ref[...], columns, preferred_element_type=f32)
            out[:, plane] = rows.astype(bf16).reshape(count, height, width)

    return pl.pallas_call(
        kernel,
        grid=(size_y // count,),
        in_specs=[
            pl.BlockSpec((count * height, Y), lambda j: (j, 0)),
            pl.BlockSpec(modes.shape, lambda j: (0, 0, 0, 0, 0, 0)),
        ]
        + tied(after),
        out_specs=pl.BlockSpec((count, planes, height, width), lambda j: (j, 0, 0, 0)),
        out_shape=jax.ShapeDtypeStruct((size_y, planes, height, width), bf16),
        compiler_params=params(24),
        cost_estimate=takes(4),
        name="y_inverse",
    )(table, modes, *after)


def y_inverse_parts(me, table, modes, size_y, after):
    blocks, halves, planes, _, count, width = modes.shape
    height = Y // size_y
    shape = (planes, height, width)

    def kernel(me_ref, table_ref, modes_ref, *refs):
        outs = refs[len(after) : -6]
        held, lines, ready, table_in, lines_in, ready_out = refs[-6:]
        copies = []
        for block in range(blocks):
            for h in range(halves):
                for plane in range(planes):
                    copies.append(
                        pltpu.make_async_copy(
                            modes_ref.at[block, h, plane],
                            lines.at[plane, block, h],
                            lines_in.at[(block * halves + h) * planes + plane],
                        )
                    )
                    copies[-1].start()
        tables = fetch_blocks(
            table_ref, held, table_in, lambda s: lax.rem(me_ref[0] + s, size_y)
        )
        for copy in copies:
            copy.wait()
        results = []
        for s in range(size_y):
            tables[s].wait()
            for plane in range(planes):
                columns = lines[plane].reshape(Y, width)
                rows = jnp.dot(held[s], columns, preferred_element_type=f32)
                ready[s, plane] = rows.astype(bf16)
            results.append(pltpu.make_async_copy(ready.at[s], outs[s], ready_out.at[s]))
            results[s].start()
        for result in results:
            result.wait()

    anywhere = pl.BlockSpec(memory_space=pl.ANY)
    out_shape = [jax.ShapeDtypeStruct(shape, bf16)] * size_y
    return pl.pallas_call(
        kernel,
        in_specs=[pl.BlockSpec(memory_space=pltpu.SMEM), anywhere, anywhere] + tied(after),
        out_specs=[anywhere] * len(out_shape),
        out_shape=out_shape,
        scratch_shapes=[
            pltpu.VMEM((size_y, height, Y), bf16),
            pltpu.VMEM((planes, blocks, halves, 2, count, width), bf16),
            pltpu.VMEM((size_y,) + shape, bf16),
            pltpu.SemaphoreType.DMA((size_y,)),
            pltpu.SemaphoreType.DMA((blocks * halves * planes,)),
            pltpu.SemaphoreType.DMA((size_y,)),
        ],
        compiler_params=params(),
        cost_estimate=takes(4),
        name="y_inverse_parts",
    )(me, table, modes, *after)


def x_transform(table, modes, after):
    blocks, _, _, count, width = modes.shape

    def kernel(table_ref, modes_ref, *refs):
        spectrum_ref = refs[-1]
        rows = jnp.concatenate(
            [modes_ref[block, 0].reshape(2 * count, width) for block in range(blocks)], axis=1
        )
        spectrum = jnp.dot(rows, table_ref[...], preferred_element_type=f32)
        spectrum_ref[0] = spectrum.reshape(2, count, X)

    return pl.pallas_call(
        kernel,
        grid=(2,),
        in_specs=[
            pl.BlockSpec((X, X), lambda j: (0, 0)),
            pl.BlockSpec((blocks, 1, 2, count, width), lambda j: (0, j, 0, 0, 0)),
        ]
        + tied(after),
        out_specs=pl.BlockSpec((1, 2, count, X), lambda j: (j, 0, 0, 0)),
        out_shape=jax.ShapeDtypeStruct((2, 2, count, X), f32),
        compiler_params=params(24),
        cost_estimate=takes(3),
        name="x_transform",
    )(table, modes, *after)


def turned(field, axis, tz, ty, tx, wave):
    index = [tz, ty, tx]
    sign = 1.0 if index[axis] == 0 else -1.0
    index[axis] = 1 - index[axis]
    value = field[index[0], index[1], :, index[2] * HALF_X : (index[2] + 1) * HALF_X]
    return value * (wave * sign)


CURL = {
    0: ((1, 2), (0, 1)),
    1: ((0, 0), (2, 2)),
    2: ((2, 1), (1, 0)),
}


def curl_kernel(axes, where_ref, table_ref, plus_ref, minus_ref, back_ref):
    blocks, _, _, count, width = back_ref.shape
    base = where_ref[0] + pl.program_id(0) * count
    depth = where_ref[1]
    mode_y = lax.broadcasted_iota(jnp.int32, (count, HALF_X), 0) + base
    mode_x = lax.broadcasted_iota(jnp.int32, (count, HALF_X), 1)
    wave_y = mode_y.astype(f32) * (2.0 * math.pi / Y)
    wave_x = mode_x.astype(f32) * (2.0 * math.pi / X)
    wave_z = jnp.full((count, HALF_X), depth, jnp.int32).astype(f32) * (2.0 * math.pi / Z)
    square = wave_x * wave_x + wave_y * wave_y + wave_z * wave_z
    doubling = (
        jnp.where(mode_x == 0, 1.0, 2.0)
        * jnp.where(mode_y == 0, 1.0, 2.0)
        * jnp.where(wave_z == 0.0, 1.0, 2.0)
    )
    weight = jnp.where(square > 0, doubling / jnp.where(square > 0, square, 1.0), 0.0)
    waves = [wave_z * weight, wave_y * weight, wave_x * weight]
    rows = []
    for tz in range(2):
        for ty in range(2):
            parts = []
            for tx in range(2):
                parts.append(
                    (
                        turned(plus_ref, axes[0], tz, ty, tx, waves[axes[0]])
                        - turned(minus_ref, axes[1], tz, ty, tx, waves[axes[1]])
                    ).astype(bf16)
                )
            rows.append(jnp.concatenate(parts, axis=1))
    rows = jnp.concatenate(rows, axis=0)
    back = jnp.dot(rows, table_ref[...], preferred_element_type=f32).astype(bf16)
    for block in range(blocks):
        back_ref[block] = back[:, block * width : (block + 1) * width].reshape(2, 2, count, width)


def curl_inverse(where, table, spectra, component, blocks, after):
    (plus_axis, plus), (minus_axis, minus) = CURL[component]
    total = spectra[plus].shape[2]
    width = X // blocks
    count = 96 if total % 96 == 0 else total
    spec = pl.BlockSpec((2, 2, count, X), lambda j: (0, 0, j, 0))

    def kernel(*refs):
        curl_kernel((plus_axis, minus_axis), *refs[:4], refs[-1])

    return pl.pallas_call(
        kernel,
        grid=(total // count,),
        in_specs=[
            pl.BlockSpec(memory_space=pltpu.SMEM),
            pl.BlockSpec((X, X), lambda j: (0, 0)),
            spec,
            spec,
        ]
        + tied(after),
        out_specs=pl.BlockSpec((blocks, 2, 2, count, width), lambda j: (0, 0, 0, j, 0)),
        out_shape=jax.ShapeDtypeStruct((blocks, 2, 2, total, width), bf16),
        compiler_params=params(24),
        cost_estimate=takes(4),
        name="curl_inverse",
    )(where, table, spectra[plus], spectra[minus], *after)


def side_columns(planes):
    width = planes[0].shape[1]
    row = lax.broadcasted_iota(jnp.int32, (2 * Z, width), 0)
    lane = lax.broadcasted_iota(jnp.int32, (2 * Z, width), 1)
    total = None
    for n in range(Z):
        pick = ((row == n) & (lane == 0)) | ((row == n + Z) & (lane == width - 1))
        part = lax.dot_general(
            pick.astype(f32).astype(bf16),
            planes[n],
            (((1,), (1,)), ((), ())),
            preferred_element_type=f32,
        )
        total = part if total is None else total + part
    return total[:Z].astype(bf16), total[Z:].astype(bf16)


def spread_columns(low, high, first, layers, width):
    row = lax.broadcasted_iota(jnp.int32, (2 * Z, layers * width), 0)
    column = lax.broadcasted_iota(jnp.int32, (2 * Z, layers * width), 1)
    place = jnp.zeros((2 * Z, layers * width), f32)
    for n in range(layers):
        place = place + jnp.where((row == first + n) & (column == n * width), -0.5, 0.0)
        place = place + jnp.where(
            (row == first + n + Z) & (column == (n + 1) * width - 1), 0.5, 0.0
        )
    both = jnp.concatenate([low, high], axis=0).astype(bf16)
    spread = lax.dot_general(
        both, place.astype(bf16), (((0,), (0,)), ((), ())), preferred_element_type=f32
    )
    return [spread[:, n * width : (n + 1) * width] for n in range(layers)]


def edges_kernel(field_ref, *refs):
    first_column_ref, last_column_ref = refs[-2:]
    first, last = side_columns([field_ref[0, n] for n in range(Z)])
    first_column_ref[0] = first
    last_column_ref[0] = last


def edge_columns(field, components, after):
    _, _, height, width = field.shape
    shape = jax.ShapeDtypeStruct((components, Z, height), bf16)
    spec = pl.BlockSpec((1, Z, height), lambda i: (i, 0, 0))
    return pl.pallas_call(
        edges_kernel,
        grid=(components,),
        in_specs=[pl.BlockSpec((1, Z, height, width), lambda i: (i, 0, 0, 0))] + tied(after),
        out_specs=[spec, spec],
        out_shape=[shape, shape],
        compiler_params=params(),
        cost_estimate=takes(4),
        name="edge_columns",
    )(field, *after)


def exchange(first, last, axis):
    count = lax.axis_size(axis)
    up = [(i, (i + 1) % count) for i in range(count)]
    down = [((i + 1) % count, i) for i in range(count)]
    return lax.ppermute(last, axis, up), lax.ppermute(first, axis, down)


def adjoint_kernel(planes_ref, cotangent_ref, *refs):
    adjoint_ref, short_ref, first_x, last_x, first_y, last_y, held = refs
    _, height, width = held.shape
    scale = 1.0 / (X * Y * Z)
    base = pl.program_id(0) * ROWS
    for row, rows, columns in tiles(ROWS, width):
        place = pl.ds(pl.multiple_of(base + row, 16), 16)
        layers = depth_inverse(
            [planes_ref[2 * k, rows, columns].astype(f32) for k in range(KZ)],
            [planes_ref[2 * k + 1, rows, columns].astype(f32) for k in range(KZ)],
        )
        for n in range(Z):
            value = cotangent_ref[0, n, rows, columns] + layers[n] * scale
            adjoint_ref[n, rows, columns] = value
            short_ref[n, rows, columns] = value.astype(bf16)
            held[n, place, columns] = value.astype(bf16)

    @pl.when(pl.program_id(0) == pl.num_programs(0) - 1)
    def _():
        first, last = side_columns([held[n] for n in range(Z)])
        first_x[0] = first
        last_x[0] = last
        top = [held[n, 0:16, :].astype(f32)[0:1] for n in range(Z)]
        bottom = [held[n, height - 16 : height, :].astype(f32)[15:16] for n in range(Z)]
        first_y[0] = jnp.concatenate(top, 0).astype(bf16)
        last_y[0] = jnp.concatenate(bottom, 0).astype(bf16)


def make_adjoint(me, parts, cotangent, component, edges, after):
    whole = len(parts) == 1
    planes, height, width = parts[0].shape
    column = jax.ShapeDtypeStruct((3, Z, height), bf16)
    row = jax.ShapeDtypeStruct((3, Z, width), bf16)
    column_spec = pl.BlockSpec((1, Z, height), lambda j: (component, 0, 0))
    row_spec = pl.BlockSpec((1, Z, width), lambda j: (component, 0, 0))
    first_edge = 2 + len(parts)

    def kernel(me_ref, *refs):
        part_refs, cotangent_ref = refs[: len(parts)], refs[len(parts)]
        outs, held, spectrum = refs[-8:-2], refs[-2], refs[-1]
        if whole:
            spectrum = part_refs[0]
        else:
            for s, part in enumerate(part_refs):
                source = lax.rem(me_ref[0] + len(parts) - s, len(parts))
                spectrum[pl.ds(source * planes, planes)] = part[...]
        adjoint_kernel(spectrum, cotangent_ref, *outs, held)

    return pl.pallas_call(
        kernel,
        grid=(height // ROWS,),
        in_specs=[pl.BlockSpec(memory_space=pltpu.SMEM)]
        + [pl.BlockSpec((planes, ROWS, width), lambda j: (0, j, 0))] * len(parts)
        + [pl.BlockSpec((1, Z, ROWS, width), lambda j: (component, 0, j, 0))]
        + tied(edges)
        + tied(after),
        out_specs=[
            pl.BlockSpec((Z, ROWS, width), lambda j: (0, j, 0)),
            pl.BlockSpec((Z, ROWS, width), lambda j: (0, j, 0)),
            column_spec,
            column_spec,
            row_spec,
            row_spec,
        ],
        out_shape=[
            jax.ShapeDtypeStruct((Z, height, width), f32),
            jax.ShapeDtypeStruct((Z, height, width), bf16),
            column,
            column,
            row,
            row,
        ],
        input_output_aliases={first_edge + n: 2 + n for n in range(len(edges))},
        scratch_shapes=[
            pltpu.VMEM((Z, height, width), bf16),
            pltpu.VMEM((Z, ROWS, width), bf16),
        ],
        compiler_params=params(),
        cost_estimate=takes(5),
        name="make_adjoint",
    )(me, *parts, cotangent, *edges, *after)


def pick_row(rows, n):
    index = lax.broadcasted_iota(jnp.int32, rows.shape, 0)
    return jnp.sum(jnp.where(index == n, rows.astype(f32), 0.0), axis=0, keepdims=True)


def with_end_rows(slope, low, high):
    height, width = slope.shape
    row = lax.broadcasted_iota(jnp.int32, (8, width), 0)
    top = slope[:8] - jnp.where(row == 0, low, 0.0)
    bottom = slope[height - 8 :] + jnp.where(row == 7, high, 0.0)
    return jnp.concatenate([top, slope[8 : height - 8], bottom], axis=0)


LAYERS = 8


def grad_vort_kernel(
    component,
    slope_x,
    slope_y,
    velocity,
    velocity_above,
    velocity_below,
    adjoint,
    low_x,
    high_x,
    low_y,
    high_y,
    *refs,
):
    before, after = refs
    height, width = velocity.shape[2], velocity.shape[3]
    factor = 0.5 * step_size
    first = pl.program_id(0) * LAYERS
    ends = spread_columns(
        low_x[0].astype(f32) * step_size, high_x[0].astype(f32) * step_size, first, LAYERS, width
    )
    layers = velocity[0]
    stacked = layers.reshape(LAYERS * height, width)
    deep = [velocity_below[0, 0]] + [layers[k] for k in range(LAYERS)] + [velocity_above[0, 0]]
    inner = jnp.dot(stacked, slope_x[...], preferred_element_type=f32)
    for k in range(LAYERS):
        n = first + k
        value = adjoint[k]
        along_x = inner[k * height : (k + 1) * height] + ends[k]
        along_y = jnp.dot(slope_y[...], layers[k], preferred_element_type=f32)
        along_y = with_end_rows(
            along_y, pick_row(low_y[0], n) * factor, pick_row(high_y[0], n) * factor
        )
        along_z = (deep[k + 2].astype(f32) - deep[k].astype(f32)) * factor
        for j, slope in enumerate((along_x, along_y, along_z)):
            term = value * slope
            if j == component:
                term = term + value
            if before is not None:
                term = before[j, k].astype(f32) + term
            after[j, k] = term.astype(after.dtype)


def add_grad_vort(component, slopes, velocity, adjoint, halos, before, after, kind):
    _, _, height, width = velocity.shape
    slope_x, slope_y = slopes
    whole = lambda shape: pl.BlockSpec(shape, lambda n: (0,) * len(shape))
    column = pl.BlockSpec((1, Z, height), lambda n: (component, 0, 0))
    row = pl.BlockSpec((1, Z, width), lambda n: (component, 0, 0))
    sums = pl.BlockSpec((3, LAYERS, height, width), lambda n: (0, n, 0, 0))
    layer_above = lambda n: lax.rem((n + 1) * LAYERS, Z)
    layer_below = lambda n: lax.rem(n * LAYERS + Z - 1, Z)
    operands = [slope_x, slope_y, velocity, velocity, velocity, adjoint, *halos]
    in_specs = [
        whole((width, width)),
        whole((height, height)),
        pl.BlockSpec((1, LAYERS, height, width), lambda n: (component, n, 0, 0)),
        pl.BlockSpec((1, 1, height, width), lambda n: (component, layer_above(n), 0, 0)),
        pl.BlockSpec((1, 1, height, width), lambda n: (component, layer_below(n), 0, 0)),
        pl.BlockSpec((LAYERS, height, width), lambda n: (n, 0, 0)),
        column,
        column,
        row,
        row,
    ]
    if before is not None:
        operands.append(before)
        in_specs.append(sums)

    def kernel(*refs):
        grad_vort_kernel(component, *refs[:10], None if before is None else refs[10], refs[-1])

    return pl.pallas_call(
        kernel,
        grid=(Z // LAYERS,),
        in_specs=in_specs + tied(after),
        out_specs=sums,
        out_shape=jax.ShapeDtypeStruct((3, Z, height, width), kind),
        compiler_params=params(),
        cost_estimate=takes(9),
        name="add_grad_vort",
    )(*operands, *after)


def grad_vel_kernel(
    count, slope_x, slope_y, vorticity, vorticity_above, vorticity_below, *refs
):
    adjoints, edges = refs[: 3 * count], refs[3 * count :]
    vort_low_x, vort_high_x, vort_low_y, vort_high_y, low_x, high_x, low_y, high_y = edges[:8]
    after = refs[-1]
    _, _, height, width = vorticity.shape
    first = pl.program_id(0) * LAYERS
    factor = -0.5 * step_size

    def times(one, other):
        return one.astype(f32) * other.astype(f32)

    for c in range(count):
        here, above, below = adjoints[3 * c : 3 * c + 3]
        ends = spread_columns(
            times(vort_low_x[0], low_x[c]) * -step_size,
            times(vort_high_x[0], high_x[c]) * -step_size,
            first,
            LAYERS,
            width,
        )
        deep = [times(vorticity_below[0, 0], below[0])]
        along_x = []
        along_y = []
        for k in range(LAYERS):
            value = here[k].astype(f32)
            along_x.append((vorticity[0, k].astype(f32) * value).astype(bf16))
            along_y.append((vorticity[1, k].astype(f32) * value).astype(bf16))
            deep.append(vorticity[2, k].astype(f32) * value)
        deep.append(times(vorticity_above[0, 0], above[0]))
        along_x = jnp.dot(
            jnp.concatenate(along_x, axis=0), slope_x[...], preferred_element_type=f32
        )
        for k in range(LAYERS):
            n = first + k
            total = jnp.dot(slope_y[...], along_y[k], preferred_element_type=f32)
            total = total + along_x[k * height : (k + 1) * height] + ends[k]
            after[c, k] = total + (deep[k + 2] - deep[k]) * factor
            low = pick_row(vort_low_y[0], n) * pick_row(low_y[c], n)
            high = pick_row(vort_high_y[0], n) * pick_row(high_y[c], n)
            after[c, k, 0:1, :] = after[c, k, 0:1, :] - low * factor
            after[c, k, height - 1 : height, :] = (
                after[c, k, height - 1 : height, :] + high * factor
            )


def write_grad_vel(slopes, vorticity, adjoints, saved_halos, halos, after):
    _, _, height, width = vorticity.shape
    count = len(adjoints)
    whole = lambda shape: pl.BlockSpec(shape, lambda n: (0,) * len(shape))
    saved_column = pl.BlockSpec((1, Z, height), lambda n: (3, 0, 0))
    saved_row = pl.BlockSpec((1, Z, width), lambda n: (3, 0, 0))
    layer_above = lambda n: lax.rem((n + 1) * LAYERS, Z)
    layer_below = lambda n: lax.rem(n * LAYERS + Z - 1, Z)
    operands = [*slopes, vorticity, vorticity, vorticity]
    in_specs = [
        whole((width, width)),
        whole((height, height)),
        pl.BlockSpec((3, LAYERS, height, width), lambda n: (0, n, 0, 0)),
        pl.BlockSpec((1, 1, height, width), lambda n: (2, layer_above(n), 0, 0)),
        pl.BlockSpec((1, 1, height, width), lambda n: (2, layer_below(n), 0, 0)),
    ]
    for adjoint in adjoints:
        operands = operands + [adjoint] * 3
        in_specs = in_specs + [
            pl.BlockSpec((LAYERS, height, width), lambda n: (n, 0, 0)),
            pl.BlockSpec((1, height, width), lambda n: (layer_above(n), 0, 0)),
            pl.BlockSpec((1, height, width), lambda n: (layer_below(n), 0, 0)),
        ]
    operands = operands + list(saved_halos) + list(halos)
    in_specs = in_specs + [saved_column, saved_column, saved_row, saved_row]
    in_specs = in_specs + [whole((count, Z, height))] * 2 + [whole((count, Z, width))] * 2

    def kernel(*refs):
        grad_vel_kernel(count, *refs)

    return pl.pallas_call(
        kernel,
        grid=(Z // LAYERS,),
        in_specs=in_specs + tied(after),
        out_specs=pl.BlockSpec((count, LAYERS, height, width), lambda n: (0, n, 0, 0)),
        out_shape=jax.ShapeDtypeStruct((count, Z, height, width), f32),
        compiler_params=params(),
        cost_estimate=takes(12),
        name="write_grad_vel",
    )(*operands, *after)


def pair_exchange(parts, axis, mine):
    count = lax.axis_size(axis)
    kept = lax.dynamic_index_in_dim(parts, mine, 1, keepdims=False)
    sent = lax.dynamic_index_in_dim(parts, 1 - mine, 1, keepdims=False)
    got = lax.ppermute(sent, axis, [(i, i ^ 1) for i in range(count)])
    return jnp.where(mine == 0, jnp.stack([kept, got], 1), jnp.stack([got, kept], 1))


def shifted(parts, axis):
    count = lax.axis_size(axis)
    return [parts[0]] + [
        lax.ppermute(parts[s], axis, [(i, (i + s) % count) for i in range(count)])
        for s in range(1, count)
    ]


def local(cot_vort, cot_vel, vorticity, velocity):
    size_x = lax.axis_size("gx")
    size_y = lax.axis_size("gy")
    planes = Z // size_y
    halves = size_y // KZ
    _, _, height, width = cot_vel.shape
    modes = HALF_Y // (size_x * halves)
    place_x = lax.axis_index("gx")
    place_y = lax.axis_index("gy")
    half = lax.rem(place_y, halves)
    me = place_y.astype(jnp.int32).reshape(1)
    where = jnp.stack([(place_x * halves + half) * modes, place_y // halves]).astype(jnp.int32)

    y_table, y_back_table = y_tables(size_x * halves)
    x_table, x_back_table = x_tables()
    slopes = [slope_matrix(width), np.ascontiguousarray(slope_matrix(height).T)]
    slopes = [(slope * np.float32(step_size)).astype(slope.dtype) for slope in slopes]

    layers = depth_transform(cot_vel, FORWARD_ORDER[0])

    velocity_first, velocity_last = edge_columns(velocity, 3, (layers,))
    vorticity_first, vorticity_last = edge_columns(vorticity, 1, (layers,))
    low_x, high_x = exchange(
        jnp.concatenate([velocity_first, vorticity_first]),
        jnp.concatenate([velocity_last, vorticity_last]),
        "gx",
    )
    low_y, high_y = exchange(
        jnp.concatenate([velocity[:, :, 0], vorticity[1:2, :, 0]]),
        jnp.concatenate([velocity[:, :, height - 1], vorticity[1:2, :, height - 1]]),
        "gy",
    )
    saved_halos = (low_x, high_x, low_y, high_y)
    early = ((low_x, high_x), (low_y, high_y), ())

    columns = layers.reshape(size_y, planes, height, width)
    columns = lax.all_to_all(columns, "gy", 0, 0, tiled=True)
    sent = []
    for place in range(3):
        if place > 0:
            layers = depth_transform(cot_vel, FORWARD_ORDER[place], me, size_y, (sent[-1],))
            columns = shifted(layers, "gy")
        if place == 0:
            parts = y_transform(y_table, columns, size_x, halves, early[place])
        else:
            parts = y_transform_parts(me, y_table, columns, size_x, halves, early[place])
        parts = parts.reshape(size_x, 2, 2, modes, width)
        sent.append(parts if halves == 1 else pair_exchange(parts, "gy", half))

    def spectrum(place, after):
        lines = lax.all_to_all(sent[place], "gx", 0, 0, tiled=True)
        return x_transform(x_table, lines, after)

    def curl(component, after):
        return curl_inverse(where, x_back_table, spectra, component, size_x, after)

    def back(filtered):
        parts = lax.all_to_all(filtered, "gx", 0, 0, tiled=True)
        if halves == 2:
            parts = pair_exchange(parts, "gy", half)
        return parts.reshape(size_x, halves, planes, 2, modes, width)

    def rows_of(component, modes_back, after):
        if component == BACK_ORDER[2]:
            return [y_inverse(y_back_table, modes_back, size_y, after)]
        return y_inverse_parts(me, y_back_table, modes_back, size_y, after)

    def layers_of(rows):
        if len(rows) == 1:
            return [lax.all_to_all(rows[0], "gy", 0, 0, tiled=True).reshape(Z, height, width)]
        return shifted(rows, "gy")

    one, two, three = BACK_ORDER
    spectra = {FORWARD_ORDER[0]: spectrum(0, (sent[1],))}
    spectra[FORWARD_ORDER[1]] = spectrum(1, (sent[2],))
    curl_one = curl(one, ())
    spectra[FORWARD_ORDER[2]] = spectrum(2, (curl_one,))
    curl_two = curl(two, ())
    rows_one = rows_of(one, back(curl_one), (curl_two,))
    layers_one = layers_of(rows_one)
    curl_three = curl(three, tuple(layers_one))

    def vort_of(component, adjoint, before, after):
        kind = f32 if component == three else bf16
        return add_grad_vort(
            component, slopes, velocity, adjoint, saved_halos, before, after, kind
        )

    adjoint_one, short_one, *edges = make_adjoint(me, layers_one, cot_vort, one, [], ())
    rows_two = rows_of(two, back(curl_two), (adjoint_one,))
    layers_two = layers_of(rows_two)
    rows_three = rows_of(three, back(curl_three), tuple(layers_two))
    grad_vort = vort_of(one, adjoint_one, None, (rows_two[0],))
    adjoint_two, short_two, *edges = make_adjoint(
        me, layers_two, cot_vort, two, edges, (rows_three[0],)
    )
    grad_vort = vort_of(two, adjoint_two, grad_vort, ())
    adjoint_three, short_three, *edges = make_adjoint(
        me, layers_of(rows_three), cot_vort, three, edges, (grad_vort,)
    )
    halos = exchange(edges[0], edges[1], "gx") + exchange(edges[2], edges[3], "gy")
    grad_vort = vort_of(three, adjoint_three, grad_vort, ())
    shorts = {one: short_one, two: short_two, three: short_three}
    grad_vel = write_grad_vel(
        [-slope for slope in slopes], vorticity, [shorts[i] for i in range(3)], saved_halos, halos, (grad_vort,)
    )
    return grad_vort, grad_vel


def solution(mesh):
    spec = P(None, None, "gy", "gx")
    return jax.shard_map(
        local,
        mesh=mesh,
        in_specs=(spec, spec, spec, spec),
        out_specs=(spec, spec),
        check_vma=False,
    )
```

```python
import math

import jax
import jax.numpy as jnp
import ml_dtypes
import numpy as np
from jax import lax
from jax.experimental import pallas as pl
from jax.experimental.pallas import tpu as pltpu
from jax.sharding import PartitionSpec as P

X = 1024
Y = 1536
Z = 16
HALF_X = X // 2
HALF_Y = Y // 2
KZ = Z // 2

step_size = 0.5

f32 = jnp.float32
bf16 = jnp.bfloat16

FORWARD_ORDER = (0, 1, 2)
BACK_ORDER = (2, 0, 1)


def params(megabytes=56):
    return pltpu.CompilerParams(vmem_limit_bytes=megabytes * 1024 * 1024)


def takes(microseconds):
    return pl.CostEstimate(flops=1, bytes_accessed=int(microseconds * 3.0e6), transcendentals=0)


def tied(after):
    return [pl.BlockSpec(memory_space=pl.ANY)] * len(after)


def trig(first, second, length):
    angle = (np.outer(first, second) % length) * (2.0 * math.pi / length)
    return np.cos(angle), np.sin(angle)


def y_tables(blocks):
    cosine, sine = trig(np.arange(HALF_Y), np.arange(Y), Y)
    both = np.stack([cosine.reshape(blocks, -1, Y), sine.reshape(blocks, -1, Y)], 1).reshape(Y, Y)
    both = both.astype(ml_dtypes.bfloat16)
    return both, np.ascontiguousarray(both.T)


def x_tables():
    cosine, sine = trig(np.arange(X), np.arange(HALF_X), X)
    both = np.concatenate([cosine, sine], 1).astype(ml_dtypes.bfloat16)
    return both, np.ascontiguousarray(both.T)


def slope_matrix(size):
    return ((np.eye(size, k=-1) - np.eye(size, k=1)) * 0.5).astype(ml_dtypes.bfloat16)


def combine(terms):
    total = None
    for factor, value in terms:
        if abs(factor) < 1e-12:
            continue
        if abs(factor - 1.0) < 1e-12:
            part = value
        elif abs(factor + 1.0) < 1e-12:
            part = -value
        else:
            part = value * factor
        total = part if total is None else total + part
    return total


def depth_forward(values):
    even = [values[0]] + [values[n] + values[Z - n] for n in range(1, 8)] + [values[8]]
    odd = [None] + [values[n] - values[Z - n] for n in range(1, 8)]
    even_sum = [even[n] + even[8 - n] for n in range(4)] + [even[4]]
    even_dif = [even[n] - even[8 - n] for n in range(4)]
    odd_sum = [None] + [odd[n] + odd[8 - n] for n in range(1, 4)] + [odd[4]]
    odd_dif = [None] + [odd[n] - odd[8 - n] for n in range(1, 4)]
    result = []
    for k in range(KZ):
        folded = even_sum if k % 2 == 0 else even_dif
        cos_part = combine([(math.cos(math.pi * k * n / 8), folded[n]) for n in range(len(folded))])
        folded = odd_dif if k % 2 == 0 else odd_sum
        sin_part = combine(
            [(math.sin(math.pi * k * n / 8), folded[n]) for n in range(1, len(folded))]
        )
        result.append((cos_part, sin_part))
    return result


def depth_inverse(cos_parts, sin_parts):
    layers = [None] * Z
    cos_sum, sin_sum = [None] * 9, [None] * 9
    for n in range(5):
        evens = combine([(math.cos(math.pi * k * n / 8), cos_parts[k]) for k in range(0, KZ, 2)])
        odds = combine([(math.cos(math.pi * k * n / 8), cos_parts[k]) for k in range(1, KZ, 2)])
        if n == 4:
            cos_sum[4] = evens
        else:
            cos_sum[n] = evens + odds
            cos_sum[8 - n] = evens - odds
    for n in range(1, 5):
        evens = combine([(math.sin(math.pi * k * n / 8), sin_parts[k]) for k in range(0, KZ, 2)])
        odds = combine([(math.sin(math.pi * k * n / 8), sin_parts[k]) for k in range(1, KZ, 2)])
        if n == 4:
            sin_sum[4] = odds
        else:
            sin_sum[n] = odds + evens
            sin_sum[8 - n] = odds - evens
    layers[0], layers[8] = cos_sum[0], cos_sum[8]
    for n in range(1, 8):
        layers[n] = cos_sum[n] + sin_sum[n]
        layers[Z - n] = cos_sum[n] - sin_sum[n]
    return layers


ROWS = 96


def tiles(height, width):
    for row in range(0, height, 16):
        for column in range(0, width, 128):
            yield row, pl.ds(row, 16), pl.ds(column, 128)


def depth_forward_kernel(values_ref, planes_ref):
    _, _, height, width = values_ref.shape
    for _, rows, columns in tiles(height, width):
        spectrum = depth_forward([values_ref[0, n, rows, columns] for n in range(Z)])
        for k, (cos_part, sin_part) in enumerate(spectrum):
            planes_ref[2 * k, rows, columns] = cos_part.astype(bf16)
            if sin_part is None:
                sin_part = jnp.zeros_like(cos_part)
            planes_ref[2 * k + 1, rows, columns] = sin_part.astype(bf16)


def depth_transform(values, component, me=None, size_y=1, after=()):
    _, _, height, width = values.shape
    planes = Z // size_y
    shifted_out = me is not None

    def kernel(*refs):
        if not shifted_out:
            depth_forward_kernel(*refs)
            return
        me_ref, values_ref, outs, held = refs[0], refs[1], refs[2 + len(after) : -1], refs[-1]
        depth_forward_kernel(values_ref, held)
        for s, out in enumerate(outs):
            target = lax.rem(me_ref[0] + s, size_y)
            out[...] = held[pl.ds(target * planes, planes)]

    block = (Z // size_y, ROWS, width)
    out_spec = pl.BlockSpec(block, lambda j: (0, j, 0))
    out_shape = jax.ShapeDtypeStruct((planes, height, width), bf16)
    smem = pl.BlockSpec(memory_space=pltpu.SMEM)
    return pl.pallas_call(
        kernel,
        grid=(height // ROWS,),
        in_specs=([smem] if shifted_out else [])
        + [pl.BlockSpec((1, Z, ROWS, width), lambda j: (component, 0, j, 0))]
        + tied(after),
        out_specs=[out_spec] * size_y if shifted_out else out_spec,
        out_shape=[out_shape] * size_y if shifted_out else out_shape,
        scratch_shapes=[pltpu.VMEM((Z, ROWS, width), bf16)] if shifted_out else [],
        compiler_params=params(),
        cost_estimate=takes(3),
        name="depth_transform",
    )(*(([me] if shifted_out else []) + [values, *after]))


def fetch_blocks(table_ref, held, arrived, order):
    count, rows, _ = held.shape
    copies = []
    for s in range(count):
        place = pl.ds(pl.multiple_of(order(s) * rows, rows), rows)
        copies.append(pltpu.make_async_copy(table_ref.at[place], held.at[s], arrived.at[s]))
        copies[s].start()
    return copies


def y_transform(table, columns, blocks, halves, after):
    _, planes, _, width = columns.shape
    modes = HALF_Y // (blocks * halves)
    rows = Y // blocks

    def kernel(table_ref, columns_ref, *refs):
        out = refs[-1]
        for plane in range(planes):
            column = columns_ref[:, plane].reshape(Y, width)
            part = jnp.dot(table_ref[...], column, preferred_element_type=f32)
            out[0, :, plane] = part.astype(bf16).reshape(halves, 2, modes, width)

    return pl.pallas_call(
        kernel,
        grid=(blocks,),
        in_specs=[
            pl.BlockSpec((rows, Y), lambda j: (j, 0)),
            pl.BlockSpec(columns.shape, lambda j: (0, 0, 0, 0)),
        ]
        + tied(after),
        out_specs=pl.BlockSpec((1, halves, planes, 2, modes, width), lambda j: (j, 0, 0, 0, 0, 0)),
        out_shape=jax.ShapeDtypeStruct((blocks, halves, planes, 2, modes, width), bf16),
        compiler_params=params(24),
        cost_estimate=takes(4),
        name="y_transform",
    )(table, columns, *after)


def y_transform_parts(me, table, columns, blocks, halves, after):
    size_y = len(columns)
    planes, height, width = columns[0].shape[-3:]
    modes = HALF_Y // (blocks * halves)
    rows = Y // blocks
    shape = (blocks, halves, planes, 2, modes, width)

    def kernel(me_ref, table_ref, *refs):
        parts = refs[: len(columns)]
        out, held, lines, ready, table_in, lines_in, ready_out = refs[-7:]
        copies = []
        for s in range(size_y):
            source = lax.rem(me_ref[0] + size_y - s, size_y)
            place = pl.ds(pl.multiple_of(source * height, height), height)
            for plane in range(planes):
                copies.append(
                    pltpu.make_async_copy(
                        parts[s].at[plane],
                        lines.at[plane, place],
                        lines_in.at[s * planes + plane],
                    )
                )
                copies[-1].start()
        tables = fetch_blocks(table_ref, held, table_in, lambda s: s)
        for copy in copies:
            copy.wait()
        results = []
        for s in range(blocks):
            tables[s].wait()
            for plane in range(planes):
                part = jnp.dot(held[s], lines[plane], preferred_element_type=f32)
                ready[s, :, plane] = part.astype(bf16).reshape(halves, 2, modes, width)
            results.append(pltpu.make_async_copy(ready.at[s], out.at[s], ready_out.at[s]))
            results[s].start()
        for result in results:
            result.wait()

    anywhere = pl.BlockSpec(memory_space=pl.ANY)
    return pl.pallas_call(
        kernel,
        in_specs=[pl.BlockSpec(memory_space=pltpu.SMEM), anywhere]
        + [anywhere] * len(columns)
        + tied(after),
        out_specs=anywhere,
        out_shape=jax.ShapeDtypeStruct(shape, bf16),
        scratch_shapes=[
            pltpu.VMEM((blocks, rows, Y), bf16),
            pltpu.VMEM((planes, Y, width), bf16),
            pltpu.VMEM(shape, bf16),
            pltpu.SemaphoreType.DMA((blocks,)),
            pltpu.SemaphoreType.DMA((size_y * planes,)),
            pltpu.SemaphoreType.DMA((blocks,)),
        ],
        compiler_params=params(),
        cost_estimate=takes(5),
        name="y_transform_parts",
    )(me, table, *columns, *after)


def y_inverse(table, modes, size_y, after):
    planes, width = modes.shape[2], modes.shape[5]
    height = Y // size_y
    count = 384 // height

    def kernel(table_ref, modes_ref, *refs):
        out = refs[-1]
        for plane in range(planes):
            columns = modes_ref[:, :, plane].reshape(Y, width)
            rows = jnp.dot(table_ref[...], columns, preferred_element_type=f32)
            out[:, plane] = rows.astype(bf16).reshape(count, height, width)

    return pl.pallas_call(
        kernel,
        grid=(size_y // count,),
        in_specs=[
            pl.BlockSpec((count * height, Y), lambda j: (j, 0)),
            pl.BlockSpec(modes.shape, lambda j: (0, 0, 0, 0, 0, 0)),
        ]
        + tied(after),
        out_specs=pl.BlockSpec((count, planes, height, width), lambda j: (j, 0, 0, 0)),
        out_shape=jax.ShapeDtypeStruct((size_y, planes, height, width), bf16),
        compiler_params=params(24),
        cost_estimate=takes(4),
        name="y_inverse",
    )(table, modes, *after)


def y_inverse_parts(me, table, modes, size_y, after):
    blocks, halves, planes, _, count, width = modes.shape
    height = Y // size_y
    shape = (planes, height, width)

    def kernel(me_ref, table_ref, modes_ref, *refs):
        outs = refs[len(after) : -6]
        held, lines, ready, table_in, lines_in, ready_out = refs[-6:]
        copies = []
        for block in range(blocks):
            for h in range(halves):
                for plane in range(planes):
                    copies.append(
                        pltpu.make_async_copy(
                            modes_ref.at[block, h, plane],
                            lines.at[plane, block, h],
                            lines_in.at[(block * halves + h) * planes + plane],
                        )
                    )
                    copies[-1].start()
        tables = fetch_blocks(
            table_ref, held, table_in, lambda s: lax.rem(me_ref[0] + s, size_y)
        )
        for copy in copies:
            copy.wait()
        results = []
        for s in range(size_y):
            tables[s].wait()
            for plane in range(planes):
                columns = lines[plane].reshape(Y, width)
                rows = jnp.dot(held[s], columns, preferred_element_type=f32)
                ready[s, plane] = rows.astype(bf16)
            results.append(pltpu.make_async_copy(ready.at[s], outs[s], ready_out.at[s]))
            results[s].start()
        for result in results:
            result.wait()

    anywhere = pl.BlockSpec(memory_space=pl.ANY)
    out_shape = [jax.ShapeDtypeStruct(shape, bf16)] * size_y
    return pl.pallas_call(
        kernel,
        in_specs=[pl.BlockSpec(memory_space=pltpu.SMEM), anywhere, anywhere] + tied(after),
        out_specs=[anywhere] * len(out_shape),
        out_shape=out_shape,
        scratch_shapes=[
            pltpu.VMEM((size_y, height, Y), bf16),
            pltpu.VMEM((planes, blocks, halves, 2, count, width), bf16),
            pltpu.VMEM((size_y,) + shape, bf16),
            pltpu.SemaphoreType.DMA((size_y,)),
            pltpu.SemaphoreType.DMA((blocks * halves * planes,)),
            pltpu.SemaphoreType.DMA((size_y,)),
        ],
        compiler_params=params(),
        cost_estimate=takes(4),
        name="y_inverse_parts",
    )(me, table, modes, *after)


def x_transform(table, modes, after):
    blocks, _, _, count, width = modes.shape

    def kernel(table_ref, modes_ref, *refs):
        spectrum_ref = refs[-1]
        rows = jnp.concatenate(
            [modes_ref[block, 0].reshape(2 * count, width) for block in range(blocks)], axis=1
        )
        spectrum = jnp.dot(rows, table_ref[...], preferred_element_type=f32)
        spectrum_ref[0] = spectrum.reshape(2, count, X)

    return pl.pallas_call(
        kernel,
        grid=(2,),
        in_specs=[
            pl.BlockSpec((X, X), lambda j: (0, 0)),
            pl.BlockSpec((blocks, 1, 2, count, width), lambda j: (0, j, 0, 0, 0)),
        ]
        + tied(after),
        out_specs=pl.BlockSpec((1, 2, count, X), lambda j: (j, 0, 0, 0)),
        out_shape=jax.ShapeDtypeStruct((2, 2, count, X), f32),
        compiler_params=params(24),
        cost_estimate=takes(3),
        name="x_transform",
    )(table, modes, *after)


def turned(field, axis, tz, ty, tx, wave):
    index = [tz, ty, tx]
    sign = 1.0 if index[axis] == 0 else -1.0
    index[axis] = 1 - index[axis]
    value = field[index[0], index[1], :, index[2] * HALF_X : (index[2] + 1) * HALF_X]
    return value * (wave * sign)


CURL = {
    0: ((1, 2), (0, 1)),
    1: ((0, 0), (2, 2)),
    2: ((2, 1), (1, 0)),
}


def curl_kernel(axes, where_ref, table_ref, plus_ref, minus_ref, back_ref):
    blocks, _, _, count, width = back_ref.shape
    base = where_ref[0] + pl.program_id(0) * count
    depth = where_ref[1]
    mode_y = lax.broadcasted_iota(jnp.int32, (count, HALF_X), 0) + base
    mode_x = lax.broadcasted_iota(jnp.int32, (count, HALF_X), 1)
    wave_y = mode_y.astype(f32) * (2.0 * math.pi / Y)
    wave_x = mode_x.astype(f32) * (2.0 * math.pi / X)
    wave_z = jnp.full((count, HALF_X), depth, jnp.int32).astype(f32) * (2.0 * math.pi / Z)
    square = wave_x * wave_x + wave_y * wave_y + wave_z * wave_z
    doubling = (
        jnp.where(mode_x == 0, 1.0, 2.0)
        * jnp.where(mode_y == 0, 1.0, 2.0)
        * jnp.where(wave_z == 0.0, 1.0, 2.0)
    )
    weight = jnp.where(square > 0, doubling / jnp.where(square > 0, square, 1.0), 0.0)
    waves = [wave_z * weight, wave_y * weight, wave_x * weight]
    rows = []
    for tz in range(2):
        for ty in range(2):
            parts = []
            for tx in range(2):
                parts.append(
                    (
                        turned(plus_ref, axes[0], tz, ty, tx, waves[axes[0]])
                        - turned(minus_ref, axes[1], tz, ty, tx, waves[axes[1]])
                    ).astype(bf16)
                )
            rows.append(jnp.concatenate(parts, axis=1))
    rows = jnp.concatenate(rows, axis=0)
    back = jnp.dot(rows, table_ref[...], preferred_element_type=f32).astype(bf16)
    for block in range(blocks):
        back_ref[block] = back[:, block * width : (block + 1) * width].reshape(2, 2, count, width)


def curl_inverse(where, table, spectra, component, blocks, after):
    (plus_axis, plus), (minus_axis, minus) = CURL[component]
    total = spectra[plus].shape[2]
    width = X // blocks
    count = 96 if total % 96 == 0 else total
    spec = pl.BlockSpec((2, 2, count, X), lambda j: (0, 0, j, 0))

    def kernel(*refs):
        curl_kernel((plus_axis, minus_axis), *refs[:4], refs[-1])

    return pl.pallas_call(
        kernel,
        grid=(total // count,),
        in_specs=[
            pl.BlockSpec(memory_space=pltpu.SMEM),
            pl.BlockSpec((X, X), lambda j: (0, 0)),
            spec,
            spec,
        ]
        + tied(after),
        out_specs=pl.BlockSpec((blocks, 2, 2, count, width), lambda j: (0, 0, 0, j, 0)),
        out_shape=jax.ShapeDtypeStruct((blocks, 2, 2, total, width), bf16),
        compiler_params=params(24),
        cost_estimate=takes(4),
        name="curl_inverse",
    )(where, table, spectra[plus], spectra[minus], *after)


def side_columns(planes):
    width = planes[0].shape[1]
    row = lax.broadcasted_iota(jnp.int32, (2 * Z, width), 0)
    lane = lax.broadcasted_iota(jnp.int32, (2 * Z, width), 1)
    total = None
    for n in range(Z):
        pick = ((row == n) & (lane == 0)) | ((row == n + Z) & (lane == width - 1))
        part = lax.dot_general(
            pick.astype(f32).astype(bf16),
            planes[n],
            (((1,), (1,)), ((), ())),
            preferred_element_type=f32,
        )
        total = part if total is None else total + part
    return total[:Z].astype(bf16), total[Z:].astype(bf16)


def spread_columns(low, high, first, layers, width):
    row = lax.broadcasted_iota(jnp.int32, (2 * Z, layers * width), 0)
    column = lax.broadcasted_iota(jnp.int32, (2 * Z, layers * width), 1)
    place = jnp.zeros((2 * Z, layers * width), f32)
    for n in range(layers):
        place = place + jnp.where((row == first + n) & (column == n * width), -0.5, 0.0)
        place = place + jnp.where(
            (row == first + n + Z) & (column == (n + 1) * width - 1), 0.5, 0.0
        )
    both = jnp.concatenate([low, high], axis=0).astype(bf16)
    spread = lax.dot_general(
        both, place.astype(bf16), (((0,), (0,)), ((), ())), preferred_element_type=f32
    )
    return [spread[:, n * width : (n + 1) * width] for n in range(layers)]


def edges_kernel(field_ref, *refs):
    first_column_ref, last_column_ref = refs[-2:]
    first, last = side_columns([field_ref[0, n] for n in range(Z)])
    first_column_ref[0] = first
    last_column_ref[0] = last


def edge_columns(field, components, after):
    _, _, height, width = field.shape
    shape = jax.ShapeDtypeStruct((components, Z, height), bf16)
    spec = pl.BlockSpec((1, Z, height), lambda i: (i, 0, 0))
    return pl.pallas_call(
        edges_kernel,
        grid=(components,),
        in_specs=[pl.BlockSpec((1, Z, height, width), lambda i: (i, 0, 0, 0))] + tied(after),
        out_specs=[spec, spec],
        out_shape=[shape, shape],
        compiler_params=params(),
        cost_estimate=takes(4),
        name="edge_columns",
    )(field, *after)


def exchange(first, last, axis):
    count = lax.axis_size(axis)
    up = [(i, (i + 1) % count) for i in range(count)]
    down = [((i + 1) % count, i) for i in range(count)]
    return lax.ppermute(last, axis, up), lax.ppermute(first, axis, down)


def adjoint_kernel(planes_ref, cotangent_ref, *refs):
    adjoint_ref, short_ref, first_x, last_x, first_y, last_y, held = refs
    _, height, width = held.shape
    scale = 1.0 / (X * Y * Z)
    base = pl.program_id(0) * ROWS
    for row, rows, columns in tiles(ROWS, width):
        place = pl.ds(pl.multiple_of(base + row, 16), 16)
        layers = depth_inverse(
            [planes_ref[2 * k, rows, columns].astype(f32) for k in range(KZ)],
            [planes_ref[2 * k + 1, rows, columns].astype(f32) for k in range(KZ)],
        )
        for n in range(Z):
            value = cotangent_ref[0, n, rows, columns] + layers[n] * scale
            adjoint_ref[n, rows, columns] = value
            short_ref[n, rows, columns] = value.astype(bf16)
            held[n, place, columns] = value.astype(bf16)

    @pl.when(pl.program_id(0) == pl.num_programs(0) - 1)
    def _():
        first, last = side_columns([held[n] for n in range(Z)])
        first_x[0] = first
        last_x[0] = last
        top = [held[n, 0:16, :].astype(f32)[0:1] for n in range(Z)]
        bottom = [held[n, height - 16 : height, :].astype(f32)[15:16] for n in range(Z)]
        first_y[0] = jnp.concatenate(top, 0).astype(bf16)
        last_y[0] = jnp.concatenate(bottom, 0).astype(bf16)


def make_adjoint(me, parts, cotangent, component, edges, after):
    whole = len(parts) == 1
    planes, height, width = parts[0].shape
    column = jax.ShapeDtypeStruct((3, Z, height), bf16)
    row = jax.ShapeDtypeStruct((3, Z, width), bf16)
    column_spec = pl.BlockSpec((1, Z, height), lambda j: (component, 0, 0))
    row_spec = pl.BlockSpec((1, Z, width), lambda j: (component, 0, 0))
    first_edge = 2 + len(parts)

    def kernel(me_ref, *refs):
        part_refs, cotangent_ref = refs[: len(parts)], refs[len(parts)]
        outs, held, spectrum = refs[-8:-2], refs[-2], refs[-1]
        if whole:
            spectrum = part_refs[0]
        else:
            for s, part in enumerate(part_refs):
                source = lax.rem(me_ref[0] + len(parts) - s, len(parts))
                spectrum[pl.ds(source * planes, planes)] = part[...]
        adjoint_kernel(spectrum, cotangent_ref, *outs, held)

    return pl.pallas_call(
        kernel,
        grid=(height // ROWS,),
        in_specs=[pl.BlockSpec(memory_space=pltpu.SMEM)]
        + [pl.BlockSpec((planes, ROWS, width), lambda j: (0, j, 0))] * len(parts)
        + [pl.BlockSpec((1, Z, ROWS, width), lambda j: (component, 0, j, 0))]
        + tied(edges)
        + tied(after),
        out_specs=[
            pl.BlockSpec((Z, ROWS, width), lambda j: (0, j, 0)),
            pl.BlockSpec((Z, ROWS, width), lambda j: (0, j, 0)),
            column_spec,
            column_spec,
            row_spec,
            row_spec,
        ],
        out_shape=[
            jax.ShapeDtypeStruct((Z, height, width), f32),
            jax.ShapeDtypeStruct((Z, height, width), bf16),
            column,
            column,
            row,
            row,
        ],
        input_output_aliases={first_edge + n: 2 + n for n in range(len(edges))},
        scratch_shapes=[
            pltpu.VMEM((Z, height, width), bf16),
            pltpu.VMEM((Z, ROWS, width), bf16),
        ],
        compiler_params=params(),
        cost_estimate=takes(5),
        name="make_adjoint",
    )(me, *parts, cotangent, *edges, *after)


def pick_row(rows, n):
    index = lax.broadcasted_iota(jnp.int32, rows.shape, 0)
    return jnp.sum(jnp.where(index == n, rows.astype(f32), 0.0), axis=0, keepdims=True)


def with_end_rows(slope, low, high):
    height, width = slope.shape
    row = lax.broadcasted_iota(jnp.int32, (8, width), 0)
    top = slope[:8] - jnp.where(row == 0, low, 0.0)
    bottom = slope[height - 8 :] + jnp.where(row == 7, high, 0.0)
    return jnp.concatenate([top, slope[8 : height - 8], bottom], axis=0)


LAYERS = 8


def grad_vort_kernel(
    component,
    slope_x,
    slope_y,
    velocity,
    velocity_above,
    velocity_below,
    adjoint,
    low_x,
    high_x,
    low_y,
    high_y,
    *refs,
):
    before, after = refs
    height, width = velocity.shape[2], velocity.shape[3]
    factor = 0.5 * step_size
    first = pl.program_id(0) * LAYERS
    ends = spread_columns(
        low_x[0].astype(f32) * step_size, high_x[0].astype(f32) * step_size, first, LAYERS, width
    )
    layers = velocity[0]
    stacked = layers.reshape(LAYERS * height, width)
    deep = [velocity_below[0, 0]] + [layers[k] for k in range(LAYERS)] + [velocity_above[0, 0]]
    inner = jnp.dot(stacked, slope_x[...], preferred_element_type=f32)
    for k in range(LAYERS):
        n = first + k
        value = adjoint[k]
        along_x = inner[k * height : (k + 1) * height] + ends[k]
        along_y = jnp.dot(slope_y[...], layers[k], preferred_element_type=f32)
        along_y = with_end_rows(
            along_y, pick_row(low_y[0], n) * factor, pick_row(high_y[0], n) * factor
        )
        along_z = (deep[k + 2].astype(f32) - deep[k].astype(f32)) * factor
        for j, slope in enumerate((along_x, along_y, along_z)):
            term = value * slope
            if j == component:
                term = term + value
            if before is not None:
                term = before[j, k].astype(f32) + term
            after[j, k] = term.astype(after.dtype)


def add_grad_vort(component, slopes, velocity, adjoint, halos, before, after, kind):
    _, _, height, width = velocity.shape
    slope_x, slope_y = slopes
    whole = lambda shape: pl.BlockSpec(shape, lambda n: (0,) * len(shape))
    column = pl.BlockSpec((1, Z, height), lambda n: (component, 0, 0))
    row = pl.BlockSpec((1, Z, width), lambda n: (component, 0, 0))
    sums = pl.BlockSpec((3, LAYERS, height, width), lambda n: (0, n, 0, 0))
    layer_above = lambda n: lax.rem((n + 1) * LAYERS, Z)
    layer_below = lambda n: lax.rem(n * LAYERS + Z - 1, Z)
    operands = [slope_x, slope_y, velocity, velocity, velocity, adjoint, *halos]
    in_specs = [
        whole((width, width)),
        whole((height, height)),
        pl.BlockSpec((1, LAYERS, height, width), lambda n: (component, n, 0, 0)),
        pl.BlockSpec((1, 1, height, width), lambda n: (component, layer_above(n), 0, 0)),
        pl.BlockSpec((1, 1, height, width), lambda n: (component, layer_below(n), 0, 0)),
        pl.BlockSpec((LAYERS, height, width), lambda n: (n, 0, 0)),
        column,
        column,
        row,
        row,
    ]
    if before is not None:
        operands.append(before)
        in_specs.append(sums)

    def kernel(*refs):
        grad_vort_kernel(component, *refs[:10], None if before is None else refs[10], refs[-1])

    return pl.pallas_call(
        kernel,
        grid=(Z // LAYERS,),
        in_specs=in_specs + tied(after),
        out_specs=sums,
        out_shape=jax.ShapeDtypeStruct((3, Z, height, width), kind),
        compiler_params=params(),
        cost_estimate=takes(9),
        name="add_grad_vort",
    )(*operands, *after)


def grad_vel_kernel(
    count, slope_x, slope_y, vorticity, vorticity_above, vorticity_below, *refs
):
    adjoints, edges = refs[: 3 * count], refs[3 * count :]
    vort_low_x, vort_high_x, vort_low_y, vort_high_y, low_x, high_x, low_y, high_y = edges[:8]
    after = refs[-1]
    _, _, height, width = vorticity.shape
    first = pl.program_id(0) * LAYERS
    factor = -0.5 * step_size

    def times(one, other):
        return one.astype(f32) * other.astype(f32)

    for c in range(count):
        here, above, below = adjoints[3 * c : 3 * c + 3]
        ends = spread_columns(
            times(vort_low_x[0], low_x[c]) * -step_size,
            times(vort_high_x[0], high_x[c]) * -step_size,
            first,
            LAYERS,
            width,
        )
        deep = [times(vorticity_below[0, 0], below[0])]
        along_x = []
        along_y = []
        for k in range(LAYERS):
            value = here[k].astype(f32)
            along_x.append((vorticity[0, k].astype(f32) * value).astype(bf16))
            along_y.append((vorticity[1, k].astype(f32) * value).astype(bf16))
            deep.append(vorticity[2, k].astype(f32) * value)
        deep.append(times(vorticity_above[0, 0], above[0]))
        along_x = jnp.dot(
            jnp.concatenate(along_x, axis=0), slope_x[...], preferred_element_type=f32
        )
        for k in range(LAYERS):
            n = first + k
            total = jnp.dot(slope_y[...], along_y[k], preferred_element_type=f32)
            total = total + along_x[k * height : (k + 1) * height] + ends[k]
            after[c, k] = total + (deep[k + 2] - deep[k]) * factor
            low = pick_row(vort_low_y[0], n) * pick_row(low_y[c], n)
            high = pick_row(vort_high_y[0], n) * pick_row(high_y[c], n)
            after[c, k, 0:1, :] = after[c, k, 0:1, :] - low * factor
            after[c, k, height - 1 : height, :] = (
                after[c, k, height - 1 : height, :] + high * factor
            )


def write_grad_vel(slopes, vorticity, adjoints, saved_halos, halos, after):
    _, _, height, width = vorticity.shape
    count = len(adjoints)
    whole = lambda shape: pl.BlockSpec(shape, lambda n: (0,) * len(shape))
    saved_column = pl.BlockSpec((1, Z, height), lambda n: (3, 0, 0))
    saved_row = pl.BlockSpec((1, Z, width), lambda n: (3, 0, 0))
    layer_above = lambda n: lax.rem((n + 1) * LAYERS, Z)
    layer_below = lambda n: lax.rem(n * LAYERS + Z - 1, Z)
    operands = [*slopes, vorticity, vorticity, vorticity]
    in_specs = [
        whole((width, width)),
        whole((height, height)),
        pl.BlockSpec((3, LAYERS, height, width), lambda n: (0, n, 0, 0)),
        pl.BlockSpec((1, 1, height, width), lambda n: (2, layer_above(n), 0, 0)),
        pl.BlockSpec((1, 1, height, width), lambda n: (2, layer_below(n), 0, 0)),
    ]
    for adjoint in adjoints:
        operands = operands + [adjoint] * 3
        in_specs = in_specs + [
            pl.BlockSpec((LAYERS, height, width), lambda n: (n, 0, 0)),
            pl.BlockSpec((1, height, width), lambda n: (layer_above(n), 0, 0)),
            pl.BlockSpec((1, height, width), lambda n: (layer_below(n), 0, 0)),
        ]
    operands = operands + list(saved_halos) + list(halos)
    in_specs = in_specs + [saved_column, saved_column, saved_row, saved_row]
    in_specs = in_specs + [whole((count, Z, height))] * 2 + [whole((count, Z, width))] * 2

    def kernel(*refs):
        grad_vel_kernel(count, *refs)

    return pl.pallas_call(
        kernel,
        grid=(Z // LAYERS,),
        in_specs=in_specs + tied(after),
        out_specs=pl.BlockSpec((count, LAYERS, height, width), lambda n: (0, n, 0, 0)),
        out_shape=jax.ShapeDtypeStruct((count, Z, height, width), f32),
        compiler_params=params(),
        cost_estimate=takes(12),
        name="write_grad_vel",
    )(*operands, *after)


def pair_exchange(parts, axis, mine):
    count = lax.axis_size(axis)
    kept = lax.dynamic_index_in_dim(parts, mine, 1, keepdims=False)
    sent = lax.dynamic_index_in_dim(parts, 1 - mine, 1, keepdims=False)
    got = lax.ppermute(sent, axis, [(i, i ^ 1) for i in range(count)])
    return jnp.where(mine == 0, jnp.stack([kept, got], 1), jnp.stack([got, kept], 1))


def shifted(parts, axis):
    count = lax.axis_size(axis)
    return [parts[0]] + [
        lax.ppermute(parts[s], axis, [(i, (i + s) % count) for i in range(count)])
        for s in range(1, count)
    ]


def local(cot_vort, cot_vel, vorticity, velocity):
    size_x = lax.axis_size("gx")
    size_y = lax.axis_size("gy")
    planes = Z // size_y
    halves = size_y // KZ
    _, _, height, width = cot_vel.shape
    modes = HALF_Y // (size_x * halves)
    place_x = lax.axis_index("gx")
    place_y = lax.axis_index("gy")
    half = lax.rem(place_y, halves)
    me = place_y.astype(jnp.int32).reshape(1)
    where = jnp.stack([(place_x * halves + half) * modes, place_y // halves]).astype(jnp.int32)

    y_table, y_back_table = y_tables(size_x * halves)
    x_table, x_back_table = x_tables()
    slopes = [slope_matrix(width), np.ascontiguousarray(slope_matrix(height).T)]
    slopes = [(slope * np.float32(step_size)).astype(slope.dtype) for slope in slopes]

    layers = depth_transform(cot_vel, FORWARD_ORDER[0])

    velocity_first, velocity_last = edge_columns(velocity, 3, (layers,))
    vorticity_first, vorticity_last = edge_columns(vorticity, 1, (layers,))
    low_x, high_x = exchange(
        jnp.concatenate([velocity_first, vorticity_first]),
        jnp.concatenate([velocity_last, vorticity_last]),
        "gx",
    )
    low_y, high_y = exchange(
        jnp.concatenate([velocity[:, :, 0], vorticity[1:2, :, 0]]),
        jnp.concatenate([velocity[:, :, height - 1], vorticity[1:2, :, height - 1]]),
        "gy",
    )
    saved_halos = (low_x, high_x, low_y, high_y)
    early = ((low_x, high_x), (low_y, high_y), ())

    columns = layers.reshape(size_y, planes, height, width)
    columns = lax.all_to_all(columns, "gy", 0, 0, tiled=True)
    sent = []
    for place in range(3):
        if place > 0:
            layers = depth_transform(cot_vel, FORWARD_ORDER[place], me, size_y, (sent[-1],))
            columns = shifted(layers, "gy")
        if place == 0:
            parts = y_transform(y_table, columns, size_x, halves, early[place])
        else:
            parts = y_transform_parts(me, y_table, columns, size_x, halves, early[place])
        parts = parts.reshape(size_x, 2, 2, modes, width)
        sent.append(parts if halves == 1 else pair_exchange(parts, "gy", half))

    def spectrum(place, after):
        lines = lax.all_to_all(sent[place], "gx", 0, 0, tiled=True)
        return x_transform(x_table, lines, after)

    third = shifted(
        [
            lax.dynamic_index_in_dim(sent[2], lax.rem(place_x + s, size_x), 0, keepdims=False)
            for s in range(size_x)
        ],
        "gx",
    )
    sources = lax.rem(place_x + size_x - jnp.arange(size_x), size_x)
    third_lines = jnp.take(jnp.stack(third), sources, axis=0)

    def curl(component, after):
        return curl_inverse(where, x_back_table, spectra, component, size_x, after)

    def back(filtered):
        parts = lax.all_to_all(filtered, "gx", 0, 0, tiled=True)
        if halves == 2:
            parts = pair_exchange(parts, "gy", half)
        return parts.reshape(size_x, halves, planes, 2, modes, width)

    def rows_of(component, modes_back, after):
        if component == BACK_ORDER[2]:
            return [y_inverse(y_back_table, modes_back, size_y, after)]
        return y_inverse_parts(me, y_back_table, modes_back, size_y, after)

    def layers_of(rows):
        if len(rows) == 1:
            return [lax.all_to_all(rows[0], "gy", 0, 0, tiled=True).reshape(Z, height, width)]
        return shifted(rows, "gy")

    one, two, three = BACK_ORDER
    spectra = {FORWARD_ORDER[0]: spectrum(0, (sent[1],))}
    spectra[FORWARD_ORDER[1]] = spectrum(1, (third[size_x // 2],))
    curl_one = curl(one, ())
    spectra[FORWARD_ORDER[2]] = x_transform(x_table, third_lines, (curl_one,))
    curl_two = curl(two, ())
    rows_one = rows_of(one, back(curl_one), (curl_two,))
    layers_one = layers_of(rows_one)
    curl_three = curl(three, tuple(layers_one))

    def vort_of(component, adjoint, before, after):
        kind = f32 if component == three else bf16
        return add_grad_vort(
            component, slopes, velocity, adjoint, saved_halos, before, after, kind
        )

    adjoint_one, short_one, *edges = make_adjoint(me, layers_one, cot_vort, one, [], ())
    rows_two = rows_of(two, back(curl_two), (adjoint_one,))
    layers_two = layers_of(rows_two)
    rows_three = rows_of(three, back(curl_three), tuple(layers_two))
    grad_vort = vort_of(one, adjoint_one, None, (rows_two[0],))
    adjoint_two, short_two, *edges = make_adjoint(
        me, layers_two, cot_vort, two, edges, (rows_three[0],)
    )
    grad_vort = vort_of(two, adjoint_two, grad_vort, ())
    adjoint_three, short_three, *edges = make_adjoint(
        me, layers_of(rows_three), cot_vort, three, edges, (grad_vort,)
    )
    halos = exchange(edges[0], edges[1], "gx") + exchange(edges[2], edges[3], "gy")
    grad_vort = vort_of(three, adjoint_three, grad_vort, ())
    shorts = {one: short_one, two: short_two, three: short_three}
    grad_vel = write_grad_vel(
        [-slope for slope in slopes], vorticity, [shorts[i] for i in range(3)], saved_halos, halos, (grad_vort,)
    )
    return grad_vort, grad_vel


def solution(mesh):
    spec = P(None, None, "gy", "gx")
    return jax.shard_map(
        local,
        mesh=mesh,
        in_specs=(spec, spec, spec, spec),
        out_specs=(spec, spec),
        check_vma=False,
    )
```
